32 devices in a mesh: lon: 16 (over z, y, core), lat: 2 (over x).
Axes of the slice: x: 2, y: 2, z: 4, core: 2. Of those that a mesh axis runs over, the one named last changes fastest.
Arguments:
- field_in: bfloat16 [4, 24, 36864], P(None, 'lat', 'lon'), may hold values from -6 to 6
- norm1_gain: float32 [192], replicated, may hold values from 0.25 to 1.75
- qkv_weight: bfloat16 [192, 576], replicated, may hold values from -0.4375 to 0.4375
- proj_weight: bfloat16 [192, 192], replicated, may hold values from -0.4375 to 0.4375
- earth_bias: float32 [4, 2, 6, 20736], P('lat'), may hold values from -4 to 320, as said below
- norm2_gain: float32 [192], replicated, may hold values from 0.25 to 1.75
- fc1_weight: bfloat16 [192, 768], replicated, may hold values from -0.4375 to 0.4375
- fc2_weight: bfloat16 [768, 192], replicated, may hold values from -0.21875 to 0.21875
Outputs:
- block_out: bfloat16 [4, 24, 36864], P(None, 'lat', 'lon')
The draws below stay inside these ranges and needn't reach their ends.
Inputs may be any that keep to these rules, and one draw needn't show every extreme that they name: `earth_bias`: bias table entries.
All inputs are finite; a program needn't handle non-finite values.
Results may differ from the reference program's by a relative error of at most 0.014.
Values may be sent and summed in bfloat16 or wider, within the bound.
No kernel may reach another device: no remote copies, remote signals or barrier semaphores. Data moves between devices by JAX's collectives and lax.ppermute only.
A program may use at most 128 MiB of HBM per device.

```python
import jax
import jax.numpy as jnp
from jax import lax

C = 192
HEADS = 6
MLP_UNITS = 768
WIN_LEV = 2
WIN_LAT = 6
WIN_LON = 12
PAIRS = 20736
LEVELS = 4
LAT = 24
LON = 192
NLATW = 4
ZWIN = 2


def draw_earth_bias(key, part):
    shape = (NLATW, ZWIN, HEADS, PAIRS)
    keys = jax.random.split(jax.random.fold_in(key, 7), 1)
    base = jnp.clip(jax.random.normal(keys[0], shape, jnp.float32), -4.0, 4.0)
    return base


def block_levels(stream_key, extent, cuts, low, high):
    level = 1.0
    for axis_at, blocks in cuts:
        heights = jax.random.uniform(jax.random.fold_in(jax.random.fold_in(stream_key, 6), axis_at), (blocks,), jnp.float32, low / len(cuts), high / len(cuts))
        level = level * jnp.repeat(jnp.exp(heights), extent[axis_at] // blocks).reshape((-1,) + (1,) * (len(extent) - 1 - axis_at))
    return level


def gaussian(rng, shape, scale, most, pieces=(), kind=jnp.bfloat16):
    loudness = block_levels(rng, shape, pieces, -0.22, 0.18) if pieces else 1.0
    drawn = jax.random.normal(rng, shape, jnp.float32) * scale * loudness
    return jnp.minimum(jnp.maximum(drawn, -most), most).astype(kind)


def setup_inputs(seed: int = 0) -> dict:
    streams_of = jax.random.split(jax.random.key(seed), 9)
    field_in = gaussian(streams_of[0], (LEVELS, LAT, LON * C), 1.0, 6.0, ((1, 2), (2, 16)))
    norm1_gain = jnp.clip(1.0 + 0.15 * jax.random.normal(streams_of[1], (C,), jnp.float32), 0.25, 1.75)
    qkv_weight = gaussian(streams_of[2], (C, 3 * C), C ** -0.5, 0.4375)
    proj_weight = gaussian(streams_of[3], (C, C), C ** -0.5, 0.4375)
    earth_bias = draw_earth_bias(jax.random.fold_in(streams_of[8], 71), 0)
    norm2_gain = jnp.clip(1.0 + 0.15 * jax.random.normal(streams_of[5], (C,), jnp.float32), 0.25, 1.75)
    fc1_weight = gaussian(streams_of[6], (C, MLP_UNITS), C ** -0.5, 0.4375)
    fc2_weight = gaussian(streams_of[7], (MLP_UNITS, C), MLP_UNITS ** -0.5, 0.21875)
    return dict(field_in=field_in, norm1_gain=norm1_gain, qkv_weight=qkv_weight, proj_weight=proj_weight, earth_bias=earth_bias, norm2_gain=norm2_gain, fc1_weight=fc1_weight, fc2_weight=fc2_weight)


def row_regions(orig, total, padded):
    tail = 4 if padded else 2
    edge = WIN_LAT // 2
    return jnp.where(orig < 0, 3, jnp.where(orig < edge, 2, jnp.where(orig < total - edge, 0, jnp.where(orig < total, 1, tail))))

def level_regions(levels):
    place = jnp.arange(levels)
    return jnp.where(place < levels - 2, 0, jnp.where(place == levels - 2, 1, 2))

def layer_norm(values, gain):
    center = values - lax.optimization_barrier(jnp.mean(values, axis=-1, keepdims=True))
    spread = lax.optimization_barrier(jnp.mean(center * center, axis=-1, keepdims=True))
    return center * lax.rsqrt(spread + 1e-05) * gain.astype(jnp.float32)

def attend(tile, gain, qkv_weight, proj_weight, bias_types, level_lab, row_lab):
    levels, rows, flat = tile.shape
    chans = qkv_weight.shape[0]
    cols = flat // chans
    heads = bias_types.shape[2]
    head_dim = chans // heads
    zwin = levels // WIN_LEV
    rwin = rows // WIN_LAT
    cwin = cols // WIN_LON
    tokens = WIN_LEV * WIN_LAT * WIN_LON
    grid = tile.reshape(zwin, WIN_LEV, rwin, WIN_LAT, cwin, WIN_LON, chans)
    windows = grid.transpose(0, 2, 4, 1, 3, 5, 6).reshape(-1, chans)
    normed = layer_norm(windows.astype(jnp.float32), gain).astype(jnp.bfloat16)
    qkv = jnp.dot(normed, qkv_weight, preferred_element_type=jnp.float32).astype(jnp.bfloat16)
    qkv = lax.optimization_barrier(qkv).astype(jnp.float32)
    qkv = qkv.reshape(zwin, rwin, cwin, tokens, 3, heads, head_dim)
    query = qkv[:, :, :, :, 0]
    keys = qkv[:, :, :, :, 1]
    values = qkv[:, :, :, :, 2]
    scores = jnp.einsum('abcqhd,abckhd->bachqk', query, keys) * head_dim ** (-0.5)
    table = bias_types.reshape(rwin, zwin, heads, tokens, tokens)
    scores = scores + table[:, :, None]
    zlab = level_lab.reshape(zwin, WIN_LEV)
    rlab = row_lab.reshape(rwin, WIN_LAT)
    label = zlab[None, :, :, None, None] * 8 + rlab[:, None, None, :, None] + jnp.zeros((1, 1, 1, 1, WIN_LON), jnp.int32)
    label = label.reshape(rwin, zwin, tokens)
    allowed = label[:, :, :, None] == label[:, :, None, :]
    scores = jnp.where(allowed[:, :, None, None], scores, -1000000000.0)
    probs = jax.nn.softmax(scores, axis=-1).astype(jnp.bfloat16)
    probs = lax.optimization_barrier(probs).astype(jnp.float32)
    mixed = jnp.einsum('bachqk,abckhd->abcqhd', probs, values).astype(jnp.bfloat16).reshape(-1, chans)
    proj = jnp.dot(mixed, proj_weight, preferred_element_type=jnp.float32).astype(jnp.bfloat16)
    back = proj.reshape(zwin, rwin, cwin, WIN_LEV, WIN_LAT, WIN_LON, chans).transpose(0, 3, 1, 4, 2, 5, 6)
    return back.reshape(levels, rows, flat)

def finish(tile, attn, gain, fc1_weight, fc2_weight):
    chans = fc1_weight.shape[0]
    resid = (tile.astype(jnp.float32) + attn.astype(jnp.float32)).astype(jnp.bfloat16)
    resid = lax.optimization_barrier(resid).reshape(-1, chans)
    normed = layer_norm(resid.astype(jnp.float32), gain).astype(jnp.bfloat16)
    hidden = jax.nn.gelu(jnp.dot(normed, fc1_weight, preferred_element_type=jnp.float32)).astype(jnp.bfloat16)
    result = resid.astype(jnp.float32) + jnp.dot(hidden, fc2_weight, preferred_element_type=jnp.float32)
    return result.astype(jnp.bfloat16).reshape(tile.shape)

def reference(field_in, norm1_gain, qkv_weight, proj_weight, earth_bias, norm2_gain, fc1_weight, fc2_weight):
    shift_lanes = WIN_LON // 2 * C
    rolled = jnp.roll(field_in, (-1, -(WIN_LAT // 2), -shift_lanes), axis=(0, 1, 2))
    level_lab = level_regions(LEVELS)
    row_lab = row_regions((jnp.arange(LAT) + WIN_LAT // 2) % LAT, LAT, False).reshape(NLATW, WIN_LAT)
    blocks = rolled.reshape(LEVELS, NLATW, WIN_LAT, LON * C).transpose(1, 0, 2, 3)

    def one_block(items):
        block, table, labels = items
        attn = attend(block, norm1_gain, qkv_weight, proj_weight, table[None], level_lab, labels)
        return finish(block, attn, norm2_gain, fc1_weight, fc2_weight)
    done = lax.map(one_block, (blocks, earth_bias, row_lab))
    done = done.transpose(1, 0, 2, 3).reshape(LEVELS, LAT, LON * C)
    return jnp.roll(done, (1, WIN_LAT // 2, shift_lanes), axis=(0, 1, 2))
```

```python
import functools

import jax
import jax.numpy as jnp
from jax import lax
from jax.experimental import pallas as pl
from jax.experimental.pallas import tpu as pltpu
from jax.sharding import PartitionSpec as P

LEVELS = 4
WIN_LEV = 2
WIN_LAT = 6
WIN_LON = 12
EDGE = WIN_LAT // 2
HALF = WIN_LON // 2
TOKENS = WIN_LEV * WIN_LAT * WIN_LON
QUERIES = TOKENS // 2
LOG2E = 1.4426950408889634
LANES = 128
SPARE = 64
NT = (((1,), (1,)), ((), ()))


def moved(x, lat_by, lon_by):
    lats, lons = lax.axis_size("lat"), lax.axis_size("lon")
    if lat_by == 0:
        return lax.ppermute(x, "lon", [(i, (i + lon_by) % lons) for i in range(lons)])
    if lon_by == 0:
        return lax.ppermute(x, "lat", [(i, (i + lat_by) % lats) for i in range(lats)])
    pairs = [
        (b * lats + a, (b + lon_by) % lons * lats + (a + lat_by) % lats)
        for b in range(lons)
        for a in range(lats)
    ]
    return lax.ppermute(x, ("lon", "lat"), pairs)


def table_kernel(last_ref, bias_ref, table_ref):
    heads = bias_ref.shape[2]
    width = 9 * LANES
    lane = lax.broadcasted_iota(jnp.int32, (1, LANES), 1)
    last = jnp.where(last_ref[0] > 0, -1e9, 0.0).astype(jnp.float32)

    def penalty(first, lev, side, wrap):
        key = lane + first
        key_lev = (key >= QUERIES).astype(jnp.int32)
        key_side = ((key - key_lev * QUERIES) >= QUERIES // 2).astype(jnp.int32)
        out = jnp.zeros((1, LANES), jnp.float32)
        if lev is not None:
            out = jnp.where(key_lev != lev, -1e9, out)
        if wrap:
            out = out + jnp.where(key_side != side, last, 0.0)
        return out

    for k in range(2):
        for p in range(2):
            masks = {}
            for lev in range(2):
                for side in range(2):
                    masks[lev, side] = [
                        penalty(first, lev if p == 1 else None, side, k == 1)
                        for first in (0, LANES)
                    ]
            for c in range(TOKENS // 8):
                tiles = [
                    bias_ref[k, p, :, c * width + u * LANES : c * width + (u + 1) * LANES]
                    for u in range(9)
                ]
                for r in range(8):
                    i = 8 * c + r
                    shift = 16 * r
                    nxt = tiles[r + 1]
                    main = tiles[r]
                    if r:
                        main = pltpu.roll(main, LANES - shift, 1)
                        nxt = pltpu.roll(nxt, LANES - shift, 1)
                        main = jnp.where(lane < LANES - shift, main, nxt)
                    lev = i // QUERIES
                    row = i % QUERIES // WIN_LON
                    col = i % WIN_LON
                    side = col // HALF
                    place = lev * 36 + row * HALF + col % HALF
                    mask = masks[lev, row // EDGE]
                    at = pl.ds(place, heads, stride=QUERIES)
                    table_ref[k, p, 1 - side, 0, at, :] = main * LOG2E + mask[0]
                    table_ref[k, p, 1 - side, 1, at, :] = nxt * LOG2E + mask[1]


def layer_norm(values, gain):
    center = values - jnp.mean(values, axis=-1, keepdims=True)
    spread = jnp.mean(center * center, axis=-1, keepdims=True)
    return center * lax.rsqrt(spread + 1e-05) * gain


def block_kernel(
    chans,
    heads,
    own_a,
    own_b,
    west_a,
    west_b,
    east_a,
    east_b,
    gain1_ref,
    wq_ref,
    wk_ref,
    wv_ref,
    proj_ref,
    table_ref,
    gain2_ref,
    fc1_ref,
    fc2_ref,
    out_ref,
    keys_ref,
    own_ref,
    res_ref,
):
    head_dim = chans // heads
    low = lax.broadcasted_iota(jnp.int32, (1, LANES), 1) < SPARE

    def tokens_of(ref, side, first, count):
        both = [ref[side, part, first : first + count] for part in range(2)]
        return jnp.concatenate([both[0], both[1][:, : chans - LANES]], axis=1)

    def fill(ref, row, col, cols):
        for pair in range(cols // 2):
            both = ref[row, :, pair * 2 * chans : (pair + 1) * 2 * chans].astype(jnp.float32)
            first, middle, final = (both[:, u * LANES : (u + 1) * LANES] for u in range(3))
            yield col + 2 * pair, (first, middle)
            middle, final = pltpu.roll(middle, SPARE, 1), pltpu.roll(final, SPARE, 1)
            yield col + 2 * pair + 1, (jnp.where(low, middle, final), final)

    for row in range(WIN_LAT):
        own, west, east = ((own_a, west_a, east_a), (own_b, west_b, east_b))[row // EDGE]
        r = row % EDGE
        blocks = list(fill(west, r, 0, HALF)) + list(fill(own, r, HALF, WIN_LON))
        blocks += list(fill(east, r, HALF + WIN_LON, HALF))
        for col, block in blocks:
            side = col // WIN_LON
            for part in range(2):
                at = pl.ds(row * WIN_LON + col % WIN_LON, LEVELS, stride=QUERIES)
                keys_ref[side, part, at, :] = block[part]
            mine = col - HALF
            if 0 <= mine < WIN_LON:
                side = mine // HALF
                place = row * HALF + mine % HALF
                for part in range(2):
                    own_ref[side, part, pl.ds(4 + place, LEVELS, stride=36), :] = block[part]
                    own_ref[side, part, pl.ds(148 + place, 1), :] = block[part][:1]

    gain1 = gain1_ref[...]
    lane = lax.broadcasted_iota(jnp.int32, (1, chans), 1)
    ones = (lax.broadcasted_iota(jnp.int32, (1, 2 * LANES), 1) == chans).astype(jnp.float32)
    mixed = []
    for side in range(2):
        normed = layer_norm(tokens_of(keys_ref, side, 0, LEVELS * QUERIES), gain1)
        normed = jnp.concatenate([normed[QUERIES:], normed[:QUERIES]], axis=0)
        normed = normed.astype(jnp.bfloat16)
        keys = jnp.dot(normed, wk_ref[...], preferred_element_type=jnp.float32)
        values = jnp.dot(normed, wv_ref[...], preferred_element_type=jnp.float32) + ones
        own = layer_norm(tokens_of(own_ref, side, 40, 144), gain1).astype(jnp.bfloat16)
        query = jnp.dot(own, wq_ref[...], preferred_element_type=jnp.float32)
        query = query * (head_dim ** (-0.5) * LOG2E)
        for p in range(2):
            q = query[p * QUERIES : (p + 1) * QUERIES]
            k = keys[p * TOKENS : (p + 1) * TOKENS].astype(jnp.bfloat16)
            v = values[p * TOKENS : (p + 1) * TOKENS].astype(jnp.bfloat16)
            picked = [
                jnp.where((lane >= h * head_dim) & (lane < (h + 1) * head_dim), q, 0.0)
                for h in range(heads)
            ]
            picked = jnp.concatenate(picked, axis=0).astype(jnp.bfloat16)
            scores = lax.dot_general(picked, k, NT, preferred_element_type=jnp.float32)
            bias = table_ref[0, p, side]
            scores = scores + jnp.concatenate([bias[0], bias[1, :, : TOKENS - LANES]], axis=1)
            top = jnp.max(scores, axis=1, keepdims=True)
            probs = jnp.exp2(scores - top).astype(jnp.bfloat16)
            got = jnp.dot(probs, v, preferred_element_type=jnp.float32)
            out = jnp.zeros((QUERIES, chans), jnp.float32)
            for h in range(heads):
                part = got[h * QUERIES : (h + 1) * QUERIES]
                scaled = part[:, :chans] * (1.0 / part[:, chans : chans + 1])
                inside = (lane >= h * head_dim) & (lane < (h + 1) * head_dim)
                out = jnp.where(inside, scaled, out)
            mixed.append(out)
    mixed = jnp.concatenate(mixed, axis=0).astype(jnp.bfloat16)
    attn = jnp.dot(mixed, proj_ref[...], preferred_element_type=jnp.float32)
    attn = attn.astype(jnp.bfloat16).astype(jnp.float32)
    resid = jnp.concatenate([tokens_of(own_ref, side, 40, 144) for side in range(2)], axis=0) + attn
    resid = resid.astype(jnp.bfloat16).astype(jnp.float32)
    normed = layer_norm(resid, gain2_ref[...]).astype(jnp.bfloat16)
    hidden = jnp.dot(normed, fc1_ref[...], preferred_element_type=jnp.float32)
    hidden = jax.nn.gelu(hidden).astype(jnp.bfloat16)
    result = resid + jnp.dot(hidden, fc2_ref[...], preferred_element_type=jnp.float32)
    for side in range(2):
        mine = result[side * 144 : (side + 1) * 144]
        for part, lanes in enumerate((slice(0, LANES), slice(LANES, chans))):
            width = min(LANES, chans - part * LANES)
            res_ref[side, part, 40:184, :width] = mine[:, lanes]
            res_ref[side, part, 0:40, :width] = mine[104:144, lanes]
    for row in range(WIN_LAT):
        for pair in range(WIN_LON // 2):
            tiles = []
            for col in (2 * pair, 2 * pair + 1):
                at = pl.ds(4 + row * HALF + col % HALF, LEVELS, stride=36)
                tiles += [res_ref[col // HALF, part, at, :] for part in range(2)]
            shifted = [pltpu.roll(x, SPARE, 1) for x in tiles[2:]]
            tiles = [tiles[0], jnp.where(low, tiles[1], shifted[0])]
            tiles.append(jnp.where(low, shifted[0], shifted[1]))
            tiles = jnp.concatenate(tiles, axis=1).astype(jnp.bfloat16)
            out_ref[row, :, pair * 2 * chans : (pair + 1) * 2 * chans] = tiles


def rows_of(ref_rows, at):
    shape = (EDGE,) + ref_rows.shape[1:]
    return pl.BlockSpec(shape, lambda _: (at, 0, 0))


def whole(x):
    return pl.BlockSpec(x.shape, lambda _: (0,) * x.ndim)


def run_block(pieces, table, at, weights, chans, heads):
    arrays = [x for x, _ in pieces]
    specs = [rows_of(x, where) for x, where in pieces]
    gain1, wq, wk, wv, proj, gain2, fc1, fc2 = weights
    table_spec = pl.BlockSpec((1,) + table.shape[1:], lambda _: (at, 0, 0, 0, 0, 0))
    before, after = (gain1, wq, wk, wv, proj), (gain2, fc1, fc2)
    out = jax.ShapeDtypeStruct((WIN_LAT,) + arrays[0].shape[1:], jnp.bfloat16)
    return pl.pallas_call(
        functools.partial(block_kernel, chans, heads),
        out_shape=out,
        grid=(1,),
        in_specs=specs + [whole(x) for x in before] + [table_spec] + [whole(x) for x in after],
        out_specs=whole(out),
        scratch_shapes=[
            pltpu.VMEM((2, 2, LEVELS * QUERIES, LANES), jnp.float32),
            pltpu.VMEM((2, 2, 184, LANES), jnp.float32),
            pltpu.VMEM((2, 2, 184, LANES), jnp.float32),
        ],
        compiler_params=pltpu.CompilerParams(vmem_limit_bytes=40 * 2**20),
        cost_estimate=pl.CostEstimate(flops=400_000_000, bytes_accessed=3_000_000, transcendentals=500_000),
        name="swin_rows",
    )(*arrays, *before, table, *after)


def shards(
    field_in, norm1_gain, qkv_weight, proj_weight, earth_bias, norm2_gain, fc1_weight, fc2_weight
):
    levels, rows, flat = field_in.shape
    chans = qkv_weight.shape[0]
    heads = earth_bias.shape[2]
    half = HALF * chans
    field = jnp.transpose(field_in, (1, 0, 2))
    east = moved(field[EDGE:, :, :half], 0, -1)
    west = moved(field[EDGE:, :, half:], 0, 1)
    south = moved(field[:EDGE], -1, 0)
    south_east = moved(field[:EDGE, :, :half], -1, -1)
    south_west = moved(field[:EDGE, :, half:], -1, 1)
    last = (lax.axis_index("lat") == lax.axis_size("lat") - 1).astype(jnp.int32).reshape(1)
    windows = rows // WIN_LAT
    table = pl.pallas_call(
        table_kernel,
        out_shape=jax.ShapeDtypeStruct((windows, 2, 2, 2, heads * QUERIES, LANES), jnp.float32),
        in_specs=[
            pl.BlockSpec(memory_space=pltpu.SMEM),
            pl.BlockSpec(memory_space=pltpu.VMEM),
        ],
        out_specs=pl.BlockSpec(memory_space=pltpu.VMEM),
        compiler_params=pltpu.CompilerParams(vmem_limit_bytes=40 * 2**20),
        cost_estimate=pl.CostEstimate(flops=4_000_000, bytes_accessed=6_000_000, transcendentals=0),
        name="bias_tables",
    )(last, earth_bias)
    wq = qkv_weight[:, :chans]
    wk = qkv_weight[:, chans : 2 * chans]
    wv = jnp.pad(qkv_weight[:, 2 * chans :], ((0, 0), (0, 2 * LANES - chans)))
    weights = (
        norm1_gain.reshape(1, chans),
        wq,
        wk,
        wv,
        proj_weight,
        norm2_gain.reshape(1, chans),
        fc1_weight,
        fc2_weight,
    )
    straddle = [(field, 3), (south, 0), (west, 2), (south_west, 0), (east, 2), (south_east, 0)]
    lower = run_block(straddle, table, 1, weights, chans, heads)
    top = moved(lower[EDGE:], 1, 0)
    inner = [(field, 1), (field, 2), (west, 0), (west, 1), (east, 0), (east, 1)]
    upper = run_block(inner, table, 0, weights, chans, heads)
    done = jnp.concatenate([top, upper, lower[:EDGE]], axis=0)
    return jnp.transpose(done, (1, 0, 2))


def solution(mesh):
    in_specs = (P(None, "lat", "lon"), P(), P(), P(), P("lat", None, None, None), P(), P(), P())
    out_specs = P(None, "lat", "lon")
    return jax.shard_map(shards, mesh=mesh, in_specs=in_specs, out_specs=out_specs, check_vma=False)
```

```python
import functools

import jax
import jax.numpy as jnp
from jax import lax
from jax.experimental import pallas as pl
from jax.experimental.pallas import tpu as pltpu
from jax.sharding import PartitionSpec as P

LEVELS = 4
WIN_LEV = 2
WIN_LAT = 6
WIN_LON = 12
EDGE = WIN_LAT // 2
HALF = WIN_LON // 2
TOKENS = WIN_LEV * WIN_LAT * WIN_LON
QUERIES = TOKENS // 2
LOG2E = 1.4426950408889634
LANES = 128
SPARE = 64
NT = (((1,), (1,)), ((), ()))


def moved(x, axis, by):
    size = lax.axis_size(axis)
    return lax.ppermute(x, axis, [(i, (i + by) % size) for i in range(size)])


def swapped(x, axis, first):
    size = lax.axis_size(axis)
    pairs = []
    for i in range(first, size, 2):
        j = (i + 1) % size
        pairs += [(i, j), (j, i)]
    return lax.ppermute(x, axis, pairs)


def table_kernel(last_ref, bias_ref, table_ref):
    heads = bias_ref.shape[2]
    width = 9 * LANES
    lane = lax.broadcasted_iota(jnp.int32, (1, LANES), 1)
    last = jnp.where(last_ref[0] > 0, -1e9, 0.0).astype(jnp.float32)

    def penalty(first, lev, side, wrap):
        key = lane + first
        key_lev = (key >= QUERIES).astype(jnp.int32)
        key_side = ((key - key_lev * QUERIES) >= QUERIES // 2).astype(jnp.int32)
        out = jnp.zeros((1, LANES), jnp.float32)
        if lev is not None:
            out = jnp.where(key_lev != lev, -1e9, out)
        if wrap:
            out = out + jnp.where(key_side != side, last, 0.0)
        return out

    for k in range(2):
        for p in range(2):
            masks = {}
            for lev in range(2):
                for side in range(2):
                    masks[lev, side] = [
                        penalty(first, lev if p == 1 else None, side, k == 1)
                        for first in (0, LANES)
                    ]
            for c in range(TOKENS // 8):
                tiles = [
                    bias_ref[k, p, :, c * width + u * LANES : c * width + (u + 1) * LANES]
                    for u in range(9)
                ]
                for r in range(8):
                    i = 8 * c + r
                    shift = 16 * r
                    nxt = tiles[r + 1]
                    main = tiles[r]
                    if r:
                        main = pltpu.roll(main, LANES - shift, 1)
                        nxt = pltpu.roll(nxt, LANES - shift, 1)
                        main = jnp.where(lane < LANES - shift, main, nxt)
                    lev = i // QUERIES
                    row = i % QUERIES // WIN_LON
                    col = i % WIN_LON
                    side = col // HALF
                    place = lev * 36 + row * HALF + col % HALF
                    mask = masks[lev, row // EDGE]
                    at = pl.ds(place, heads, stride=QUERIES)
                    table_ref[k, p, 1 - side, 0, at, :] = main * LOG2E + mask[0]
                    table_ref[k, p, 1 - side, 1, at, :] = nxt * LOG2E + mask[1]


def layer_norm(values, gain):
    center = values - jnp.mean(values, axis=-1, keepdims=True)
    spread = jnp.mean(center * center, axis=-1, keepdims=True)
    return center * lax.rsqrt(spread + 1e-05) * gain


def side_kernel(
    chans,
    heads,
    windows,
    right_ref,
    own_piece,
    halo_piece,
    gain1_ref,
    qkv_ref,
    proj_ref,
    table_ref,
    gain2_ref,
    fc1_ref,
    fc2_ref,
    out_ref,
    keys_ref,
    own_ref,
    res_ref,
):
    head_dim = chans // heads
    low = lax.broadcasted_iota(jnp.int32, (1, LANES), 1) < SPARE
    right = right_ref[0]
    halo_at = right * HALF
    own_at = HALF - halo_at

    def tokens_of(ref, at, first, count):
        both = [ref[at, part, first : first + count] for part in range(2)]
        return jnp.concatenate([both[0], both[1][:, : chans - LANES]], axis=1)

    def split(ref, row):
        for pair in range(HALF // 2):
            both = ref[row, :, pair * 2 * chans : (pair + 1) * 2 * chans].astype(jnp.float32)
            first, middle, final = (both[:, u * LANES : (u + 1) * LANES] for u in range(3))
            yield 2 * pair, (first, middle)
            middle, final = pltpu.roll(middle, SPARE, 1), pltpu.roll(final, SPARE, 1)
            yield 2 * pair + 1, (jnp.where(low, middle, final), final)

    for n in range(len(windows)):
        for row in range(WIN_LAT):
            for col, block in split(halo_piece, n * WIN_LAT + row):
                at = pl.ds(row * WIN_LON + col + halo_at, LEVELS, stride=QUERIES)
                for part in range(2):
                    keys_ref[n, part, at, :] = block[part]
            for col, block in split(own_piece, n * WIN_LAT + row):
                at = pl.ds(row * WIN_LON + col + own_at, LEVELS, stride=QUERIES)
                place = row * HALF + col
                for part in range(2):
                    keys_ref[n, part, at, :] = block[part]
                    own_ref[n, part, pl.ds(4 + place, LEVELS, stride=36), :] = block[part]
                    own_ref[n, part, pl.ds(148 + place, 1), :] = block[part][:1]

    gain1 = gain1_ref[...]
    lane = lax.broadcasted_iota(jnp.int32, (1, chans), 1)
    ones = jnp.ones((LEVELS * QUERIES, 2 * LANES - chans), jnp.float32)
    mixed = []
    for n in range(len(windows)):
        normed = layer_norm(tokens_of(keys_ref, n, 0, LEVELS * QUERIES), gain1)
        normed = jnp.concatenate([normed[QUERIES:], normed[:QUERIES]], axis=0)
        normed = normed.astype(jnp.bfloat16)
        keys = jnp.dot(normed, qkv_ref[:, chans : 2 * chans], preferred_element_type=jnp.float32)
        values = jnp.dot(normed, qkv_ref[:, 2 * chans :], preferred_element_type=jnp.float32)
        values = jnp.concatenate([values, ones], axis=1)
        own = layer_norm(tokens_of(own_ref, n, 40, 144), gain1).astype(jnp.bfloat16)
        query = jnp.dot(own, qkv_ref[:, :chans], preferred_element_type=jnp.float32)
        query = query * (head_dim ** (-0.5) * LOG2E)
        for p in range(2):
            q = query[p * QUERIES : (p + 1) * QUERIES]
            k = keys[p * TOKENS : (p + 1) * TOKENS].astype(jnp.bfloat16)
            v = values[p * TOKENS : (p + 1) * TOKENS].astype(jnp.bfloat16)
            picked = [
                jnp.where((lane >= h * head_dim) & (lane < (h + 1) * head_dim), q, 0.0)
                for h in range(heads)
            ]
            picked = jnp.concatenate(picked, axis=0).astype(jnp.bfloat16)
            scores = lax.dot_general(picked, k, NT, preferred_element_type=jnp.float32)
            table = [table_ref[windows[n], p, right, part] for part in range(2)]
            table = jnp.concatenate([table[0], table[1][:, : TOKENS - LANES]], axis=1)
            scores = scores + table
            top = jnp.max(scores, axis=1, keepdims=True)
            probs = jnp.exp2(scores - top).astype(jnp.bfloat16)
            got = jnp.dot(probs, v, preferred_element_type=jnp.float32)
            out = jnp.zeros((QUERIES, chans), jnp.float32)
            for h in range(heads):
                part = got[h * QUERIES : (h + 1) * QUERIES]
                scaled = part[:, :chans] * (1.0 / part[:, chans : chans + 1])
                inside = (lane >= h * head_dim) & (lane < (h + 1) * head_dim)
                out = jnp.where(inside, scaled, out)
            mixed.append(out)
    mixed = jnp.concatenate(mixed, axis=0).astype(jnp.bfloat16)
    attn = jnp.dot(mixed, proj_ref[...], preferred_element_type=jnp.float32)
    attn = attn.astype(jnp.bfloat16).astype(jnp.float32)
    tokens = [tokens_of(own_ref, n, 40, 144) for n in range(len(windows))]
    resid = jnp.concatenate(tokens, axis=0) + attn
    resid = resid.astype(jnp.bfloat16).astype(jnp.float32)
    normed = layer_norm(resid, gain2_ref[...]).astype(jnp.bfloat16)
    hidden = jnp.dot(normed, fc1_ref[...], preferred_element_type=jnp.float32)
    hidden = jax.nn.gelu(hidden).astype(jnp.bfloat16)
    result = lax.dot_general(hidden, fc2_ref[...], NT, preferred_element_type=jnp.float32)
    result = resid + result
    for n in range(len(windows)):
        mine = result[n * 144 : (n + 1) * 144]
        for part, lanes in enumerate((slice(0, LANES), slice(LANES, chans))):
            width = min(LANES, chans - part * LANES)
            res_ref[n, part, 40:184, :width] = mine[:, lanes]
            res_ref[n, part, 0:40, :width] = mine[104:144, lanes]
        for row in range(WIN_LAT):
            for pair in range(HALF // 2):
                tiles = []
                for col in (2 * pair, 2 * pair + 1):
                    at = pl.ds(4 + row * HALF + col, LEVELS, stride=36)
                    tiles += [res_ref[n, part, at, :] for part in range(2)]
                shifted = [pltpu.roll(x, SPARE, 1) for x in tiles[2:]]
                tiles = [tiles[0], jnp.where(low, tiles[1], shifted[0])]
                tiles.append(jnp.where(low, shifted[0], shifted[1]))
                tiles = jnp.concatenate(tiles, axis=1).astype(jnp.bfloat16)
                out_ref[n * WIN_LAT + row, :, pair * 2 * chans : (pair + 1) * 2 * chans] = tiles


def run_side(right, own, halo, table, windows, weights, chans, heads):
    count = len(windows)
    first = windows[0]
    assert list(windows) == list(range(first, first + count)) and first % count == 0
    rows = count * WIN_LAT
    piece = pl.BlockSpec((rows,) + own.shape[1:], lambda _: (first // count, 0, 0))

    def whole(x):
        return pl.BlockSpec(x.shape, lambda _: (0,) * len(x.shape))

    out = jax.ShapeDtypeStruct((rows,) + own.shape[1:], jnp.bfloat16)
    gain1, qkv, proj, gain2, fc1, fc2 = weights
    return pl.pallas_call(
        functools.partial(side_kernel, chans, heads, windows),
        out_shape=out,
        grid=(1,),
        in_specs=[pl.BlockSpec(memory_space=pltpu.SMEM), piece, piece]
        + [whole(x) for x in (gain1, qkv, proj, table, gain2, fc1, fc2)],
        out_specs=whole(out),
        scratch_shapes=[
            pltpu.VMEM((count, 2, LEVELS * QUERIES, LANES), jnp.float32),
            pltpu.VMEM((count, 2, 184, LANES), jnp.float32),
            pltpu.VMEM((count, 2, 184, LANES), jnp.float32),
        ],
        compiler_params=pltpu.CompilerParams(vmem_limit_bytes=32 * 2**20),
        cost_estimate=pl.CostEstimate(
            flops=200_000_000 * count, bytes_accessed=3_000_000, transcendentals=250_000 * count
        ),
        name="swin_side",
    )(right, own, halo, gain1, qkv, proj, table, gain2, fc1, fc2)


def shards(
    field_in, norm1_gain, qkv_weight, proj_weight, earth_bias, norm2_gain, fc1_weight, fc2_weight
):
    levels, rows, flat = field_in.shape
    chans = qkv_weight.shape[0]
    heads = earth_bias.shape[2]
    half = HALF * chans
    field = jnp.transpose(field_in, (1, 0, 2))
    south = moved(field[:EDGE], "lat", -1)
    odd = lax.axis_index("lon") % 2
    last = (lax.axis_index("lat") == lax.axis_size("lat") - 1).astype(jnp.int32).reshape(1)
    table = pl.pallas_call(
        table_kernel,
        out_shape=jax.ShapeDtypeStruct((2, 2, 2, 2, heads * QUERIES, LANES), jnp.float32),
        in_specs=[
            pl.BlockSpec(memory_space=pltpu.SMEM),
            pl.BlockSpec(memory_space=pltpu.VMEM),
        ],
        out_specs=pl.BlockSpec(memory_space=pltpu.VMEM),
        compiler_params=pltpu.CompilerParams(vmem_limit_bytes=32 * 2**20),
        cost_estimate=pl.CostEstimate(flops=4_000_000, bytes_accessed=6_000_000, transcendentals=0),
        name="bias_tables",
    )(last, earth_bias)
    tokens = jnp.concatenate([field[EDGE:], south], axis=0)
    left, right = tokens[:, :, :half], tokens[:, :, half:]
    near = jnp.where(odd == 1, left, right)
    far = jnp.where(odd == 1, right, left)
    far_halo = swapped(far, "lon", 1)
    near_halo = swapped(near, "lon", 0)
    weights = (
        norm1_gain.reshape(1, chans),
        qkv_weight,
        proj_weight,
        norm2_gain.reshape(1, chans),
        fc1_weight,
        jnp.transpose(fc2_weight),
    )
    near_right, far_right = (1 - odd).reshape(1), odd.reshape(1)
    near_done = run_side(near_right, near, near_halo, table, (0, 1), weights, chans, heads)
    far_low = run_side(far_right, far, far_halo, table, (1,), weights, chans, heads)
    top = moved(jnp.stack([near_done[WIN_LAT + EDGE :], far_low[EDGE:]]), "lat", 1)
    far_high = run_side(far_right, far, far_halo, table, (0,), weights, chans, heads)
    near_all = jnp.concatenate([top[0], near_done[: WIN_LAT + EDGE]], axis=0)
    far_all = jnp.concatenate([top[1], far_high, far_low[:EDGE]], axis=0)
    done = jnp.where(
        odd == 1,
        jnp.concatenate([near_all, far_all], axis=2),
        jnp.concatenate([far_all, near_all], axis=2),
    )
    return jnp.transpose(done, (1, 0, 2))


def solution(mesh):
    in_specs = (P(None, "lat", "lon"), P(), P(), P(), P("lat", None, None, None), P(), P(), P())
    out_specs = P(None, "lat", "lon")
    return jax.shard_map(shards, mesh=mesh, in_specs=in_specs, out_specs=out_specs, check_vma=False)
```

```python
import functools

import jax
import jax.numpy as jnp
from jax import lax
from jax.experimental import pallas as pl
from jax.experimental.pallas import tpu as pltpu
from jax.sharding import PartitionSpec as P

LEVELS = 4
WIN_LEV = 2
WIN_LAT = 6
WIN_LON = 12
EDGE = WIN_LAT // 2
HALF = WIN_LON // 2
TOKENS = WIN_LEV * WIN_LAT * WIN_LON
QUERIES = TOKENS // 2
LOG2E = 1.4426950408889634
LANES = 128
SPARE = 64
NT = (((1,), (1,)), ((), ()))


def moved(x, axis, by):
    size = lax.axis_size(axis)
    return lax.ppermute(x, axis, [(i, (i + by) % size) for i in range(size)])


def swapped(x, axis, first):
    size = lax.axis_size(axis)
    pairs = []
    for i in range(first, size, 2):
        j = (i + 1) % size
        pairs += [(i, j), (j, i)]
    return lax.ppermute(x, axis, pairs)


def table_kernel(last_ref, bias_ref, field_ref, table_ref, kept_ref):
    kept_ref[...] = field_ref[EDGE:]
    heads = bias_ref.shape[2]
    width = 9 * LANES
    lane = lax.broadcasted_iota(jnp.int32, (1, LANES), 1)
    last = jnp.where(last_ref[0] > 0, -1e9, 0.0).astype(jnp.float32)

    def penalty(first, lev, side, wrap):
        key = lane + first
        key_lev = (key >= QUERIES).astype(jnp.int32)
        key_side = ((key - key_lev * QUERIES) >= QUERIES // 2).astype(jnp.int32)
        out = jnp.zeros((1, LANES), jnp.float32)
        if lev is not None:
            out = jnp.where(key_lev != lev, -1e9, out)
        if wrap:
            out = out + jnp.where(key_side != side, last, 0.0)
        return out

    for k in range(2):
        for p in range(2):
            masks = {}
            for lev in range(2):
                for side in range(2):
                    masks[lev, side] = [
                        penalty(first, lev if p == 1 else None, side, k == 1)
                        for first in (0, LANES)
                    ]
            for c in range(TOKENS // 8):
                tiles = [
                    bias_ref[k, p, :, c * width + u * LANES : c * width + (u + 1) * LANES]
                    for u in range(9)
                ]
                for r in range(8):
                    i = 8 * c + r
                    shift = 16 * r
                    nxt = tiles[r + 1]
                    main = tiles[r]
                    if r:
                        main = pltpu.roll(main, LANES - shift, 1)
                        nxt = pltpu.roll(nxt, LANES - shift, 1)
                        main = jnp.where(lane < LANES - shift, main, nxt)
                    lev = i // QUERIES
                    row = i % QUERIES // WIN_LON
                    col = i % WIN_LON
                    side = col // HALF
                    place = lev * 36 + row * HALF + col % HALF
                    mask = masks[lev, row // EDGE]
                    at = pl.ds(place, heads, stride=QUERIES)
                    table_ref[k, p, 1 - side, 0, at, :] = main * LOG2E + mask[0]
                    table_ref[k, p, 1 - side, 1, at, :] = nxt * LOG2E + mask[1]


def layer_norm(values, gain):
    center = values - jnp.mean(values, axis=-1, keepdims=True)
    spread = jnp.mean(center * center, axis=-1, keepdims=True)
    return center * lax.rsqrt(spread + 1e-05) * gain


def side_kernel(
    chans,
    heads,
    windows,
    right_ref,
    own_piece,
    halo_piece,
    gain1_ref,
    qkv_ref,
    proj_ref,
    table_ref,
    gain2_ref,
    fc1_ref,
    fc2_ref,
    out_ref,
    keys_ref,
    own_ref,
    res_ref,
):
    head_dim = chans // heads
    low = lax.broadcasted_iota(jnp.int32, (1, LANES), 1) < SPARE
    right = right_ref[0]
    halo_at = right * HALF
    own_at = HALF - halo_at

    def tokens_of(ref, at, first, count):
        both = [ref[at, part, first : first + count] for part in range(2)]
        return jnp.concatenate([both[0], both[1][:, : chans - LANES]], axis=1)

    def split(ref, row):
        for pair in range(HALF // 2):
            both = ref[row, :, pair * 2 * chans : (pair + 1) * 2 * chans].astype(jnp.float32)
            first, middle, final = (both[:, u * LANES : (u + 1) * LANES] for u in range(3))
            yield 2 * pair, (first, middle)
            middle, final = pltpu.roll(middle, SPARE, 1), pltpu.roll(final, SPARE, 1)
            yield 2 * pair + 1, (jnp.where(low, middle, final), final)

    for n in range(len(windows)):
        for row in range(WIN_LAT):
            for col, block in split(halo_piece, windows[n] * WIN_LAT + row):
                at = pl.ds(row * WIN_LON + col + halo_at, LEVELS, stride=QUERIES)
                for part in range(2):
                    keys_ref[n, part, at, :] = block[part]
            for col, block in split(own_piece, windows[n] * WIN_LAT + row):
                at = pl.ds(row * WIN_LON + col + own_at, LEVELS, stride=QUERIES)
                place = row * HALF + col
                for part in range(2):
                    keys_ref[n, part, at, :] = block[part]
                    own_ref[n, part, pl.ds(4 + place, LEVELS, stride=36), :] = block[part]
                    own_ref[n, part, pl.ds(148 + place, 1), :] = block[part][:1]

    gain1 = gain1_ref[...]
    lane = lax.broadcasted_iota(jnp.int32, (1, chans), 1)
    ones = jnp.ones((LEVELS * QUERIES, 2 * LANES - chans), jnp.float32)
    mixed = []
    for n in range(len(windows)):
        normed = layer_norm(tokens_of(keys_ref, n, 0, LEVELS * QUERIES), gain1)
        normed = jnp.concatenate([normed[QUERIES:], normed[:QUERIES]], axis=0)
        normed = normed.astype(jnp.bfloat16)
        keys = jnp.dot(normed, qkv_ref[:, chans : 2 * chans], preferred_element_type=jnp.float32)
        values = jnp.dot(normed, qkv_ref[:, 2 * chans :], preferred_element_type=jnp.float32)
        values = jnp.concatenate([values, ones], axis=1)
        own = layer_norm(tokens_of(own_ref, n, 40, 144), gain1).astype(jnp.bfloat16)
        query = jnp.dot(own, qkv_ref[:, :chans], preferred_element_type=jnp.float32)
        query = query * (head_dim ** (-0.5) * LOG2E)
        for p in range(2):
            q = query[p * QUERIES : (p + 1) * QUERIES]
            k = keys[p * TOKENS : (p + 1) * TOKENS].astype(jnp.bfloat16)
            v = values[p * TOKENS : (p + 1) * TOKENS].astype(jnp.bfloat16)
            picked = [
                jnp.where((lane >= h * head_dim) & (lane < (h + 1) * head_dim), q, 0.0)
                for h in range(heads)
            ]
            picked = jnp.concatenate(picked, axis=0).astype(jnp.bfloat16)
            scores = lax.dot_general(picked, k, NT, preferred_element_type=jnp.float32)
            table = [table_ref[windows[n], p, right, part] for part in range(2)]
            table = jnp.concatenate([table[0], table[1][:, : TOKENS - LANES]], axis=1)
            scores = scores + table
            top = jnp.max(scores, axis=1, keepdims=True)
            probs = jnp.exp2(scores - top).astype(jnp.bfloat16)
            got = jnp.dot(probs, v, preferred_element_type=jnp.float32)
            out = jnp.zeros((QUERIES, chans), jnp.float32)
            for h in range(heads):
                part = got[h * QUERIES : (h + 1) * QUERIES]
                scaled = part[:, :chans] * (1.0 / part[:, chans : chans + 1])
                inside = (lane >= h * head_dim) & (lane < (h + 1) * head_dim)
                out = jnp.where(inside, scaled, out)
            mixed.append(out)
    mixed = jnp.concatenate(mixed, axis=0).astype(jnp.bfloat16)
    attn = jnp.dot(mixed, proj_ref[...], preferred_element_type=jnp.float32)
    attn = attn.astype(jnp.bfloat16).astype(jnp.float32)
    tokens = [tokens_of(own_ref, n, 40, 144) for n in range(len(windows))]
    resid = jnp.concatenate(tokens, axis=0) + attn
    resid = resid.astype(jnp.bfloat16).astype(jnp.float32)
    normed = layer_norm(resid, gain2_ref[...]).astype(jnp.bfloat16)
    hidden = jnp.dot(normed, fc1_ref[...], preferred_element_type=jnp.float32)
    hidden = jax.nn.gelu(hidden).astype(jnp.bfloat16)
    result = lax.dot_general(hidden, fc2_ref[...], NT, preferred_element_type=jnp.float32)
    result = resid + result
    for n in range(len(windows)):
        mine = result[n * 144 : (n + 1) * 144]
        for part, lanes in enumerate((slice(0, LANES), slice(LANES, chans))):
            width = min(LANES, chans - part * LANES)
            res_ref[n, part, 40:184, :width] = mine[:, lanes]
            res_ref[n, part, 0:40, :width] = mine[104:144, lanes]
        for row in range(WIN_LAT):
            for pair in range(HALF // 2):
                tiles = []
                for col in (2 * pair, 2 * pair + 1):
                    at = pl.ds(4 + row * HALF + col, LEVELS, stride=36)
                    tiles += [res_ref[n, part, at, :] for part in range(2)]
                shifted = [pltpu.roll(x, SPARE, 1) for x in tiles[2:]]
                tiles = [tiles[0], jnp.where(low, tiles[1], shifted[0])]
                tiles.append(jnp.where(low, shifted[0], shifted[1]))
                tiles = jnp.concatenate(tiles, axis=1).astype(jnp.bfloat16)
                out_ref[n * WIN_LAT + row, :, pair * 2 * chans : (pair + 1) * 2 * chans] = tiles


def run_side(right, own, halo, table, windows, weights, chans, heads):
    count = len(windows)
    vmem = pl.BlockSpec(memory_space=pltpu.VMEM)
    out = jax.ShapeDtypeStruct((count * WIN_LAT,) + own.shape[1:], jnp.bfloat16)
    gain1, qkv, proj, gain2, fc1, fc2 = weights
    return pl.pallas_call(
        functools.partial(side_kernel, chans, heads, windows),
        out_shape=out,
        in_specs=[pl.BlockSpec(memory_space=pltpu.SMEM)] + [vmem] * 9,
        out_specs=vmem,
        scratch_shapes=[
            pltpu.VMEM((count, 2, LEVELS * QUERIES, LANES), jnp.float32),
            pltpu.VMEM((count, 2, 184, LANES), jnp.float32),
            pltpu.VMEM((count, 2, 184, LANES), jnp.float32),
        ],
        compiler_params=pltpu.CompilerParams(vmem_limit_bytes=32 * 2**20),
        cost_estimate=pl.CostEstimate(
            flops=200_000_000 * count, bytes_accessed=3_000_000, transcendentals=250_000 * count
        ),
        name="swin_side",
    )(right, own, halo, gain1, qkv, proj, table, gain2, fc1, fc2)


def shards(
    field_in, norm1_gain, qkv_weight, proj_weight, earth_bias, norm2_gain, fc1_weight, fc2_weight
):
    levels, rows, flat = field_in.shape
    chans = qkv_weight.shape[0]
    heads = earth_bias.shape[2]
    half = HALF * chans
    field = jnp.transpose(field_in, (1, 0, 2))
    south = moved(field[:EDGE], "lat", -1)
    odd = lax.axis_index("lon") % 2
    last = (lax.axis_index("lat") == lax.axis_size("lat") - 1).astype(jnp.int32).reshape(1)
    vmem = pl.BlockSpec(memory_space=pltpu.VMEM)
    table, kept = pl.pallas_call(
        table_kernel,
        out_shape=[
            jax.ShapeDtypeStruct((2, 2, 2, 2, heads * QUERIES, LANES), jnp.float32),
            jax.ShapeDtypeStruct((rows - EDGE, levels, flat), field.dtype),
        ],
        in_specs=[pl.BlockSpec(memory_space=pltpu.SMEM), vmem, vmem],
        out_specs=[vmem, vmem],
        compiler_params=pltpu.CompilerParams(vmem_limit_bytes=32 * 2**20),
        cost_estimate=pl.CostEstimate(flops=4_000_000, bytes_accessed=6_000_000, transcendentals=0),
        name="bias_tables",
    )(last, earth_bias, field)
    tokens = jnp.concatenate([kept, south], axis=0)
    left, right = tokens[:, :, :half], tokens[:, :, half:]
    near = jnp.where(odd == 1, left, right)
    far = jnp.where(odd == 1, right, left)
    far_halo = swapped(far, "lon", 1)
    near_halo = swapped(near, "lon", 0)
    weights = (
        norm1_gain.reshape(1, chans),
        qkv_weight,
        proj_weight,
        norm2_gain.reshape(1, chans),
        fc1_weight,
        jnp.transpose(fc2_weight),
    )
    near_right, far_right = (1 - odd).reshape(1), odd.reshape(1)
    near_done = run_side(near_right, near, near_halo, table, (0, 1), weights, chans, heads)
    far_halo, near_done = lax.optimization_barrier((far_halo, near_done))
    far_low = run_side(far_right, far, far_halo, table, (1,), weights, chans, heads)
    top = moved(jnp.stack([near_done[WIN_LAT + EDGE :], far_low[EDGE:]]), "lat", 1)
    far_high = run_side(far_right, far, far_halo, table, (0,), weights, chans, heads)
    near_all = jnp.concatenate([top[0], near_done[: WIN_LAT + EDGE]], axis=0)
    far_all = jnp.concatenate([top[1], far_high, far_low[:EDGE]], axis=0)
    done = jnp.where(
        odd == 1,
        jnp.concatenate([near_all, far_all], axis=2),
        jnp.concatenate([far_all, near_all], axis=2),
    )
    return jnp.transpose(done, (1, 0, 2))


def solution(mesh):
    in_specs = (P(None, "lat", "lon"), P(), P(), P(), P("lat", None, None, None), P(), P(), P())
    out_specs = P(None, "lat", "lon")
    return jax.shard_map(shards, mesh=mesh, in_specs=in_specs, out_specs=out_specs, check_vma=False)
```

```python
import functools

import jax
import jax.numpy as jnp
from jax import lax
from jax.experimental import pallas as pl
from jax.experimental.pallas import tpu as pltpu
from jax.sharding import PartitionSpec as P

LEVELS = 4
WIN_LEV = 2
WIN_LAT = 6
WIN_LON = 12
EDGE = WIN_LAT // 2
HALF = WIN_LON // 2
TOKENS = WIN_LEV * WIN_LAT * WIN_LON
QUERIES = TOKENS // 2
LOG2E = 1.4426950408889634
LANES = 128
SPARE = 64
NT = (((1,), (1,)), ((), ()))


def moved(x, axis, by):
    size = lax.axis_size(axis)
    return lax.ppermute(x, axis, [(i, (i + by) % size) for i in range(size)])


def swapped(x, axis, first):
    size = lax.axis_size(axis)
    pairs = []
    for i in range(first, size, 2):
        j = (i + 1) % size
        pairs += [(i, j), (j, i)]
    return lax.ppermute(x, axis, pairs)


def table_kernel(last_ref, bias_ref, field_ref, table_out, kept_ref, table_ref, sems):
    kept_ref[...] = field_ref[EDGE:]
    heads = bias_ref.shape[2]
    width = 9 * LANES
    lane = lax.broadcasted_iota(jnp.int32, (1, LANES), 1)
    last = jnp.where(last_ref[0] > 0, -1e9, 0.0).astype(jnp.float32)

    def penalty(first, lev, side, wrap):
        key = lane + first
        key_lev = (key >= QUERIES).astype(jnp.int32)
        key_side = ((key - key_lev * QUERIES) >= QUERIES // 2).astype(jnp.int32)
        out = jnp.zeros((1, LANES), jnp.float32)
        if lev is not None:
            out = jnp.where(key_lev != lev, -1e9, out)
        if wrap:
            out = out + jnp.where(key_side != side, last, 0.0)
        return out

    copies = []
    for k in range(2):
        for p in range(2):
            masks = {}
            for lev in range(2):
                for side in range(2):
                    masks[lev, side] = [
                        penalty(first, lev if p == 1 else None, side, k == 1)
                        for first in (0, LANES)
                    ]
            for c in range(TOKENS // 8):
                tiles = [
                    bias_ref[k, p, :, c * width + u * LANES : c * width + (u + 1) * LANES]
                    for u in range(9)
                ]
                for r in range(8):
                    i = 8 * c + r
                    shift = 16 * r
                    nxt = tiles[r + 1]
                    main = tiles[r]
                    if r:
                        main = pltpu.roll(main, LANES - shift, 1)
                        nxt = pltpu.roll(nxt, LANES - shift, 1)
                        main = jnp.where(lane < LANES - shift, main, nxt)
                    lev = i // QUERIES
                    row = i % QUERIES // WIN_LON
                    col = i % WIN_LON
                    side = col // HALF
                    place = lev * 36 + row * HALF + col % HALF
                    mask = masks[lev, row // EDGE]
                    at = pl.ds(place, heads, stride=QUERIES)
                    table_ref[k, p, 1 - side, 0, at, :] = main * LOG2E + mask[0]
                    table_ref[k, p, 1 - side, 1, at, :] = nxt * LOG2E + mask[1]
            copies.append(pltpu.make_async_copy(table_ref.at[k, p], table_out.at[k, p], sems.at[k, p]))
            copies[-1].start()
    for copy in copies:
        copy.wait()


def layer_norm(values, gain):
    center = values - jnp.mean(values, axis=-1, keepdims=True)
    spread = jnp.mean(center * center, axis=-1, keepdims=True)
    return center * lax.rsqrt(spread + 1e-05) * gain


def side_kernel(
    chans,
    heads,
    windows,
    right_ref,
    own_piece,
    halo_piece,
    gain1_ref,
    gain2_ref,
    qkv_any,
    table_any,
    proj_any,
    fc1_any,
    fc2_any,
    out_ref,
    keys_ref,
    own_ref,
    res_ref,
    qkv_ref,
    table_ref,
    proj_ref,
    fc1_ref,
    fc2_ref,
    sems,
):
    head_dim = chans // heads
    low = lax.broadcasted_iota(jnp.int32, (1, LANES), 1) < SPARE
    right = right_ref[0]

    def fetch(source, target, sem):
        copy = pltpu.make_async_copy(source, target, sems.at[sem])
        copy.start()
        return copy

    qkv_copy = fetch(qkv_any, qkv_ref, 0)
    table_copies = {}
    for n in range(len(windows)):
        for p in range(2):
            source = table_any.at[windows[n], p, right]
            table_copies[n, p] = fetch(source, table_ref.at[n, p], 4 + 2 * n + p)
    late_copies = [
        fetch(proj_any, proj_ref, 1),
        fetch(fc1_any, fc1_ref, 2),
        fetch(fc2_any, fc2_ref, 3),
    ]
    halo_at = right * HALF
    own_at = HALF - halo_at

    def tokens_of(ref, at, first, count):
        both = [ref[at, part, first : first + count] for part in range(2)]
        return jnp.concatenate([both[0], both[1][:, : chans - LANES]], axis=1)

    def split(ref, row):
        for pair in range(HALF // 2):
            both = ref[row, :, pair * 2 * chans : (pair + 1) * 2 * chans].astype(jnp.float32)
            first, middle, final = (both[:, u * LANES : (u + 1) * LANES] for u in range(3))
            yield 2 * pair, (first, middle)
            middle, final = pltpu.roll(middle, SPARE, 1), pltpu.roll(final, SPARE, 1)
            yield 2 * pair + 1, (jnp.where(low, middle, final), final)

    for n in range(len(windows)):
        for row in range(WIN_LAT):
            for col, block in split(halo_piece, windows[n] * WIN_LAT + row):
                at = pl.ds(row * WIN_LON + col + halo_at, LEVELS, stride=QUERIES)
                for part in range(2):
                    keys_ref[n, part, at, :] = block[part]
            for col, block in split(own_piece, windows[n] * WIN_LAT + row):
                at = pl.ds(row * WIN_LON + col + own_at, LEVELS, stride=QUERIES)
                place = row * HALF + col
                for part in range(2):
                    keys_ref[n, part, at, :] = block[part]
                    own_ref[n, part, pl.ds(4 + place, LEVELS, stride=36), :] = block[part]
                    own_ref[n, part, pl.ds(148 + place, 1), :] = block[part][:1]

    gain1 = gain1_ref[...]
    lane = lax.broadcasted_iota(jnp.int32, (1, chans), 1)
    ones = jnp.ones((LEVELS * QUERIES, 2 * LANES - chans), jnp.float32)
    mixed = []
    qkv_copy.wait()
    for n in range(len(windows)):
        normed = layer_norm(tokens_of(keys_ref, n, 0, LEVELS * QUERIES), gain1)
        normed = jnp.concatenate([normed[QUERIES:], normed[:QUERIES]], axis=0)
        normed = normed.astype(jnp.bfloat16)
        keys = jnp.dot(normed, qkv_ref[:, chans : 2 * chans], preferred_element_type=jnp.float32)
        values = jnp.dot(normed, qkv_ref[:, 2 * chans :], preferred_element_type=jnp.float32)
        values = jnp.concatenate([values, ones], axis=1)
        own = layer_norm(tokens_of(own_ref, n, 40, 144), gain1).astype(jnp.bfloat16)
        query = jnp.dot(own, qkv_ref[:, :chans], preferred_element_type=jnp.float32)
        query = query * (head_dim ** (-0.5) * LOG2E)
        for p in range(2):
            q = query[p * QUERIES : (p + 1) * QUERIES]
            k = keys[p * TOKENS : (p + 1) * TOKENS].astype(jnp.bfloat16)
            v = values[p * TOKENS : (p + 1) * TOKENS].astype(jnp.bfloat16)
            picked = [
                jnp.where((lane >= h * head_dim) & (lane < (h + 1) * head_dim), q, 0.0)
                for h in range(heads)
            ]
            picked = jnp.concatenate(picked, axis=0).astype(jnp.bfloat16)
            scores = lax.dot_general(picked, k, NT, preferred_element_type=jnp.float32)
            table_copies[n, p].wait()
            table = [table_ref[n, p, part] for part in range(2)]
            table = jnp.concatenate([table[0], table[1][:, : TOKENS - LANES]], axis=1)
            scores = scores + table
            top = jnp.max(scores, axis=1, keepdims=True)
            probs = jnp.exp2(scores - top).astype(jnp.bfloat16)
            got = jnp.dot(probs, v, preferred_element_type=jnp.float32)
            out = jnp.zeros((QUERIES, chans), jnp.float32)
            for h in range(heads):
                part = got[h * QUERIES : (h + 1) * QUERIES]
                scaled = part[:, :chans] * (1.0 / part[:, chans : chans + 1])
                inside = (lane >= h * head_dim) & (lane < (h + 1) * head_dim)
                out = jnp.where(inside, scaled, out)
            mixed.append(out)
    mixed = jnp.concatenate(mixed, axis=0).astype(jnp.bfloat16)
    for copy in late_copies:
        copy.wait()
    attn = jnp.dot(mixed, proj_ref[...], preferred_element_type=jnp.float32)
    attn = attn.astype(jnp.bfloat16).astype(jnp.float32)
    tokens = [tokens_of(own_ref, n, 40, 144) for n in range(len(windows))]
    resid = jnp.concatenate(tokens, axis=0) + attn
    resid = resid.astype(jnp.bfloat16).astype(jnp.float32)
    normed = layer_norm(resid, gain2_ref[...]).astype(jnp.bfloat16)
    hidden = jnp.dot(normed, fc1_ref[...], preferred_element_type=jnp.float32)
    hidden = jax.nn.gelu(hidden).astype(jnp.bfloat16)
    result = lax.dot_general(hidden, fc2_ref[...], NT, preferred_element_type=jnp.float32)
    result = resid + result
    for n in range(len(windows)):
        mine = result[n * 144 : (n + 1) * 144]
        for part, lanes in enumerate((slice(0, LANES), slice(LANES, chans))):
            width = min(LANES, chans - part * LANES)
            res_ref[n, part, 40:184, :width] = mine[:, lanes]
            res_ref[n, part, 0:40, :width] = mine[104:144, lanes]
        for row in range(WIN_LAT):
            for pair in range(HALF // 2):
                tiles = []
                for col in (2 * pair, 2 * pair + 1):
                    at = pl.ds(4 + row * HALF + col, LEVELS, stride=36)
                    tiles += [res_ref[n, part, at, :] for part in range(2)]
                shifted = [pltpu.roll(x, SPARE, 1) for x in tiles[2:]]
                tiles = [tiles[0], jnp.where(low, tiles[1], shifted[0])]
                tiles.append(jnp.where(low, shifted[0], shifted[1]))
                tiles = jnp.concatenate(tiles, axis=1).astype(jnp.bfloat16)
                out_ref[n * WIN_LAT + row, :, pair * 2 * chans : (pair + 1) * 2 * chans] = tiles


def run_side(right, own, halo, table, windows, weights, chans, heads):
    count = len(windows)
    vmem = pl.BlockSpec(memory_space=pltpu.VMEM)
    out = jax.ShapeDtypeStruct((count * WIN_LAT,) + own.shape[1:], jnp.bfloat16)
    gain1, qkv, proj, gain2, fc1, fc2 = weights
    return pl.pallas_call(
        functools.partial(side_kernel, chans, heads, windows),
        out_shape=out,
        in_specs=[pl.BlockSpec(memory_space=pltpu.SMEM)]
        + [vmem] * 4
        + [pl.BlockSpec(memory_space=pl.ANY)] * 5,
        out_specs=vmem,
        scratch_shapes=[
            pltpu.VMEM((count, 2, LEVELS * QUERIES, LANES), jnp.float32),
            pltpu.VMEM((count, 2, 184, LANES), jnp.float32),
            pltpu.VMEM((count, 2, 184, LANES), jnp.float32),
            pltpu.VMEM(qkv.shape, qkv.dtype),
            pltpu.VMEM((count, 2) + table.shape[3:], table.dtype),
            pltpu.VMEM(proj.shape, proj.dtype),
            pltpu.VMEM(fc1.shape, fc1.dtype),
            pltpu.VMEM(fc2.shape, fc2.dtype),
            pltpu.SemaphoreType.DMA((4 + 2 * count,)),
        ],
        compiler_params=pltpu.CompilerParams(vmem_limit_bytes=24 * 2**20),
        cost_estimate=pl.CostEstimate(
            flops=200_000_000 * count, bytes_accessed=3_000_000, transcendentals=250_000 * count
        ),
        name="swin_side",
    )(right, own, halo, gain1, gain2, qkv, table, proj, fc1, fc2)


def shards(
    field_in, norm1_gain, qkv_weight, proj_weight, earth_bias, norm2_gain, fc1_weight, fc2_weight
):
    levels, rows, flat = field_in.shape
    chans = qkv_weight.shape[0]
    heads = earth_bias.shape[2]
    half = HALF * chans
    field = jnp.transpose(field_in, (1, 0, 2))
    south = moved(field[:EDGE], "lat", -1)
    odd = lax.axis_index("lon") % 2
    last = (lax.axis_index("lat") == lax.axis_size("lat") - 1).astype(jnp.int32).reshape(1)
    vmem = pl.BlockSpec(memory_space=pltpu.VMEM)
    table_shape = (2, 2, 2, 2, heads * QUERIES, LANES)
    table, kept = pl.pallas_call(
        table_kernel,
        out_shape=[
            jax.ShapeDtypeStruct(table_shape, jnp.float32),
            jax.ShapeDtypeStruct((rows - EDGE, levels, flat), field.dtype),
        ],
        in_specs=[pl.BlockSpec(memory_space=pltpu.SMEM), vmem, vmem],
        out_specs=[pl.BlockSpec(memory_space=pl.ANY), vmem],
        scratch_shapes=[
            pltpu.VMEM(table_shape, jnp.float32),
            pltpu.SemaphoreType.DMA((2, 2)),
        ],
        compiler_params=pltpu.CompilerParams(vmem_limit_bytes=32 * 2**20),
        cost_estimate=pl.CostEstimate(flops=4_000_000, bytes_accessed=6_000_000, transcendentals=0),
        name="bias_tables",
    )(last, earth_bias, field)
    tokens = jnp.concatenate([kept, south], axis=0)
    left, right = tokens[:, :, :half], tokens[:, :, half:]
    near = jnp.where(odd == 1, left, right)
    far = jnp.where(odd == 1, right, left)
    far_halo = swapped(far, "lon", 1)
    near_halo = swapped(near, "lon", 0)
    weights = (
        norm1_gain.reshape(1, chans),
        qkv_weight,
        proj_weight,
        norm2_gain.reshape(1, chans),
        fc1_weight,
        jnp.transpose(fc2_weight),
    )
    near_right, far_right = (1 - odd).reshape(1), odd.reshape(1)
    near_done = run_side(near_right, near, near_halo, table, (0, 1), weights, chans, heads)
    far_halo, near_done = lax.optimization_barrier((far_halo, near_done))
    far_low = run_side(far_right, far, far_halo, table, (1,), weights, chans, heads)
    top = moved(jnp.stack([near_done[WIN_LAT + EDGE :], far_low[EDGE:]]), "lat", 1)
    far_high = run_side(far_right, far, far_halo, table, (0,), weights, chans, heads)
    near_all = jnp.concatenate([top[0], near_done[: WIN_LAT + EDGE]], axis=0)
    far_all = jnp.concatenate([top[1], far_high, far_low[:EDGE]], axis=0)
    done = jnp.where(
        odd == 1,
        jnp.concatenate([near_all, far_all], axis=2),
        jnp.concatenate([far_all, near_all], axis=2),
    )
    return jnp.transpose(done, (1, 0, 2))


def solution(mesh):
    in_specs = (P(None, "lat", "lon"), P(), P(), P(), P("lat", None, None, None), P(), P(), P())
    out_specs = P(None, "lat", "lon")
    return jax.shard_map(shards, mesh=mesh, in_specs=in_specs, out_specs=out_specs, check_vma=False)
```

```python
import functools

import jax
import jax.numpy as jnp
from jax import lax
from jax.experimental import pallas as pl
from jax.experimental.pallas import tpu as pltpu
from jax.sharding import PartitionSpec as P

LEVELS = 4
WIN_LEV = 2
WIN_LAT = 6
WIN_LON = 12
EDGE = WIN_LAT // 2
HALF = WIN_LON // 2
TOKENS = WIN_LEV * WIN_LAT * WIN_LON
QUERIES = TOKENS // 2
LOG2E = 1.4426950408889634
LANES = 128
SPARE = 64
NT = (((1,), (1,)), ((), ()))


def moved(x, axis, by):
    size = lax.axis_size(axis)
    return lax.ppermute(x, axis, [(i, (i + by) % size) for i in range(size)])


def swapped(x, axis, first):
    size = lax.axis_size(axis)
    pairs = []
    for i in range(first, size, 2):
        j = (i + 1) % size
        pairs += [(i, j), (j, i)]
    return lax.ppermute(x, axis, pairs)


def half_places(place_ref, half):
    odd = place_ref[1]
    return pl.multiple_of((1 - odd) * half, LANES), pl.multiple_of(odd * half, LANES)


def pack_kernel(place_ref, south_ref, near_in, far_in, near_ref, far_ref):
    near_at, far_at = half_places(place_ref, near_ref.shape[2])
    rows = near_ref.shape[0] - EDGE
    near_ref[:rows] = near_in[:rows]
    far_ref[:rows] = far_in[:rows]
    near_ref[rows:] = south_ref[:, :, pl.ds(near_at, near_ref.shape[2])]
    far_ref[rows:] = south_ref[:, :, pl.ds(far_at, far_ref.shape[2])]


def last_kernel(place_ref, top_ref, done_ref, out_ref, sems):
    half = top_ref.shape[3]
    copies = []
    for n, at in enumerate(half_places(place_ref, half)):
        target = out_ref.at[:EDGE, :, pl.ds(at, half)]
        copies.append(pltpu.make_async_copy(top_ref.at[n], target, sems.at[n]))
        copies[-1].start()
    for copy in copies:
        copy.wait()


def table_kernel(place_ref, bias_ref, field_ref, table_ref, near_ref, far_ref):
    rows = field_ref.shape[0] - EDGE
    near_at, far_at = half_places(place_ref, near_ref.shape[2])
    near_ref[:rows] = field_ref[EDGE:, :, pl.ds(near_at, near_ref.shape[2])]
    far_ref[:rows] = field_ref[EDGE:, :, pl.ds(far_at, far_ref.shape[2])]
    heads = bias_ref.shape[2]
    width = 9 * LANES
    lane = lax.broadcasted_iota(jnp.int32, (1, LANES), 1)
    last = jnp.where(place_ref[0] > 0, -1e9, 0.0).astype(jnp.float32)

    def penalty(first, lev, side, wrap):
        key = lane + first
        key_lev = (key >= QUERIES).astype(jnp.int32)
        key_side = ((key - key_lev * QUERIES) >= QUERIES // 2).astype(jnp.int32)
        out = jnp.zeros((1, LANES), jnp.float32)
        if lev is not None:
            out = jnp.where(key_lev != lev, -1e9, out)
        if wrap:
            out = out + jnp.where(key_side != side, last, 0.0)
        return out

    for k in range(2):
        for p in range(2):
            masks = {}
            for lev in range(2):
                for side in range(2):
                    masks[lev, side] = [
                        penalty(first, lev if p == 1 else None, side, k == 1)
                        for first in (0, LANES)
                    ]
            for c in range(TOKENS // 8):
                tiles = [
                    bias_ref[k, p, :, c * width + u * LANES : c * width + (u + 1) * LANES]
                    for u in range(9)
                ]
                for r in range(8):
                    i = 8 * c + r
                    shift = 16 * r
                    nxt = tiles[r + 1]
                    main = tiles[r]
                    if r:
                        main = pltpu.roll(main, LANES - shift, 1)
                        nxt = pltpu.roll(nxt, LANES - shift, 1)
                        main = jnp.where(lane < LANES - shift, main, nxt)
                    lev = i // QUERIES
                    row = i % QUERIES // WIN_LON
                    col = i % WIN_LON
                    side = col // HALF
                    place = lev * 36 + row * HALF + col % HALF
                    mask = masks[lev, row // EDGE]
                    at = pl.ds(place, heads, stride=QUERIES)
                    table_ref[k, p, 1 - side, 0, at, :] = main * LOG2E + mask[0]
                    table_ref[k, p, 1 - side, 1, at, :] = nxt * LOG2E + mask[1]


def layer_norm(values, gain):
    center = values - jnp.mean(values, axis=-1, keepdims=True)
    spread = jnp.mean(center * center, axis=-1, keepdims=True)
    return center * lax.rsqrt(spread + 1e-05) * gain


def side_kernel(
    chans,
    heads,
    windows,
    part_of,
    place_ref,
    own_piece,
    halo_piece,
    gain1_ref,
    qkv_ref,
    proj_ref,
    table_ref,
    gain2_ref,
    fc1_ref,
    fc2_ref,
    *rest,
):
    if part_of == "near":
        out_ref, keys_ref, own_ref, res_ref = rest
    elif part_of == "low":
        near_ref, out_ref, send_ref, keys_ref, own_ref, res_ref = rest
    else:
        near_ref, low_ref, done_ref, keys_ref, own_ref, res_ref, out_ref, sems = rest
        half = near_ref.shape[2]
        near_at, far_at = half_places(place_ref, half)
        done_near = done_ref.at[:, :, pl.ds(near_at, half)]
        done_far = done_ref.at[:, :, pl.ds(far_at, half)]
        copies = [
            pltpu.make_async_copy(
                near_ref.at[: WIN_LAT + EDGE], done_near.at[EDGE:], sems.at[0]
            ),
            pltpu.make_async_copy(
                low_ref.at[:EDGE], done_far.at[WIN_LAT + EDGE :], sems.at[1]
            ),
            pltpu.make_async_copy(
                out_ref, done_far.at[EDGE : WIN_LAT + EDGE], sems.at[2]
            ),
        ]
        for copy in copies[:2]:
            copy.start()
    head_dim = chans // heads
    low = lax.broadcasted_iota(jnp.int32, (1, LANES), 1) < SPARE
    right = 1 - place_ref[1] if part_of == "near" else place_ref[1]
    halo_at = right * HALF
    own_at = HALF - halo_at

    def tokens_of(ref, at, first, count):
        both = [ref[at, part, first : first + count] for part in range(2)]
        return jnp.concatenate([both[0], both[1][:, : chans - LANES]], axis=1)

    def split(ref, row):
        for pair in range(HALF // 2):
            both = ref[row, :, pair * 2 * chans : (pair + 1) * 2 * chans].astype(jnp.float32)
            first, middle, final = (both[:, u * LANES : (u + 1) * LANES] for u in range(3))
            yield 2 * pair, (first, middle)
            middle, final = pltpu.roll(middle, SPARE, 1), pltpu.roll(final, SPARE, 1)
            yield 2 * pair + 1, (jnp.where(low, middle, final), final)

    for n in range(len(windows)):
        for row in range(WIN_LAT):
            for col, block in split(halo_piece, n * WIN_LAT + row):
                at = pl.ds(row * WIN_LON + col + halo_at, LEVELS, stride=QUERIES)
                for part in range(2):
                    keys_ref[n, part, at, :] = block[part]
            for col, block in split(own_piece, n * WIN_LAT + row):
                at = pl.ds(row * WIN_LON + col + own_at, LEVELS, stride=QUERIES)
                place = row * HALF + col
                for part in range(2):
                    keys_ref[n, part, at, :] = block[part]
                    own_ref[n, part, pl.ds(4 + place, LEVELS, stride=36), :] = block[part]
                    own_ref[n, part, pl.ds(148 + place, 1), :] = block[part][:1]

    gain1 = gain1_ref[...]
    lane = lax.broadcasted_iota(jnp.int32, (1, chans), 1)
    ones = jnp.ones((LEVELS * QUERIES, 2 * LANES - chans), jnp.float32)
    mixed = []
    for n in range(len(windows)):
        normed = layer_norm(tokens_of(keys_ref, n, 0, LEVELS * QUERIES), gain1)
        normed = jnp.concatenate([normed[QUERIES:], normed[:QUERIES]], axis=0)
        normed = normed.astype(jnp.bfloat16)
        keys = jnp.dot(normed, qkv_ref[:, chans : 2 * chans], preferred_element_type=jnp.float32)
        values = jnp.dot(normed, qkv_ref[:, 2 * chans :], preferred_element_type=jnp.float32)
        values = jnp.concatenate([values, ones], axis=1)
        own = layer_norm(tokens_of(own_ref, n, 40, 144), gain1).astype(jnp.bfloat16)
        query = jnp.dot(own, qkv_ref[:, :chans], preferred_element_type=jnp.float32)
        query = query * (head_dim ** (-0.5) * LOG2E)
        for p in range(2):
            q = query[p * QUERIES : (p + 1) * QUERIES]
            k = keys[p * TOKENS : (p + 1) * TOKENS].astype(jnp.bfloat16)
            v = values[p * TOKENS : (p + 1) * TOKENS].astype(jnp.bfloat16)
            picked = [
                jnp.where((lane >= h * head_dim) & (lane < (h + 1) * head_dim), q, 0.0)
                for h in range(heads)
            ]
            picked = jnp.concatenate(picked, axis=0).astype(jnp.bfloat16)
            scores = lax.dot_general(picked, k, NT, preferred_element_type=jnp.float32)
            table = [table_ref[windows[n], p, right, part] for part in range(2)]
            table = jnp.concatenate([table[0], table[1][:, : TOKENS - LANES]], axis=1)
            scores = scores + table
            top = jnp.max(scores, axis=1, keepdims=True)
            probs = jnp.exp2(scores - top).astype(jnp.bfloat16)
            got = jnp.dot(probs, v, preferred_element_type=jnp.float32)
            out = jnp.zeros((QUERIES, chans), jnp.float32)
            for h in range(heads):
                part = got[h * QUERIES : (h + 1) * QUERIES]
                scaled = part[:, :chans] * (1.0 / part[:, chans : chans + 1])
                inside = (lane >= h * head_dim) & (lane < (h + 1) * head_dim)
                out = jnp.where(inside, scaled, out)
            mixed.append(out)
    mixed = jnp.concatenate(mixed, axis=0).astype(jnp.bfloat16)
    attn = jnp.dot(mixed, proj_ref[...], preferred_element_type=jnp.float32)
    attn = attn.astype(jnp.bfloat16).astype(jnp.float32)
    tokens = [tokens_of(own_ref, n, 40, 144) for n in range(len(windows))]
    resid = jnp.concatenate(tokens, axis=0) + attn
    resid = resid.astype(jnp.bfloat16).astype(jnp.float32)
    normed = layer_norm(resid, gain2_ref[...]).astype(jnp.bfloat16)
    hidden = jnp.dot(normed, fc1_ref[...], preferred_element_type=jnp.float32)
    hidden = jax.nn.gelu(hidden).astype(jnp.bfloat16)
    result = lax.dot_general(hidden, fc2_ref[...], NT, preferred_element_type=jnp.float32)
    result = resid + result
    for n in range(len(windows)):
        mine = result[n * 144 : (n + 1) * 144]
        for part, lanes in enumerate((slice(0, LANES), slice(LANES, chans))):
            width = min(LANES, chans - part * LANES)
            res_ref[n, part, 40:184, :width] = mine[:, lanes]
            res_ref[n, part, 0:40, :width] = mine[104:144, lanes]
        for row in range(WIN_LAT):
            for pair in range(HALF // 2):
                tiles = []
                for col in (2 * pair, 2 * pair + 1):
                    at = pl.ds(4 + row * HALF + col, LEVELS, stride=36)
                    tiles += [res_ref[n, part, at, :] for part in range(2)]
                shifted = [pltpu.roll(x, SPARE, 1) for x in tiles[2:]]
                tiles = [tiles[0], jnp.where(low, tiles[1], shifted[0])]
                tiles.append(jnp.where(low, shifted[0], shifted[1]))
                tiles = jnp.concatenate(tiles, axis=1).astype(jnp.bfloat16)
                out_ref[n * WIN_LAT + row, :, pair * 2 * chans : (pair + 1) * 2 * chans] = tiles
    if part_of == "low":
        send_ref[0] = near_ref[WIN_LAT + EDGE :]
        send_ref[1] = out_ref[EDGE:]
    elif part_of == "high":
        copies[2].start()
        for copy in copies:
            copy.wait()


def run_side(place, own, halo, table, windows, part_of, weights, chans, heads, before):
    count = len(windows)
    first = windows[0]
    assert list(windows) == list(range(first, first + count)) and first % count == 0
    rows = count * WIN_LAT
    piece = pl.BlockSpec((rows,) + own.shape[1:], lambda _: (first // count, 0, 0))

    def whole(x):
        return pl.BlockSpec(x.shape, lambda _: (0,) * len(x.shape))

    anywhere = pl.BlockSpec(memory_space=pl.ANY)
    out = jax.ShapeDtypeStruct((rows,) + own.shape[1:], own.dtype)
    send = jax.ShapeDtypeStruct((2, EDGE) + own.shape[1:], own.dtype)
    done = jax.ShapeDtypeStruct(own.shape[:2] + (2 * own.shape[2],), own.dtype)
    outs = {"near": [out], "low": [out, send], "high": [done]}[part_of]
    extra = [pltpu.VMEM(out.shape, out.dtype), pltpu.SemaphoreType.DMA((3,))]
    gain1, qkv, proj, gain2, fc1, fc2 = weights
    operands = (gain1, qkv, proj, table, gain2, fc1, fc2) + before
    return pl.pallas_call(
        functools.partial(side_kernel, chans, heads, windows, part_of),
        out_shape=outs,
        grid=(1,),
        in_specs=[pl.BlockSpec(memory_space=pltpu.SMEM), piece, piece]
        + [whole(x) for x in operands],
        out_specs=[anywhere] if part_of == "high" else [whole(x) for x in outs],
        scratch_shapes=[
            pltpu.VMEM((count, 2, LEVELS * QUERIES, LANES), jnp.float32),
            pltpu.VMEM((count, 2, 184, LANES), jnp.float32),
            pltpu.VMEM((count, 2, 184, LANES), jnp.float32),
        ]
        + (extra if part_of == "high" else []),
        compiler_params=pltpu.CompilerParams(vmem_limit_bytes=32 * 2**20),
        cost_estimate=pl.CostEstimate(
            flops=200_000_000 * count, bytes_accessed=3_000_000, transcendentals=250_000 * count
        ),
        name="swin_" + part_of,
    )(place, own, halo, *operands)


def shards(
    field_in, norm1_gain, qkv_weight, proj_weight, earth_bias, norm2_gain, fc1_weight, fc2_weight
):
    levels, rows, flat = field_in.shape
    chans = qkv_weight.shape[0]
    heads = earth_bias.shape[2]
    half = HALF * chans
    field = jnp.transpose(field_in, (1, 0, 2))
    south = moved(field[:EDGE], "lat", -1)
    odd = lax.axis_index("lon") % 2
    last = (lax.axis_index("lat") == lax.axis_size("lat") - 1).astype(jnp.int32)
    place = jnp.stack([last, odd])
    smem, vmem = (pl.BlockSpec(memory_space=m) for m in (pltpu.SMEM, pltpu.VMEM))
    piece = jax.ShapeDtypeStruct((rows, levels, half), field.dtype)
    table, near, far = pl.pallas_call(
        table_kernel,
        out_shape=[
            jax.ShapeDtypeStruct((2, 2, 2, 2, heads * QUERIES, LANES), jnp.float32),
            piece,
            piece,
        ],
        in_specs=[smem, vmem, vmem],
        out_specs=[vmem] * 3,
        compiler_params=pltpu.CompilerParams(vmem_limit_bytes=32 * 2**20),
        cost_estimate=pl.CostEstimate(flops=4_000_000, bytes_accessed=6_000_000, transcendentals=0),
        name="bias_tables",
    )(place, earth_bias, field)
    near, far = pl.pallas_call(
        pack_kernel,
        out_shape=[piece, piece],
        in_specs=[smem] + [vmem] * 3,
        out_specs=[vmem] * 2,
        cost_estimate=pl.CostEstimate(flops=0, bytes_accessed=500_000, transcendentals=0),
        name="pack_halves",
    )(place, south, near, far)
    far_halo = swapped(far, "lon", 1)
    near_halo = swapped(near, "lon", 0)
    weights = (
        norm1_gain.reshape(1, chans),
        qkv_weight,
        proj_weight,
        norm2_gain.reshape(1, chans),
        fc1_weight,
        jnp.transpose(fc2_weight),
    )
    (near_done,) = run_side(
        place, near, near_halo, table, (0, 1), "near", weights, chans, heads, ()
    )
    far_low, send = run_side(
        place, far, far_halo, table, (1,), "low", weights, chans, heads, (near_done,)
    )
    top = moved(send, "lat", 1)
    (done,) = run_side(
        place, far, far_halo, table, (0,), "high", weights, chans, heads, (near_done, far_low)
    )
    anywhere = pl.BlockSpec(memory_space=pl.ANY)
    done = pl.pallas_call(
        last_kernel,
        out_shape=jax.ShapeDtypeStruct(done.shape, done.dtype),
        in_specs=[smem, anywhere, anywhere],
        out_specs=anywhere,
        scratch_shapes=[pltpu.SemaphoreType.DMA((2,))],
        input_output_aliases={2: 0},
        cost_estimate=pl.CostEstimate(flops=0, bytes_accessed=100_000, transcendentals=0),
        name="last_rows",
    )(place, top, done)
    return jnp.transpose(done, (1, 0, 2))


def solution(mesh):
    in_specs = (P(None, "lat", "lon"), P(), P(), P(), P("lat", None, None, None), P(), P(), P())
    out_specs = P(None, "lat", "lon")
    return jax.shard_map(shards, mesh=mesh, in_specs=in_specs, out_specs=out_specs, check_vma=False)
```

```python
import functools

import jax
import jax.numpy as jnp
from jax import lax
from jax.experimental import pallas as pl
from jax.experimental.pallas import tpu as pltpu
from jax.sharding import PartitionSpec as P

LEVELS = 4
WIN_LEV = 2
WIN_LAT = 6
WIN_LON = 12
EDGE = WIN_LAT // 2
HALF = WIN_LON // 2
TOKENS = WIN_LEV * WIN_LAT * WIN_LON
QUERIES = TOKENS // 2
LOG2E = 1.4426950408889634
LANES = 128
SPARE = 64
VMEM_BYTES = 8 * 2**20
NT = (((1,), (1,)), ((), ()))


def moved(x, axis, by):
    size = lax.axis_size(axis)
    return lax.ppermute(x, axis, [(i, (i + by) % size) for i in range(size)])


def swapped(x, axis, first):
    size = lax.axis_size(axis)
    pairs = []
    for i in range(first, size, 2):
        j = (i + 1) % size
        pairs += [(i, j), (j, i)]
    return lax.ppermute(x, axis, pairs)


def half_places(place_ref, half):
    odd = place_ref[1]
    return pl.multiple_of((1 - odd) * half, LANES), pl.multiple_of(odd * half, LANES)


def pack_kernel(place_ref, south_ref, near_in, far_in, near_ref, far_ref):
    near_at, far_at = half_places(place_ref, near_ref.shape[2])
    rows = near_ref.shape[0] - EDGE
    near_ref[:rows] = near_in[:rows]
    far_ref[:rows] = far_in[:rows]
    near_ref[rows:] = south_ref[:, :, pl.ds(near_at, near_ref.shape[2])]
    far_ref[rows:] = south_ref[:, :, pl.ds(far_at, far_ref.shape[2])]


def last_kernel(place_ref, top_ref, done_ref, out_ref, sems):
    half = top_ref.shape[3]
    copies = []
    for n, at in enumerate(half_places(place_ref, half)):
        target = out_ref.at[:EDGE, :, pl.ds(at, half)]
        copies.append(pltpu.make_async_copy(top_ref.at[n], target, sems.at[n]))
        copies[-1].start()
    for copy in copies:
        copy.wait()


def table_kernel(place_ref, bias_ref, field_ref, table_ref, near_ref, far_ref):
    rows = field_ref.shape[0] - EDGE
    near_at, far_at = half_places(place_ref, near_ref.shape[2])
    near_ref[:rows] = field_ref[EDGE:, :, pl.ds(near_at, near_ref.shape[2])]
    far_ref[:rows] = field_ref[EDGE:, :, pl.ds(far_at, far_ref.shape[2])]
    heads = bias_ref.shape[2]
    width = 9 * LANES
    lane = lax.broadcasted_iota(jnp.int32, (1, LANES), 1)
    last = jnp.where(place_ref[0] > 0, -1e9, 0.0).astype(jnp.float32)

    def penalty(first, lev, side, wrap):
        key = lane + first
        key_lev = (key >= QUERIES).astype(jnp.int32)
        key_side = ((key - key_lev * QUERIES) >= QUERIES // 2).astype(jnp.int32)
        out = jnp.zeros((1, LANES), jnp.float32)
        if lev is not None:
            out = jnp.where(key_lev != lev, -1e9, out)
        if wrap:
            out = out + jnp.where(key_side != side, last, 0.0)
        return out

    for k in range(2):
        for p in range(2):
            masks = {}
            for lev in range(2):
                for side in range(2):
                    masks[lev, side] = [
                        penalty(first, lev if p == 1 else None, side, k == 1)
                        for first in (0, LANES)
                    ]
            for c in range(TOKENS // 8):
                tiles = [
                    bias_ref[k, p, :, c * width + u * LANES : c * width + (u + 1) * LANES]
                    for u in range(9)
                ]
                for r in range(8):
                    i = 8 * c + r
                    shift = 16 * r
                    nxt = tiles[r + 1]
                    main = tiles[r]
                    if r:
                        main = pltpu.roll(main, LANES - shift, 1)
                        nxt = pltpu.roll(nxt, LANES - shift, 1)
                        main = jnp.where(lane < LANES - shift, main, nxt)
                    lev = i // QUERIES
                    row = i % QUERIES // WIN_LON
                    col = i % WIN_LON
                    side = col // HALF
                    place = lev * 36 + row * HALF + col % HALF
                    mask = masks[lev, row // EDGE]
                    at = pl.ds(place, heads, stride=QUERIES)
                    table_ref[k, p, 1 - side, 0, at, :] = main * LOG2E + mask[0]
                    table_ref[k, p, 1 - side, 1, at, :] = nxt * LOG2E + mask[1]


def layer_norm(values, gain):
    center = values - jnp.mean(values, axis=-1, keepdims=True)
    spread = jnp.mean(center * center, axis=-1, keepdims=True)
    return center * lax.rsqrt(spread + 1e-05) * gain


def side_kernel(
    chans,
    heads,
    windows,
    part_of,
    place_ref,
    own_piece,
    halo_piece,
    gain1_ref,
    qkv_ref,
    proj_ref,
    table_ref,
    gain2_ref,
    fc1_ref,
    fc2_ref,
    *rest,
):
    if part_of == "near":
        out_ref, keys_ref, own_ref, res_ref = rest
    elif part_of == "low":
        near_ref, out_ref, send_ref, keys_ref, own_ref, res_ref = rest
    else:
        near_ref, low_ref, done_ref, keys_ref, own_ref, res_ref, out_ref, sems = rest
        half = near_ref.shape[2]
        near_at, far_at = half_places(place_ref, half)
        done_near = done_ref.at[:, :, pl.ds(near_at, half)]
        done_far = done_ref.at[:, :, pl.ds(far_at, half)]
        copies = [
            pltpu.make_async_copy(
                near_ref.at[: WIN_LAT + EDGE], done_near.at[EDGE:], sems.at[0]
            ),
            pltpu.make_async_copy(
                low_ref.at[:EDGE], done_far.at[WIN_LAT + EDGE :], sems.at[1]
            ),
            pltpu.make_async_copy(
                out_ref, done_far.at[EDGE : WIN_LAT + EDGE], sems.at[2]
            ),
        ]
        for copy in copies[:2]:
            copy.start()
    head_dim = chans // heads
    low = lax.broadcasted_iota(jnp.int32, (1, LANES), 1) < SPARE
    right = 1 - place_ref[1] if part_of == "near" else place_ref[1]
    halo_at = right * HALF
    own_at = HALF - halo_at

    def tokens_of(ref, at, first, count):
        both = [ref[at, part, first : first + count] for part in range(2)]
        return jnp.concatenate([both[0], both[1][:, : chans - LANES]], axis=1)

    def split(ref, row):
        for pair in range(HALF // 2):
            both = ref[row, :, pair * 2 * chans : (pair + 1) * 2 * chans].astype(jnp.float32)
            first, middle, final = (both[:, u * LANES : (u + 1) * LANES] for u in range(3))
            yield 2 * pair, (first, middle)
            middle, final = pltpu.roll(middle, SPARE, 1), pltpu.roll(final, SPARE, 1)
            yield 2 * pair + 1, (jnp.where(low, middle, final), final)

    for n in range(len(windows)):
        for row in range(WIN_LAT):
            for col, block in split(halo_piece, n * WIN_LAT + row):
                at = pl.ds(row * WIN_LON + col + halo_at, LEVELS, stride=QUERIES)
                for part in range(2):
                    keys_ref[n, part, at, :] = block[part]
            for col, block in split(own_piece, n * WIN_LAT + row):
                at = pl.ds(row * WIN_LON + col + own_at, LEVELS, stride=QUERIES)
                place = row * HALF + col
                for part in range(2):
                    keys_ref[n, part, at, :] = block[part]
                    own_ref[n, part, pl.ds(4 + place, LEVELS, stride=36), :] = block[part]
                    own_ref[n, part, pl.ds(148 + place, 1), :] = block[part][:1]

    gain1 = gain1_ref[...]
    lane = lax.broadcasted_iota(jnp.int32, (1, chans), 1)
    ones = jnp.ones((LEVELS * QUERIES, 2 * LANES - chans), jnp.float32)
    mixed = []
    for n in range(len(windows)):
        normed = layer_norm(tokens_of(keys_ref, n, 0, LEVELS * QUERIES), gain1)
        normed = jnp.concatenate([normed[QUERIES:], normed[:QUERIES]], axis=0)
        normed = normed.astype(jnp.bfloat16)
        keys = jnp.dot(normed, qkv_ref[:, chans : 2 * chans], preferred_element_type=jnp.float32)
        values = jnp.dot(normed, qkv_ref[:, 2 * chans :], preferred_element_type=jnp.float32)
        values = jnp.concatenate([values, ones], axis=1)
        own = layer_norm(tokens_of(own_ref, n, 40, 144), gain1).astype(jnp.bfloat16)
        query = jnp.dot(own, qkv_ref[:, :chans], preferred_element_type=jnp.float32)
        query = query * (head_dim ** (-0.5) * LOG2E)
        for p in range(2):
            q = query[p * QUERIES : (p + 1) * QUERIES]
            k = keys[p * TOKENS : (p + 1) * TOKENS].astype(jnp.bfloat16)
            v = values[p * TOKENS : (p + 1) * TOKENS].astype(jnp.bfloat16)
            picked = [
                jnp.where((lane >= h * head_dim) & (lane < (h + 1) * head_dim), q, 0.0)
                for h in range(heads)
            ]
            picked = jnp.concatenate(picked, axis=0).astype(jnp.bfloat16)
            scores = lax.dot_general(picked, k, NT, preferred_element_type=jnp.float32)
            table = [table_ref[windows[n], p, right, part] for part in range(2)]
            table = jnp.concatenate([table[0], table[1][:, : TOKENS - LANES]], axis=1)
            scores = scores + table
            top = jnp.max(scores, axis=1, keepdims=True)
            probs = jnp.exp2(scores - top).astype(jnp.bfloat16)
            got = jnp.dot(probs, v, preferred_element_type=jnp.float32)
            out = jnp.zeros((QUERIES, chans), jnp.float32)
            for h in range(heads):
                part = got[h * QUERIES : (h + 1) * QUERIES]
                scaled = part[:, :chans] * (1.0 / part[:, chans : chans + 1])
                inside = (lane >= h * head_dim) & (lane < (h + 1) * head_dim)
                out = jnp.where(inside, scaled, out)
            mixed.append(out)
    mixed = jnp.concatenate(mixed, axis=0).astype(jnp.bfloat16)
    attn = jnp.dot(mixed, proj_ref[...], preferred_element_type=jnp.float32)
    attn = attn.astype(jnp.bfloat16).astype(jnp.float32)
    tokens = [tokens_of(own_ref, n, 40, 144) for n in range(len(windows))]
    resid = jnp.concatenate(tokens, axis=0) + attn
    resid = resid.astype(jnp.bfloat16).astype(jnp.float32)
    normed = layer_norm(resid, gain2_ref[...]).astype(jnp.bfloat16)
    hidden = jnp.dot(normed, fc1_ref[...], preferred_element_type=jnp.float32)
    hidden = jax.nn.gelu(hidden).astype(jnp.bfloat16)
    result = lax.dot_general(hidden, fc2_ref[...], NT, preferred_element_type=jnp.float32)
    result = resid + result
    for n in range(len(windows)):
        mine = result[n * 144 : (n + 1) * 144]
        for part, lanes in enumerate((slice(0, LANES), slice(LANES, chans))):
            width = min(LANES, chans - part * LANES)
            res_ref[n, part, 40:184, :width] = mine[:, lanes]
            res_ref[n, part, 0:40, :width] = mine[104:144, lanes]
        for row in range(WIN_LAT):
            for pair in range(HALF // 2):
                tiles = []
                for col in (2 * pair, 2 * pair + 1):
                    at = pl.ds(4 + row * HALF + col, LEVELS, stride=36)
                    tiles += [res_ref[n, part, at, :] for part in range(2)]
                shifted = [pltpu.roll(x, SPARE, 1) for x in tiles[2:]]
                tiles = [tiles[0], jnp.where(low, tiles[1], shifted[0])]
                tiles.append(jnp.where(low, shifted[0], shifted[1]))
                tiles = jnp.concatenate(tiles, axis=1).astype(jnp.bfloat16)
                out_ref[n * WIN_LAT + row, :, pair * 2 * chans : (pair + 1) * 2 * chans] = tiles
    if part_of == "low":
        send_ref[0] = near_ref[WIN_LAT + EDGE :]
        send_ref[1] = out_ref[EDGE:]
    elif part_of == "high":
        copies[2].start()
        for copy in copies:
            copy.wait()


def run_side(place, own, halo, table, windows, part_of, weights, chans, heads, before):
    count = len(windows)
    first = windows[0]
    assert list(windows) == list(range(first, first + count)) and first % count == 0
    rows = count * WIN_LAT
    piece = pl.BlockSpec((rows,) + own.shape[1:], lambda _: (first // count, 0, 0))

    def whole(x):
        return pl.BlockSpec(x.shape, lambda _: (0,) * len(x.shape))

    anywhere = pl.BlockSpec(memory_space=pl.ANY)
    out = jax.ShapeDtypeStruct((rows,) + own.shape[1:], own.dtype)
    send = jax.ShapeDtypeStruct((2, EDGE) + own.shape[1:], own.dtype)
    done = jax.ShapeDtypeStruct(own.shape[:2] + (2 * own.shape[2],), own.dtype)
    outs = {"near": [out], "low": [out, send], "high": [done]}[part_of]
    extra = [pltpu.VMEM(out.shape, out.dtype), pltpu.SemaphoreType.DMA((3,))]
    gain1, qkv, proj, gain2, fc1, fc2 = weights
    operands = (gain1, qkv, proj, table, gain2, fc1, fc2) + before
    return pl.pallas_call(
        functools.partial(side_kernel, chans, heads, windows, part_of),
        out_shape=outs,
        grid=(1,),
        in_specs=[pl.BlockSpec(memory_space=pltpu.SMEM), piece, piece]
        + [whole(x) for x in operands],
        out_specs=[anywhere] if part_of == "high" else [whole(x) for x in outs],
        scratch_shapes=[
            pltpu.VMEM((count, 2, LEVELS * QUERIES, LANES), jnp.float32),
            pltpu.VMEM((count, 2, 184, LANES), jnp.float32),
            pltpu.VMEM((count, 2, 184, LANES), jnp.float32),
        ]
        + (extra if part_of == "high" else []),
        compiler_params=pltpu.CompilerParams(vmem_limit_bytes=VMEM_BYTES),
        cost_estimate=pl.CostEstimate(
            flops=200_000_000 * count, bytes_accessed=3_000_000, transcendentals=250_000 * count
        ),
        name="swin_" + part_of,
    )(place, own, halo, *operands)


def shards(
    field_in, norm1_gain, qkv_weight, proj_weight, earth_bias, norm2_gain, fc1_weight, fc2_weight
):
    levels, rows, flat = field_in.shape
    chans = qkv_weight.shape[0]
    heads = earth_bias.shape[2]
    half = HALF * chans
    field = jnp.transpose(field_in, (1, 0, 2))
    south = moved(field[:EDGE], "lat", -1)
    odd = lax.axis_index("lon") % 2
    last = (lax.axis_index("lat") == lax.axis_size("lat") - 1).astype(jnp.int32)
    place = jnp.stack([last, odd])
    smem, vmem = (pl.BlockSpec(memory_space=m) for m in (pltpu.SMEM, pltpu.VMEM))
    piece = jax.ShapeDtypeStruct((rows, levels, half), field.dtype)
    table, near, far = pl.pallas_call(
        table_kernel,
        out_shape=[
            jax.ShapeDtypeStruct((2, 2, 2, 2, heads * QUERIES, LANES), jnp.float32),
            piece,
            piece,
        ],
        in_specs=[smem, vmem, vmem],
        out_specs=[vmem] * 3,
        compiler_params=pltpu.CompilerParams(vmem_limit_bytes=VMEM_BYTES),
        cost_estimate=pl.CostEstimate(flops=4_000_000, bytes_accessed=6_000_000, transcendentals=0),
        name="bias_tables",
    )(place, earth_bias, field)
    near, far = pl.pallas_call(
        pack_kernel,
        out_shape=[piece, piece],
        in_specs=[smem] + [vmem] * 3,
        out_specs=[vmem] * 2,
        compiler_params=pltpu.CompilerParams(vmem_limit_bytes=VMEM_BYTES),
        cost_estimate=pl.CostEstimate(flops=0, bytes_accessed=500_000, transcendentals=0),
        name="pack_halves",
    )(place, south, near, far)
    far_halo = swapped(far, "lon", 1)
    near_halo = swapped(near, "lon", 0)
    weights = (
        norm1_gain.reshape(1, chans),
        qkv_weight,
        proj_weight,
        norm2_gain.reshape(1, chans),
        fc1_weight,
        jnp.transpose(fc2_weight),
    )
    (near_done,) = run_side(
        place, near, near_halo, table, (0, 1), "near", weights, chans, heads, ()
    )
    far_low, send = run_side(
        place, far, far_halo, table, (1,), "low", weights, chans, heads, (near_done,)
    )
    top = moved(send, "lat", 1)
    (done,) = run_side(
        place, far, far_halo, table, (0,), "high", weights, chans, heads, (near_done, far_low)
    )
    anywhere = pl.BlockSpec(memory_space=pl.ANY)
    done = pl.pallas_call(
        last_kernel,
        out_shape=jax.ShapeDtypeStruct(done.shape, done.dtype),
        in_specs=[smem, anywhere, anywhere],
        out_specs=anywhere,
        scratch_shapes=[pltpu.SemaphoreType.DMA((2,))],
        input_output_aliases={2: 0},
        compiler_params=pltpu.CompilerParams(vmem_limit_bytes=VMEM_BYTES),
        cost_estimate=pl.CostEstimate(flops=0, bytes_accessed=100_000, transcendentals=0),
        name="last_rows",
    )(place, top, done)
    return jnp.transpose(done, (1, 0, 2))


def solution(mesh):
    in_specs = (P(None, "lat", "lon"), P(), P(), P(), P("lat", None, None, None), P(), P(), P())
    out_specs = P(None, "lat", "lon")
    return jax.shard_map(shards, mesh=mesh, in_specs=in_specs, out_specs=out_specs, check_vma=False)
```

```python
import functools

import jax
import jax.numpy as jnp
from jax import lax
from jax.experimental import pallas as pl
from jax.experimental.pallas import tpu as pltpu
from jax.sharding import PartitionSpec as P

LEVELS = 4
WIN_LEV = 2
WIN_LAT = 6
WIN_LON = 12
EDGE = WIN_LAT // 2
HALF = WIN_LON // 2
TOKENS = WIN_LEV * WIN_LAT * WIN_LON
QUERIES = TOKENS // 2
LOG2E = 1.4426950408889634
GELU_0 = 0.7978845608028654
GELU_1 = 0.044715 * GELU_0
LANES = 128
SPARE = 64
VMEM_BYTES = 8 * 2**20
NT = (((1,), (1,)), ((), ()))


def moved(x, axis, by):
    size = lax.axis_size(axis)
    return lax.ppermute(x, axis, [(i, (i + by) % size) for i in range(size)])


def swapped(x, axis, first):
    size = lax.axis_size(axis)
    pairs = []
    for i in range(first, size, 2):
        j = (i + 1) % size
        pairs += [(i, j), (j, i)]
    return lax.ppermute(x, axis, pairs)


def half_places(half):
    odd = lax.rem(lax.axis_index("lon"), 2)
    return pl.multiple_of((1 - odd) * half, LANES), pl.multiple_of(odd * half, LANES)


def pack_kernel(which, south_ref, kept_ref, *rest):
    piece_ref = rest[-1]
    at = half_places(piece_ref.shape[2])[which]
    rows = piece_ref.shape[0] - EDGE
    piece_ref[:rows] = kept_ref[:rows]
    piece_ref[rows:] = south_ref[:, :, pl.ds(at, piece_ref.shape[2])]


def last_kernel(top_ref, high_ref, done_ref, out_ref, sems):
    half = top_ref.shape[3]
    near_at, far_at = half_places(half)
    near_out, far_out = (out_ref.at[:, :, pl.ds(at, half)] for at in (near_at, far_at))
    copies = [
        pltpu.make_async_copy(top_ref.at[0], near_out.at[:EDGE], sems.at[0]),
        pltpu.make_async_copy(top_ref.at[1], far_out.at[:EDGE], sems.at[1]),
        pltpu.make_async_copy(high_ref, far_out.at[EDGE : EDGE + WIN_LAT], sems.at[2]),
    ]
    for copy in copies:
        copy.start()
    for copy in copies:
        copy.wait()


def table_kernel(bias_ref, field_ref, table_ref, near_ref, far_ref):
    rows = field_ref.shape[0] - EDGE
    near_at, far_at = half_places(near_ref.shape[2])
    near_ref[:rows] = field_ref[EDGE:, :, pl.ds(near_at, near_ref.shape[2])]
    far_ref[:rows] = field_ref[EDGE:, :, pl.ds(far_at, far_ref.shape[2])]
    heads = bias_ref.shape[2]
    width = 9 * LANES
    lane = lax.broadcasted_iota(jnp.int32, (1, LANES), 1)
    is_last = lax.axis_index("lat") == lax.axis_size("lat") - 1
    last = jnp.where(is_last, -1e9, 0.0).astype(jnp.float32)

    def penalty(first, lev, side, wrap):
        key = lane + first
        key_lev = (key >= QUERIES).astype(jnp.int32)
        key_side = ((key - key_lev * QUERIES) >= QUERIES // 2).astype(jnp.int32)
        out = jnp.zeros((1, LANES), jnp.float32)
        if lev is not None:
            out = jnp.where(key_lev != lev, -1e9, out)
        if wrap:
            out = out + jnp.where(key_side != side, last, 0.0)
        return out

    for k in range(2):
        for p in range(2):
            masks = {}
            for lev in range(2):
                for side in range(2):
                    masks[lev, side] = [
                        penalty(first, lev if p == 1 else None, side, k == 1)
                        for first in (0, LANES)
                    ]
            for c in range(TOKENS // 8):
                tiles = [
                    bias_ref[k, p, :, c * width + u * LANES : c * width + (u + 1) * LANES]
                    for u in range(9)
                ]
                for r in range(8):
                    i = 8 * c + r
                    shift = 16 * r
                    nxt = tiles[r + 1]
                    main = tiles[r]
                    if r:
                        main = pltpu.roll(main, LANES - shift, 1)
                        nxt = pltpu.roll(nxt, LANES - shift, 1)
                        main = jnp.where(lane < LANES - shift, main, nxt)
                    lev = i // QUERIES
                    row = i % QUERIES // WIN_LON
                    col = i % WIN_LON
                    side = col // HALF
                    place = lev * 36 + row * HALF + col % HALF
                    mask = masks[lev, row // EDGE]
                    at = pl.ds(place, heads, stride=QUERIES)
                    table_ref[k, p, 1 - side, 0, at, :] = main * LOG2E + mask[0]
                    table_ref[k, p, 1 - side, 1, at, :] = nxt * LOG2E + mask[1]


def layer_norm(values, gain):
    center = values - jnp.mean(values, axis=-1, keepdims=True)
    spread = jnp.mean(center * center, axis=-1, keepdims=True)
    return center * lax.rsqrt(spread + 1e-05) * gain


def gelu(x):
    half = 0.5 * x
    return half + half * jnp.tanh(x * (GELU_0 + GELU_1 * (x * x)))


def side_kernel(
    chans,
    heads,
    windows,
    part_of,
    own_piece,
    halo_piece,
    gain1_ref,
    qkv_ref,
    proj_ref,
    table_ref,
    gain2_ref,
    fc1_ref,
    fc2_ref,
    *rest,
):
    if part_of == "near":
        out_ref, keys_ref, own_ref, res_ref = rest
    elif part_of == "low":
        near_ref, out_ref, send_ref, keys_ref, own_ref, res_ref = rest
    else:
        near_ref, low_ref, out_ref, done_ref, keys_ref, own_ref, res_ref, sems = rest
        half = near_ref.shape[2]
        near_at, far_at = half_places(half)
        done_near = done_ref.at[:, :, pl.ds(near_at, half)]
        done_far = done_ref.at[:, :, pl.ds(far_at, half)]
        copies = [
            pltpu.make_async_copy(
                near_ref.at[: WIN_LAT + EDGE], done_near.at[EDGE:], sems.at[0]
            ),
            pltpu.make_async_copy(
                low_ref.at[:EDGE], done_far.at[WIN_LAT + EDGE :], sems.at[1]
            ),
        ]
        for copy in copies:
            copy.start()
    head_dim = chans // heads
    low = lax.broadcasted_iota(jnp.int32, (1, LANES), 1) < SPARE
    odd = lax.rem(lax.axis_index("lon"), 2)
    right = 1 - odd if part_of == "near" else odd
    halo_at = right * HALF
    own_at = HALF - halo_at

    def tokens_of(ref, at, first, count):
        both = [ref[at, part, first : first + count] for part in range(2)]
        return jnp.concatenate([both[0], both[1][:, : chans - LANES]], axis=1)

    def split(ref, row):
        for pair in range(HALF // 2):
            both = ref[row, :, pair * 2 * chans : (pair + 1) * 2 * chans].astype(jnp.float32)
            first, middle, final = (both[:, u * LANES : (u + 1) * LANES] for u in range(3))
            yield 2 * pair, (first, middle)
            middle, final = pltpu.roll(middle, SPARE, 1), pltpu.roll(final, SPARE, 1)
            yield 2 * pair + 1, (jnp.where(low, middle, final), final)

    for n in range(len(windows)):
        for row in range(WIN_LAT):
            for col, block in split(halo_piece, n * WIN_LAT + row):
                at = pl.ds(row * WIN_LON + col + halo_at, LEVELS, stride=QUERIES)
                for part in range(2):
                    keys_ref[n, part, at, :] = block[part]
            for col, block in split(own_piece, n * WIN_LAT + row):
                at = pl.ds(row * WIN_LON + col + own_at, LEVELS, stride=QUERIES)
                place = row * HALF + col
                for part in range(2):
                    keys_ref[n, part, at, :] = block[part]
                    own_ref[n, part, pl.ds(4 + place, LEVELS, stride=36), :] = block[part]
                    own_ref[n, part, pl.ds(148 + place, 1), :] = block[part][:1]

    gain1 = gain1_ref[...]
    lane = lax.broadcasted_iota(jnp.int32, (1, chans), 1)
    ones = jnp.ones((LEVELS * QUERIES, 2 * LANES - chans), jnp.float32)
    mixed = []
    for n in range(len(windows)):
        normed = layer_norm(tokens_of(keys_ref, n, 0, LEVELS * QUERIES), gain1)
        normed = jnp.concatenate([normed[QUERIES:], normed[:QUERIES]], axis=0)
        normed = normed.astype(jnp.bfloat16)
        keys = jnp.dot(normed, qkv_ref[:, chans : 2 * chans], preferred_element_type=jnp.float32)
        values = jnp.dot(normed, qkv_ref[:, 2 * chans :], preferred_element_type=jnp.float32)
        values = jnp.concatenate([values, ones], axis=1)
        own = layer_norm(tokens_of(own_ref, n, 40, 144), gain1).astype(jnp.bfloat16)
        query = jnp.dot(own, qkv_ref[:, :chans], preferred_element_type=jnp.float32)
        query = query * (head_dim ** (-0.5) * LOG2E)
        for p in range(2):
            q = query[p * QUERIES : (p + 1) * QUERIES]
            k = keys[p * TOKENS : (p + 1) * TOKENS].astype(jnp.bfloat16)
            v = values[p * TOKENS : (p + 1) * TOKENS].astype(jnp.bfloat16)
            picked = [
                jnp.where((lane >= h * head_dim) & (lane < (h + 1) * head_dim), q, 0.0)
                for h in range(heads)
            ]
            picked = jnp.concatenate(picked, axis=0).astype(jnp.bfloat16)
            scores = lax.dot_general(picked, k, NT, preferred_element_type=jnp.float32)
            table = [table_ref[windows[n], p, right, part] for part in range(2)]
            table = jnp.concatenate([table[0], table[1][:, : TOKENS - LANES]], axis=1)
            scores = scores + table
            top = jnp.max(scores, axis=1, keepdims=True)
            probs = jnp.exp2(scores - top).astype(jnp.bfloat16)
            got = jnp.dot(probs, v, preferred_element_type=jnp.float32)
            out = jnp.zeros((QUERIES, chans), jnp.float32)
            for h in range(heads):
                part = got[h * QUERIES : (h + 1) * QUERIES]
                scaled = part[:, :chans] * (1.0 / part[:, chans : chans + 1])
                inside = (lane >= h * head_dim) & (lane < (h + 1) * head_dim)
                out = jnp.where(inside, scaled, out)
            mixed.append(out)
    mixed = jnp.concatenate(mixed, axis=0).astype(jnp.bfloat16)
    attn = jnp.dot(mixed, proj_ref[...], preferred_element_type=jnp.float32)
    attn = attn.astype(jnp.bfloat16).astype(jnp.float32)
    tokens = [tokens_of(own_ref, n, 40, 144) for n in range(len(windows))]
    resid = jnp.concatenate(tokens, axis=0) + attn
    resid = resid.astype(jnp.bfloat16).astype(jnp.float32)
    normed = layer_norm(resid, gain2_ref[...]).astype(jnp.bfloat16)
    hidden = jnp.dot(normed, fc1_ref[...], preferred_element_type=jnp.float32)
    hidden = gelu(hidden).astype(jnp.bfloat16)
    result = lax.dot_general(hidden, fc2_ref[...], NT, preferred_element_type=jnp.float32)
    result = resid + result
    for n in range(len(windows)):
        mine = result[n * 144 : (n + 1) * 144]
        for part, lanes in enumerate((slice(0, LANES), slice(LANES, chans))):
            width = min(LANES, chans - part * LANES)
            res_ref[n, part, 40:184, :width] = mine[:, lanes]
            res_ref[n, part, 0:40, :width] = mine[104:144, lanes]
        for row in range(WIN_LAT):
            for pair in range(HALF // 2):
                tiles = []
                for col in (2 * pair, 2 * pair + 1):
                    at = pl.ds(4 + row * HALF + col, LEVELS, stride=36)
                    tiles += [res_ref[n, part, at, :] for part in range(2)]
                shifted = [pltpu.roll(x, SPARE, 1) for x in tiles[2:]]
                tiles = [tiles[0], jnp.where(low, tiles[1], shifted[0])]
                tiles.append(jnp.where(low, shifted[0], shifted[1]))
                tiles = jnp.concatenate(tiles, axis=1).astype(jnp.bfloat16)
                out_ref[n * WIN_LAT + row, :, pair * 2 * chans : (pair + 1) * 2 * chans] = tiles
    if part_of == "low":
        send_ref[0] = near_ref[WIN_LAT + EDGE :]
        send_ref[1] = out_ref[EDGE:]
    elif part_of == "high":
        for copy in copies:
            copy.wait()


def run_side(own, halo, table, windows, part_of, weights, chans, heads, before):
    count = len(windows)
    first = windows[0]
    assert list(windows) == list(range(first, first + count)) and first % count == 0
    rows = count * WIN_LAT
    piece = pl.BlockSpec((rows,) + own.shape[1:], lambda _: (first // count, 0, 0))

    def whole(x):
        return pl.BlockSpec(x.shape, lambda _: (0,) * len(x.shape))

    anywhere = pl.BlockSpec(memory_space=pl.ANY)
    out = jax.ShapeDtypeStruct((rows,) + own.shape[1:], own.dtype)
    send = jax.ShapeDtypeStruct((2, EDGE) + own.shape[1:], own.dtype)
    done = jax.ShapeDtypeStruct(own.shape[:2] + (2 * own.shape[2],), own.dtype)
    outs = {"near": [out], "low": [out, send], "high": [out, done]}[part_of]
    extra = [pltpu.SemaphoreType.DMA((2,))]
    gain1, qkv, proj, gain2, fc1, fc2 = weights
    operands = (gain1, qkv, proj, table, gain2, fc1, fc2) + before
    return pl.pallas_call(
        functools.partial(side_kernel, chans, heads, windows, part_of),
        out_shape=outs,
        grid=(1,),
        in_specs=[piece, piece] + [whole(x) for x in operands],
        out_specs=[whole(out), anywhere] if part_of == "high" else [whole(x) for x in outs],
        scratch_shapes=[
            pltpu.VMEM((count, 2, LEVELS * QUERIES, LANES), jnp.float32),
            pltpu.VMEM((count, 2, 184, LANES), jnp.float32),
            pltpu.VMEM((count, 2, 184, LANES), jnp.float32),
        ]
        + (extra if part_of == "high" else []),
        compiler_params=pltpu.CompilerParams(vmem_limit_bytes=VMEM_BYTES),
        cost_estimate=pl.CostEstimate(
            flops=200_000_000 * count, bytes_accessed=3_000_000, transcendentals=250_000 * count
        ),
        name="swin_" + part_of,
    )(own, halo, *operands)


def shards(
    field_in, norm1_gain, qkv_weight, proj_weight, earth_bias, norm2_gain, fc1_weight, fc2_weight
):
    levels, rows, flat = field_in.shape
    chans = qkv_weight.shape[0]
    heads = earth_bias.shape[2]
    half = HALF * chans
    field = jnp.transpose(field_in, (1, 0, 2))
    south = moved(field[:EDGE], "lat", -1)
    vmem = pl.BlockSpec(memory_space=pltpu.VMEM)
    piece = jax.ShapeDtypeStruct((rows, levels, half), field.dtype)
    table, near, far = pl.pallas_call(
        table_kernel,
        out_shape=[
            jax.ShapeDtypeStruct((2, 2, 2, 2, heads * QUERIES, LANES), jnp.float32),
            piece,
            piece,
        ],
        in_specs=[vmem, vmem],
        out_specs=[vmem] * 3,
        compiler_params=pltpu.CompilerParams(vmem_limit_bytes=VMEM_BYTES),
        cost_estimate=pl.CostEstimate(flops=4_000_000, bytes_accessed=6_000_000, transcendentals=0),
        name="bias_tables",
    )(earth_bias, field)
    anywhere = pl.BlockSpec(memory_space=pl.ANY)

    def pack(which, kept, *after):
        return pl.pallas_call(
            functools.partial(pack_kernel, which),
            out_shape=piece,
            in_specs=[vmem] * 2 + [anywhere] * len(after),
            out_specs=vmem,
            compiler_params=pltpu.CompilerParams(vmem_limit_bytes=VMEM_BYTES),
            cost_estimate=pl.CostEstimate(flops=0, bytes_accessed=250_000, transcendentals=0),
            name="pack_half",
        )(south, kept, *after)

    far = pack(1, far)
    near = pack(0, near, far)
    far_halo = swapped(far, "lon", 1)
    near_halo = swapped(near, "lon", 0)
    weights = (
        norm1_gain.reshape(1, chans),
        qkv_weight,
        proj_weight,
        norm2_gain.reshape(1, chans),
        fc1_weight,
        jnp.transpose(fc2_weight),
    )
    (near_done,) = run_side(
        near, near_halo, table, (0, 1), "near", weights, chans, heads, ()
    )
    far_low, send = run_side(
        far, far_halo, table, (1,), "low", weights, chans, heads, (near_done,)
    )
    top = moved(send, "lat", 1)
    far_high, done = run_side(
        far, far_halo, table, (0,), "high", weights, chans, heads, (near_done, far_low)
    )
    done = pl.pallas_call(
        last_kernel,
        out_shape=jax.ShapeDtypeStruct(done.shape, done.dtype),
        in_specs=[anywhere] * 3,
        out_specs=anywhere,
        scratch_shapes=[pltpu.SemaphoreType.DMA((3,))],
        input_output_aliases={2: 0},
        compiler_params=pltpu.CompilerParams(vmem_limit_bytes=VMEM_BYTES),
        cost_estimate=pl.CostEstimate(flops=0, bytes_accessed=200_000, transcendentals=0),
        name="last_rows",
    )(top, far_high, done)
    return jnp.transpose(done, (1, 0, 2))


def solution(mesh):
    in_specs = (P(None, "lat", "lon"), P(), P(), P(), P("lat", None, None, None), P(), P(), P())
    out_specs = P(None, "lat", "lon")
    return jax.shard_map(shards, mesh=mesh, in_specs=in_specs, out_specs=out_specs, check_vma=False)
```

```python
import functools

import jax
import jax.numpy as jnp
from jax import lax
from jax.experimental import pallas as pl
from jax.experimental.pallas import tpu as pltpu
from jax.sharding import PartitionSpec as P

LEVELS = 4
WIN_LEV = 2
WIN_LAT = 6
WIN_LON = 12
EDGE = WIN_LAT // 2
HALF = WIN_LON // 2
TOKENS = WIN_LEV * WIN_LAT * WIN_LON
QUERIES = TOKENS // 2
LOG2E = 1.4426950408889634
GELU_0 = 0.7978845608028654
GELU_1 = 0.044715 * GELU_0
LANES = 128
SPARE = 64
VMEM_BYTES = 8 * 2**20
NT = (((1,), (1,)), ((), ()))


def moved(x, axis, by):
    size = lax.axis_size(axis)
    return lax.ppermute(x, axis, [(i, (i + by) % size) for i in range(size)])


def swapped(x, axis, first):
    size = lax.axis_size(axis)
    pairs = []
    for i in range(first, size, 2):
        j = (i + 1) % size
        pairs += [(i, j), (j, i)]
    return lax.ppermute(x, axis, pairs)


def half_places(half):
    odd = lax.rem(lax.axis_index("lon"), 2)
    return pl.multiple_of((1 - odd) * half, LANES), pl.multiple_of(odd * half, LANES)


def pack_kernel(which, south_ref, kept_ref, *rest):
    piece_ref = rest[-1]
    at = half_places(piece_ref.shape[2])[which]
    rows = piece_ref.shape[0] - EDGE
    piece_ref[:rows] = kept_ref[:rows]
    piece_ref[rows:] = south_ref[:, :, pl.ds(at, piece_ref.shape[2])]


def last_kernel(top_ref, high_ref, done_ref, out_ref, sems):
    half = top_ref.shape[3]
    near_at, far_at = half_places(half)
    near_out, far_out = (out_ref.at[:, :, pl.ds(at, half)] for at in (near_at, far_at))
    copies = [
        pltpu.make_async_copy(top_ref.at[0], near_out.at[:EDGE], sems.at[0]),
        pltpu.make_async_copy(top_ref.at[1], far_out.at[:EDGE], sems.at[1]),
        pltpu.make_async_copy(high_ref, far_out.at[EDGE : EDGE + WIN_LAT], sems.at[2]),
    ]
    for copy in copies:
        copy.start()
    for copy in copies:
        copy.wait()


def table_kernel(count, *refs):
    bias_any, field_any, *weights_any = refs[: 2 + count]
    table_ref, near_ref, far_ref, *weights_ref = refs[2 + count : 5 + 2 * count]
    bias_ref, sems, side_sems = refs[5 + 2 * count :]
    windows, heads = bias_any.shape[:2]
    copies = {}
    for k in range(windows):
        for h in range(heads):
            target = bias_ref.at[k, pl.ds(2 * h, 2)]
            copies[k, h] = pltpu.make_async_copy(bias_any.at[k, h], target, sems.at[k, h])
            copies[k, h].start()
    rows, half = field_any.shape[0] - EDGE, near_ref.shape[2]
    near_at, far_at = half_places(half)
    fetches = [
        (field_any.at[EDGE:, :, pl.ds(far_at, half)], far_ref.at[:rows]),
        (field_any.at[EDGE:, :, pl.ds(near_at, half)], near_ref.at[:rows]),
    ]
    fetches += list(zip(weights_any, weights_ref))
    fetches = [
        pltpu.make_async_copy(source, target, side_sems.at[n])
        for n, (source, target) in enumerate(fetches)
    ]
    for copy in fetches:
        copy.start()
    width = 9 * LANES
    lane = lax.broadcasted_iota(jnp.int32, (8, LANES), 1)
    upper = lax.rem(lax.broadcasted_iota(jnp.int32, (8, LANES), 0), 2) == 1
    is_last = lax.axis_index("lat") == lax.axis_size("lat") - 1
    last = jnp.where(is_last, -1e9, 0.0).astype(jnp.float32)

    def penalty(first, lev, side, wrap):
        key = lane + first
        key_lev = (key >= QUERIES).astype(jnp.int32)
        key_side = ((key - key_lev * QUERIES) >= QUERIES // 2).astype(jnp.int32)
        out = jnp.where(upper & (key_lev != lev), -1e9, jnp.zeros((8, LANES), jnp.float32))
        if wrap:
            out = out + jnp.where(key_side != side, last, 0.0)
        return out

    for k in range(windows):
        masks = {
            (lev, side, part): penalty(part * LANES, lev, side, k == windows - 1)
            for lev in range(2)
            for side in range(2)
            for part in range(2)
        }
        for h in range(heads):
            copies[k, h].wait()
        for first in range(0, 2 * heads, 8):
            count = min(8, 2 * heads - first)
            for c in range(TOKENS // 8):
                tiles = []
                for u in range(9):
                    at = c * width + u * LANES
                    tiles.append(bias_ref[k, first : first + count, at : at + LANES] * LOG2E)
                for r in range(8):
                    i = 8 * c + r
                    shift = 16 * r
                    nxt = tiles[r + 1]
                    main = tiles[r]
                    if r:
                        main = pltpu.roll(main, LANES - shift, 1)
                        nxt = pltpu.roll(nxt, LANES - shift, 1)
                        main = jnp.where(lane[:count] < LANES - shift, main, nxt)
                    lev = i // QUERIES
                    row = i % QUERIES // WIN_LON
                    col = i % WIN_LON
                    side = col // HALF
                    place = first * QUERIES + lev * 36 + row * HALF + col % HALF
                    at = pl.ds(place, count, stride=QUERIES)
                    for part, piece in enumerate((main, nxt)):
                        mask = masks[lev, row // EDGE, part]
                        table_ref[k, 1 - side, part, at, :] = piece + mask[:count]
    for copy in fetches:
        copy.wait()


def layer_norm(values, gain):
    center = values - jnp.mean(values, axis=-1, keepdims=True)
    spread = jnp.mean(center * center, axis=-1, keepdims=True)
    return center * lax.rsqrt(spread + 1e-05) * gain


def gelu(x):
    half = 0.5 * x
    return half + half * jnp.tanh(x * (GELU_0 + GELU_1 * (x * x)))


def side_kernel(
    chans,
    heads,
    windows,
    part_of,
    own_piece,
    halo_piece,
    gain1_ref,
    qkv_ref,
    proj_ref,
    table_ref,
    gain2_ref,
    fc1_ref,
    fc2_ref,
    *rest,
):
    if part_of == "near":
        out_ref, keys_ref, own_ref, res_ref = rest
    elif part_of == "low":
        near_ref, out_ref, send_ref, keys_ref, own_ref, res_ref = rest
    else:
        near_ref, low_ref, out_ref, done_ref, keys_ref, own_ref, res_ref, sems = rest
        half = near_ref.shape[2]
        near_at, far_at = half_places(half)
        done_near = done_ref.at[:, :, pl.ds(near_at, half)]
        done_far = done_ref.at[:, :, pl.ds(far_at, half)]
        copies = [
            pltpu.make_async_copy(
                near_ref.at[: WIN_LAT + EDGE], done_near.at[EDGE:], sems.at[0]
            ),
            pltpu.make_async_copy(
                low_ref.at[:EDGE], done_far.at[WIN_LAT + EDGE :], sems.at[1]
            ),
        ]
        for copy in copies:
            copy.start()
    head_dim = chans // heads
    low = lax.broadcasted_iota(jnp.int32, (1, LANES), 1) < SPARE
    odd = lax.rem(lax.axis_index("lon"), 2)
    right = 1 - odd if part_of == "near" else odd
    halo_at = right * HALF
    own_at = HALF - halo_at

    def tokens_of(ref, at, first, count):
        both = [ref[at, part, first : first + count] for part in range(2)]
        return jnp.concatenate([both[0], both[1][:, : chans - LANES]], axis=1)

    def split(ref, row):
        for pair in range(HALF // 2):
            both = ref[row, :, pair * 2 * chans : (pair + 1) * 2 * chans].astype(jnp.float32)
            first, middle, final = (both[:, u * LANES : (u + 1) * LANES] for u in range(3))
            yield 2 * pair, (first, middle)
            middle, final = pltpu.roll(middle, SPARE, 1), pltpu.roll(final, SPARE, 1)
            yield 2 * pair + 1, (jnp.where(low, middle, final), final)

    for n in range(len(windows)):
        for row in range(WIN_LAT):
            for col, block in split(halo_piece, n * WIN_LAT + row):
                at = pl.ds(row * WIN_LON + col + halo_at, LEVELS, stride=QUERIES)
                for part in range(2):
                    keys_ref[n, part, at, :] = block[part]
            for col, block in split(own_piece, n * WIN_LAT + row):
                at = pl.ds(row * WIN_LON + col + own_at, LEVELS, stride=QUERIES)
                place = row * HALF + col
                for part in range(2):
                    keys_ref[n, part, at, :] = block[part]
                    own_ref[n, part, pl.ds(4 + place, LEVELS, stride=36), :] = block[part]
                    own_ref[n, part, pl.ds(148 + place, 1), :] = block[part][:1]

    gain1 = gain1_ref[...]
    lane = lax.broadcasted_iota(jnp.int32, (1, chans), 1)
    ones = jnp.ones((LEVELS * QUERIES, 2 * LANES - chans), jnp.float32)
    mixed = []
    for n in range(len(windows)):
        normed = layer_norm(tokens_of(keys_ref, n, 0, LEVELS * QUERIES), gain1)
        normed = jnp.concatenate([normed[QUERIES:], normed[:QUERIES]], axis=0)
        normed = normed.astype(jnp.bfloat16)
        keys = jnp.dot(normed, qkv_ref[:, chans : 2 * chans], preferred_element_type=jnp.float32)
        values = jnp.dot(normed, qkv_ref[:, 2 * chans :], preferred_element_type=jnp.float32)
        values = jnp.concatenate([values, ones], axis=1)
        own = layer_norm(tokens_of(own_ref, n, 40, 144), gain1).astype(jnp.bfloat16)
        query = jnp.dot(own, qkv_ref[:, :chans], preferred_element_type=jnp.float32)
        query = query * (head_dim ** (-0.5) * LOG2E)
        for p in range(2):
            q = query[p * QUERIES : (p + 1) * QUERIES]
            k = keys[p * TOKENS : (p + 1) * TOKENS].astype(jnp.bfloat16)
            v = values[p * TOKENS : (p + 1) * TOKENS].astype(jnp.bfloat16)
            picked = [
                jnp.where((lane >= h * head_dim) & (lane < (h + 1) * head_dim), q, 0.0)
                for h in range(heads)
            ]
            picked = jnp.concatenate(picked, axis=0).astype(jnp.bfloat16)
            scores = lax.dot_general(picked, k, NT, preferred_element_type=jnp.float32)
            table = []
            for part in range(2):
                firsts = [(2 * h + p) * QUERIES for h in range(heads)]
                pieces = [table_ref[windows[n], right, part, f : f + QUERIES] for f in firsts]
                table.append(jnp.concatenate(pieces, axis=0))
            table = jnp.concatenate([table[0], table[1][:, : TOKENS - LANES]], axis=1)
            scores = scores + table
            top = jnp.max(scores, axis=1, keepdims=True)
            probs = jnp.exp2(scores - top).astype(jnp.bfloat16)
            got = jnp.dot(probs, v, preferred_element_type=jnp.float32)
            out = jnp.zeros((QUERIES, chans), jnp.float32)
            for h in range(heads):
                part = got[h * QUERIES : (h + 1) * QUERIES]
                scaled = part[:, :chans] * (1.0 / part[:, chans : chans + 1])
                inside = (lane >= h * head_dim) & (lane < (h + 1) * head_dim)
                out = jnp.where(inside, scaled, out)
            mixed.append(out)
    mixed = jnp.concatenate(mixed, axis=0).astype(jnp.bfloat16)
    attn = jnp.dot(mixed, proj_ref[...], preferred_element_type=jnp.float32)
    attn = attn.astype(jnp.bfloat16).astype(jnp.float32)
    tokens = [tokens_of(own_ref, n, 40, 144) for n in range(len(windows))]
    resid = jnp.concatenate(tokens, axis=0) + attn
    resid = resid.astype(jnp.bfloat16).astype(jnp.float32)
    normed = layer_norm(resid, gain2_ref[...]).astype(jnp.bfloat16)
    hidden = jnp.dot(normed, fc1_ref[...], preferred_element_type=jnp.float32)
    hidden = gelu(hidden).astype(jnp.bfloat16)
    result = lax.dot_general(hidden, fc2_ref[...], NT, preferred_element_type=jnp.float32)
    result = resid + result
    for n in range(len(windows)):
        mine = result[n * 144 : (n + 1) * 144]
        for part, lanes in enumerate((slice(0, LANES), slice(LANES, chans))):
            width = min(LANES, chans - part * LANES)
            res_ref[n, part, 40:184, :width] = mine[:, lanes]
            res_ref[n, part, 0:40, :width] = mine[104:144, lanes]
        for row in range(WIN_LAT):
            for pair in range(HALF // 2):
                tiles = []
                for col in (2 * pair, 2 * pair + 1):
                    at = pl.ds(4 + row * HALF + col, LEVELS, stride=36)
                    tiles += [res_ref[n, part, at, :] for part in range(2)]
                shifted = [pltpu.roll(x, SPARE, 1) for x in tiles[2:]]
                tiles = [tiles[0], jnp.where(low, tiles[1], shifted[0])]
                tiles.append(jnp.where(low, shifted[0], shifted[1]))
                tiles = jnp.concatenate(tiles, axis=1).astype(jnp.bfloat16)
                out_ref[n * WIN_LAT + row, :, pair * 2 * chans : (pair + 1) * 2 * chans] = tiles
    if part_of == "low":
        send_ref[0] = near_ref[WIN_LAT + EDGE :]
        send_ref[1] = out_ref[EDGE:]
    elif part_of == "high":
        for copy in copies:
            copy.wait()


def run_side(own, halo, table, windows, part_of, weights, chans, heads, before):
    count = len(windows)
    first = windows[0]
    assert list(windows) == list(range(first, first + count)) and first % count == 0
    rows = count * WIN_LAT
    piece = pl.BlockSpec((rows,) + own.shape[1:], lambda _: (first // count, 0, 0))

    def whole(x):
        return pl.BlockSpec(x.shape, lambda _: (0,) * len(x.shape))

    anywhere = pl.BlockSpec(memory_space=pl.ANY)
    out = jax.ShapeDtypeStruct((rows,) + own.shape[1:], own.dtype)
    send = jax.ShapeDtypeStruct((2, EDGE) + own.shape[1:], own.dtype)
    done = jax.ShapeDtypeStruct(own.shape[:2] + (2 * own.shape[2],), own.dtype)
    outs = {"near": [out], "low": [out, send], "high": [out, done]}[part_of]
    extra = [pltpu.SemaphoreType.DMA((2,))]
    gain1, qkv, proj, gain2, fc1, fc2 = weights
    operands = (gain1, qkv, proj, table, gain2, fc1, fc2) + before
    return pl.pallas_call(
        functools.partial(side_kernel, chans, heads, windows, part_of),
        out_shape=outs,
        grid=(1,),
        in_specs=[piece, piece] + [whole(x) for x in operands],
        out_specs=[whole(out), anywhere] if part_of == "high" else [whole(x) for x in outs],
        scratch_shapes=[
            pltpu.VMEM((count, 2, LEVELS * QUERIES, LANES), jnp.float32),
            pltpu.VMEM((count, 2, 184, LANES), jnp.float32),
            pltpu.VMEM((count, 2, 184, LANES), jnp.float32),
        ]
        + (extra if part_of == "high" else []),
        compiler_params=pltpu.CompilerParams(vmem_limit_bytes=VMEM_BYTES),
        cost_estimate=pl.CostEstimate(
            flops=200_000_000 * count, bytes_accessed=3_000_000, transcendentals=250_000 * count
        ),
        name="swin_" + part_of,
    )(own, halo, *operands)


def shards(
    field_in, norm1_gain, qkv_weight, proj_weight, earth_bias, norm2_gain, fc1_weight, fc2_weight
):
    levels, rows, flat = field_in.shape
    chans = qkv_weight.shape[0]
    heads = earth_bias.shape[2]
    half = HALF * chans
    field = jnp.transpose(field_in, (1, 0, 2))
    south = moved(field[:EDGE], "lat", -1)
    weights = (
        norm1_gain.reshape(1, chans),
        qkv_weight,
        proj_weight,
        norm2_gain.reshape(1, chans),
        fc1_weight,
        jnp.transpose(fc2_weight),
    )
    vmem = pl.BlockSpec(memory_space=pltpu.VMEM)
    anywhere = pl.BlockSpec(memory_space=pl.ANY)
    piece = jax.ShapeDtypeStruct((rows, levels, half), field.dtype)
    table = jax.ShapeDtypeStruct((2, 2, 2, 2 * heads * QUERIES, LANES), jnp.float32)
    sources = (jnp.transpose(earth_bias, (0, 2, 1, 3)), field) + weights
    sources = [pltpu.with_memory_space_constraint(x, pltpu.HBM) for x in sources]
    outs = [table, piece, piece] + [jax.ShapeDtypeStruct(x.shape, x.dtype) for x in weights]
    table, near, far, *weights = pl.pallas_call(
        functools.partial(table_kernel, len(weights)),
        out_shape=outs,
        in_specs=[pl.BlockSpec(memory_space=pltpu.HBM)] * len(sources),
        out_specs=[vmem] * len(outs),
        scratch_shapes=[
            pltpu.VMEM((2, 2 * heads, earth_bias.shape[3]), jnp.float32),
            pltpu.SemaphoreType.DMA((2, heads)),
            pltpu.SemaphoreType.DMA((2 + len(weights),)),
        ],
        compiler_params=pltpu.CompilerParams(vmem_limit_bytes=VMEM_BYTES),
        cost_estimate=pl.CostEstimate(flops=4_000_000, bytes_accessed=6_000_000, transcendentals=0),
        name="bias_tables",
    )(*sources)

    def pack(which, kept, *after):
        return pl.pallas_call(
            functools.partial(pack_kernel, which),
            out_shape=piece,
            in_specs=[vmem] * 2 + [anywhere] * len(after),
            out_specs=vmem,
            compiler_params=pltpu.CompilerParams(vmem_limit_bytes=VMEM_BYTES),
            cost_estimate=pl.CostEstimate(flops=0, bytes_accessed=250_000, transcendentals=0),
            name="pack_half",
        )(south, kept, *after)

    far = pack(1, far)
    near = pack(0, near, far)
    far_halo = swapped(far, "lon", 1)
    near_halo = swapped(near, "lon", 0)
    (near_done,) = run_side(
        near, near_halo, table, (0, 1), "near", weights, chans, heads, ()
    )
    far_low, send = run_side(
        far, far_halo, table, (1,), "low", weights, chans, heads, (near_done,)
    )
    top = moved(send, "lat", 1)
    far_high, done = run_side(
        far, far_halo, table, (0,), "high", weights, chans, heads, (near_done, far_low)
    )
    done = pl.pallas_call(
        last_kernel,
        out_shape=jax.ShapeDtypeStruct(done.shape, done.dtype),
        in_specs=[anywhere] * 3,
        out_specs=anywhere,
        scratch_shapes=[pltpu.SemaphoreType.DMA((3,))],
        input_output_aliases={2: 0},
        compiler_params=pltpu.CompilerParams(vmem_limit_bytes=VMEM_BYTES),
        cost_estimate=pl.CostEstimate(flops=0, bytes_accessed=200_000, transcendentals=0),
        name="last_rows",
    )(top, far_high, done)
    return jnp.transpose(done, (1, 0, 2))


def solution(mesh):
    in_specs = (P(None, "lat", "lon"), P(), P(), P(), P("lat", None, None, None), P(), P(), P())
    out_specs = P(None, "lat", "lon")
    return jax.shard_map(shards, mesh=mesh, in_specs=in_specs, out_specs=out_specs, check_vma=False)
```

```python
import functools

import jax
import jax.numpy as jnp
from jax import lax
from jax.experimental import pallas as pl
from jax.experimental.pallas import tpu as pltpu
from jax.sharding import PartitionSpec as P

LEVELS = 4
WIN_LEV = 2
WIN_LAT = 6
WIN_LON = 12
EDGE = WIN_LAT // 2
HALF = WIN_LON // 2
TOKENS = WIN_LEV * WIN_LAT * WIN_LON
QUERIES = TOKENS // 2
LOG2E = 1.4426950408889634
GELU_0 = 0.7978845608028654
GELU_1 = 0.044715 * GELU_0
LANES = 128
SPARE = 64
VMEM_BYTES = 8 * 2**20
NT = (((1,), (1,)), ((), ()))


def moved(x, axis, by):
    size = lax.axis_size(axis)
    return lax.ppermute(x, axis, [(i, (i + by) % size) for i in range(size)])


def swapped(x, axis, first, ways=(True, True)):
    size = lax.axis_size(axis)
    pairs = []
    for i in range(first, size, 2):
        j = (i + 1) % size
        pairs += [(i, j)] * ways[0] + [(j, i)] * ways[1]
    return lax.ppermute(x, axis, pairs)


def half_places(half):
    odd = lax.rem(lax.axis_index("lon"), 2)
    return pl.multiple_of((1 - odd) * half, LANES), pl.multiple_of(odd * half, LANES)


def pack_kernel(which, south_ref, kept_ref, *rest):
    piece_ref = rest[-1]
    at = half_places(piece_ref.shape[2])[which]
    rows = piece_ref.shape[0] - EDGE
    piece_ref[:rows] = kept_ref[:rows]
    piece_ref[rows:] = south_ref[:, :, pl.ds(at, piece_ref.shape[2])]


def pick_kernel(even_ref, odd_ref, out_ref):
    odd = lax.rem(lax.axis_index("lon"), 2)

    @pl.when(odd == 0)
    def _():
        out_ref[...] = even_ref[...]

    @pl.when(odd == 1)
    def _():
        out_ref[...] = odd_ref[...]


def last_kernel(top_ref, high_ref, done_ref, out_ref, sems):
    half = top_ref.shape[3]
    near_at, far_at = half_places(half)
    near_out, far_out = (out_ref.at[:, :, pl.ds(at, half)] for at in (near_at, far_at))
    copies = [
        pltpu.make_async_copy(top_ref.at[0], near_out.at[:EDGE], sems.at[0]),
        pltpu.make_async_copy(top_ref.at[1], far_out.at[:EDGE], sems.at[1]),
        pltpu.make_async_copy(high_ref, far_out.at[EDGE : EDGE + WIN_LAT], sems.at[2]),
    ]
    for copy in copies:
        copy.start()
    for copy in copies:
        copy.wait()


def table_kernel(count, *refs):
    bias_any, field_any, *weights_any = refs[: 2 + count]
    table_ref, near_ref, far_ref, *weights_ref = refs[2 + count : 5 + 2 * count]
    bias_ref, sems, side_sems = refs[5 + 2 * count :]
    windows, heads = bias_any.shape[:2]
    copies = {}
    for k in range(windows):
        for h in range(heads):
            target = bias_ref.at[k, pl.ds(2 * h, 2)]
            copies[k, h] = pltpu.make_async_copy(bias_any.at[k, h], target, sems.at[k, h])
            copies[k, h].start()
    rows, half = field_any.shape[0] - EDGE, near_ref.shape[2]
    near_at, far_at = half_places(half)
    fetches = [
        (field_any.at[EDGE:, :, pl.ds(far_at, half)], far_ref.at[:rows]),
        (field_any.at[EDGE:, :, pl.ds(near_at, half)], near_ref.at[:rows]),
    ]
    fetches += list(zip(weights_any, weights_ref))
    fetches = [
        pltpu.make_async_copy(source, target, side_sems.at[n])
        for n, (source, target) in enumerate(fetches)
    ]
    for copy in fetches:
        copy.start()
    width = 9 * LANES
    lane = lax.broadcasted_iota(jnp.int32, (8, LANES), 1)
    upper = lax.rem(lax.broadcasted_iota(jnp.int32, (8, LANES), 0), 2) == 1
    is_last = lax.axis_index("lat") == lax.axis_size("lat") - 1
    last = jnp.where(is_last, -1e9, 0.0).astype(jnp.float32)

    def penalty(first, lev, side, wrap):
        key = lane + first
        key_lev = (key >= QUERIES).astype(jnp.int32)
        key_side = ((key - key_lev * QUERIES) >= QUERIES // 2).astype(jnp.int32)
        out = jnp.where(upper & (key_lev != lev), -1e9, jnp.zeros((8, LANES), jnp.float32))
        if wrap:
            out = out + jnp.where(key_side != side, last, 0.0)
        return out

    for k in range(windows):
        masks = {
            (lev, side, part): penalty(part * LANES, lev, side, k == windows - 1)
            for lev in range(2)
            for side in range(2)
            for part in range(2)
        }
        for first in range(0, 2 * heads, 8):
            count = min(8, 2 * heads - first)
            for h in range(first // 2, (first + count) // 2):
                copies[k, h].wait()
            for c in range(TOKENS // 8):
                tiles = []
                for u in range(9):
                    at = c * width + u * LANES
                    tiles.append(bias_ref[k, first : first + count, at : at + LANES] * LOG2E)
                for r in range(8):
                    i = 8 * c + r
                    shift = 16 * r
                    nxt = tiles[r + 1]
                    main = tiles[r]
                    if r:
                        main = pltpu.roll(main, LANES - shift, 1)
                        nxt = pltpu.roll(nxt, LANES - shift, 1)
                        main = jnp.where(lane[:count] < LANES - shift, main, nxt)
                    lev = i // QUERIES
                    row = i % QUERIES // WIN_LON
                    col = i % WIN_LON
                    side = col // HALF
                    place = first * QUERIES + lev * 36 + row * HALF + col % HALF
                    at = pl.ds(place, count, stride=QUERIES)
                    for part, piece in enumerate((main, nxt)):
                        mask = masks[lev, row // EDGE, part]
                        table_ref[k, 1 - side, part, at, :] = piece + mask[:count]
    for copy in fetches:
        copy.wait()


def layer_norm(values, gain):
    center = values - jnp.mean(values, axis=-1, keepdims=True)
    spread = jnp.mean(center * center, axis=-1, keepdims=True)
    return center * lax.rsqrt(spread + 1e-05) * gain


def gelu(x):
    half = 0.5 * x
    return half + half * jnp.tanh(x * (GELU_0 + GELU_1 * (x * x)))


def side_kernel(
    chans,
    heads,
    windows,
    part_of,
    own_piece,
    *rest,
):
    lon = lax.axis_index("lon")
    if part_of == "seam":
        halo_piece, *rest, far_in, out_ref, far_out, keys_ref, own_ref, res_ref = rest
        refs = rest + [out_ref, keys_ref, own_ref, res_ref]
        far_out[...] = far_in[...]

        @pl.when(lon == 0)
        def _():
            side_body(chans, heads, windows, "near", own_piece, halo_piece, *refs)

    elif part_of == "near":
        halo_piece, *rest, seam_ref, out_ref, keys_ref, own_ref, res_ref = rest
        refs = rest + [out_ref, keys_ref, own_ref, res_ref]

        @pl.when(lon != 0)
        def _():
            side_body(chans, heads, windows, "near", own_piece, halo_piece, *refs)

        @pl.when(lon == 0)
        def _():
            out_ref[...] = seam_ref[...]

    else:
        side_body(chans, heads, windows, part_of, own_piece, *rest)


def side_body(
    chans,
    heads,
    windows,
    part_of,
    own_piece,
    halo_piece,
    gain1_ref,
    qkv_ref,
    proj_ref,
    table_ref,
    gain2_ref,
    fc1_ref,
    fc2_ref,
    *rest,
):
    if part_of == "near":
        out_ref, keys_ref, own_ref, res_ref = rest
    elif part_of == "low":
        near_ref, out_ref, send_ref, keys_ref, own_ref, res_ref = rest
    else:
        near_ref, low_ref, out_ref, done_ref, keys_ref, own_ref, res_ref, sems = rest
        half = near_ref.shape[2]
        near_at, far_at = half_places(half)
        done_near = done_ref.at[:, :, pl.ds(near_at, half)]
        done_far = done_ref.at[:, :, pl.ds(far_at, half)]
        copies = [
            pltpu.make_async_copy(
                near_ref.at[: WIN_LAT + EDGE], done_near.at[EDGE:], sems.at[0]
            ),
            pltpu.make_async_copy(
                low_ref.at[:EDGE], done_far.at[WIN_LAT + EDGE :], sems.at[1]
            ),
        ]
        for copy in copies:
            copy.start()
    head_dim = chans // heads
    low = lax.broadcasted_iota(jnp.int32, (1, LANES), 1) < SPARE
    odd = lax.rem(lax.axis_index("lon"), 2)
    right = 1 - odd if part_of == "near" else odd
    halo_at = right * HALF
    own_at = HALF - halo_at

    def tokens_of(ref, at, first, count):
        both = [ref[at, part, first : first + count] for part in range(2)]
        return jnp.concatenate([both[0], both[1][:, : chans - LANES]], axis=1)

    def split(ref, row):
        for pair in range(HALF // 2):
            both = ref[row, :, pair * 2 * chans : (pair + 1) * 2 * chans].astype(jnp.float32)
            first, middle, final = (both[:, u * LANES : (u + 1) * LANES] for u in range(3))
            yield 2 * pair, (first, middle)
            middle, final = pltpu.roll(middle, SPARE, 1), pltpu.roll(final, SPARE, 1)
            yield 2 * pair + 1, (jnp.where(low, middle, final), final)

    for n in range(len(windows)):
        for row in range(WIN_LAT):
            for col, block in split(halo_piece, n * WIN_LAT + row):
                at = pl.ds(row * WIN_LON + col + halo_at, LEVELS, stride=QUERIES)
                for part in range(2):
                    keys_ref[n, part, at, :] = block[part]
            for col, block in split(own_piece, n * WIN_LAT + row):
                at = pl.ds(row * WIN_LON + col + own_at, LEVELS, stride=QUERIES)
                place = row * HALF + col
                for part in range(2):
                    keys_ref[n, part, at, :] = block[part]
                    own_ref[n, part, pl.ds(4 + place, LEVELS, stride=36), :] = block[part]
                    own_ref[n, part, pl.ds(148 + place, 1), :] = block[part][:1]

    gain1 = gain1_ref[...]
    lane = lax.broadcasted_iota(jnp.int32, (1, chans), 1)
    ones = jnp.ones((LEVELS * QUERIES, 2 * LANES - chans), jnp.float32)
    mixed = []
    for n in range(len(windows)):
        normed = layer_norm(tokens_of(keys_ref, n, 0, LEVELS * QUERIES), gain1)
        normed = jnp.concatenate([normed[QUERIES:], normed[:QUERIES]], axis=0)
        normed = normed.astype(jnp.bfloat16)
        keys = jnp.dot(normed, qkv_ref[:, chans : 2 * chans], preferred_element_type=jnp.float32)
        values = jnp.dot(normed, qkv_ref[:, 2 * chans :], preferred_element_type=jnp.float32)
        values = jnp.concatenate([values, ones], axis=1)
        own = layer_norm(tokens_of(own_ref, n, 40, 144), gain1).astype(jnp.bfloat16)
        query = jnp.dot(own, qkv_ref[:, :chans], preferred_element_type=jnp.float32)
        query = query * (head_dim ** (-0.5) * LOG2E)
        for p in range(2):
            q = query[p * QUERIES : (p + 1) * QUERIES]
            k = keys[p * TOKENS : (p + 1) * TOKENS].astype(jnp.bfloat16)
            v = values[p * TOKENS : (p + 1) * TOKENS].astype(jnp.bfloat16)
            picked = [
                jnp.where((lane >= h * head_dim) & (lane < (h + 1) * head_dim), q, 0.0)
                for h in range(heads)
            ]
            picked = jnp.concatenate(picked, axis=0).astype(jnp.bfloat16)
            scores = lax.dot_general(picked, k, NT, preferred_element_type=jnp.float32)
            table = []
            for part in range(2):
                firsts = [(2 * h + p) * QUERIES for h in range(heads)]
                pieces = [table_ref[windows[n], right, part, f : f + QUERIES] for f in firsts]
                table.append(jnp.concatenate(pieces, axis=0))
            table = jnp.concatenate([table[0], table[1][:, : TOKENS - LANES]], axis=1)
            scores = scores + table
            top = jnp.max(scores, axis=1, keepdims=True)
            probs = jnp.exp2(scores - top).astype(jnp.bfloat16)
            got = jnp.dot(probs, v, preferred_element_type=jnp.float32)
            out = jnp.zeros((QUERIES, chans), jnp.float32)
            for h in range(heads):
                part = got[h * QUERIES : (h + 1) * QUERIES]
                scaled = part[:, :chans] * (1.0 / part[:, chans : chans + 1])
                inside = (lane >= h * head_dim) & (lane < (h + 1) * head_dim)
                out = jnp.where(inside, scaled, out)
            mixed.append(out)
    mixed = jnp.concatenate(mixed, axis=0).astype(jnp.bfloat16)
    attn = jnp.dot(mixed, proj_ref[...], preferred_element_type=jnp.float32)
    attn = attn.astype(jnp.bfloat16).astype(jnp.float32)
    tokens = [tokens_of(own_ref, n, 40, 144) for n in range(len(windows))]
    resid = jnp.concatenate(tokens, axis=0) + attn
    resid = resid.astype(jnp.bfloat16).astype(jnp.float32)
    normed = layer_norm(resid, gain2_ref[...]).astype(jnp.bfloat16)
    hidden = jnp.dot(normed, fc1_ref[...], preferred_element_type=jnp.float32)
    hidden = gelu(hidden).astype(jnp.bfloat16)
    result = lax.dot_general(hidden, fc2_ref[...], NT, preferred_element_type=jnp.float32)
    result = resid + result
    for n in range(len(windows)):
        mine = result[n * 144 : (n + 1) * 144]
        for part, lanes in enumerate((slice(0, LANES), slice(LANES, chans))):
            width = min(LANES, chans - part * LANES)
            res_ref[n, part, 40:184, :width] = mine[:, lanes]
            res_ref[n, part, 0:40, :width] = mine[104:144, lanes]
        for row in range(WIN_LAT):
            for pair in range(HALF // 2):
                tiles = []
                for col in (2 * pair, 2 * pair + 1):
                    at = pl.ds(4 + row * HALF + col, LEVELS, stride=36)
                    tiles += [res_ref[n, part, at, :] for part in range(2)]
                shifted = [pltpu.roll(x, SPARE, 1) for x in tiles[2:]]
                tiles = [tiles[0], jnp.where(low, tiles[1], shifted[0])]
                tiles.append(jnp.where(low, shifted[0], shifted[1]))
                tiles = jnp.concatenate(tiles, axis=1).astype(jnp.bfloat16)
                out_ref[n * WIN_LAT + row, :, pair * 2 * chans : (pair + 1) * 2 * chans] = tiles
    if part_of == "low":
        send_ref[0] = near_ref[WIN_LAT + EDGE :]
        send_ref[1] = out_ref[EDGE:]
    elif part_of == "high":
        for copy in copies:
            copy.wait()


def run_side(own, halo, table, windows, part_of, weights, chans, heads, before):
    count = len(windows)
    first = windows[0]
    assert list(windows) == list(range(first, first + count)) and first % count == 0
    rows = count * WIN_LAT
    piece = pl.BlockSpec((rows,) + own.shape[1:], lambda _: (first // count, 0, 0))

    def whole(x):
        return pl.BlockSpec(x.shape, lambda _: (0,) * len(x.shape))

    anywhere = pl.BlockSpec(memory_space=pl.ANY)
    out = jax.ShapeDtypeStruct((rows,) + own.shape[1:], own.dtype)
    send = jax.ShapeDtypeStruct((2, EDGE) + own.shape[1:], own.dtype)
    done = jax.ShapeDtypeStruct(own.shape[:2] + (2 * own.shape[2],), own.dtype)
    outs = {"seam": [out, own], "near": [out], "low": [out, send], "high": [out, done]}[part_of]
    extra = [pltpu.SemaphoreType.DMA((2,))]
    gain1, qkv, proj, gain2, fc1, fc2 = weights
    operands = (gain1, qkv, proj, table, gain2, fc1, fc2) + before
    return pl.pallas_call(
        functools.partial(side_kernel, chans, heads, windows, part_of),
        out_shape=[jax.ShapeDtypeStruct(x.shape, x.dtype) for x in outs],
        grid=(1,),
        in_specs=[piece, piece] + [whole(x) for x in operands],
        out_specs=[whole(out), anywhere] if part_of == "high" else [whole(x) for x in outs],
        scratch_shapes=[
            pltpu.VMEM((count, 2, LEVELS * QUERIES, LANES), jnp.float32),
            pltpu.VMEM((count, 2, 184, LANES), jnp.float32),
            pltpu.VMEM((count, 2, 184, LANES), jnp.float32),
        ]
        + (extra if part_of == "high" else []),
        compiler_params=pltpu.CompilerParams(vmem_limit_bytes=VMEM_BYTES),
        cost_estimate=pl.CostEstimate(
            flops=200_000_000 * count, bytes_accessed=3_000_000, transcendentals=250_000 * count
        ),
        name="swin_" + part_of,
    )(own, halo, *operands)


def shards(
    field_in, norm1_gain, qkv_weight, proj_weight, earth_bias, norm2_gain, fc1_weight, fc2_weight
):
    levels, rows, flat = field_in.shape
    chans = qkv_weight.shape[0]
    heads = earth_bias.shape[2]
    half = HALF * chans
    field = jnp.transpose(field_in, (1, 0, 2))
    south = moved(field[:EDGE], "lat", -1)
    weights = (
        norm1_gain.reshape(1, chans),
        qkv_weight,
        proj_weight,
        norm2_gain.reshape(1, chans),
        fc1_weight,
        jnp.transpose(fc2_weight),
    )
    vmem = pl.BlockSpec(memory_space=pltpu.VMEM)
    anywhere = pl.BlockSpec(memory_space=pl.ANY)
    piece = jax.ShapeDtypeStruct((rows, levels, half), field.dtype)
    table = jax.ShapeDtypeStruct((2, 2, 2, 2 * heads * QUERIES, LANES), jnp.float32)
    sources = (jnp.transpose(earth_bias, (0, 2, 1, 3)), field) + weights
    sources = [pltpu.with_memory_space_constraint(x, pltpu.HBM) for x in sources]
    outs = [table, piece, piece] + [jax.ShapeDtypeStruct(x.shape, x.dtype) for x in weights]
    table, near, far, *weights = pl.pallas_call(
        functools.partial(table_kernel, len(weights)),
        out_shape=outs,
        in_specs=[pl.BlockSpec(memory_space=pltpu.HBM)] * len(sources),
        out_specs=[vmem] * len(outs),
        scratch_shapes=[
            pltpu.VMEM((2, 2 * heads, earth_bias.shape[3]), jnp.float32),
            pltpu.SemaphoreType.DMA((2, heads)),
            pltpu.SemaphoreType.DMA((2 + len(weights),)),
        ],
        compiler_params=pltpu.CompilerParams(vmem_limit_bytes=VMEM_BYTES),
        cost_estimate=pl.CostEstimate(flops=4_000_000, bytes_accessed=6_000_000, transcendentals=0),
        name="bias_tables",
    )(*sources)

    def pack(which, kept, *after):
        return pl.pallas_call(
            functools.partial(pack_kernel, which),
            out_shape=piece,
            in_specs=[vmem] * 2 + [anywhere] * len(after),
            out_specs=vmem,
            compiler_params=pltpu.CompilerParams(vmem_limit_bytes=VMEM_BYTES),
            cost_estimate=pl.CostEstimate(flops=0, bytes_accessed=250_000, transcendentals=0),
            name="pack_half",
        )(south, kept, *after)

    def pick(even, odd):
        return pl.pallas_call(
            pick_kernel,
            out_shape=piece,
            in_specs=[vmem] * 2,
            out_specs=vmem,
            compiler_params=pltpu.CompilerParams(vmem_limit_bytes=VMEM_BYTES),
            cost_estimate=pl.CostEstimate(flops=0, bytes_accessed=350_000, transcendentals=0),
            name="pick_halo",
        )(even, odd)

    far = pack(1, far)
    near = pack(0, near, far)
    near_halo = swapped(near, "lon", 0)
    halo_even = swapped(far, "lon", 1, (True, False))
    seam_done, far_later = run_side(
        near, near_halo, table, (0, 1), "seam", weights, chans, heads, (far,)
    )
    halo_odd = swapped(far_later, "lon", 1, (False, True))
    (near_done,) = run_side(
        near, near_halo, table, (0, 1), "near", weights, chans, heads, (seam_done,)
    )
    far_halo = pick(halo_even, halo_odd)
    far_low, send = run_side(
        far, far_halo, table, (1,), "low", weights, chans, heads, (near_done,)
    )
    top = moved(send, "lat", 1)
    far_high, done = run_side(
        far, far_halo, table, (0,), "high", weights, chans, heads, (near_done, far_low)
    )
    done = pl.pallas_call(
        last_kernel,
        out_shape=jax.ShapeDtypeStruct(done.shape, done.dtype),
        in_specs=[anywhere] * 3,
        out_specs=anywhere,
        scratch_shapes=[pltpu.SemaphoreType.DMA((3,))],
        input_output_aliases={2: 0},
        compiler_params=pltpu.CompilerParams(vmem_limit_bytes=VMEM_BYTES),
        cost_estimate=pl.CostEstimate(flops=0, bytes_accessed=200_000, transcendentals=0),
        name="last_rows",
    )(top, far_high, done)
    return jnp.transpose(done, (1, 0, 2))


def solution(mesh):
    in_specs = (P(None, "lat", "lon"), P(), P(), P(), P("lat", None, None, None), P(), P(), P())
    out_specs = P(None, "lat", "lon")
    return jax.shard_map(shards, mesh=mesh, in_specs=in_specs, out_specs=out_specs, check_vma=False)
```

```python
import functools

import jax
import jax.numpy as jnp
from jax import lax
from jax.experimental import pallas as pl
from jax.experimental.pallas import tpu as pltpu
from jax.sharding import PartitionSpec as P

LEVELS = 4
WIN_LEV = 2
WIN_LAT = 6
WIN_LON = 12
EDGE = WIN_LAT // 2
HALF = WIN_LON // 2
TOKENS = WIN_LEV * WIN_LAT * WIN_LON
QUERIES = TOKENS // 2
LOG2E = 1.4426950408889634
GELU_0 = 0.7978845608028654
GELU_1 = 0.044715 * GELU_0
LANES = 128
SPARE = 64
VMEM_BYTES = 8 * 2**20
NT = (((1,), (1,)), ((), ()))


def moved(x, axis, by):
    size = lax.axis_size(axis)
    return lax.ppermute(x, axis, [(i, (i + by) % size) for i in range(size)])


def swapped(x, axis, first):
    size = lax.axis_size(axis)
    pairs = []
    for i in range(first, size, 2):
        j = (i + 1) % size
        pairs += [(i, j), (j, i)]
    return lax.ppermute(x, axis, pairs)


def half_places(half):
    odd = lax.rem(lax.axis_index("lon"), 2)
    return pl.multiple_of((1 - odd) * half, LANES), pl.multiple_of(odd * half, LANES)


def pack_kernel(which, south_ref, kept_ref, *rest):
    piece_ref = rest[-1]
    at = half_places(piece_ref.shape[2])[which]
    rows = piece_ref.shape[0] - EDGE
    piece_ref[:rows] = kept_ref[:rows]
    piece_ref[rows:] = south_ref[:, :, pl.ds(at, piece_ref.shape[2])]


def last_kernel(top_ref, high_ref, near_low_ref, far_low_ref, out_ref, sems):
    half = top_ref.shape[3]
    copies = []
    for n, at in enumerate(half_places(half)):
        target = out_ref.at[:, :, pl.ds(at, half)]
        low_ref = (near_low_ref, far_low_ref)[n]
        for source, first in (
            (high_ref.at[n], EDGE),
            (low_ref.at[0, :EDGE], EDGE + WIN_LAT),
            (top_ref.at[n], 0),
        ):
            rows = pl.ds(first, source.shape[0])
            copy = pltpu.make_async_copy(source, target.at[rows], sems.at[len(copies)])
            copy.start()
            copies.append(copy)
    for copy in copies:
        copy.wait()


def table_kernel(count, *refs):
    bias_any, field_any, *weights_any = refs[: 2 + count]
    table_ref, near_ref, far_ref, *weights_ref = refs[2 + count : 5 + 2 * count]
    bias_ref, sems, side_sems = refs[5 + 2 * count :]
    windows, heads, tiles = bias_any.shape[:3]
    lines = bias_ref.shape[0]
    flat = bias_any.reshape(lines, LANES)
    parts = 2 * windows
    copies = []
    for n in range(parts):
        at = pl.ds(n * (lines // parts), lines // parts)
        copies.append(pltpu.make_async_copy(flat.at[at], bias_ref.at[at], sems.at[n]))
        copies[-1].start()
    rows, half = field_any.shape[0] - EDGE, near_ref.shape[2]
    near_at, far_at = half_places(half)
    fetches = [
        (field_any.at[EDGE:, :, pl.ds(far_at, half)], far_ref.at[:rows]),
        (field_any.at[EDGE:, :, pl.ds(near_at, half)], near_ref.at[:rows]),
    ]
    fetches += list(zip(weights_any, weights_ref))
    fetches = [
        pltpu.make_async_copy(source, target, side_sems.at[n])
        for n, (source, target) in enumerate(fetches)
    ]
    for copy in fetches:
        copy.start()
    blocks = WIN_LEV * WIN_LAT // 2
    lane = lax.broadcasted_iota(jnp.int32, (blocks, LANES), 1)
    block = lax.broadcasted_iota(jnp.int32, (blocks, LANES), 0)
    is_last = lax.axis_index("lat") == lax.axis_size("lat") - 1
    last = jnp.where(is_last, -1e9, 0.0).astype(jnp.float32)

    def penalty(part, second, levels, wrap):
        key = lane + part * LANES
        key_lev = key // QUERIES
        key_side = (key - key_lev * QUERIES) // (QUERIES // 2)
        row = 2 * block + second
        lev = row // WIN_LAT
        side = (row - lev * WIN_LAT) // EDGE
        out = jnp.zeros((blocks, LANES), jnp.float32)
        if levels:
            out = jnp.where(key_lev != lev, -1e9, out)
        if wrap:
            out = out + jnp.where(key_side != side, last, 0.0)
        return out

    for k in range(windows):
        masks = {
            (p, part, second): penalty(part, second, p == 1, k == windows - 1)
            for p in range(2)
            for part in range(2)
            for second in range(2)
        }
        for h in range(heads):
            if h % (heads // 2) == 0:
                copies[2 * k + h // (heads // 2)].wait()
            for p in range(2):
                base = (k * heads + h) * 2 * tiles + p
                for third in range(3):
                    line = base + third * 18
                    pieces = [
                        bias_ref[pl.ds(line + 2 * u, blocks, stride=54), :] * LOG2E
                        for u in range(9)
                    ]
                    for r in range(8):
                        shift = 16 * r
                        main, nxt = pieces[r], pieces[r + 1]
                        if r:
                            main = pltpu.roll(main, LANES - shift, 1)
                            nxt = pltpu.roll(nxt, LANES - shift, 1)
                            main = jnp.where(lane < LANES - shift, main, nxt)
                        second, col = divmod(8 * third + r, WIN_LON)
                        side = col // HALF
                        place = h * QUERIES + HALF * second + col % HALF
                        at = pl.ds(place, blocks, stride=WIN_LON)
                        for part, piece in enumerate((main, nxt)):
                            filled = piece + masks[p, part, second]
                            table_ref[k, p, 1 - side, part, at, :] = filled
    for copy in fetches:
        copy.wait()


def layer_norm(values, gain):
    center = values - jnp.mean(values, axis=-1, keepdims=True)
    spread = jnp.mean(center * center, axis=-1, keepdims=True)
    return center * lax.rsqrt(spread + 1e-05) * gain


def gelu(x):
    half = 0.5 * x
    return half + half * jnp.tanh(x * (GELU_0 + GELU_1 * (x * x)))


def units_kernel(chans, heads, units, lower, *refs):
    count = len(units)
    pieces, refs = refs[: 2 * count], refs[2 * count :]
    gain1_ref, qkv_ref, proj_ref, gain2_ref, fc1_ref, fc2_ref, table_ref, *refs = refs
    if lower:
        lower_ref, out_ref, send_ref, keys_ref, own_ref, res_ref = refs
    else:
        out_ref, keys_ref, own_ref, res_ref = refs
    head_dim = chans // heads
    low = lax.broadcasted_iota(jnp.int32, (1, LANES), 1) < SPARE
    odd = lax.rem(lax.axis_index("lon"), 2)
    rights = [1 - odd if near else odd for near, _ in units]

    def tokens_of(ref, at, first, count):
        both = [ref[at, part, first : first + count] for part in range(2)]
        return jnp.concatenate([both[0], both[1][:, : chans - LANES]], axis=1)

    def split(ref, row):
        for pair in range(HALF // 2):
            both = ref[row, :, pair * 2 * chans : (pair + 1) * 2 * chans].astype(jnp.float32)
            first, middle, final = (both[:, u * LANES : (u + 1) * LANES] for u in range(3))
            yield 2 * pair, (first, middle)
            middle, final = pltpu.roll(middle, SPARE, 1), pltpu.roll(final, SPARE, 1)
            yield 2 * pair + 1, (jnp.where(low, middle, final), final)

    for n, (_, window) in enumerate(units):
        own_piece, halo_piece = pieces[2 * n], pieces[2 * n + 1]
        halo_at = rights[n] * HALF
        own_at = HALF - halo_at
        for row in range(WIN_LAT):
            for col, block in split(halo_piece, window * WIN_LAT + row):
                at = pl.ds(row * WIN_LON + col + halo_at, LEVELS, stride=QUERIES)
                for part in range(2):
                    keys_ref[n, part, at, :] = block[part]
            for col, block in split(own_piece, window * WIN_LAT + row):
                at = pl.ds(row * WIN_LON + col + own_at, LEVELS, stride=QUERIES)
                place = row * HALF + col
                for part in range(2):
                    keys_ref[n, part, at, :] = block[part]
                    own_ref[n, part, pl.ds(4 + place, LEVELS, stride=36), :] = block[part]
                    own_ref[n, part, pl.ds(148 + place, 1), :] = block[part][:1]

    gain1 = gain1_ref[...]
    lane = lax.broadcasted_iota(jnp.int32, (1, chans), 1)
    ones = jnp.ones((LEVELS * QUERIES, 2 * LANES - chans), jnp.float32)
    mixed = []
    for n, (_, window) in enumerate(units):
        normed = layer_norm(tokens_of(keys_ref, n, 0, LEVELS * QUERIES), gain1)
        normed = jnp.concatenate([normed[QUERIES:], normed[:QUERIES]], axis=0)
        normed = normed.astype(jnp.bfloat16)
        keys = jnp.dot(normed, qkv_ref[:, chans : 2 * chans], preferred_element_type=jnp.float32)
        values = jnp.dot(normed, qkv_ref[:, 2 * chans :], preferred_element_type=jnp.float32)
        values = jnp.concatenate([values, ones], axis=1)
        own = layer_norm(tokens_of(own_ref, n, 40, 144), gain1).astype(jnp.bfloat16)
        query = jnp.dot(own, qkv_ref[:, :chans], preferred_element_type=jnp.float32)
        query = query * (head_dim ** (-0.5) * LOG2E)
        for p in range(2):
            q = query[p * QUERIES : (p + 1) * QUERIES]
            k = keys[p * TOKENS : (p + 1) * TOKENS].astype(jnp.bfloat16)
            v = values[p * TOKENS : (p + 1) * TOKENS].astype(jnp.bfloat16)
            picked = [
                jnp.where((lane >= h * head_dim) & (lane < (h + 1) * head_dim), q, 0.0)
                for h in range(heads)
            ]
            picked = jnp.concatenate(picked, axis=0).astype(jnp.bfloat16)
            scores = lax.dot_general(picked, k, NT, preferred_element_type=jnp.float32)
            table = [table_ref[window, p, rights[n], part] for part in range(2)]
            table = jnp.concatenate([table[0], table[1][:, : TOKENS - LANES]], axis=1)
            scores = scores + table
            top = jnp.max(scores, axis=1, keepdims=True)
            probs = jnp.exp2(scores - top).astype(jnp.bfloat16)
            got = jnp.dot(probs, v, preferred_element_type=jnp.float32)
            out = jnp.zeros((QUERIES, chans), jnp.float32)
            for h in range(heads):
                part = got[h * QUERIES : (h + 1) * QUERIES]
                scaled = part[:, :chans] * (1.0 / part[:, chans : chans + 1])
                inside = (lane >= h * head_dim) & (lane < (h + 1) * head_dim)
                out = jnp.where(inside, scaled, out)
            mixed.append(out)
    mixed = jnp.concatenate(mixed, axis=0).astype(jnp.bfloat16)
    attn = jnp.dot(mixed, proj_ref[...], preferred_element_type=jnp.float32)
    attn = attn.astype(jnp.bfloat16).astype(jnp.float32)
    tokens = [tokens_of(own_ref, n, 40, 144) for n in range(count)]
    resid = jnp.concatenate(tokens, axis=0) + attn
    resid = resid.astype(jnp.bfloat16).astype(jnp.float32)
    normed = layer_norm(resid, gain2_ref[...]).astype(jnp.bfloat16)
    hidden = jnp.dot(normed, fc1_ref[...], preferred_element_type=jnp.float32)
    hidden = gelu(hidden).astype(jnp.bfloat16)
    result = lax.dot_general(hidden, fc2_ref[...], NT, preferred_element_type=jnp.float32)
    result = resid + result
    for n in range(count):
        mine = result[n * 144 : (n + 1) * 144]
        for part, lanes in enumerate((slice(0, LANES), slice(LANES, chans))):
            width = min(LANES, chans - part * LANES)
            res_ref[n, part, 40:184, :width] = mine[:, lanes]
            res_ref[n, part, 0:40, :width] = mine[104:144, lanes]
        for row in range(WIN_LAT):
            for pair in range(HALF // 2):
                tiles = []
                for col in (2 * pair, 2 * pair + 1):
                    at = pl.ds(4 + row * HALF + col, LEVELS, stride=36)
                    tiles += [res_ref[n, part, at, :] for part in range(2)]
                shifted = [pltpu.roll(x, SPARE, 1) for x in tiles[2:]]
                tiles = [tiles[0], jnp.where(low, tiles[1], shifted[0])]
                tiles.append(jnp.where(low, shifted[0], shifted[1]))
                tiles = jnp.concatenate(tiles, axis=1).astype(jnp.bfloat16)
                out_ref[n, row, :, pair * 2 * chans : (pair + 1) * 2 * chans] = tiles
    if lower:
        send_ref[0] = lower_ref[0, EDGE:]
        send_ref[1] = out_ref[0, EDGE:]


def run_units(units, near, far, table, weights, chans, heads, *lower):
    count = len(units)
    pieces = [x for is_near, _ in units for x in (near if is_near else far)]
    piece = pieces[0]
    out = jax.ShapeDtypeStruct((count, WIN_LAT) + piece.shape[1:], piece.dtype)
    send = jax.ShapeDtypeStruct((2, EDGE) + piece.shape[1:], piece.dtype)
    operands = (*pieces, *weights, table, *lower)
    vmem = pl.BlockSpec(memory_space=pltpu.VMEM)
    outs = [out, send] if lower else [out]
    return pl.pallas_call(
        functools.partial(units_kernel, chans, heads, units, bool(lower)),
        out_shape=outs,
        in_specs=[vmem] * len(operands),
        out_specs=[vmem] * len(outs),
        scratch_shapes=[
            pltpu.VMEM((count, 2, LEVELS * QUERIES, LANES), jnp.float32),
            pltpu.VMEM((count, 2, 184, LANES), jnp.float32),
            pltpu.VMEM((count, 2, 184, LANES), jnp.float32),
        ],
        compiler_params=pltpu.CompilerParams(vmem_limit_bytes=VMEM_BYTES),
        cost_estimate=pl.CostEstimate(
            flops=200_000_000 * count, bytes_accessed=3_000_000, transcendentals=250_000 * count
        ),
        name="swin_windows",
    )(*operands)


def shards(
    field_in, norm1_gain, qkv_weight, proj_weight, earth_bias, norm2_gain, fc1_weight, fc2_weight
):
    levels, rows, flat = field_in.shape
    chans = qkv_weight.shape[0]
    heads = earth_bias.shape[2]
    half = HALF * chans
    field = jnp.transpose(field_in, (1, 0, 2))
    south = moved(field[:EDGE], "lat", -1)
    weights = (
        norm1_gain.reshape(1, chans),
        qkv_weight,
        proj_weight,
        norm2_gain.reshape(1, chans),
        fc1_weight,
        jnp.transpose(fc2_weight),
    )
    vmem = pl.BlockSpec(memory_space=pltpu.VMEM)
    anywhere = pl.BlockSpec(memory_space=pl.ANY)
    piece = jax.ShapeDtypeStruct((rows, levels, half), field.dtype)
    table = jax.ShapeDtypeStruct((2, 2, 2, 2, heads * QUERIES, LANES), jnp.float32)
    windows, zwin, _, entries = earth_bias.shape
    tiles = entries // LANES
    bias = earth_bias.reshape(windows, zwin, heads, tiles, LANES).transpose(0, 2, 3, 1, 4)
    sources = (bias, field) + weights
    sources = [pltpu.with_memory_space_constraint(x, pltpu.HBM) for x in sources]
    outs = [table, piece, piece] + [jax.ShapeDtypeStruct(x.shape, x.dtype) for x in weights]
    table, near, far, *weights = pl.pallas_call(
        functools.partial(table_kernel, len(weights)),
        out_shape=outs,
        in_specs=[pl.BlockSpec(memory_space=pltpu.HBM)] * len(sources),
        out_specs=[vmem] * len(outs),
        scratch_shapes=[
            pltpu.VMEM((bias.size // LANES, LANES), jnp.float32),
            pltpu.SemaphoreType.DMA((2 * windows,)),
            pltpu.SemaphoreType.DMA((2 + len(weights),)),
        ],
        compiler_params=pltpu.CompilerParams(vmem_limit_bytes=VMEM_BYTES),
        cost_estimate=pl.CostEstimate(flops=4_000_000, bytes_accessed=6_000_000, transcendentals=0),
        name="bias_tables",
    )(*sources)

    def pack(which, kept, *after):
        return pl.pallas_call(
            functools.partial(pack_kernel, which),
            out_shape=piece,
            in_specs=[vmem] * 2 + [anywhere] * len(after),
            out_specs=vmem,
            compiler_params=pltpu.CompilerParams(vmem_limit_bytes=VMEM_BYTES),
            cost_estimate=pl.CostEstimate(flops=0, bytes_accessed=250_000, transcendentals=0),
            name="pack_half",
        )(south, kept, *after)

    far = pack(1, far)
    near = pack(0, near, far)
    far_halo = swapped(far, "lon", 1)
    near_halo = swapped(near, "lon", 0)
    near, far = (near, near_halo), (far, far_halo)
    common = (near, far, table, weights, chans, heads)
    (near_low,) = run_units(((True, 1),), *common)
    far_low, send = run_units(((False, 1),), *common, near_low)
    top = moved(send, "lat", 1)
    (high,) = run_units(((True, 0), (False, 0)), *common)
    done = pl.pallas_call(
        last_kernel,
        out_shape=jax.ShapeDtypeStruct(field.shape, field.dtype),
        in_specs=[vmem] * 4,
        out_specs=anywhere,
        scratch_shapes=[pltpu.SemaphoreType.DMA((6,))],
        compiler_params=pltpu.CompilerParams(vmem_limit_bytes=VMEM_BYTES),
        cost_estimate=pl.CostEstimate(flops=0, bytes_accessed=400_000, transcendentals=0),
        name="last_rows",
    )(top, high, near_low, far_low)
    return jnp.transpose(done, (1, 0, 2))


def solution(mesh):
    in_specs = (P(None, "lat", "lon"), P(), P(), P(), P("lat", None, None, None), P(), P(), P())
    out_specs = P(None, "lat", "lon")
    return jax.shard_map(shards, mesh=mesh, in_specs=in_specs, out_specs=out_specs, check_vma=False)
```

```python
import functools

import jax
import jax.numpy as jnp
from jax import lax
from jax.experimental import pallas as pl
from jax.experimental.pallas import tpu as pltpu
from jax.sharding import PartitionSpec as P

LEVELS = 4
WIN_LEV = 2
WIN_LAT = 6
WIN_LON = 12
EDGE = WIN_LAT // 2
HALF = WIN_LON // 2
TOKENS = WIN_LEV * WIN_LAT * WIN_LON
QUERIES = TOKENS // 2
LOG2E = 1.4426950408889634
GELU_0 = 0.7978845608028654
GELU_1 = 0.044715 * GELU_0
LANES = 128
SPARE = 64
VMEM_BYTES = 8 * 2**20
NT = (((1,), (1,)), ((), ()))


def moved(x, axis, by):
    size = lax.axis_size(axis)
    return lax.ppermute(x, axis, [(i, (i + by) % size) for i in range(size)])


def swapped(x, axis, first):
    size = lax.axis_size(axis)
    pairs = []
    for i in range(first, size, 2):
        j = (i + 1) % size
        pairs += [(i, j), (j, i)]
    return lax.ppermute(x, axis, pairs)


def half_places(half):
    odd = lax.rem(lax.axis_index("lon"), 2)
    return pl.multiple_of((1 - odd) * half, LANES), pl.multiple_of(odd * half, LANES)


def pack_kernel(which, south_ref, kept_ref, *rest):
    piece_ref = rest[-1]
    at = half_places(piece_ref.shape[2])[which]
    rows = piece_ref.shape[0] - EDGE
    piece_ref[:rows] = kept_ref[:rows]
    piece_ref[rows:] = south_ref[:, :, pl.ds(at, piece_ref.shape[2])]


def last_kernel(top_ref, high_ref, near_low_ref, far_low_ref, out_ref, sems):
    half = top_ref.shape[3]
    copies = []
    for n, at in enumerate(half_places(half)):
        target = out_ref.at[:, :, pl.ds(at, half)]
        low_ref = (near_low_ref, far_low_ref)[n]
        for source, first in (
            (high_ref.at[n], EDGE),
            (low_ref.at[0, :EDGE], EDGE + WIN_LAT),
            (top_ref.at[n], 0),
        ):
            rows = pl.ds(first, source.shape[0])
            copy = pltpu.make_async_copy(source, target.at[rows], sems.at[len(copies)])
            copy.start()
            copies.append(copy)
    for copy in copies:
        copy.wait()


def table_kernel(count, *refs):
    bias_any, field_any, *weights_any = refs[: 2 + count]
    table_ref, near_ref, far_ref, *weights_ref = refs[2 + count : 5 + 2 * count]
    bias_ref, sems, side_sems = refs[5 + 2 * count :]
    windows, heads, tiles = bias_any.shape[:3]
    lines = bias_ref.shape[0]
    flat = bias_any.reshape(lines, LANES)
    parts = heads * windows
    copies = []
    for n in range(parts):
        at = pl.ds(n * (lines // parts), lines // parts)
        copies.append(pltpu.make_async_copy(flat.at[at], bias_ref.at[at], sems.at[n]))
        copies[-1].start()
    rows, half = field_any.shape[0] - EDGE, near_ref.shape[2]
    near_at, far_at = half_places(half)
    fetches = [
        (field_any.at[EDGE:, :, pl.ds(far_at, half)], far_ref.at[:rows]),
        (field_any.at[EDGE:, :, pl.ds(near_at, half)], near_ref.at[:rows]),
    ]
    fetches += list(zip(weights_any, weights_ref))
    fetches = [
        pltpu.make_async_copy(source, target, side_sems.at[n])
        for n, (source, target) in enumerate(fetches)
    ]
    for copy in fetches:
        copy.start()
    blocks = WIN_LEV * WIN_LAT // 2
    lane = lax.broadcasted_iota(jnp.int32, (blocks, LANES), 1)
    block = lax.broadcasted_iota(jnp.int32, (blocks, LANES), 0)
    is_last = lax.axis_index("lat") == lax.axis_size("lat") - 1
    last = jnp.where(is_last, -1e9, 0.0).astype(jnp.float32)

    def penalty(part, second, levels, wrap):
        key = lane + part * LANES
        key_lev = key // QUERIES
        key_side = (key - key_lev * QUERIES) // (QUERIES // 2)
        row = 2 * block + second
        lev = row // WIN_LAT
        side = (row - lev * WIN_LAT) // EDGE
        out = jnp.zeros((blocks, LANES), jnp.float32)
        if levels:
            out = jnp.where(key_lev != lev, -1e9, out)
        if wrap:
            out = out + jnp.where(key_side != side, last, 0.0)
        return out

    for k in range(windows):
        masks = {
            (p, part, second): penalty(part, second, p == 1, k == windows - 1)
            for p in range(2)
            for part in range(2)
            for second in range(2)
        }
        for h in range(heads):
            copies[k * heads + h].wait()
            for p in range(2):
                base = (k * heads + h) * 2 * tiles + p
                for third in range(3):
                    line = base + third * 18
                    pieces = [
                        bias_ref[pl.ds(line + 2 * u, blocks, stride=54), :] * LOG2E
                        for u in range(9)
                    ]
                    for r in range(8):
                        shift = 16 * r
                        main, nxt = pieces[r], pieces[r + 1]
                        if r:
                            main = pltpu.roll(main, LANES - shift, 1)
                            nxt = pltpu.roll(nxt, LANES - shift, 1)
                            main = jnp.where(lane < LANES - shift, main, nxt)
                        second, col = divmod(8 * third + r, WIN_LON)
                        side = col // HALF
                        place = h * QUERIES + HALF * second + col % HALF
                        at = pl.ds(place, blocks, stride=WIN_LON)
                        for part, piece in enumerate((main, nxt)):
                            filled = piece + masks[p, part, second]
                            table_ref[k, p, 1 - side, part, at, :] = filled
    for copy in fetches:
        copy.wait()


def layer_norm(values, gain):
    chans = values.shape[1]
    ones = jnp.ones((chans, chans), jnp.bfloat16)

    def mean(x):
        total = jnp.dot(x.astype(jnp.bfloat16), ones, preferred_element_type=jnp.float32)
        return total * (1.0 / chans)

    center = values - mean(values)
    return center * lax.rsqrt(mean(center * center) + 1e-05) * gain


def gelu(x):
    half = 0.5 * x
    return half + half * jnp.tanh(x * (GELU_0 + GELU_1 * (x * x)))


def units_kernel(chans, heads, units, lower, *refs):
    count = len(units)
    pieces, refs = refs[: 2 * count], refs[2 * count :]
    gain1_ref, qkv_ref, proj_ref, gain2_ref, fc1_ref, fc2_ref, table_ref, *refs = refs
    if lower:
        lower_ref, out_ref, send_ref, keys_ref, own_ref, res_ref = refs
    else:
        out_ref, keys_ref, own_ref, res_ref = refs
    head_dim = chans // heads
    low = lax.broadcasted_iota(jnp.int32, (1, LANES), 1) < SPARE
    odd = lax.rem(lax.axis_index("lon"), 2)
    rights = [1 - odd if near else odd for near, _ in units]

    def tokens_of(ref, at, first, count):
        both = [ref[at, part, first : first + count] for part in range(2)]
        return jnp.concatenate([both[0], both[1][:, : chans - LANES]], axis=1)

    def split(ref, row):
        for pair in range(HALF // 2):
            both = ref[row, :, pair * 2 * chans : (pair + 1) * 2 * chans].astype(jnp.float32)
            first, middle, final = (both[:, u * LANES : (u + 1) * LANES] for u in range(3))
            yield 2 * pair, (first, middle)
            middle, final = pltpu.roll(middle, SPARE, 1), pltpu.roll(final, SPARE, 1)
            yield 2 * pair + 1, (jnp.where(low, middle, final), final)

    for n, (_, window) in enumerate(units):
        own_piece, halo_piece = pieces[2 * n], pieces[2 * n + 1]
        halo_at = rights[n] * HALF
        own_at = HALF - halo_at
        for row in range(WIN_LAT):
            for col, block in split(halo_piece, window * WIN_LAT + row):
                at = pl.ds(row * WIN_LON + col + halo_at, LEVELS, stride=QUERIES)
                for part in range(2):
                    keys_ref[n, part, at, :] = block[part]
            for col, block in split(own_piece, window * WIN_LAT + row):
                at = pl.ds(row * WIN_LON + col + own_at, LEVELS, stride=QUERIES)
                place = row * HALF + col
                for part in range(2):
                    keys_ref[n, part, at, :] = block[part]
                    own_ref[n, part, pl.ds(4 + place, LEVELS, stride=36), :] = block[part]
                    own_ref[n, part, pl.ds(148 + place, 1), :] = block[part][:1]

    gain1 = gain1_ref[...]
    lane = lax.broadcasted_iota(jnp.int32, (1, chans), 1)
    ones = jnp.ones((LEVELS * QUERIES, 2 * LANES - chans), jnp.float32)
    mixed = []
    for n, (_, window) in enumerate(units):
        normed = layer_norm(tokens_of(keys_ref, n, 0, LEVELS * QUERIES), gain1)
        normed = jnp.concatenate([normed[QUERIES:], normed[:QUERIES]], axis=0)
        normed = normed.astype(jnp.bfloat16)
        keys = jnp.dot(normed, qkv_ref[:, chans : 2 * chans], preferred_element_type=jnp.float32)
        values = jnp.dot(normed, qkv_ref[:, 2 * chans :], preferred_element_type=jnp.float32)
        values = jnp.concatenate([values, ones], axis=1)
        own = layer_norm(tokens_of(own_ref, n, 40, 144), gain1).astype(jnp.bfloat16)
        query = jnp.dot(own, qkv_ref[:, :chans], preferred_element_type=jnp.float32)
        query = query * (head_dim ** (-0.5) * LOG2E)
        for p in range(2):
            q = query[p * QUERIES : (p + 1) * QUERIES]
            k = keys[p * TOKENS : (p + 1) * TOKENS].astype(jnp.bfloat16)
            v = values[p * TOKENS : (p + 1) * TOKENS].astype(jnp.bfloat16)
            picked = [
                jnp.where((lane >= h * head_dim) & (lane < (h + 1) * head_dim), q, 0.0)
                for h in range(heads)
            ]
            picked = jnp.concatenate(picked, axis=0).astype(jnp.bfloat16)
            scores = lax.dot_general(picked, k, NT, preferred_element_type=jnp.float32)
            table = [table_ref[window, p, rights[n], part] for part in range(2)]
            table = jnp.concatenate([table[0], table[1][:, : TOKENS - LANES]], axis=1)
            scores = scores + table
            top = jnp.max(scores, axis=1, keepdims=True)
            probs = jnp.exp2(scores - top).astype(jnp.bfloat16)
            got = jnp.dot(probs, v, preferred_element_type=jnp.float32)
            out, total = got[:QUERIES, :chans], got[:QUERIES, chans : chans + 1]
            for h in range(1, heads):
                part = got[h * QUERIES : (h + 1) * QUERIES]
                out = jnp.where(lane >= h * head_dim, part[:, :chans], out)
                total = jnp.where(lane >= h * head_dim, part[:, chans : chans + 1], total)
            mixed.append(out / total)
    mixed = jnp.concatenate(mixed, axis=0).astype(jnp.bfloat16)
    attn = jnp.dot(mixed, proj_ref[...], preferred_element_type=jnp.float32)
    attn = attn.astype(jnp.bfloat16).astype(jnp.float32)
    tokens = [tokens_of(own_ref, n, 40, 144) for n in range(count)]
    resid = jnp.concatenate(tokens, axis=0) + attn
    resid = resid.astype(jnp.bfloat16).astype(jnp.float32)
    normed = layer_norm(resid, gain2_ref[...]).astype(jnp.bfloat16)
    hidden = jnp.dot(normed, fc1_ref[...], preferred_element_type=jnp.float32)
    hidden = gelu(hidden).astype(jnp.bfloat16)
    result = lax.dot_general(hidden, fc2_ref[...], NT, preferred_element_type=jnp.float32)
    result = resid + result
    for n in range(count):
        mine = result[n * 144 : (n + 1) * 144]
        for part, lanes in enumerate((slice(0, LANES), slice(LANES, chans))):
            width = min(LANES, chans - part * LANES)
            res_ref[n, part, 40:184, :width] = mine[:, lanes]
            res_ref[n, part, 0:40, :width] = mine[104:144, lanes]
        for row in range(WIN_LAT):
            for pair in range(HALF // 2):
                tiles = []
                for col in (2 * pair, 2 * pair + 1):
                    at = pl.ds(4 + row * HALF + col, LEVELS, stride=36)
                    tiles += [res_ref[n, part, at, :] for part in range(2)]
                shifted = [pltpu.roll(x, SPARE, 1) for x in tiles[2:]]
                tiles = [tiles[0], jnp.where(low, tiles[1], shifted[0])]
                tiles.append(jnp.where(low, shifted[0], shifted[1]))
                tiles = jnp.concatenate(tiles, axis=1).astype(jnp.bfloat16)
                out_ref[n, row, :, pair * 2 * chans : (pair + 1) * 2 * chans] = tiles
    if lower:
        send_ref[0] = lower_ref[0, EDGE:]
        send_ref[1] = out_ref[0, EDGE:]


def run_units(units, near, far, table, weights, chans, heads, *lower):
    count = len(units)
    pieces = [x for is_near, _ in units for x in (near if is_near else far)]
    piece = pieces[0]
    out = jax.ShapeDtypeStruct((count, WIN_LAT) + piece.shape[1:], piece.dtype)
    send = jax.ShapeDtypeStruct((2, EDGE) + piece.shape[1:], piece.dtype)
    operands = (*pieces, *weights, table, *lower)
    vmem = pl.BlockSpec(memory_space=pltpu.VMEM)
    outs = [out, send] if lower else [out]
    return pl.pallas_call(
        functools.partial(units_kernel, chans, heads, units, bool(lower)),
        out_shape=outs,
        in_specs=[vmem] * len(operands),
        out_specs=[vmem] * len(outs),
        scratch_shapes=[
            pltpu.VMEM((count, 2, LEVELS * QUERIES, LANES), jnp.float32),
            pltpu.VMEM((count, 2, 184, LANES), jnp.float32),
            pltpu.VMEM((count, 2, 184, LANES), jnp.float32),
        ],
        compiler_params=pltpu.CompilerParams(vmem_limit_bytes=VMEM_BYTES),
        cost_estimate=pl.CostEstimate(
            flops=200_000_000 * count, bytes_accessed=3_000_000, transcendentals=250_000 * count
        ),
        name="swin_windows",
    )(*operands)


def shards(
    field_in, norm1_gain, qkv_weight, proj_weight, earth_bias, norm2_gain, fc1_weight, fc2_weight
):
    levels, rows, flat = field_in.shape
    chans = qkv_weight.shape[0]
    heads = earth_bias.shape[2]
    half = HALF * chans
    field = jnp.transpose(field_in, (1, 0, 2))
    south = moved(field[:EDGE], "lat", -1)
    weights = (
        norm1_gain.reshape(1, chans),
        qkv_weight,
        proj_weight,
        norm2_gain.reshape(1, chans),
        fc1_weight,
        jnp.transpose(fc2_weight),
    )
    vmem = pl.BlockSpec(memory_space=pltpu.VMEM)
    anywhere = pl.BlockSpec(memory_space=pl.ANY)
    piece = jax.ShapeDtypeStruct((rows, levels, half), field.dtype)
    table = jax.ShapeDtypeStruct((2, 2, 2, 2, heads * QUERIES, LANES), jnp.float32)
    windows, zwin, _, entries = earth_bias.shape
    tiles = entries // LANES
    bias = earth_bias.reshape(windows, zwin, heads, tiles, LANES).transpose(0, 2, 3, 1, 4)
    sources = (bias, field) + weights
    sources = [pltpu.with_memory_space_constraint(x, pltpu.HBM) for x in sources]
    outs = [table, piece, piece] + [jax.ShapeDtypeStruct(x.shape, x.dtype) for x in weights]
    table, near, far, *weights = pl.pallas_call(
        functools.partial(table_kernel, len(weights)),
        out_shape=outs,
        in_specs=[pl.BlockSpec(memory_space=pltpu.HBM)] * len(sources),
        out_specs=[vmem] * len(outs),
        scratch_shapes=[
            pltpu.VMEM((bias.size // LANES, LANES), jnp.float32),
            pltpu.SemaphoreType.DMA((heads * windows,)),
            pltpu.SemaphoreType.DMA((2 + len(weights),)),
        ],
        compiler_params=pltpu.CompilerParams(vmem_limit_bytes=VMEM_BYTES),
        cost_estimate=pl.CostEstimate(flops=4_000_000, bytes_accessed=6_000_000, transcendentals=0),
        name="bias_tables",
    )(*sources)

    def pack(which, kept, *after):
        return pl.pallas_call(
            functools.partial(pack_kernel, which),
            out_shape=piece,
            in_specs=[vmem] * 2 + [anywhere] * len(after),
            out_specs=vmem,
            compiler_params=pltpu.CompilerParams(vmem_limit_bytes=VMEM_BYTES),
            cost_estimate=pl.CostEstimate(flops=0, bytes_accessed=250_000, transcendentals=0),
            name="pack_half",
        )(south, kept, *after)

    far = pack(1, far)
    near = pack(0, near, far)
    far_halo = swapped(far, "lon", 1)
    near_halo = swapped(near, "lon", 0)
    near, far = (near, near_halo), (far, far_halo)
    common = (near, far, table, weights, chans, heads)
    (near_low,) = run_units(((True, 1),), *common)
    far_low, send = run_units(((False, 1),), *common, near_low)
    top = moved(send, "lat", 1)
    (high,) = run_units(((True, 0), (False, 0)), *common)
    done = pl.pallas_call(
        last_kernel,
        out_shape=jax.ShapeDtypeStruct(field.shape, field.dtype),
        in_specs=[vmem] * 4,
        out_specs=anywhere,
        scratch_shapes=[pltpu.SemaphoreType.DMA((6,))],
        compiler_params=pltpu.CompilerParams(vmem_limit_bytes=VMEM_BYTES),
        cost_estimate=pl.CostEstimate(flops=0, bytes_accessed=400_000, transcendentals=0),
        name="last_rows",
    )(top, high, near_low, far_low)
    return jnp.transpose(done, (1, 0, 2))


def solution(mesh):
    in_specs = (P(None, "lat", "lon"), P(), P(), P(), P("lat", None, None, None), P(), P(), P())
    out_specs = P(None, "lat", "lon")
    return jax.shard_map(shards, mesh=mesh, in_specs=in_specs, out_specs=out_specs, check_vma=False)
```

```python
import functools

import jax
import jax.numpy as jnp
from jax import lax
from jax.experimental import pallas as pl
from jax.experimental.pallas import tpu as pltpu
from jax.sharding import PartitionSpec as P

LEVELS = 4
WIN_LEV = 2
WIN_LAT = 6
WIN_LON = 12
EDGE = WIN_LAT // 2
HALF = WIN_LON // 2
TOKENS = WIN_LEV * WIN_LAT * WIN_LON
QUERIES = TOKENS // 2
LOG2E = 1.4426950408889634
GELU_0 = 0.7978845608028654
GELU_1 = 0.044715 * GELU_0
LANES = 128
SPARE = 64
VMEM_BYTES = 8 * 2**20
NT = (((1,), (1,)), ((), ()))


def moved(x, axis, by):
    size = lax.axis_size(axis)
    return lax.ppermute(x, axis, [(i, (i + by) % size) for i in range(size)])


def swapped(x, axis, first):
    size = lax.axis_size(axis)
    pairs = []
    for i in range(first, size, 2):
        j = (i + 1) % size
        pairs += [(i, j), (j, i)]
    return lax.ppermute(x, axis, pairs)


def half_places(half):
    odd = lax.rem(lax.axis_index("lon"), 2)
    return pl.multiple_of((1 - odd) * half, LANES), pl.multiple_of(odd * half, LANES)


def pack_kernel(which, south_ref, kept_ref, *rest):
    piece_ref = rest[-1]
    at = half_places(piece_ref.shape[2])[which]
    rows = piece_ref.shape[0] - EDGE
    piece_ref[:rows] = kept_ref[:rows]
    piece_ref[rows:] = south_ref[:, :, pl.ds(at, piece_ref.shape[2])]


def last_kernel(top_ref, high_ref, near_low_ref, far_low_ref, out_ref, sems):
    half = top_ref.shape[3]
    copies = []
    for n, at in enumerate(half_places(half)):
        target = out_ref.at[:, :, pl.ds(at, half)]
        low_ref = (near_low_ref, far_low_ref)[n]
        for source, first in (
            (high_ref.at[n], EDGE),
            (low_ref.at[0, :EDGE], EDGE + WIN_LAT),
            (top_ref.at[n], 0),
        ):
            rows = pl.ds(first, source.shape[0])
            copy = pltpu.make_async_copy(source, target.at[rows], sems.at[len(copies)])
            copy.start()
            copies.append(copy)
    for copy in copies:
        copy.wait()


def table_kernel(count, *refs):
    bias_any, field_any, *weights_any = refs[: 2 + count]
    table_ref, near_ref, far_ref, *weights_ref = refs[2 + count : 5 + 2 * count]
    bias_ref, sems, side_sems = refs[5 + 2 * count :]
    windows, heads, tiles = bias_any.shape[:3]
    lines = bias_ref.shape[0]
    flat = bias_any.reshape(lines, LANES)
    parts = windows
    copies = []
    for n in range(parts):
        at = pl.ds(n * (lines // parts), lines // parts)
        copies.append(pltpu.make_async_copy(flat.at[at], bias_ref.at[at], sems.at[n]))
        copies[-1].start()
    rows, half = field_any.shape[0] - EDGE, near_ref.shape[2]
    near_at, far_at = half_places(half)
    fetches = [
        (field_any.at[EDGE:, :, pl.ds(far_at, half)], far_ref.at[:rows]),
        (field_any.at[EDGE:, :, pl.ds(near_at, half)], near_ref.at[:rows]),
    ]
    fetches += list(zip(weights_any, weights_ref))
    fetches = [
        pltpu.make_async_copy(source, target, side_sems.at[n])
        for n, (source, target) in enumerate(fetches)
    ]
    for copy in fetches:
        copy.start()
    blocks = WIN_LEV * WIN_LAT // 2
    lane = lax.broadcasted_iota(jnp.int32, (blocks, LANES), 1)
    block = lax.broadcasted_iota(jnp.int32, (blocks, LANES), 0)
    is_last = lax.axis_index("lat") == lax.axis_size("lat") - 1
    last = jnp.where(is_last, -1e9, 0.0).astype(jnp.float32)

    def penalty(part, second, levels, wrap):
        key = lane + part * LANES
        key_lev = key // QUERIES
        key_side = (key - key_lev * QUERIES) // (QUERIES // 2)
        row = 2 * block + second
        lev = row // WIN_LAT
        side = (row - lev * WIN_LAT) // EDGE
        out = jnp.zeros((blocks, LANES), jnp.float32)
        if levels:
            out = jnp.where(key_lev != lev, -1e9, out)
        if wrap:
            out = out + jnp.where(key_side != side, last, 0.0)
        return out

    for k in range(windows):
        masks = {
            (p, part, second): penalty(part, second, p == 1, k == windows - 1)
            for p in range(2)
            for part in range(2)
            for second in range(2)
        }
        copies[k].wait()
        for h in range(heads):
            for p in range(2):
                base = (k * heads + h) * 2 * tiles + p
                for third in range(3):
                    line = base + third * 18
                    pieces = [
                        bias_ref[pl.ds(line + 2 * u, blocks, stride=54), :] * LOG2E
                        for u in range(9)
                    ]
                    for r in range(8):
                        shift = 16 * r
                        main, nxt = pieces[r], pieces[r + 1]
                        if r:
                            main = pltpu.roll(main, LANES - shift, 1)
                            nxt = pltpu.roll(nxt, LANES - shift, 1)
                            main = jnp.where(lane < LANES - shift, main, nxt)
                        second, col = divmod(8 * third + r, WIN_LON)
                        side = col // HALF
                        place = h * QUERIES + HALF * second + col % HALF
                        at = pl.ds(place, blocks, stride=WIN_LON)
                        for part, piece in enumerate((main, nxt)):
                            filled = piece + masks[p, part, second]
                            table_ref[k, p, 1 - side, part, at, :] = filled
    for copy in fetches:
        copy.wait()


def layer_norm(values, gain):
    center = values - jnp.mean(values, axis=-1, keepdims=True)
    spread = jnp.mean(center * center, axis=-1, keepdims=True)
    return center * lax.rsqrt(spread + 1e-05) * gain


def gelu(x):
    half = 0.5 * x
    return half + half * jnp.tanh(x * (GELU_0 + GELU_1 * (x * x)))


def units_kernel(chans, heads, units, lower, *refs):
    count = len(units)
    pieces, refs = refs[: 2 * count], refs[2 * count :]
    gain1_ref, qkv_ref, proj_ref, gain2_ref, fc1_ref, fc2_ref, table_ref, *refs = refs
    if lower:
        lower_ref, out_ref, send_ref, keys_ref, own_ref, res_ref = refs
    else:
        out_ref, keys_ref, own_ref, res_ref = refs
    head_dim = chans // heads
    low = lax.broadcasted_iota(jnp.int32, (1, LANES), 1) < SPARE
    odd = lax.rem(lax.axis_index("lon"), 2)
    rights = [1 - odd if near else odd for near, _ in units]

    def tokens_of(ref, at, first, count):
        both = [ref[at, part, first : first + count] for part in range(2)]
        return jnp.concatenate([both[0], both[1][:, : chans - LANES]], axis=1)

    def split(ref, row):
        for pair in range(HALF // 2):
            both = ref[row, :, pair * 2 * chans : (pair + 1) * 2 * chans].astype(jnp.float32)
            first, middle, final = (both[:, u * LANES : (u + 1) * LANES] for u in range(3))
            yield 2 * pair, (first, middle)
            middle, final = pltpu.roll(middle, SPARE, 1), pltpu.roll(final, SPARE, 1)
            yield 2 * pair + 1, (jnp.where(low, middle, final), final)

    for n, (_, window) in enumerate(units):
        own_piece, halo_piece = pieces[2 * n], pieces[2 * n + 1]
        halo_at = rights[n] * HALF
        own_at = HALF - halo_at
        for row in range(WIN_LAT):
            for col, block in split(halo_piece, window * WIN_LAT + row):
                at = pl.ds(row * WIN_LON + col + halo_at, LEVELS, stride=QUERIES)
                for part in range(2):
                    keys_ref[n, part, at, :] = block[part]
            for col, block in split(own_piece, window * WIN_LAT + row):
                at = pl.ds(row * WIN_LON + col + own_at, LEVELS, stride=QUERIES)
                place = row * HALF + col
                for part in range(2):
                    keys_ref[n, part, at, :] = block[part]
                    own_ref[n, part, pl.ds(4 + place, LEVELS, stride=36), :] = block[part]
                    own_ref[n, part, pl.ds(148 + place, 1), :] = block[part][:1]

    gain1 = gain1_ref[...]
    lane = lax.broadcasted_iota(jnp.int32, (1, chans), 1)
    ones = jnp.ones((TOKENS, 2 * LANES - chans), jnp.float32)
    mixed = []
    for n, (_, window) in enumerate(units):
        normed = []
        for p in range(2):
            levels = [(2 * p + 1 + lev) % LEVELS for lev in range(WIN_LEV)]
            parts = [tokens_of(keys_ref, n, lev * QUERIES, QUERIES) for lev in levels]
            parts = [layer_norm(x, gain1) for x in parts]
            normed.append(jnp.concatenate(parts, axis=0).astype(jnp.bfloat16))
        normed = jnp.concatenate(normed, axis=0)
        keys = jnp.dot(normed, qkv_ref[:, chans : 2 * chans], preferred_element_type=jnp.float32)
        values = jnp.dot(normed, qkv_ref[:, 2 * chans :], preferred_element_type=jnp.float32)
        own = layer_norm(tokens_of(own_ref, n, 40, 144), gain1).astype(jnp.bfloat16)
        query = jnp.dot(own, qkv_ref[:, :chans], preferred_element_type=jnp.float32)
        query = query * (head_dim ** (-0.5) * LOG2E)
        for p in range(2):
            q = query[p * QUERIES : (p + 1) * QUERIES]
            k = keys[p * TOKENS : (p + 1) * TOKENS].astype(jnp.bfloat16)
            v = jnp.concatenate([values[p * TOKENS : (p + 1) * TOKENS], ones], axis=1)
            v = v.astype(jnp.bfloat16)
            picked = [
                jnp.where((lane >= h * head_dim) & (lane < (h + 1) * head_dim), q, 0.0)
                for h in range(heads)
            ]
            picked = jnp.concatenate(picked, axis=0).astype(jnp.bfloat16)
            scores = lax.dot_general(picked, k, NT, preferred_element_type=jnp.float32)
            probs = []
            for h in range(heads):
                at = slice(h * QUERIES, (h + 1) * QUERIES)
                bias = [table_ref[window, p, rights[n], part, at] for part in range(2)]
                bias = jnp.concatenate([bias[0], bias[1][:, : TOKENS - LANES]], axis=1)
                part = scores[at] + bias
                probs.append(jnp.exp2(part - jnp.max(part, axis=1, keepdims=True)))
            probs = jnp.concatenate(probs, axis=0).astype(jnp.bfloat16)
            got = jnp.dot(probs, v, preferred_element_type=jnp.float32)
            out = None
            for h in range(heads):
                part = got[h * QUERIES : (h + 1) * QUERIES]
                scaled = part[:, :chans] * (1.0 / part[:, chans : chans + 1])
                out = jnp.where(lane >= h * head_dim, scaled, out) if h else scaled
            mixed.append(out)
    mixed = jnp.concatenate(mixed, axis=0).astype(jnp.bfloat16)
    attn = jnp.dot(mixed, proj_ref[...], preferred_element_type=jnp.float32)
    attn = attn.astype(jnp.bfloat16).astype(jnp.float32)
    resid, normed = [], []
    for n in range(count):
        part = tokens_of(own_ref, n, 40, 144) + attn[n * 144 : (n + 1) * 144]
        resid.append(part.astype(jnp.bfloat16).astype(jnp.float32))
        normed.append(layer_norm(resid[n], gain2_ref[...]).astype(jnp.bfloat16))
    result, normed = jnp.concatenate(resid, axis=0), jnp.concatenate(normed, axis=0)
    for first in range(0, fc1_ref.shape[1], 2 * LANES):
        units_at = slice(first, first + 2 * LANES)
        hidden = jnp.dot(normed, fc1_ref[:, units_at], preferred_element_type=jnp.float32)
        hidden = gelu(hidden).astype(jnp.bfloat16)
        result = result + lax.dot_general(
            hidden, fc2_ref[:, units_at], NT, preferred_element_type=jnp.float32
        )
    for n in range(count):
        mine = result[n * 144 : (n + 1) * 144]
        for part, lanes in enumerate((slice(0, LANES), slice(LANES, chans))):
            width = min(LANES, chans - part * LANES)
            res_ref[n, part, 40:184, :width] = mine[:, lanes]
            res_ref[n, part, 0:40, :width] = mine[104:144, lanes]
        for row in range(WIN_LAT):
            for pair in range(HALF // 2):
                tiles = []
                for col in (2 * pair, 2 * pair + 1):
                    at = pl.ds(4 + row * HALF + col, LEVELS, stride=36)
                    tiles += [res_ref[n, part, at, :] for part in range(2)]
                shifted = [pltpu.roll(x, SPARE, 1) for x in tiles[2:]]
                tiles = [tiles[0], jnp.where(low, tiles[1], shifted[0])]
                tiles.append(jnp.where(low, shifted[0], shifted[1]))
                tiles = jnp.concatenate(tiles, axis=1).astype(jnp.bfloat16)
                out_ref[n, row, :, pair * 2 * chans : (pair + 1) * 2 * chans] = tiles
    if lower:
        send_ref[0] = lower_ref[0, EDGE:]
        send_ref[1] = out_ref[0, EDGE:]


def run_units(units, near, far, table, weights, chans, heads, *lower):
    count = len(units)
    pieces = [x for is_near, _ in units for x in (near if is_near else far)]
    piece = pieces[0]
    out = jax.ShapeDtypeStruct((count, WIN_LAT) + piece.shape[1:], piece.dtype)
    send = jax.ShapeDtypeStruct((2, EDGE) + piece.shape[1:], piece.dtype)
    operands = (*pieces, *weights, table, *lower)
    vmem = pl.BlockSpec(memory_space=pltpu.VMEM)
    outs = [out, send] if lower else [out]
    return pl.pallas_call(
        functools.partial(units_kernel, chans, heads, units, bool(lower)),
        out_shape=outs,
        in_specs=[vmem] * len(operands),
        out_specs=[vmem] * len(outs),
        scratch_shapes=[
            pltpu.VMEM((count, 2, LEVELS * QUERIES, LANES), jnp.float32),
            pltpu.VMEM((count, 2, 184, LANES), jnp.float32),
            pltpu.VMEM((count, 2, 184, LANES), jnp.float32),
        ],
        compiler_params=pltpu.CompilerParams(vmem_limit_bytes=VMEM_BYTES),
        cost_estimate=pl.CostEstimate(
            flops=200_000_000 * count, bytes_accessed=3_000_000, transcendentals=250_000 * count
        ),
        name="swin_windows",
    )(*operands)


def shards(
    field_in, norm1_gain, qkv_weight, proj_weight, earth_bias, norm2_gain, fc1_weight, fc2_weight
):
    levels, rows, flat = field_in.shape
    chans = qkv_weight.shape[0]
    heads = earth_bias.shape[2]
    half = HALF * chans
    field = jnp.transpose(field_in, (1, 0, 2))
    south = moved(field[:EDGE], "lat", -1)
    weights = (
        norm1_gain.reshape(1, chans),
        qkv_weight,
        proj_weight,
        norm2_gain.reshape(1, chans),
        fc1_weight,
        jnp.transpose(fc2_weight),
    )
    vmem = pl.BlockSpec(memory_space=pltpu.VMEM)
    anywhere = pl.BlockSpec(memory_space=pl.ANY)
    piece = jax.ShapeDtypeStruct((rows, levels, half), field.dtype)
    table = jax.ShapeDtypeStruct((2, 2, 2, 2, heads * QUERIES, LANES), jnp.float32)
    windows, zwin, _, entries = earth_bias.shape
    tiles = entries // LANES
    bias = earth_bias.reshape(windows, zwin, heads, tiles, LANES).transpose(0, 2, 3, 1, 4)
    sources = (bias, field) + weights
    sources = [pltpu.with_memory_space_constraint(x, pltpu.HBM) for x in sources]
    outs = [table, piece, piece] + [jax.ShapeDtypeStruct(x.shape, x.dtype) for x in weights]
    table, near, far, *weights = pl.pallas_call(
        functools.partial(table_kernel, len(weights)),
        out_shape=outs,
        in_specs=[pl.BlockSpec(memory_space=pltpu.HBM)] * len(sources),
        out_specs=[vmem] * len(outs),
        scratch_shapes=[
            pltpu.VMEM((bias.size // LANES, LANES), jnp.float32),
            pltpu.SemaphoreType.DMA((2 * windows,)),
            pltpu.SemaphoreType.DMA((2 + len(weights),)),
        ],
        compiler_params=pltpu.CompilerParams(vmem_limit_bytes=VMEM_BYTES),
        cost_estimate=pl.CostEstimate(flops=4_000_000, bytes_accessed=6_000_000, transcendentals=0),
        name="bias_tables",
    )(*sources)

    def pack(which, kept, *after):
        return pl.pallas_call(
            functools.partial(pack_kernel, which),
            out_shape=piece,
            in_specs=[vmem] * 2 + [anywhere] * len(after),
            out_specs=vmem,
            compiler_params=pltpu.CompilerParams(vmem_limit_bytes=VMEM_BYTES),
            cost_estimate=pl.CostEstimate(flops=0, bytes_accessed=250_000, transcendentals=0),
            name="pack_half",
        )(south, kept, *after)

    far = pack(1, far)
    near = pack(0, near, far)
    far_halo = swapped(far, "lon", 1)
    near_halo = swapped(near, "lon", 0)
    near, far = (near, near_halo), (far, far_halo)
    common = (near, far, table, weights, chans, heads)
    (near_low,) = run_units(((True, 1),), *common)
    far_low, send = run_units(((False, 1),), *common, near_low)
    top = moved(send, "lat", 1)
    (high,) = run_units(((True, 0), (False, 0)), *common)
    done = pl.pallas_call(
        last_kernel,
        out_shape=jax.ShapeDtypeStruct(field.shape, field.dtype),
        in_specs=[vmem] * 4,
        out_specs=anywhere,
        scratch_shapes=[pltpu.SemaphoreType.DMA((6,))],
        compiler_params=pltpu.CompilerParams(vmem_limit_bytes=VMEM_BYTES),
        cost_estimate=pl.CostEstimate(flops=0, bytes_accessed=400_000, transcendentals=0),
        name="last_rows",
    )(top, high, near_low, far_low)
    return jnp.transpose(done, (1, 0, 2))


def solution(mesh):
    in_specs = (P(None, "lat", "lon"), P(), P(), P(), P("lat", None, None, None), P(), P(), P())
    out_specs = P(None, "lat", "lon")
    return jax.shard_map(shards, mesh=mesh, in_specs=in_specs, out_specs=out_specs, check_vma=False)
```

```python
import functools

import jax
import jax.numpy as jnp
from jax import lax
from jax.experimental import pallas as pl
from jax.experimental.pallas import tpu as pltpu
from jax.sharding import PartitionSpec as P

LEVELS = 4
WIN_LEV = 2
WIN_LAT = 6
WIN_LON = 12
EDGE = WIN_LAT // 2
HALF = WIN_LON // 2
TOKENS = WIN_LEV * WIN_LAT * WIN_LON
QUERIES = TOKENS // 2
LOG2E = 1.4426950408889634
GELU_0 = 0.7978845608028654
GELU_1 = 0.044715 * GELU_0
LANES = 128
SPARE = 64
VMEM_BYTES = 8 * 2**20
NT = (((1,), (1,)), ((), ()))


def moved(x, axis, by):
    size = lax.axis_size(axis)
    return lax.ppermute(x, axis, [(i, (i + by) % size) for i in range(size)])


def swapped(x, axis, first):
    size = lax.axis_size(axis)
    pairs = []
    for i in range(first, size, 2):
        j = (i + 1) % size
        pairs += [(i, j), (j, i)]
    return lax.ppermute(x, axis, pairs)


def half_places(half):
    odd = lax.rem(lax.axis_index("lon"), 2)
    return pl.multiple_of((1 - odd) * half, LANES), pl.multiple_of(odd * half, LANES)


def pack_kernel(which, south_ref, kept_ref, *rest):
    piece_ref = rest[-1]
    at = half_places(piece_ref.shape[2])[which]
    rows = piece_ref.shape[0] - EDGE
    piece_ref[:rows] = kept_ref[:rows]
    piece_ref[rows:] = south_ref[:, :, pl.ds(at, piece_ref.shape[2])]


def last_kernel(top_ref, high_ref, near_low_ref, far_low_ref, out_ref, sems):
    half = top_ref.shape[3]
    copies = []
    for n, at in enumerate(half_places(half)):
        target = out_ref.at[:, :, pl.ds(at, half)]
        low_ref = (near_low_ref, far_low_ref)[n]
        for source, first in (
            (high_ref.at[n], EDGE),
            (low_ref.at[0, :EDGE], EDGE + WIN_LAT),
            (top_ref.at[n], 0),
        ):
            rows = pl.ds(first, source.shape[0])
            copy = pltpu.make_async_copy(source, target.at[rows], sems.at[len(copies)])
            copy.start()
            copies.append(copy)
    for copy in copies:
        copy.wait()


def build_tables(bias_ref, table_ref, heads, wrap):
    lines = bias_ref.shape[0] // heads
    blocks = WIN_LEV * WIN_LAT // 2
    lane = lax.broadcasted_iota(jnp.int32, (blocks, LANES), 1)
    block = lax.broadcasted_iota(jnp.int32, (blocks, LANES), 0)
    is_last = lax.axis_index("lat") == lax.axis_size("lat") - 1
    last = jnp.where(is_last, -1e9, 0.0).astype(jnp.float32)

    def penalty(part, second, levels):
        key = lane + part * LANES
        key_lev = key // QUERIES
        key_side = (key - key_lev * QUERIES) // (QUERIES // 2)
        row = 2 * block + second
        lev = row // WIN_LAT
        side = (row - lev * WIN_LAT) // EDGE
        out = jnp.zeros((blocks, LANES), jnp.float32)
        if levels:
            out = jnp.where(key_lev != lev, -1e9, out)
        if wrap:
            out = out + jnp.where(key_side != side, last, 0.0)
        return out

    masks = {
        (p, part, second): penalty(part, second, p == 1)
        for p in range(2)
        for part in range(2)
        for second in range(2)
    }
    for h in range(heads):
        for p in range(2):
            for third in range(3):
                line = h * lines + p + third * 18
                pieces = [
                    bias_ref[pl.ds(line + 2 * u, blocks, stride=54), :] * LOG2E for u in range(9)
                ]
                for r in range(8):
                    shift = 16 * r
                    main, nxt = pieces[r], pieces[r + 1]
                    if r:
                        main = pltpu.roll(main, LANES - shift, 1)
                        nxt = pltpu.roll(nxt, LANES - shift, 1)
                        main = jnp.where(lane < LANES - shift, main, nxt)
                    second, col = divmod(8 * third + r, WIN_LON)
                    side = col // HALF
                    place = h * QUERIES + HALF * second + col % HALF
                    at = pl.ds(place, blocks, stride=WIN_LON)
                    for part, piece in enumerate((main, nxt)):
                        table_ref[p, 1 - side, part, at, :] = piece + masks[p, part, second]


def table_kernel(count, heads, *refs):
    bias_any, field_any, *weights_any = refs[: 2 + count]
    table_ref, inner_ref, near_ref, far_ref, *weights_ref = refs[2 + count : 6 + 2 * count]
    bias_ref, sems = refs[6 + 2 * count :]
    lines = bias_ref.shape[0]
    flat = bias_any.reshape(2 * lines, LANES)
    rows, half = field_any.shape[0] - EDGE, near_ref.shape[2]
    near_at, far_at = half_places(half)
    fetches = [
        (flat.at[pl.ds(lines, lines)], bias_ref),
        (field_any.at[EDGE:, :, pl.ds(far_at, half)], far_ref.at[:rows]),
        (field_any.at[EDGE:, :, pl.ds(near_at, half)], near_ref.at[:rows]),
        (flat.at[pl.ds(0, lines)], inner_ref),
    ]
    fetches += list(zip(weights_any, weights_ref))
    fetches = [
        pltpu.make_async_copy(source, target, sems.at[n])
        for n, (source, target) in enumerate(fetches)
    ]
    for copy in fetches:
        copy.start()
    fetches[0].wait()
    build_tables(bias_ref, table_ref, heads, True)
    for copy in fetches[1:]:
        copy.wait()


def layer_norm(values, gain):
    center = values - jnp.mean(values, axis=-1, keepdims=True)
    spread = jnp.mean(center * center, axis=-1, keepdims=True)
    return center * lax.rsqrt(spread + 1e-05) * gain


def gelu(x):
    half = 0.5 * x
    return half + half * jnp.tanh(x * (GELU_0 + GELU_1 * (x * x)))


def units_kernel(chans, heads, units, extra, *refs):
    count = len(units)
    pieces, refs = refs[: 2 * count], refs[2 * count :]
    gain1_ref, qkv_ref, proj_ref, gain2_ref, fc1_ref, fc2_ref, table_ref, *refs = refs
    if extra:
        extra_ref, out_ref, extra_out, keys_ref, own_ref, res_ref = refs
    else:
        out_ref, keys_ref, own_ref, res_ref = refs
    if extra == "tables":
        build_tables(extra_ref, extra_out, heads, False)
    head_dim = chans // heads
    low = lax.broadcasted_iota(jnp.int32, (1, LANES), 1) < SPARE
    odd = lax.rem(lax.axis_index("lon"), 2)
    rights = [1 - odd if near else odd for near, _ in units]

    def tokens_of(ref, at, first, count):
        both = [ref[at, part, first : first + count] for part in range(2)]
        return jnp.concatenate([both[0], both[1][:, : chans - LANES]], axis=1)

    def split(ref, row):
        for pair in range(HALF // 2):
            both = ref[row, :, pair * 2 * chans : (pair + 1) * 2 * chans].astype(jnp.float32)
            first, middle, final = (both[:, u * LANES : (u + 1) * LANES] for u in range(3))
            yield 2 * pair, (first, middle)
            middle, final = pltpu.roll(middle, SPARE, 1), pltpu.roll(final, SPARE, 1)
            yield 2 * pair + 1, (jnp.where(low, middle, final), final)

    for n, (_, window) in enumerate(units):
        own_piece, halo_piece = pieces[2 * n], pieces[2 * n + 1]
        halo_at = rights[n] * HALF
        own_at = HALF - halo_at
        for row in range(WIN_LAT):
            for col, block in split(halo_piece, window * WIN_LAT + row):
                at = pl.ds(row * WIN_LON + col + halo_at, LEVELS, stride=QUERIES)
                for part in range(2):
                    keys_ref[n, part, at, :] = block[part]
            for col, block in split(own_piece, window * WIN_LAT + row):
                at = pl.ds(row * WIN_LON + col + own_at, LEVELS, stride=QUERIES)
                place = row * HALF + col
                for part in range(2):
                    keys_ref[n, part, at, :] = block[part]
                    own_ref[n, part, pl.ds(4 + place, LEVELS, stride=36), :] = block[part]
                    own_ref[n, part, pl.ds(148 + place, 1), :] = block[part][:1]

    gain1 = gain1_ref[...]
    lane = lax.broadcasted_iota(jnp.int32, (1, chans), 1)
    ones = jnp.ones((TOKENS, 2 * LANES - chans), jnp.float32)
    mixed = []
    for n, (_, window) in enumerate(units):
        normed = []
        for p in range(2):
            levels = [(2 * p + 1 + lev) % LEVELS for lev in range(WIN_LEV)]
            parts = [tokens_of(keys_ref, n, lev * QUERIES, QUERIES) for lev in levels]
            parts = [layer_norm(x, gain1) for x in parts]
            normed.append(jnp.concatenate(parts, axis=0).astype(jnp.bfloat16))
        normed = jnp.concatenate(normed, axis=0)
        keys = jnp.dot(normed, qkv_ref[:, chans : 2 * chans], preferred_element_type=jnp.float32)
        values = jnp.dot(normed, qkv_ref[:, 2 * chans :], preferred_element_type=jnp.float32)
        own = layer_norm(tokens_of(own_ref, n, 40, 144), gain1).astype(jnp.bfloat16)
        query = jnp.dot(own, qkv_ref[:, :chans], preferred_element_type=jnp.float32)
        query = query * (head_dim ** (-0.5) * LOG2E)
        for p in range(2):
            q = query[p * QUERIES : (p + 1) * QUERIES]
            k = keys[p * TOKENS : (p + 1) * TOKENS].astype(jnp.bfloat16)
            v = jnp.concatenate([values[p * TOKENS : (p + 1) * TOKENS], ones], axis=1)
            v = v.astype(jnp.bfloat16)
            picked = [
                jnp.where((lane >= h * head_dim) & (lane < (h + 1) * head_dim), q, 0.0)
                for h in range(heads)
            ]
            picked = jnp.concatenate(picked, axis=0).astype(jnp.bfloat16)
            scores = lax.dot_general(picked, k, NT, preferred_element_type=jnp.float32)
            probs = []
            for h in range(heads):
                at = slice(h * QUERIES, (h + 1) * QUERIES)
                bias = [table_ref[p, rights[n], part, at] for part in range(2)]
                bias = jnp.concatenate([bias[0], bias[1][:, : TOKENS - LANES]], axis=1)
                part = scores[at] + bias
                probs.append(jnp.exp2(part - jnp.max(part, axis=1, keepdims=True)))
            probs = jnp.concatenate(probs, axis=0).astype(jnp.bfloat16)
            got = jnp.dot(probs, v, preferred_element_type=jnp.float32)
            out = None
            for h in range(heads):
                part = got[h * QUERIES : (h + 1) * QUERIES]
                scaled = part[:, :chans] * (1.0 / part[:, chans : chans + 1])
                out = jnp.where(lane >= h * head_dim, scaled, out) if h else scaled
            mixed.append(out)
    mixed = jnp.concatenate(mixed, axis=0).astype(jnp.bfloat16)
    attn = jnp.dot(mixed, proj_ref[...], preferred_element_type=jnp.float32)
    attn = attn.astype(jnp.bfloat16).astype(jnp.float32)
    resid, normed = [], []
    for n in range(count):
        part = tokens_of(own_ref, n, 40, 144) + attn[n * 144 : (n + 1) * 144]
        resid.append(part.astype(jnp.bfloat16).astype(jnp.float32))
        normed.append(layer_norm(resid[n], gain2_ref[...]).astype(jnp.bfloat16))
    result, normed = jnp.concatenate(resid, axis=0), jnp.concatenate(normed, axis=0)
    for first in range(0, fc1_ref.shape[1], 2 * LANES):
        units_at = slice(first, first + 2 * LANES)
        hidden = jnp.dot(normed, fc1_ref[:, units_at], preferred_element_type=jnp.float32)
        hidden = gelu(hidden).astype(jnp.bfloat16)
        result = result + lax.dot_general(
            hidden, fc2_ref[:, units_at], NT, preferred_element_type=jnp.float32
        )
    for n in range(count):
        mine = result[n * 144 : (n + 1) * 144]
        for part, lanes in enumerate((slice(0, LANES), slice(LANES, chans))):
            width = min(LANES, chans - part * LANES)
            res_ref[n, part, 40:184, :width] = mine[:, lanes]
            res_ref[n, part, 0:40, :width] = mine[104:144, lanes]
        for row in range(WIN_LAT):
            for pair in range(HALF // 2):
                tiles = []
                for col in (2 * pair, 2 * pair + 1):
                    at = pl.ds(4 + row * HALF + col, LEVELS, stride=36)
                    tiles += [res_ref[n, part, at, :] for part in range(2)]
                shifted = [pltpu.roll(x, SPARE, 1) for x in tiles[2:]]
                tiles = [tiles[0], jnp.where(low, tiles[1], shifted[0])]
                tiles.append(jnp.where(low, shifted[0], shifted[1]))
                tiles = jnp.concatenate(tiles, axis=1).astype(jnp.bfloat16)
                out_ref[n, row, :, pair * 2 * chans : (pair + 1) * 2 * chans] = tiles
    if extra == "send":
        extra_out[0] = extra_ref[0, EDGE:]
        extra_out[1] = out_ref[0, EDGE:]


def run_units(units, near, far, weights, chans, heads, table, extra=None, extra_in=None):
    count = len(units)
    pieces = [x for is_near, _ in units for x in (near if is_near else far)]
    piece = pieces[0]
    outs = [jax.ShapeDtypeStruct((count, WIN_LAT) + piece.shape[1:], piece.dtype)]
    operands = (*pieces, *weights, table)
    if extra == "send":
        outs.append(jax.ShapeDtypeStruct((2, EDGE) + piece.shape[1:], piece.dtype))
    elif extra == "tables":
        outs.append(jax.ShapeDtypeStruct(table.shape, table.dtype))
    if extra:
        operands += (extra_in,)
    vmem = pl.BlockSpec(memory_space=pltpu.VMEM)
    return pl.pallas_call(
        functools.partial(units_kernel, chans, heads, units, extra),
        out_shape=outs,
        in_specs=[vmem] * len(operands),
        out_specs=[vmem] * len(outs),
        scratch_shapes=[
            pltpu.VMEM((count, 2, LEVELS * QUERIES, LANES), jnp.float32),
            pltpu.VMEM((count, 2, 184, LANES), jnp.float32),
            pltpu.VMEM((count, 2, 184, LANES), jnp.float32),
        ],
        compiler_params=pltpu.CompilerParams(vmem_limit_bytes=VMEM_BYTES),
        cost_estimate=pl.CostEstimate(
            flops=200_000_000 * count, bytes_accessed=3_000_000, transcendentals=250_000 * count
        ),
        name="swin_windows",
    )(*operands)


def shards(
    field_in, norm1_gain, qkv_weight, proj_weight, earth_bias, norm2_gain, fc1_weight, fc2_weight
):
    levels, rows, flat = field_in.shape
    chans = qkv_weight.shape[0]
    heads = earth_bias.shape[2]
    half = HALF * chans
    field = jnp.transpose(field_in, (1, 0, 2))
    south = moved(field[:EDGE], "lat", -1)
    weights = (
        norm1_gain.reshape(1, chans),
        qkv_weight,
        proj_weight,
        norm2_gain.reshape(1, chans),
        fc1_weight,
        jnp.transpose(fc2_weight),
    )
    vmem = pl.BlockSpec(memory_space=pltpu.VMEM)
    anywhere = pl.BlockSpec(memory_space=pl.ANY)
    piece = jax.ShapeDtypeStruct((rows, levels, half), field.dtype)
    table = jax.ShapeDtypeStruct((2, 2, 2, heads * QUERIES, LANES), jnp.float32)
    windows, zwin, _, entries = earth_bias.shape
    tiles = entries // LANES
    bias = earth_bias.reshape(windows, zwin, heads, tiles, LANES).transpose(0, 2, 3, 1, 4)
    sources = (bias, field) + weights
    raw = jax.ShapeDtypeStruct((bias.size // windows // LANES, LANES), bias.dtype)
    sources = [pltpu.with_memory_space_constraint(x, pltpu.HBM) for x in sources]
    outs = [table, raw, piece, piece] + [jax.ShapeDtypeStruct(x.shape, x.dtype) for x in weights]
    table, inner, near, far, *weights = pl.pallas_call(
        functools.partial(table_kernel, len(weights), heads),
        out_shape=outs,
        in_specs=[pl.BlockSpec(memory_space=pltpu.HBM)] * len(sources),
        out_specs=[vmem] * len(outs),
        scratch_shapes=[
            pltpu.VMEM(raw.shape, raw.dtype),
            pltpu.SemaphoreType.DMA((4 + len(weights),)),
        ],
        compiler_params=pltpu.CompilerParams(vmem_limit_bytes=VMEM_BYTES),
        cost_estimate=pl.CostEstimate(flops=4_000_000, bytes_accessed=6_000_000, transcendentals=0),
        name="bias_tables",
    )(*sources)

    def pack(which, kept, *after):
        return pl.pallas_call(
            functools.partial(pack_kernel, which),
            out_shape=piece,
            in_specs=[vmem] * 2 + [anywhere] * len(after),
            out_specs=vmem,
            compiler_params=pltpu.CompilerParams(vmem_limit_bytes=VMEM_BYTES),
            cost_estimate=pl.CostEstimate(flops=0, bytes_accessed=250_000, transcendentals=0),
            name="pack_half",
        )(south, kept, *after)

    far = pack(1, far)
    near = pack(0, near, far)
    far_halo = swapped(far, "lon", 1)
    near_halo = swapped(near, "lon", 0)
    near, far = (near, near_halo), (far, far_halo)
    common = (near, far, weights, chans, heads)
    near_low, inner = run_units(((True, 1),), *common, table, "tables", inner)
    far_low, send = run_units(((False, 1),), *common, table, "send", near_low)
    top = moved(send, "lat", 1)
    (high,) = run_units(((True, 0), (False, 0)), *common, inner)
    done = pl.pallas_call(
        last_kernel,
        out_shape=jax.ShapeDtypeStruct(field.shape, field.dtype),
        in_specs=[vmem] * 4,
        out_specs=anywhere,
        scratch_shapes=[pltpu.SemaphoreType.DMA((6,))],
        compiler_params=pltpu.CompilerParams(vmem_limit_bytes=VMEM_BYTES),
        cost_estimate=pl.CostEstimate(flops=0, bytes_accessed=400_000, transcendentals=0),
        name="last_rows",
    )(top, high, near_low, far_low)
    return jnp.transpose(done, (1, 0, 2))


def solution(mesh):
    in_specs = (P(None, "lat", "lon"), P(), P(), P(), P("lat", None, None, None), P(), P(), P())
    out_specs = P(None, "lat", "lon")
    return jax.shard_map(shards, mesh=mesh, in_specs=in_specs, out_specs=out_specs, check_vma=False)
```

```python
import functools

import jax
import jax.numpy as jnp
from jax import lax
from jax.experimental import pallas as pl
from jax.experimental.pallas import tpu as pltpu
from jax.sharding import PartitionSpec as P

LEVELS = 4
WIN_LEV = 2
WIN_LAT = 6
WIN_LON = 12
EDGE = WIN_LAT // 2
HALF = WIN_LON // 2
TOKENS = WIN_LEV * WIN_LAT * WIN_LON
QUERIES = TOKENS // 2
LOG2E = 1.4426950408889634
GELU_0 = 0.7978845608028654
GELU_1 = 0.044715 * GELU_0
LANES = 128
SPARE = 64
VMEM_BYTES = 8 * 2**20
NT = (((1,), (1,)), ((), ()))


def moved(x, axis, by):
    size = lax.axis_size(axis)
    return lax.ppermute(x, axis, [(i, (i + by) % size) for i in range(size)])


def swapped(x, axis, first):
    size = lax.axis_size(axis)
    pairs = []
    for i in range(first, size, 2):
        j = (i + 1) % size
        pairs += [(i, j), (j, i)]
    return lax.ppermute(x, axis, pairs)


def half_places(half):
    odd = lax.rem(lax.axis_index("lon"), 2)
    return pl.multiple_of((1 - odd) * half, LANES), pl.multiple_of(odd * half, LANES)


def pack_kernel(which, south_ref, kept_ref, *rest):
    piece_ref = rest[-1]
    at = half_places(piece_ref.shape[2])[which]
    rows = piece_ref.shape[0] - EDGE
    piece_ref[:rows] = kept_ref[:rows]
    piece_ref[rows:] = south_ref[:, :, pl.ds(at, piece_ref.shape[2])]


def pick_kernel(both_ref, out_ref, sem):
    odd = lax.rem(lax.axis_index("lon"), 2)
    copy = pltpu.make_async_copy(both_ref.at[1 - odd], out_ref, sem)
    copy.start()
    copy.wait()


def last_kernel(top_ref, high_ref, near_low_ref, far_low_ref, out_ref, sems):
    half = top_ref.shape[3]
    copies = []
    for n, at in enumerate(half_places(half)):
        target = out_ref.at[:, :, pl.ds(at, half)]
        low_ref = (near_low_ref, far_low_ref)[n]
        for source, first in (
            (high_ref.at[n], EDGE),
            (low_ref.at[0, :EDGE], EDGE + WIN_LAT),
            (top_ref.at[n], 0),
        ):
            rows = pl.ds(first, source.shape[0])
            copy = pltpu.make_async_copy(source, target.at[rows], sems.at[len(copies)])
            copy.start()
            copies.append(copy)
    for copy in copies:
        copy.wait()


def build_tables(bias_ref, table_ref, heads, wrap):
    lines = bias_ref.shape[0] // heads
    blocks = WIN_LEV * WIN_LAT // 2
    lane = lax.broadcasted_iota(jnp.int32, (blocks, LANES), 1)
    block = lax.broadcasted_iota(jnp.int32, (blocks, LANES), 0)
    is_last = lax.axis_index("lat") == lax.axis_size("lat") - 1
    last = jnp.where(is_last, -1e9, 0.0).astype(jnp.float32)

    def penalty(part, second, levels):
        key = lane + part * LANES
        key_lev = key // QUERIES
        key_side = (key - key_lev * QUERIES) // (QUERIES // 2)
        row = 2 * block + second
        lev = row // WIN_LAT
        side = (row - lev * WIN_LAT) // EDGE
        out = jnp.zeros((blocks, LANES), jnp.float32)
        if levels:
            out = jnp.where(key_lev != lev, -1e9, out)
        if wrap:
            out = out + jnp.where(key_side != side, last, 0.0)
        return out

    masks = {
        (p, part, second): penalty(part, second, p == 1)
        for p in range(2)
        for part in range(2)
        for second in range(2)
    }
    for h in range(heads):
        for p in range(2):
            for third in range(3):
                line = h * lines + p + third * 18
                pieces = [
                    bias_ref[pl.ds(line + 2 * u, blocks, stride=54), :] * LOG2E for u in range(9)
                ]
                for r in range(8):
                    shift = 16 * r
                    main, nxt = pieces[r], pieces[r + 1]
                    if r:
                        main = pltpu.roll(main, LANES - shift, 1)
                        nxt = pltpu.roll(nxt, LANES - shift, 1)
                        main = jnp.where(lane < LANES - shift, main, nxt)
                    second, col = divmod(8 * third + r, WIN_LON)
                    side = col // HALF
                    place = h * QUERIES + HALF * second + col % HALF
                    at = pl.ds(place, blocks, stride=WIN_LON)
                    for part, piece in enumerate((main, nxt)):
                        table_ref[p, 1 - side, part, at, :] = piece + masks[p, part, second]


def table_kernel(count, heads, *refs):
    bias_any, field_any, *weights_any = refs[: 2 + count]
    table_ref, inner_ref, near_ref, far_ref, *weights_ref = refs[2 + count : 6 + 2 * count]
    bias_ref, sems = refs[6 + 2 * count :]
    lines = bias_ref.shape[0]
    flat = bias_any.reshape(2 * lines, LANES)
    rows, half = field_any.shape[0] - EDGE, near_ref.shape[2]
    near_at, far_at = half_places(half)
    fetches = [
        (flat.at[pl.ds(lines, lines)], bias_ref),
        (field_any.at[EDGE:, :, pl.ds(far_at, half)], far_ref.at[:rows]),
        (field_any.at[EDGE:, :, pl.ds(near_at, half)], near_ref.at[:rows]),
        (flat.at[pl.ds(0, lines)], inner_ref),
    ]
    fetches += list(zip(weights_any, weights_ref))
    fetches = [
        pltpu.make_async_copy(source, target, sems.at[n])
        for n, (source, target) in enumerate(fetches)
    ]
    for copy in fetches:
        copy.start()
    fetches[0].wait()
    build_tables(bias_ref, table_ref, heads, True)
    for copy in fetches[1:]:
        copy.wait()


def layer_norm(values, gain):
    center = values - jnp.mean(values, axis=-1, keepdims=True)
    spread = jnp.mean(center * center, axis=-1, keepdims=True)
    return center * lax.rsqrt(spread + 1e-05) * gain


def gelu(x):
    half = 0.5 * x
    return half + half * jnp.tanh(x * (GELU_0 + GELU_1 * (x * x)))


def units_kernel(chans, heads, units, extra, *refs):
    count = len(units)
    pieces, refs = refs[: 2 * count], refs[2 * count :]
    gain1_ref, qkv_ref, proj_ref, gain2_ref, fc1_ref, fc2_ref, table_ref, *refs = refs
    if extra:
        extra_ref, out_ref, extra_out, keys_ref, own_ref, res_ref = refs
    else:
        out_ref, keys_ref, own_ref, res_ref = refs
    if extra == "tables":
        build_tables(extra_ref, extra_out, heads, False)
    head_dim = chans // heads
    low = lax.broadcasted_iota(jnp.int32, (1, LANES), 1) < SPARE
    odd = lax.rem(lax.axis_index("lon"), 2)
    rights = [1 - odd if near else odd for near, _ in units]

    def tokens_of(ref, at, first, count):
        both = [ref[at, part, first : first + count] for part in range(2)]
        return jnp.concatenate([both[0], both[1][:, : chans - LANES]], axis=1)

    def split(ref, row):
        for pair in range(HALF // 2):
            both = ref[row, :, pair * 2 * chans : (pair + 1) * 2 * chans].astype(jnp.float32)
            first, middle, final = (both[:, u * LANES : (u + 1) * LANES] for u in range(3))
            yield 2 * pair, (first, middle)
            middle, final = pltpu.roll(middle, SPARE, 1), pltpu.roll(final, SPARE, 1)
            yield 2 * pair + 1, (jnp.where(low, middle, final), final)

    for n, (_, window) in enumerate(units):
        own_piece, halo_piece = pieces[2 * n], pieces[2 * n + 1]
        halo_at = rights[n] * HALF
        own_at = HALF - halo_at
        for row in range(WIN_LAT):
            for col, block in split(halo_piece, window * WIN_LAT + row):
                at = pl.ds(row * WIN_LON + col + halo_at, LEVELS, stride=QUERIES)
                for part in range(2):
                    keys_ref[n, part, at, :] = block[part]
            for col, block in split(own_piece, window * WIN_LAT + row):
                at = pl.ds(row * WIN_LON + col + own_at, LEVELS, stride=QUERIES)
                place = row * HALF + col
                for part in range(2):
                    keys_ref[n, part, at, :] = block[part]
                    own_ref[n, part, pl.ds(4 + place, LEVELS, stride=36), :] = block[part]
                    own_ref[n, part, pl.ds(148 + place, 1), :] = block[part][:1]

    gain1 = gain1_ref[...]
    lane = lax.broadcasted_iota(jnp.int32, (1, chans), 1)
    ones = jnp.ones((TOKENS, 2 * LANES - chans), jnp.float32)
    mixed = []
    for n, (_, window) in enumerate(units):
        normed = []
        for p in range(2):
            levels = [(2 * p + 1 + lev) % LEVELS for lev in range(WIN_LEV)]
            parts = [tokens_of(keys_ref, n, lev * QUERIES, QUERIES) for lev in levels]
            parts = [layer_norm(x, gain1) for x in parts]
            normed.append(jnp.concatenate(parts, axis=0).astype(jnp.bfloat16))
        normed = jnp.concatenate(normed, axis=0)
        keys = jnp.dot(normed, qkv_ref[:, chans : 2 * chans], preferred_element_type=jnp.float32)
        values = jnp.dot(normed, qkv_ref[:, 2 * chans :], preferred_element_type=jnp.float32)
        own = layer_norm(tokens_of(own_ref, n, 40, 144), gain1).astype(jnp.bfloat16)
        query = jnp.dot(own, qkv_ref[:, :chans], preferred_element_type=jnp.float32)
        query = query * (head_dim ** (-0.5) * LOG2E)
        for p in range(2):
            q = query[p * QUERIES : (p + 1) * QUERIES]
            k = keys[p * TOKENS : (p + 1) * TOKENS].astype(jnp.bfloat16)
            v = jnp.concatenate([values[p * TOKENS : (p + 1) * TOKENS], ones], axis=1)
            v = v.astype(jnp.bfloat16)
            picked = [
                jnp.where((lane >= h * head_dim) & (lane < (h + 1) * head_dim), q, 0.0)
                for h in range(heads)
            ]
            picked = jnp.concatenate(picked, axis=0).astype(jnp.bfloat16)
            scores = lax.dot_general(picked, k, NT, preferred_element_type=jnp.float32)
            probs = []
            for h in range(heads):
                at = slice(h * QUERIES, (h + 1) * QUERIES)
                bias = [table_ref[p, rights[n], part, at] for part in range(2)]
                bias = jnp.concatenate([bias[0], bias[1][:, : TOKENS - LANES]], axis=1)
                part = scores[at] + bias
                probs.append(jnp.exp2(part - jnp.max(part, axis=1, keepdims=True)))
            probs = jnp.concatenate(probs, axis=0).astype(jnp.bfloat16)
            got = jnp.dot(probs, v, preferred_element_type=jnp.float32)
            out = None
            for h in range(heads):
                part = got[h * QUERIES : (h + 1) * QUERIES]
                scaled = part[:, :chans] * (1.0 / part[:, chans : chans + 1])
                out = jnp.where(lane >= h * head_dim, scaled, out) if h else scaled
            mixed.append(out)
    mixed = jnp.concatenate(mixed, axis=0).astype(jnp.bfloat16)
    attn = jnp.dot(mixed, proj_ref[...], preferred_element_type=jnp.float32)
    attn = attn.astype(jnp.bfloat16).astype(jnp.float32)
    resid, normed = [], []
    for n in range(count):
        part = tokens_of(own_ref, n, 40, 144) + attn[n * 144 : (n + 1) * 144]
        resid.append(part.astype(jnp.bfloat16).astype(jnp.float32))
        normed.append(layer_norm(resid[n], gain2_ref[...]).astype(jnp.bfloat16))
    result, normed = jnp.concatenate(resid, axis=0), jnp.concatenate(normed, axis=0)
    for first in range(0, fc1_ref.shape[1], 2 * LANES):
        units_at = slice(first, first + 2 * LANES)
        hidden = jnp.dot(normed, fc1_ref[:, units_at], preferred_element_type=jnp.float32)
        hidden = gelu(hidden).astype(jnp.bfloat16)
        result = result + lax.dot_general(
            hidden, fc2_ref[:, units_at], NT, preferred_element_type=jnp.float32
        )
    for n in range(count):
        mine = result[n * 144 : (n + 1) * 144]
        for part, lanes in enumerate((slice(0, LANES), slice(LANES, chans))):
            width = min(LANES, chans - part * LANES)
            res_ref[n, part, 40:184, :width] = mine[:, lanes]
            res_ref[n, part, 0:40, :width] = mine[104:144, lanes]
        for row in range(WIN_LAT):
            for pair in range(HALF // 2):
                tiles = []
                for col in (2 * pair, 2 * pair + 1):
                    at = pl.ds(4 + row * HALF + col, LEVELS, stride=36)
                    tiles += [res_ref[n, part, at, :] for part in range(2)]
                shifted = [pltpu.roll(x, SPARE, 1) for x in tiles[2:]]
                tiles = [tiles[0], jnp.where(low, tiles[1], shifted[0])]
                tiles.append(jnp.where(low, shifted[0], shifted[1]))
                tiles = jnp.concatenate(tiles, axis=1).astype(jnp.bfloat16)
                out_ref[n, row, :, pair * 2 * chans : (pair + 1) * 2 * chans] = tiles
    if extra == "send":
        extra_out[0] = extra_ref[0, EDGE:]
        extra_out[1] = out_ref[0, EDGE:]


def run_units(units, near, far, weights, chans, heads, table, extra=None, extra_in=None):
    count = len(units)
    pieces = [x for is_near, _ in units for x in (near if is_near else far)]
    piece = pieces[0]
    outs = [jax.ShapeDtypeStruct((count, WIN_LAT) + piece.shape[1:], piece.dtype)]
    operands = (*pieces, *weights, table)
    if extra == "send":
        outs.append(jax.ShapeDtypeStruct((2, EDGE) + piece.shape[1:], piece.dtype))
    elif extra == "tables":
        outs.append(jax.ShapeDtypeStruct(table.shape, table.dtype))
    if extra:
        operands += (extra_in,)
    vmem = pl.BlockSpec(memory_space=pltpu.VMEM)
    return pl.pallas_call(
        functools.partial(units_kernel, chans, heads, units, extra),
        out_shape=outs,
        in_specs=[vmem] * len(operands),
        out_specs=[vmem] * len(outs),
        scratch_shapes=[
            pltpu.VMEM((count, 2, LEVELS * QUERIES, LANES), jnp.float32),
            pltpu.VMEM((count, 2, 184, LANES), jnp.float32),
            pltpu.VMEM((count, 2, 184, LANES), jnp.float32),
        ],
        compiler_params=pltpu.CompilerParams(vmem_limit_bytes=VMEM_BYTES),
        cost_estimate=pl.CostEstimate(
            flops=200_000_000 * count, bytes_accessed=3_000_000, transcendentals=250_000 * count
        ),
        name="swin_windows",
    )(*operands)


def shards(
    field_in, norm1_gain, qkv_weight, proj_weight, earth_bias, norm2_gain, fc1_weight, fc2_weight
):
    levels, rows, flat = field_in.shape
    chans = qkv_weight.shape[0]
    heads = earth_bias.shape[2]
    half = HALF * chans
    field = jnp.transpose(field_in, (1, 0, 2))
    south = moved(field[:EDGE], "lat", -1)
    weights = (
        norm1_gain.reshape(1, chans),
        qkv_weight,
        proj_weight,
        norm2_gain.reshape(1, chans),
        fc1_weight,
        jnp.transpose(fc2_weight),
    )
    vmem = pl.BlockSpec(memory_space=pltpu.VMEM)
    anywhere = pl.BlockSpec(memory_space=pl.ANY)
    piece = jax.ShapeDtypeStruct((rows, levels, half), field.dtype)
    table = jax.ShapeDtypeStruct((2, 2, 2, heads * QUERIES, LANES), jnp.float32)
    windows, zwin, _, entries = earth_bias.shape
    tiles = entries // LANES
    bias = earth_bias.reshape(windows, zwin, heads, tiles, LANES).transpose(0, 2, 3, 1, 4)
    sources = (bias, field) + weights
    raw = jax.ShapeDtypeStruct((bias.size // windows // LANES, LANES), bias.dtype)
    sources = [pltpu.with_memory_space_constraint(x, pltpu.HBM) for x in sources]
    outs = [table, raw, piece, piece] + [jax.ShapeDtypeStruct(x.shape, x.dtype) for x in weights]
    table, inner, near, far, *weights = pl.pallas_call(
        functools.partial(table_kernel, len(weights), heads),
        out_shape=outs,
        in_specs=[pl.BlockSpec(memory_space=pltpu.HBM)] * len(sources),
        out_specs=[vmem] * len(outs),
        scratch_shapes=[
            pltpu.VMEM(raw.shape, raw.dtype),
            pltpu.SemaphoreType.DMA((4 + len(weights),)),
        ],
        compiler_params=pltpu.CompilerParams(vmem_limit_bytes=VMEM_BYTES),
        cost_estimate=pl.CostEstimate(flops=4_000_000, bytes_accessed=6_000_000, transcendentals=0),
        name="bias_tables",
    )(*sources)

    def pack(which, kept, *after):
        return pl.pallas_call(
            functools.partial(pack_kernel, which),
            out_shape=piece,
            in_specs=[vmem] * 2 + [anywhere] * len(after),
            out_specs=vmem,
            compiler_params=pltpu.CompilerParams(vmem_limit_bytes=VMEM_BYTES),
            cost_estimate=pl.CostEstimate(flops=0, bytes_accessed=250_000, transcendentals=0),
            name="pack_half",
        )(south, kept, *after)

    far = pack(1, far)
    near = pack(0, near, far)
    far_halo = swapped(far, "lon", 1)
    lons = lax.axis_size("lon")
    both = lax.all_gather(near, "lon", axis_index_groups=[[i, i + 1] for i in range(0, lons, 2)])
    near_halo = pl.pallas_call(
        pick_kernel,
        out_shape=piece,
        in_specs=[anywhere],
        out_specs=vmem,
        scratch_shapes=[pltpu.SemaphoreType.DMA],
        compiler_params=pltpu.CompilerParams(vmem_limit_bytes=VMEM_BYTES),
        cost_estimate=pl.CostEstimate(flops=0, bytes_accessed=250_000, transcendentals=0),
        name="pick_halo",
    )(both)
    near, far = (near, near_halo), (far, far_halo)
    common = (near, far, weights, chans, heads)
    near_low, inner = run_units(((True, 1),), *common, table, "tables", inner)
    far_low, send = run_units(((False, 1),), *common, table, "send", near_low)
    top = moved(send, "lat", 1)
    (high,) = run_units(((True, 0), (False, 0)), *common, inner)
    done = pl.pallas_call(
        last_kernel,
        out_shape=jax.ShapeDtypeStruct(field.shape, field.dtype),
        in_specs=[vmem] * 4,
        out_specs=anywhere,
        scratch_shapes=[pltpu.SemaphoreType.DMA((6,))],
        compiler_params=pltpu.CompilerParams(vmem_limit_bytes=VMEM_BYTES),
        cost_estimate=pl.CostEstimate(flops=0, bytes_accessed=400_000, transcendentals=0),
        name="last_rows",
    )(top, high, near_low, far_low)
    return jnp.transpose(done, (1, 0, 2))


def solution(mesh):
    in_specs = (P(None, "lat", "lon"), P(), P(), P(), P("lat", None, None, None), P(), P(), P())
    out_specs = P(None, "lat", "lon")
    return jax.shard_map(shards, mesh=mesh, in_specs=in_specs, out_specs=out_specs, check_vma=False)
```

```python
import functools

import jax
import jax.numpy as jnp
from jax import lax
from jax.experimental import pallas as pl
from jax.experimental.pallas import tpu as pltpu
from jax.sharding import PartitionSpec as P

LEVELS = 4
WIN_LEV = 2
WIN_LAT = 6
WIN_LON = 12
EDGE = WIN_LAT // 2
HALF = WIN_LON // 2
TOKENS = WIN_LEV * WIN_LAT * WIN_LON
QUERIES = TOKENS // 2
LOG2E = 1.4426950408889634
GELU_0 = 0.7978845608028654
GELU_1 = 0.044715 * GELU_0
LANES = 128
SPARE = 64
VMEM_BYTES = 8 * 2**20
NT = (((1,), (1,)), ((), ()))


def moved(x, axis, by):
    size = lax.axis_size(axis)
    return lax.ppermute(x, axis, [(i, (i + by) % size) for i in range(size)])


def swapped(x, axis, first):
    size = lax.axis_size(axis)
    pairs = []
    for i in range(first, size, 2):
        j = (i + 1) % size
        pairs += [(i, j), (j, i)]
    return lax.ppermute(x, axis, pairs)


def half_places(half):
    odd = lax.rem(lax.axis_index("lon"), 2)
    return pl.multiple_of((1 - odd) * half, LANES), pl.multiple_of(odd * half, LANES)


def pack_kernel(which, south_ref, kept_ref, *rest):
    piece_ref = rest[-1]
    at = half_places(piece_ref.shape[2])[which]
    rows = piece_ref.shape[0] - EDGE
    piece_ref[:rows] = kept_ref[:rows]
    piece_ref[rows:] = south_ref[:, :, pl.ds(at, piece_ref.shape[2])]


def last_kernel(top_ref, high_ref, near_low_ref, far_low_ref, out_ref, sems):
    half = top_ref.shape[3]
    copies = []
    for n, at in enumerate(half_places(half)):
        target = out_ref.at[:, :, pl.ds(at, half)]
        low_ref = (near_low_ref, far_low_ref)[n]
        for source, first in (
            (high_ref.at[n], EDGE),
            (low_ref.at[0, :EDGE], EDGE + WIN_LAT),
            (top_ref.at[n], 0),
        ):
            rows = pl.ds(first, source.shape[0])
            copy = pltpu.make_async_copy(source, target.at[rows], sems.at[len(copies)])
            copy.start()
            copies.append(copy)
    for copy in copies:
        copy.wait()


def table_kernel(count, *refs):
    bias_any, field_any, *weights_any = refs[: 2 + count]
    table_ref, near_ref, far_ref, *weights_ref = refs[2 + count : 5 + 2 * count]
    bias_ref, sems, side_sems = refs[5 + 2 * count :]
    windows, heads, tiles = bias_any.shape[:3]
    lines = bias_ref.shape[0]
    flat = bias_any.reshape(lines, LANES)
    parts = windows
    copies = []
    for n in range(parts):
        at = pl.ds(n * (lines // parts), lines // parts)
        copies.append(pltpu.make_async_copy(flat.at[at], bias_ref.at[at], sems.at[n]))
        copies[-1].start()
    rows, half = field_any.shape[0] - EDGE, near_ref.shape[2]
    near_at, far_at = half_places(half)
    fetches = [
        (field_any.at[EDGE:, :, pl.ds(far_at, half)], far_ref.at[:rows]),
        (field_any.at[EDGE:, :, pl.ds(near_at, half)], near_ref.at[:rows]),
    ]
    fetches += list(zip(weights_any, weights_ref))
    fetches = [
        pltpu.make_async_copy(source, target, side_sems.at[n])
        for n, (source, target) in enumerate(fetches)
    ]
    for copy in fetches:
        copy.start()
    blocks = WIN_LEV * WIN_LAT // 2
    lane = lax.broadcasted_iota(jnp.int32, (blocks, LANES), 1)
    block = lax.broadcasted_iota(jnp.int32, (blocks, LANES), 0)
    is_last = lax.axis_index("lat") == lax.axis_size("lat") - 1
    last = jnp.where(is_last, -1e9, 0.0).astype(jnp.float32)

    def penalty(part, second, levels, wrap):
        key = lane + part * LANES
        key_lev = key // QUERIES
        key_side = (key - key_lev * QUERIES) // (QUERIES // 2)
        row = 2 * block + second
        lev = row // WIN_LAT
        side = (row - lev * WIN_LAT) // EDGE
        out = jnp.zeros((blocks, LANES), jnp.float32)
        if levels:
            out = jnp.where(key_lev != lev, -1e9, out)
        if wrap:
            out = out + jnp.where(key_side != side, last, 0.0)
        return out

    for k in range(windows):
        masks = {
            (p, part, second): penalty(part, second, p == 1, k == windows - 1)
            for p in range(2)
            for part in range(2)
            for second in range(2)
        }
        copies[k].wait()
        for h in range(heads):
            for p in range(2):
                base = (k * heads + h) * 2 * tiles + p
                for third in range(3):
                    line = base + third * 18
                    pieces = [
                        bias_ref[pl.ds(line + 2 * u, blocks, stride=54), :] * LOG2E
                        for u in range(9)
                    ]
                    for r in range(8):
                        shift = 16 * r
                        main, nxt = pieces[r], pieces[r + 1]
                        if r:
                            main = pltpu.roll(main, LANES - shift, 1)
                            nxt = pltpu.roll(nxt, LANES - shift, 1)
                            main = jnp.where(lane < LANES - shift, main, nxt)
                        second, col = divmod(8 * third + r, WIN_LON)
                        side = col // HALF
                        place = h * QUERIES + HALF * second + col % HALF
                        at = pl.ds(place, blocks, stride=WIN_LON)
                        for part, piece in enumerate((main, nxt)):
                            filled = piece + masks[p, part, second]
                            table_ref[k, p, 1 - side, part, at, :] = filled
    for copy in fetches:
        copy.wait()


def layer_norm(values, gain):
    center = values - jnp.mean(values, axis=-1, keepdims=True)
    spread = jnp.mean(center * center, axis=-1, keepdims=True)
    return center * lax.rsqrt(spread + 1e-05) * gain


def gelu(x):
    half = 0.5 * x
    return half + half * jnp.tanh(x * (GELU_0 + GELU_1 * (x * x)))


def units_kernel(chans, heads, units, lower, *refs):
    count = len(units)
    pieces, refs = refs[: 2 * count], refs[2 * count :]
    gain1_ref, qkv_ref, proj_ref, gain2_ref, fc1_ref, fc2_ref, table_ref, *refs = refs
    if lower:
        lower_ref, out_ref, send_ref, keys_ref, own_ref, res_ref = refs
    else:
        out_ref, keys_ref, own_ref, res_ref = refs
    head_dim = chans // heads
    low = lax.broadcasted_iota(jnp.int32, (1, LANES), 1) < SPARE
    odd = lax.rem(lax.axis_index("lon"), 2)
    rights = [1 - odd if near else odd for near, _ in units]

    def tokens_of(ref, at, first, count):
        both = [ref[at, part, first : first + count] for part in range(2)]
        return jnp.concatenate([both[0], both[1][:, : chans - LANES]], axis=1)

    def split(ref, row):
        for pair in range(HALF // 2):
            both = ref[row, :, pair * 2 * chans : (pair + 1) * 2 * chans].astype(jnp.float32)
            first, middle, final = (both[:, u * LANES : (u + 1) * LANES] for u in range(3))
            yield 2 * pair, (first, middle)
            middle, final = pltpu.roll(middle, SPARE, 1), pltpu.roll(final, SPARE, 1)
            yield 2 * pair + 1, (jnp.where(low, middle, final), final)

    for n, (_, window) in enumerate(units):
        own_piece, halo_piece = pieces[2 * n], pieces[2 * n + 1]
        halo_at = rights[n] * HALF
        own_at = HALF - halo_at
        for row in range(WIN_LAT):
            for col, block in split(halo_piece, window * WIN_LAT + row):
                at = pl.ds(row * WIN_LON + col + halo_at, LEVELS, stride=QUERIES)
                for part in range(2):
                    keys_ref[n, part, at, :] = block[part]
            for col, block in split(own_piece, window * WIN_LAT + row):
                at = pl.ds(row * WIN_LON + col + own_at, LEVELS, stride=QUERIES)
                place = row * HALF + col
                for part in range(2):
                    keys_ref[n, part, at, :] = block[part]
                    own_ref[n, part, pl.ds(4 + place, LEVELS, stride=36), :] = block[part]
                    own_ref[n, part, pl.ds(148 + place, 1), :] = block[part][:1]

    gain1, gain2 = gain1_ref[...], gain2_ref[...]
    lane = lax.broadcasted_iota(jnp.int32, (1, chans), 1)
    ones = jnp.ones((TOKENS, 2 * LANES - chans), jnp.float32)

    def level_window(n, window, p):
        levels = [(2 * p + 1 + lev) % LEVELS for lev in range(WIN_LEV)]
        parts = [tokens_of(keys_ref, n, lev * QUERIES, QUERIES) for lev in levels]
        parts = [layer_norm(x, gain1) for x in parts]
        normed = jnp.concatenate(parts, axis=0).astype(jnp.bfloat16)
        k = jnp.dot(normed, qkv_ref[:, chans : 2 * chans], preferred_element_type=jnp.float32)
        k = k.astype(jnp.bfloat16)
        v = jnp.dot(normed, qkv_ref[:, 2 * chans :], preferred_element_type=jnp.float32)
        v = jnp.concatenate([v, ones], axis=1).astype(jnp.bfloat16)
        tokens = tokens_of(own_ref, n, 40 + p * QUERIES, QUERIES)
        own = layer_norm(tokens, gain1).astype(jnp.bfloat16)
        q = jnp.dot(own, qkv_ref[:, :chans], preferred_element_type=jnp.float32)
        q = q * (head_dim ** (-0.5) * LOG2E)
        picked = [
            jnp.where((lane >= h * head_dim) & (lane < (h + 1) * head_dim), q, 0.0)
            for h in range(heads)
        ]
        picked = jnp.concatenate(picked, axis=0).astype(jnp.bfloat16)
        scores = lax.dot_general(picked, k, NT, preferred_element_type=jnp.float32)
        probs = []
        for h in range(heads):
            at = slice(h * QUERIES, (h + 1) * QUERIES)
            bias = [table_ref[window, p, rights[n], part, at] for part in range(2)]
            bias = jnp.concatenate([bias[0], bias[1][:, : TOKENS - LANES]], axis=1)
            part = scores[at] + bias
            probs.append(jnp.exp2(part - jnp.max(part, axis=1, keepdims=True)))
        probs = jnp.concatenate(probs, axis=0).astype(jnp.bfloat16)
        got = jnp.dot(probs, v, preferred_element_type=jnp.float32)
        mixed = None
        for h in range(heads):
            part = got[h * QUERIES : (h + 1) * QUERIES]
            scaled = part[:, :chans] * (1.0 / part[:, chans : chans + 1])
            mixed = jnp.where(lane >= h * head_dim, scaled, mixed) if h else scaled
        mixed = mixed.astype(jnp.bfloat16)
        attn = jnp.dot(mixed, proj_ref[...], preferred_element_type=jnp.float32)
        resid = tokens + attn.astype(jnp.bfloat16).astype(jnp.float32)
        result = resid = resid.astype(jnp.bfloat16).astype(jnp.float32)
        normed = layer_norm(resid, gain2).astype(jnp.bfloat16)
        for first in range(0, fc1_ref.shape[1], 2 * LANES):
            units_at = slice(first, first + 2 * LANES)
            hidden = jnp.dot(normed, fc1_ref[:, units_at], preferred_element_type=jnp.float32)
            hidden = gelu(hidden).astype(jnp.bfloat16)
            result = result + lax.dot_general(
                hidden, fc2_ref[:, units_at], NT, preferred_element_type=jnp.float32
            )
        for part, lanes in enumerate((slice(0, LANES), slice(LANES, chans))):
            width = min(LANES, chans - part * LANES)
            first = 40 + p * QUERIES
            res_ref[n, part, first : first + QUERIES, :width] = result[:, lanes]
            if p == 1:
                res_ref[n, part, 0:40, :width] = result[QUERIES - 40 :, lanes]

    for n, (_, window) in enumerate(units):
        for p in range(2):
            level_window(n, window, p)
    for n in range(count):
        for row in range(WIN_LAT):
            for pair in range(HALF // 2):
                tiles = []
                for col in (2 * pair, 2 * pair + 1):
                    at = pl.ds(4 + row * HALF + col, LEVELS, stride=36)
                    tiles += [res_ref[n, part, at, :] for part in range(2)]
                shifted = [pltpu.roll(x, SPARE, 1) for x in tiles[2:]]
                tiles = [tiles[0], jnp.where(low, tiles[1], shifted[0])]
                tiles.append(jnp.where(low, shifted[0], shifted[1]))
                tiles = jnp.concatenate(tiles, axis=1).astype(jnp.bfloat16)
                out_ref[n, row, :, pair * 2 * chans : (pair + 1) * 2 * chans] = tiles
    if lower:
        send_ref[0] = lower_ref[0, EDGE:]
        send_ref[1] = out_ref[0, EDGE:]


def run_units(units, near, far, table, weights, chans, heads, *lower):
    count = len(units)
    pieces = [x for is_near, _ in units for x in (near if is_near else far)]
    piece = pieces[0]
    out = jax.ShapeDtypeStruct((count, WIN_LAT) + piece.shape[1:], piece.dtype)
    send = jax.ShapeDtypeStruct((2, EDGE) + piece.shape[1:], piece.dtype)
    operands = (*pieces, *weights, table, *lower)
    vmem = pl.BlockSpec(memory_space=pltpu.VMEM)
    outs = [out, send] if lower else [out]
    return pl.pallas_call(
        functools.partial(units_kernel, chans, heads, units, bool(lower)),
        out_shape=outs,
        in_specs=[vmem] * len(operands),
        out_specs=[vmem] * len(outs),
        scratch_shapes=[
            pltpu.VMEM((count, 2, LEVELS * QUERIES, LANES), jnp.float32),
            pltpu.VMEM((count, 2, 184, LANES), jnp.float32),
            pltpu.VMEM((count, 2, 184, LANES), jnp.float32),
        ],
        compiler_params=pltpu.CompilerParams(vmem_limit_bytes=VMEM_BYTES),
        cost_estimate=pl.CostEstimate(
            flops=200_000_000 * count, bytes_accessed=3_000_000, transcendentals=250_000 * count
        ),
        name="swin_windows",
    )(*operands)


def shards(
    field_in, norm1_gain, qkv_weight, proj_weight, earth_bias, norm2_gain, fc1_weight, fc2_weight
):
    levels, rows, flat = field_in.shape
    chans = qkv_weight.shape[0]
    heads = earth_bias.shape[2]
    half = HALF * chans
    field = jnp.transpose(field_in, (1, 0, 2))
    south = moved(field[:EDGE], "lat", -1)
    weights = (
        norm1_gain.reshape(1, chans),
        qkv_weight,
        proj_weight,
        norm2_gain.reshape(1, chans),
        fc1_weight,
        jnp.transpose(fc2_weight),
    )
    vmem = pl.BlockSpec(memory_space=pltpu.VMEM)
    anywhere = pl.BlockSpec(memory_space=pl.ANY)
    piece = jax.ShapeDtypeStruct((rows, levels, half), field.dtype)
    table = jax.ShapeDtypeStruct((2, 2, 2, 2, heads * QUERIES, LANES), jnp.float32)
    windows, zwin, _, entries = earth_bias.shape
    tiles = entries // LANES
    bias = earth_bias.reshape(windows, zwin, heads, tiles, LANES).transpose(0, 2, 3, 1, 4)
    sources = (bias, field) + weights
    sources = [pltpu.with_memory_space_constraint(x, pltpu.HBM) for x in sources]
    outs = [table, piece, piece] + [jax.ShapeDtypeStruct(x.shape, x.dtype) for x in weights]
    table, near, far, *weights = pl.pallas_call(
        functools.partial(table_kernel, len(weights)),
        out_shape=outs,
        in_specs=[pl.BlockSpec(memory_space=pltpu.HBM)] * len(sources),
        out_specs=[vmem] * len(outs),
        scratch_shapes=[
            pltpu.VMEM((bias.size // LANES, LANES), jnp.float32),
            pltpu.SemaphoreType.DMA((2 * windows,)),
            pltpu.SemaphoreType.DMA((2 + len(weights),)),
        ],
        compiler_params=pltpu.CompilerParams(vmem_limit_bytes=VMEM_BYTES),
        cost_estimate=pl.CostEstimate(flops=4_000_000, bytes_accessed=6_000_000, transcendentals=0),
        name="bias_tables",
    )(*sources)

    def pack(which, kept, *after):
        return pl.pallas_call(
            functools.partial(pack_kernel, which),
            out_shape=piece,
            in_specs=[vmem] * 2 + [anywhere] * len(after),
            out_specs=vmem,
            compiler_params=pltpu.CompilerParams(vmem_limit_bytes=VMEM_BYTES),
            cost_estimate=pl.CostEstimate(flops=0, bytes_accessed=250_000, transcendentals=0),
            name="pack_half",
        )(south, kept, *after)

    far = pack(1, far)
    near = pack(0, near, far)
    far_halo = swapped(far, "lon", 1)
    near_halo = swapped(near, "lon", 0)
    near, far = (near, near_halo), (far, far_halo)
    common = (near, far, table, weights, chans, heads)
    (near_low,) = run_units(((True, 1),), *common)
    far_low, send = run_units(((False, 1),), *common, near_low)
    top = moved(send, "lat", 1)
    (high,) = run_units(((True, 0), (False, 0)), *common)
    done = pl.pallas_call(
        last_kernel,
        out_shape=jax.ShapeDtypeStruct(field.shape, field.dtype),
        in_specs=[vmem] * 4,
        out_specs=anywhere,
        scratch_shapes=[pltpu.SemaphoreType.DMA((6,))],
        compiler_params=pltpu.CompilerParams(vmem_limit_bytes=VMEM_BYTES),
        cost_estimate=pl.CostEstimate(flops=0, bytes_accessed=400_000, transcendentals=0),
        name="last_rows",
    )(top, high, near_low, far_low)
    return jnp.transpose(done, (1, 0, 2))


def solution(mesh):
    in_specs = (P(None, "lat", "lon"), P(), P(), P(), P("lat", None, None, None), P(), P(), P())
    out_specs = P(None, "lat", "lon")
    return jax.shard_map(shards, mesh=mesh, in_specs=in_specs, out_specs=out_specs, check_vma=False)
```

```python
import functools

import jax
import jax.numpy as jnp
from jax import lax
from jax.experimental import pallas as pl
from jax.experimental.pallas import tpu as pltpu
from jax.sharding import PartitionSpec as P

LEVELS = 4
WIN_LEV = 2
WIN_LAT = 6
WIN_LON = 12
EDGE = WIN_LAT // 2
HALF = WIN_LON // 2
TOKENS = WIN_LEV * WIN_LAT * WIN_LON
QUERIES = TOKENS // 2
LOG2E = 1.4426950408889634
GELU_0 = 0.7978845608028654
GELU_1 = 0.044715 * GELU_0
LANES = 128
SPARE = 64
VMEM_BYTES = 8 * 2**20
NT = (((1,), (1,)), ((), ()))


def moved(x, axis, by):
    size = lax.axis_size(axis)
    return lax.ppermute(x, axis, [(i, (i + by) % size) for i in range(size)])


def swapped(x, axis, first):
    size = lax.axis_size(axis)
    pairs = []
    for i in range(first, size, 2):
        j = (i + 1) % size
        pairs += [(i, j), (j, i)]
    return lax.ppermute(x, axis, pairs)


def half_places(half):
    odd = lax.rem(lax.axis_index("lon"), 2)
    return pl.multiple_of((1 - odd) * half, LANES), pl.multiple_of(odd * half, LANES)


def pack_kernel(which, south_ref, kept_ref, *rest):
    piece_ref = rest[-1]
    at = half_places(piece_ref.shape[2])[which]
    rows = piece_ref.shape[0] - EDGE
    piece_ref[:rows] = kept_ref[:rows]
    piece_ref[rows:] = south_ref[:, :, pl.ds(at, piece_ref.shape[2])]


def last_kernel(top_ref, high_ref, near_low_ref, far_low_ref, out_ref, sems):
    half = top_ref.shape[3]
    copies = []
    for n, at in enumerate(half_places(half)):
        target = out_ref.at[:, :, pl.ds(at, half)]
        low_ref = (near_low_ref, far_low_ref)[n]
        for source, first in (
            (high_ref.at[n], EDGE),
            (low_ref.at[0, :EDGE], EDGE + WIN_LAT),
            (top_ref.at[n], 0),
        ):
            rows = pl.ds(first, source.shape[0])
            copy = pltpu.make_async_copy(source, target.at[rows], sems.at[len(copies)])
            copy.start()
            copies.append(copy)
    for copy in copies:
        copy.wait()


def table_kernel(count, *refs):
    bias_any, field_any, *weights_any = refs[: 2 + count]
    table_ref, near_ref, far_ref, *weights_ref = refs[2 + count : 5 + 2 * count]
    bias_ref, sems, side_sems = refs[5 + 2 * count :]
    windows, heads, tiles = bias_any.shape[:3]
    lines = bias_ref.shape[0]
    flat = bias_any.reshape(lines, LANES)
    parts = windows
    copies = []
    for n in range(parts):
        at = pl.ds(n * (lines // parts), lines // parts)
        copies.append(pltpu.make_async_copy(flat.at[at], bias_ref.at[at], sems.at[n]))
        copies[-1].start()
    rows, half = field_any.shape[0] - EDGE, near_ref.shape[2]
    near_at, far_at = half_places(half)
    fetches = [
        (field_any.at[EDGE:, :, pl.ds(far_at, half)], far_ref.at[:rows]),
        (field_any.at[EDGE:, :, pl.ds(near_at, half)], near_ref.at[:rows]),
    ]
    fetches += list(zip(weights_any, weights_ref))
    fetches = [
        pltpu.make_async_copy(source, target, side_sems.at[n])
        for n, (source, target) in enumerate(fetches)
    ]
    for copy in fetches:
        copy.start()
    blocks = WIN_LEV * WIN_LAT // 2
    lane = lax.broadcasted_iota(jnp.int32, (blocks, LANES), 1)
    block = lax.broadcasted_iota(jnp.int32, (blocks, LANES), 0)
    is_last = lax.axis_index("lat") == lax.axis_size("lat") - 1
    last = jnp.where(is_last, -1e9, 0.0).astype(jnp.float32)

    def penalty(part, second, levels, wrap):
        key = lane + part * LANES
        key_lev = key // QUERIES
        key_side = (key - key_lev * QUERIES) // (QUERIES // 2)
        row = 2 * block + second
        lev = row // WIN_LAT
        side = (row - lev * WIN_LAT) // EDGE
        out = jnp.zeros((blocks, LANES), jnp.float32)
        if levels:
            out = jnp.where(key_lev != lev, -1e9, out)
        if wrap:
            out = out + jnp.where(key_side != side, last, 0.0)
        return out

    for k in range(windows):
        masks = {
            (p, part, second): penalty(part, second, p == 1, k == windows - 1)
            for p in range(2)
            for part in range(2)
            for second in range(2)
        }
        copies[k].wait()
        for h in range(heads):
            for p in range(2):
                base = (k * heads + h) * 2 * tiles + p
                for third in range(3):
                    line = base + third * 18
                    pieces = [
                        bias_ref[pl.ds(line + 2 * u, blocks, stride=54), :] * LOG2E
                        for u in range(9)
                    ]
                    for r in range(8):
                        shift = 16 * r
                        main, nxt = pieces[r], pieces[r + 1]
                        if r:
                            main = pltpu.roll(main, LANES - shift, 1)
                            nxt = pltpu.roll(nxt, LANES - shift, 1)
                            main = jnp.where(lane < LANES - shift, main, nxt)
                        second, col = divmod(8 * third + r, WIN_LON)
                        side = col // HALF
                        place = h * QUERIES + HALF * second + col % HALF
                        at = pl.ds(place, blocks, stride=WIN_LON)
                        for part, piece in enumerate((main, nxt)):
                            filled = piece + masks[p, part, second]
                            table_ref[k, p, 1 - side, part, at, :] = filled
    for copy in fetches:
        copy.wait()


def layer_norm(values, gain):
    center = values - jnp.mean(values, axis=-1, keepdims=True)
    spread = jnp.mean(center * center, axis=-1, keepdims=True)
    return center * lax.rsqrt(spread + 1e-05) * gain


def gelu(x):
    half = 0.5 * x
    return half + half * jnp.tanh(x * (GELU_0 + GELU_1 * (x * x)))


def units_kernel(chans, heads, units, lower, *refs):
    count = len(units)
    pieces, refs = refs[: 2 * count], refs[2 * count :]
    gain1_ref, qkv_ref, proj_ref, gain2_ref, fc1_ref, fc2_ref, table_ref, *refs = refs
    if lower:
        lower_ref, out_ref, send_ref, keys_ref, own_ref, res_ref = refs
    else:
        out_ref, keys_ref, own_ref, res_ref = refs
    head_dim = chans // heads
    low = lax.broadcasted_iota(jnp.int32, (1, LANES), 1) < SPARE
    odd = lax.rem(lax.axis_index("lon"), 2)
    rights = [1 - odd if near else odd for near, _ in units]

    def tokens_of(ref, at, first, count):
        both = [ref[at, part, first : first + count] for part in range(2)]
        return jnp.concatenate([both[0], both[1][:, : chans - LANES]], axis=1)

    def split(ref, row):
        for pair in range(HALF // 2):
            both = ref[row, :, pair * 2 * chans : (pair + 1) * 2 * chans].astype(jnp.float32)
            first, middle, final = (both[:, u * LANES : (u + 1) * LANES] for u in range(3))
            yield 2 * pair, (first, middle)
            middle, final = pltpu.roll(middle, SPARE, 1), pltpu.roll(final, SPARE, 1)
            yield 2 * pair + 1, (jnp.where(low, middle, final), final)

    for n, (_, window) in enumerate(units):
        own_piece, halo_piece = pieces[2 * n], pieces[2 * n + 1]
        halo_at = rights[n] * HALF
        own_at = HALF - halo_at
        for row in range(WIN_LAT):
            for col, block in split(halo_piece, window * WIN_LAT + row):
                at = pl.ds(row * WIN_LON + col + halo_at, LEVELS, stride=QUERIES)
                for part in range(2):
                    keys_ref[n, part, at, :] = block[part]
            for col, block in split(own_piece, window * WIN_LAT + row):
                at = pl.ds(row * WIN_LON + col + own_at, LEVELS, stride=QUERIES)
                place = row * HALF + col
                for part in range(2):
                    keys_ref[n, part, at, :] = block[part]
                    own_ref[n, part, pl.ds(4 + place, LEVELS, stride=36), :] = block[part]
                    own_ref[n, part, pl.ds(148 + place, 1), :] = block[part][:1]

    gain1 = gain1_ref[...]
    lane = lax.broadcasted_iota(jnp.int32, (1, chans), 1)
    ones = jnp.ones((TOKENS, 2 * LANES - chans), jnp.float32)
    scores, values, mixed = {}, {}, []
    for n in range(count):
        own = layer_norm(tokens_of(own_ref, n, 40, 144), gain1).astype(jnp.bfloat16)
        query = jnp.dot(own, qkv_ref[:, :chans], preferred_element_type=jnp.float32)
        normed = []
        for p in range(2):
            levels = [(2 * p + 1 + lev) % LEVELS for lev in range(WIN_LEV)]
            parts = [tokens_of(keys_ref, n, lev * QUERIES, QUERIES) for lev in levels]
            parts = [layer_norm(x, gain1) for x in parts]
            normed.append(jnp.concatenate(parts, axis=0).astype(jnp.bfloat16))
        normed = jnp.concatenate(normed, axis=0)
        keys = jnp.dot(normed, qkv_ref[:, chans : 2 * chans], preferred_element_type=jnp.float32)
        query = query * (head_dim ** (-0.5) * LOG2E)
        for p in range(2):
            q = query[p * QUERIES : (p + 1) * QUERIES]
            picked = [
                jnp.where((lane >= h * head_dim) & (lane < (h + 1) * head_dim), q, 0.0)
                for h in range(heads)
            ]
            picked = jnp.concatenate(picked, axis=0).astype(jnp.bfloat16)
            k = keys[p * TOKENS : (p + 1) * TOKENS].astype(jnp.bfloat16)
            scores[n, p] = lax.dot_general(picked, k, NT, preferred_element_type=jnp.float32)
        values[n] = jnp.dot(normed, qkv_ref[:, 2 * chans :], preferred_element_type=jnp.float32)
    got = {}
    for n, (_, window) in enumerate(units):
        for p in range(2):
            probs = []
            for h in range(heads):
                at = slice(h * QUERIES, (h + 1) * QUERIES)
                bias = [table_ref[window, p, rights[n], part, at] for part in range(2)]
                bias = jnp.concatenate([bias[0], bias[1][:, : TOKENS - LANES]], axis=1)
                part = scores[n, p][at] + bias
                probs.append(jnp.exp2(part - jnp.max(part, axis=1, keepdims=True)))
            probs = jnp.concatenate(probs, axis=0).astype(jnp.bfloat16)
            v = jnp.concatenate([values[n][p * TOKENS : (p + 1) * TOKENS], ones], axis=1)
            v = v.astype(jnp.bfloat16)
            got[n, p] = jnp.dot(probs, v, preferred_element_type=jnp.float32)
    for n in range(count):
        for p in range(2):
            out = None
            for h in range(heads):
                part = got[n, p][h * QUERIES : (h + 1) * QUERIES]
                scaled = part[:, :chans] * (1.0 / part[:, chans : chans + 1])
                out = jnp.where(lane >= h * head_dim, scaled, out) if h else scaled
            mixed.append(out)
    mixed = jnp.concatenate(mixed, axis=0).astype(jnp.bfloat16)
    attn = jnp.dot(mixed, proj_ref[...], preferred_element_type=jnp.float32)
    attn = attn.astype(jnp.bfloat16).astype(jnp.float32)
    resid, normed = [], []
    for n in range(count):
        part = tokens_of(own_ref, n, 40, 144) + attn[n * 144 : (n + 1) * 144]
        resid.append(part.astype(jnp.bfloat16).astype(jnp.float32))
        normed.append(layer_norm(resid[n], gain2_ref[...]).astype(jnp.bfloat16))
    result, normed = jnp.concatenate(resid, axis=0), jnp.concatenate(normed, axis=0)
    blocks = [slice(f, f + 2 * LANES) for f in range(0, fc1_ref.shape[1], 2 * LANES)]

    def first_product(at):
        return jnp.dot(normed, fc1_ref[:, at], preferred_element_type=jnp.float32)

    hidden = first_product(blocks[0])
    for b, at in enumerate(blocks):
        following = first_product(blocks[b + 1]) if b + 1 < len(blocks) else None
        active = gelu(hidden).astype(jnp.bfloat16)
        result = result + lax.dot_general(
            active, fc2_ref[:, at], NT, preferred_element_type=jnp.float32
        )
        hidden = following
    for n in range(count):
        mine = result[n * 144 : (n + 1) * 144]
        for part, lanes in enumerate((slice(0, LANES), slice(LANES, chans))):
            width = min(LANES, chans - part * LANES)
            res_ref[n, part, 40:184, :width] = mine[:, lanes]
            res_ref[n, part, 0:40, :width] = mine[104:144, lanes]
        for row in range(WIN_LAT):
            for pair in range(HALF // 2):
                tiles = []
                for col in (2 * pair, 2 * pair + 1):
                    at = pl.ds(4 + row * HALF + col, LEVELS, stride=36)
                    tiles += [res_ref[n, part, at, :] for part in range(2)]
                shifted = [pltpu.roll(x, SPARE, 1) for x in tiles[2:]]
                tiles = [tiles[0], jnp.where(low, tiles[1], shifted[0])]
                tiles.append(jnp.where(low, shifted[0], shifted[1]))
                tiles = jnp.concatenate(tiles, axis=1).astype(jnp.bfloat16)
                out_ref[n, row, :, pair * 2 * chans : (pair + 1) * 2 * chans] = tiles
    if lower:
        send_ref[0] = lower_ref[0, EDGE:]
        send_ref[1] = out_ref[0, EDGE:]


def run_units(units, near, far, table, weights, chans, heads, *lower):
    count = len(units)
    pieces = [x for is_near, _ in units for x in (near if is_near else far)]
    piece = pieces[0]
    out = jax.ShapeDtypeStruct((count, WIN_LAT) + piece.shape[1:], piece.dtype)
    send = jax.ShapeDtypeStruct((2, EDGE) + piece.shape[1:], piece.dtype)
    operands = (*pieces, *weights, table, *lower)
    vmem = pl.BlockSpec(memory_space=pltpu.VMEM)
    outs = [out, send] if lower else [out]
    return pl.pallas_call(
        functools.partial(units_kernel, chans, heads, units, bool(lower)),
        out_shape=outs,
        in_specs=[vmem] * len(operands),
        out_specs=[vmem] * len(outs),
        scratch_shapes=[
            pltpu.VMEM((count, 2, LEVELS * QUERIES, LANES), jnp.float32),
            pltpu.VMEM((count, 2, 184, LANES), jnp.float32),
            pltpu.VMEM((count, 2, 184, LANES), jnp.float32),
        ],
        compiler_params=pltpu.CompilerParams(vmem_limit_bytes=VMEM_BYTES),
        cost_estimate=pl.CostEstimate(
            flops=200_000_000 * count, bytes_accessed=3_000_000, transcendentals=250_000 * count
        ),
        name="swin_windows",
    )(*operands)


def shards(
    field_in, norm1_gain, qkv_weight, proj_weight, earth_bias, norm2_gain, fc1_weight, fc2_weight
):
    levels, rows, flat = field_in.shape
    chans = qkv_weight.shape[0]
    heads = earth_bias.shape[2]
    half = HALF * chans
    field = jnp.transpose(field_in, (1, 0, 2))
    south = moved(field[:EDGE], "lat", -1)
    weights = (
        norm1_gain.reshape(1, chans),
        qkv_weight,
        proj_weight,
        norm2_gain.reshape(1, chans),
        fc1_weight,
        jnp.transpose(fc2_weight),
    )
    vmem = pl.BlockSpec(memory_space=pltpu.VMEM)
    anywhere = pl.BlockSpec(memory_space=pl.ANY)
    piece = jax.ShapeDtypeStruct((rows, levels, half), field.dtype)
    table = jax.ShapeDtypeStruct((2, 2, 2, 2, heads * QUERIES, LANES), jnp.float32)
    windows, zwin, _, entries = earth_bias.shape
    tiles = entries // LANES
    bias = earth_bias.reshape(windows, zwin, heads, tiles, LANES).transpose(0, 2, 3, 1, 4)
    sources = (bias, field) + weights
    sources = [pltpu.with_memory_space_constraint(x, pltpu.HBM) for x in sources]
    outs = [table, piece, piece] + [jax.ShapeDtypeStruct(x.shape, x.dtype) for x in weights]
    table, near, far, *weights = pl.pallas_call(
        functools.partial(table_kernel, len(weights)),
        out_shape=outs,
        in_specs=[pl.BlockSpec(memory_space=pltpu.HBM)] * len(sources),
        out_specs=[vmem] * len(outs),
        scratch_shapes=[
            pltpu.VMEM((bias.size // LANES, LANES), jnp.float32),
            pltpu.SemaphoreType.DMA((2 * windows,)),
            pltpu.SemaphoreType.DMA((2 + len(weights),)),
        ],
        compiler_params=pltpu.CompilerParams(vmem_limit_bytes=VMEM_BYTES),
        cost_estimate=pl.CostEstimate(flops=4_000_000, bytes_accessed=6_000_000, transcendentals=0),
        name="bias_tables",
    )(*sources)

    def pack(which, kept, *after):
        return pl.pallas_call(
            functools.partial(pack_kernel, which),
            out_shape=piece,
            in_specs=[vmem] * 2 + [anywhere] * len(after),
            out_specs=vmem,
            compiler_params=pltpu.CompilerParams(vmem_limit_bytes=VMEM_BYTES),
            cost_estimate=pl.CostEstimate(flops=0, bytes_accessed=250_000, transcendentals=0),
            name="pack_half",
        )(south, kept, *after)

    far = pack(1, far)
    near = pack(0, near, far)
    far_halo = swapped(far, "lon", 1)
    near_halo = swapped(near, "lon", 0)
    near, far = (near, near_halo), (far, far_halo)
    common = (near, far, table, weights, chans, heads)
    (near_low,) = run_units(((True, 1),), *common)
    far_low, send = run_units(((False, 1),), *common, near_low)
    top = moved(send, "lat", 1)
    (high,) = run_units(((True, 0), (False, 0)), *common)
    done = pl.pallas_call(
        last_kernel,
        out_shape=jax.ShapeDtypeStruct(field.shape, field.dtype),
        in_specs=[vmem] * 4,
        out_specs=anywhere,
        scratch_shapes=[pltpu.SemaphoreType.DMA((6,))],
        compiler_params=pltpu.CompilerParams(vmem_limit_bytes=VMEM_BYTES),
        cost_estimate=pl.CostEstimate(flops=0, bytes_accessed=400_000, transcendentals=0),
        name="last_rows",
    )(top, high, near_low, far_low)
    return jnp.transpose(done, (1, 0, 2))


def solution(mesh):
    in_specs = (P(None, "lat", "lon"), P(), P(), P(), P("lat", None, None, None), P(), P(), P())
    out_specs = P(None, "lat", "lon")
    return jax.shard_map(shards, mesh=mesh, in_specs=in_specs, out_specs=out_specs, check_vma=False)
```

```python
import functools

import jax
import jax.numpy as jnp
from jax import lax
from jax.experimental import pallas as pl
from jax.experimental.pallas import tpu as pltpu
from jax.sharding import PartitionSpec as P

LEVELS = 4
WIN_LEV = 2
WIN_LAT = 6
WIN_LON = 12
EDGE = WIN_LAT // 2
HALF = WIN_LON // 2
TOKENS = WIN_LEV * WIN_LAT * WIN_LON
QUERIES = TOKENS // 2
LOG2E = 1.4426950408889634
GELU_0 = 0.7978845608028654
GELU_1 = 0.044715 * GELU_0
LANES = 128
SPARE = 64
VMEM_BYTES = 8 * 2**20
NT = (((1,), (1,)), ((), ()))


def moved(x, axis, by):
    size = lax.axis_size(axis)
    return lax.ppermute(x, axis, [(i, (i + by) % size) for i in range(size)])


def swapped(x, axis, first):
    size = lax.axis_size(axis)
    pairs = []
    for i in range(first, size, 2):
        j = (i + 1) % size
        pairs += [(i, j), (j, i)]
    return lax.ppermute(x, axis, pairs)


def half_places(half):
    odd = lax.rem(lax.axis_index("lon"), 2)
    return pl.multiple_of((1 - odd) * half, LANES), pl.multiple_of(odd * half, LANES)


def pack_far_kernel(south_ref, kept_ref, far_ref):
    at = half_places(far_ref.shape[2])[1]
    rows = far_ref.shape[0] - EDGE
    far_ref[:rows] = kept_ref[:rows]
    far_ref[rows:] = south_ref[:, :, pl.ds(at, far_ref.shape[2])]


def pack_near_kernel(south_ref, kept_ref, _, low_ref, high_ref):
    at = half_places(low_ref.shape[2])[0]
    high_ref[...] = kept_ref[:WIN_LAT]
    low_ref[:EDGE] = kept_ref[WIN_LAT : WIN_LAT + EDGE]
    low_ref[EDGE:] = south_ref[:, :, pl.ds(at, low_ref.shape[2])]


def last_kernel(top_ref, high_ref, near_low_ref, far_low_ref, out_ref, sems):
    half = top_ref.shape[3]
    copies = []
    for n, at in enumerate(half_places(half)):
        target = out_ref.at[:, :, pl.ds(at, half)]
        low_ref = (near_low_ref, far_low_ref)[n]
        for source, first in (
            (high_ref.at[n], EDGE),
            (low_ref.at[0, :EDGE], EDGE + WIN_LAT),
            (top_ref.at[n], 0),
        ):
            rows = pl.ds(first, source.shape[0])
            copy = pltpu.make_async_copy(source, target.at[rows], sems.at[len(copies)])
            copy.start()
            copies.append(copy)
    for copy in copies:
        copy.wait()


def build_tables(bias_ref, table_ref, heads, wrap):
    lines = bias_ref.shape[0] // heads
    blocks = WIN_LEV * WIN_LAT // 2
    lane = lax.broadcasted_iota(jnp.int32, (blocks, LANES), 1)
    block = lax.broadcasted_iota(jnp.int32, (blocks, LANES), 0)
    is_last = lax.axis_index("lat") == lax.axis_size("lat") - 1
    last = jnp.where(is_last, -1e9, 0.0).astype(jnp.float32)

    def penalty(part, second, levels):
        key = lane + part * LANES
        key_lev = key // QUERIES
        key_side = (key - key_lev * QUERIES) // (QUERIES // 2)
        row = 2 * block + second
        lev = row // WIN_LAT
        side = (row - lev * WIN_LAT) // EDGE
        out = jnp.zeros((blocks, LANES), jnp.float32)
        if levels:
            out = jnp.where(key_lev != lev, -1e9, out)
        if wrap:
            out = out + jnp.where(key_side != side, last, 0.0)
        return out

    masks = {
        (p, part, second): penalty(part, second, p == 1)
        for p in range(2)
        for part in range(2)
        for second in range(2)
    }
    for h in range(heads):
        for p in range(2):
            for third in range(3):
                line = h * lines + p + third * 18
                pieces = [
                    bias_ref[pl.ds(line + 2 * u, blocks, stride=54), :] * LOG2E for u in range(9)
                ]
                for r in range(8):
                    shift = 16 * r
                    main, nxt = pieces[r], pieces[r + 1]
                    if r:
                        main = pltpu.roll(main, LANES - shift, 1)
                        nxt = pltpu.roll(nxt, LANES - shift, 1)
                        main = jnp.where(lane < LANES - shift, main, nxt)
                    second, col = divmod(8 * third + r, WIN_LON)
                    side = col // HALF
                    place = h * QUERIES + HALF * second + col % HALF
                    at = pl.ds(place, blocks, stride=WIN_LON)
                    for part, piece in enumerate((main, nxt)):
                        table_ref[p, 1 - side, part, at, :] = piece + masks[p, part, second]


def table_kernel(count, heads, *refs):
    bias_any, field_any, *weights_any = refs[: 2 + count]
    table_ref, inner_ref, near_ref, far_ref, *weights_ref = refs[2 + count : 6 + 2 * count]
    bias_ref, sems = refs[6 + 2 * count :]
    lines = bias_ref.shape[0]
    flat = bias_any.reshape(2 * lines, LANES)
    rows, half = field_any.shape[0] - EDGE, near_ref.shape[2]
    near_at, far_at = half_places(half)
    fetches = [
        (flat.at[pl.ds(lines, lines)], bias_ref),
        (field_any.at[EDGE:, :, pl.ds(far_at, half)], far_ref.at[:rows]),
        (field_any.at[EDGE:, :, pl.ds(near_at, half)], near_ref.at[:rows]),
        (flat.at[pl.ds(0, lines)], inner_ref),
    ]
    fetches += list(zip(weights_any, weights_ref))
    fetches = [
        pltpu.make_async_copy(source, target, sems.at[n])
        for n, (source, target) in enumerate(fetches)
    ]
    for copy in fetches:
        copy.start()
    fetches[0].wait()
    build_tables(bias_ref, table_ref, heads, True)
    for copy in fetches[1:]:
        copy.wait()


def layer_norm(values, gain):
    center = values - jnp.mean(values, axis=-1, keepdims=True)
    spread = jnp.mean(center * center, axis=-1, keepdims=True)
    return center * lax.rsqrt(spread + 1e-05) * gain


def gelu(x):
    half = 0.5 * x
    return half + half * jnp.tanh(x * (GELU_0 + GELU_1 * (x * x)))


def units_kernel(chans, heads, units, extra, *refs):
    count = len(units)
    pieces, refs = refs[: 2 * count], refs[2 * count :]
    gain1_ref, qkv_ref, proj_ref, gain2_ref, fc1_ref, fc2_ref, table_ref, *refs = refs
    if extra:
        extra_ref, out_ref, extra_out, keys_ref, own_ref, res_ref = refs
    else:
        out_ref, keys_ref, own_ref, res_ref = refs
    if extra == "tables":
        build_tables(extra_ref, extra_out, heads, False)
    head_dim = chans // heads
    low = lax.broadcasted_iota(jnp.int32, (1, LANES), 1) < SPARE
    odd = lax.rem(lax.axis_index("lon"), 2)
    rights = [1 - odd if near else odd for near, _ in units]

    def tokens_of(ref, at, first, count):
        both = [ref[at, part, first : first + count] for part in range(2)]
        return jnp.concatenate([both[0], both[1][:, : chans - LANES]], axis=1)

    def split(ref, row):
        for pair in range(HALF // 2):
            both = ref[row, :, pair * 2 * chans : (pair + 1) * 2 * chans].astype(jnp.float32)
            first, middle, final = (both[:, u * LANES : (u + 1) * LANES] for u in range(3))
            yield 2 * pair, (first, middle)
            middle, final = pltpu.roll(middle, SPARE, 1), pltpu.roll(final, SPARE, 1)
            yield 2 * pair + 1, (jnp.where(low, middle, final), final)

    for n, (near, window) in enumerate(units):
        own_piece, halo_piece = pieces[2 * n], pieces[2 * n + 1]
        first = 0 if near else window * WIN_LAT
        halo_at = rights[n] * HALF
        own_at = HALF - halo_at
        for row in range(WIN_LAT):
            for col, block in split(halo_piece, first + row):
                at = pl.ds(row * WIN_LON + col + halo_at, LEVELS, stride=QUERIES)
                for part in range(2):
                    keys_ref[n, part, at, :] = block[part]
            for col, block in split(own_piece, first + row):
                at = pl.ds(row * WIN_LON + col + own_at, LEVELS, stride=QUERIES)
                place = row * HALF + col
                for part in range(2):
                    keys_ref[n, part, at, :] = block[part]
                    own_ref[n, part, pl.ds(4 + place, LEVELS, stride=36), :] = block[part]
                    own_ref[n, part, pl.ds(148 + place, 1), :] = block[part][:1]

    gain1 = gain1_ref[...]
    lane = lax.broadcasted_iota(jnp.int32, (1, chans), 1)
    ones = jnp.ones((TOKENS, 2 * LANES - chans), jnp.float32)
    scores, values, mixed = {}, {}, []
    for n in range(count):
        own = layer_norm(tokens_of(own_ref, n, 40, 144), gain1).astype(jnp.bfloat16)
        query = jnp.dot(own, qkv_ref[:, :chans], preferred_element_type=jnp.float32)
        normed = []
        for p in range(2):
            levels = [(2 * p + 1 + lev) % LEVELS for lev in range(WIN_LEV)]
            parts = [tokens_of(keys_ref, n, lev * QUERIES, QUERIES) for lev in levels]
            parts = [layer_norm(x, gain1) for x in parts]
            normed.append(jnp.concatenate(parts, axis=0).astype(jnp.bfloat16))
        normed = jnp.concatenate(normed, axis=0)
        keys = jnp.dot(normed, qkv_ref[:, chans : 2 * chans], preferred_element_type=jnp.float32)
        query = query * (head_dim ** (-0.5) * LOG2E)
        for p in range(2):
            q = query[p * QUERIES : (p + 1) * QUERIES]
            picked = [
                jnp.where((lane >= h * head_dim) & (lane < (h + 1) * head_dim), q, 0.0)
                for h in range(heads)
            ]
            picked = jnp.concatenate(picked, axis=0).astype(jnp.bfloat16)
            k = keys[p * TOKENS : (p + 1) * TOKENS].astype(jnp.bfloat16)
            scores[n, p] = lax.dot_general(picked, k, NT, preferred_element_type=jnp.float32)
        values[n] = jnp.dot(normed, qkv_ref[:, 2 * chans :], preferred_element_type=jnp.float32)
    got = {}
    for n, (_, window) in enumerate(units):
        for p in range(2):
            probs = []
            for h in range(heads):
                at = slice(h * QUERIES, (h + 1) * QUERIES)
                bias = [table_ref[p, rights[n], part, at] for part in range(2)]
                bias = jnp.concatenate([bias[0], bias[1][:, : TOKENS - LANES]], axis=1)
                part = scores[n, p][at] + bias
                probs.append(jnp.exp2(part - jnp.max(part, axis=1, keepdims=True)))
            probs = jnp.concatenate(probs, axis=0).astype(jnp.bfloat16)
            v = jnp.concatenate([values[n][p * TOKENS : (p + 1) * TOKENS], ones], axis=1)
            v = v.astype(jnp.bfloat16)
            got[n, p] = jnp.dot(probs, v, preferred_element_type=jnp.float32)
    for n in range(count):
        for p in range(2):
            out = None
            for h in range(heads):
                part = got[n, p][h * QUERIES : (h + 1) * QUERIES]
                scaled = part[:, :chans] * (1.0 / part[:, chans : chans + 1])
                out = jnp.where(lane >= h * head_dim, scaled, out) if h else scaled
            mixed.append(out)
    mixed = jnp.concatenate(mixed, axis=0).astype(jnp.bfloat16)
    attn = jnp.dot(mixed, proj_ref[...], preferred_element_type=jnp.float32)
    attn = attn.astype(jnp.bfloat16).astype(jnp.float32)
    resid, normed = [], []
    for n in range(count):
        part = tokens_of(own_ref, n, 40, 144) + attn[n * 144 : (n + 1) * 144]
        resid.append(part.astype(jnp.bfloat16).astype(jnp.float32))
        normed.append(layer_norm(resid[n], gain2_ref[...]).astype(jnp.bfloat16))
    result, normed = jnp.concatenate(resid, axis=0), jnp.concatenate(normed, axis=0)
    blocks = [slice(f, f + 2 * LANES) for f in range(0, fc1_ref.shape[1], 2 * LANES)]

    def first_product(at):
        return jnp.dot(normed, fc1_ref[:, at], preferred_element_type=jnp.float32)

    hidden = first_product(blocks[0])
    for b, at in enumerate(blocks):
        following = first_product(blocks[b + 1]) if b + 1 < len(blocks) else None
        active = gelu(hidden).astype(jnp.bfloat16)
        result = result + lax.dot_general(
            active, fc2_ref[:, at], NT, preferred_element_type=jnp.float32
        )
        hidden = following
    for n in range(count):
        mine = result[n * 144 : (n + 1) * 144]
        for part, lanes in enumerate((slice(0, LANES), slice(LANES, chans))):
            width = min(LANES, chans - part * LANES)
            res_ref[n, part, 40:184, :width] = mine[:, lanes]
            res_ref[n, part, 0:40, :width] = mine[104:144, lanes]
        for row in range(WIN_LAT):
            for pair in range(HALF // 2):
                tiles = []
                for col in (2 * pair, 2 * pair + 1):
                    at = pl.ds(4 + row * HALF + col, LEVELS, stride=36)
                    tiles += [res_ref[n, part, at, :] for part in range(2)]
                shifted = [pltpu.roll(x, SPARE, 1) for x in tiles[2:]]
                tiles = [tiles[0], jnp.where(low, tiles[1], shifted[0])]
                tiles.append(jnp.where(low, shifted[0], shifted[1]))
                tiles = jnp.concatenate(tiles, axis=1).astype(jnp.bfloat16)
                out_ref[n, row, :, pair * 2 * chans : (pair + 1) * 2 * chans] = tiles
    if extra == "send":
        extra_out[0] = extra_ref[0, EDGE:]
        extra_out[1] = out_ref[0, EDGE:]


def run_units(units, near, far, weights, chans, heads, table, extra=None, extra_in=None):
    count = len(units)
    pieces = [x for is_near, w in units for x in (near[w] if is_near else far)]
    piece = pieces[0]
    outs = [jax.ShapeDtypeStruct((count, WIN_LAT) + piece.shape[1:], piece.dtype)]
    operands = (*pieces, *weights, table)
    if extra == "send":
        outs.append(jax.ShapeDtypeStruct((2, EDGE) + piece.shape[1:], piece.dtype))
    elif extra == "tables":
        outs.append(jax.ShapeDtypeStruct(table.shape, table.dtype))
    if extra:
        operands += (extra_in,)
    vmem = pl.BlockSpec(memory_space=pltpu.VMEM)
    return pl.pallas_call(
        functools.partial(units_kernel, chans, heads, units, extra),
        out_shape=outs,
        in_specs=[vmem] * len(operands),
        out_specs=[vmem] * len(outs),
        scratch_shapes=[
            pltpu.VMEM((count, 2, LEVELS * QUERIES, LANES), jnp.float32),
            pltpu.VMEM((count, 2, 184, LANES), jnp.float32),
            pltpu.VMEM((count, 2, 184, LANES), jnp.float32),
        ],
        compiler_params=pltpu.CompilerParams(vmem_limit_bytes=VMEM_BYTES),
        cost_estimate=pl.CostEstimate(
            flops=200_000_000 * count, bytes_accessed=3_000_000, transcendentals=250_000 * count
        ),
        name="swin_windows",
    )(*operands)


def shards(
    field_in, norm1_gain, qkv_weight, proj_weight, earth_bias, norm2_gain, fc1_weight, fc2_weight
):
    levels, rows, flat = field_in.shape
    chans = qkv_weight.shape[0]
    heads = earth_bias.shape[2]
    half = HALF * chans
    field = jnp.transpose(field_in, (1, 0, 2))
    south = moved(field[:EDGE], "lat", -1)
    weights = (
        norm1_gain.reshape(1, chans),
        qkv_weight,
        proj_weight,
        norm2_gain.reshape(1, chans),
        fc1_weight,
        jnp.transpose(fc2_weight),
    )
    vmem = pl.BlockSpec(memory_space=pltpu.VMEM)
    anywhere = pl.BlockSpec(memory_space=pl.ANY)
    piece = jax.ShapeDtypeStruct((rows, levels, half), field.dtype)
    table = jax.ShapeDtypeStruct((2, 2, 2, heads * QUERIES, LANES), jnp.float32)
    windows, zwin, _, entries = earth_bias.shape
    tiles = entries // LANES
    bias = earth_bias.reshape(windows, zwin, heads, tiles, LANES).transpose(0, 2, 3, 1, 4)
    sources = (bias, field) + weights
    raw = jax.ShapeDtypeStruct((bias.size // windows // LANES, LANES), bias.dtype)
    sources = [pltpu.with_memory_space_constraint(x, pltpu.HBM) for x in sources]
    outs = [table, raw, piece, piece] + [jax.ShapeDtypeStruct(x.shape, x.dtype) for x in weights]
    table, inner, near, far, *weights = pl.pallas_call(
        functools.partial(table_kernel, len(weights), heads),
        out_shape=outs,
        in_specs=[pl.BlockSpec(memory_space=pltpu.HBM)] * len(sources),
        out_specs=[vmem] * len(outs),
        scratch_shapes=[
            pltpu.VMEM(raw.shape, raw.dtype),
            pltpu.SemaphoreType.DMA((4 + len(weights),)),
        ],
        compiler_params=pltpu.CompilerParams(vmem_limit_bytes=VMEM_BYTES),
        cost_estimate=pl.CostEstimate(flops=4_000_000, bytes_accessed=6_000_000, transcendentals=0),
        name="bias_tables",
    )(*sources)

    def pack(kernel, outs, *operands):
        return pl.pallas_call(
            kernel,
            out_shape=outs,
            in_specs=[vmem] * 2 + [anywhere] * (len(operands) - 2),
            out_specs=[vmem] * len(outs),
            compiler_params=pltpu.CompilerParams(vmem_limit_bytes=VMEM_BYTES),
            cost_estimate=pl.CostEstimate(flops=0, bytes_accessed=250_000, transcendentals=0),
            name="pack_half",
        )(*operands)

    (far,) = pack(pack_far_kernel, [piece], south, far)
    far_halo = swapped(far, "lon", 1)
    window = jax.ShapeDtypeStruct((WIN_LAT, levels, half), field.dtype)
    near_parts = pack(pack_near_kernel, [window, window], south, near, far)
    low, high = ((part, swapped(part, "lon", 0)) for part in near_parts)
    near, far = (high, low), (far, far_halo)
    common = (near, far, weights, chans, heads)
    near_low, inner = run_units(((True, 1),), *common, table, "tables", inner)
    far_low, send = run_units(((False, 1),), *common, table, "send", near_low)
    top = moved(send, "lat", 1)
    (high,) = run_units(((True, 0), (False, 0)), *common, inner)
    done = pl.pallas_call(
        last_kernel,
        out_shape=jax.ShapeDtypeStruct(field.shape, field.dtype),
        in_specs=[vmem] * 4,
        out_specs=anywhere,
        scratch_shapes=[pltpu.SemaphoreType.DMA((6,))],
        compiler_params=pltpu.CompilerParams(vmem_limit_bytes=VMEM_BYTES),
        cost_estimate=pl.CostEstimate(flops=0, bytes_accessed=400_000, transcendentals=0),
        name="last_rows",
    )(top, high, near_low, far_low)
    return jnp.transpose(done, (1, 0, 2))


def solution(mesh):
    in_specs = (P(None, "lat", "lon"), P(), P(), P(), P("lat", None, None, None), P(), P(), P())
    out_specs = P(None, "lat", "lon")
    return jax.shard_map(shards, mesh=mesh, in_specs=in_specs, out_specs=out_specs, check_vma=False)
```

```python
import functools

import jax
import jax.numpy as jnp
from jax import lax
from jax.experimental import pallas as pl
from jax.experimental.pallas import tpu as pltpu
from jax.sharding import PartitionSpec as P

LEVELS = 4
WIN_LEV = 2
WIN_LAT = 6
WIN_LON = 12
EDGE = WIN_LAT // 2
HALF = WIN_LON // 2
TOKENS = WIN_LEV * WIN_LAT * WIN_LON
QUERIES = TOKENS // 2
LOG2E = 1.4426950408889634
GELU_0 = 0.7978845608028654
GELU_1 = 0.044715 * GELU_0
LANES = 128
SPARE = 64
VMEM_BYTES = 8 * 2**20
NT = (((1,), (1,)), ((), ()))


def moved(x, axis, by):
    size = lax.axis_size(axis)
    return lax.ppermute(x, axis, [(i, (i + by) % size) for i in range(size)])


def swapped(x, axis, first):
    size = lax.axis_size(axis)
    pairs = []
    for i in range(first, size, 2):
        j = (i + 1) % size
        pairs += [(i, j), (j, i)]
    return lax.ppermute(x, axis, pairs)


def half_places(half):
    odd = lax.rem(lax.axis_index("lon"), 2)
    return pl.multiple_of((1 - odd) * half, LANES), pl.multiple_of(odd * half, LANES)


def pack_far_kernel(south_ref, kept_ref, far_ref):
    at = half_places(far_ref.shape[2])[1]
    rows = far_ref.shape[0] - EDGE
    far_ref[:rows] = kept_ref[:rows]
    far_ref[rows:] = south_ref[:, :, pl.ds(at, far_ref.shape[2])]


def pack_near_kernel(south_ref, kept_ref, _, low_ref, high_ref):
    at = half_places(low_ref.shape[2])[0]
    high_ref[...] = kept_ref[:WIN_LAT]
    low_ref[:EDGE] = kept_ref[WIN_LAT : WIN_LAT + EDGE]
    low_ref[EDGE:] = south_ref[:, :, pl.ds(at, low_ref.shape[2])]


def last_kernel(top_ref, high_ref, near_low_ref, far_low_ref, out_ref, sems):
    half = top_ref.shape[3]
    copies = []
    for n, at in enumerate(half_places(half)):
        target = out_ref.at[:, :, pl.ds(at, half)]
        low_ref = (near_low_ref, far_low_ref)[n]
        for source, first in (
            (high_ref.at[n], EDGE),
            (low_ref.at[0, :EDGE], EDGE + WIN_LAT),
            (top_ref.at[n], 0),
        ):
            rows = pl.ds(first, source.shape[0])
            copy = pltpu.make_async_copy(source, target.at[rows], sems.at[len(copies)])
            copy.start()
            copies.append(copy)
    for copy in copies:
        copy.wait()


def build_tables(bias_ref, table_ref, heads, wrap):
    lines = bias_ref.shape[0] // heads
    blocks = WIN_LEV * WIN_LAT // 2
    lane = lax.broadcasted_iota(jnp.int32, (blocks, LANES), 1)
    block = lax.broadcasted_iota(jnp.int32, (blocks, LANES), 0)
    is_last = lax.axis_index("lat") == lax.axis_size("lat") - 1
    last = jnp.where(is_last, -1e9, 0.0).astype(jnp.float32)

    def penalty(part, second, levels):
        key = lane + part * LANES
        key_lev = key // QUERIES
        key_side = (key - key_lev * QUERIES) // (QUERIES // 2)
        row = 2 * block + second
        lev = row // WIN_LAT
        side = (row - lev * WIN_LAT) // EDGE
        out = jnp.zeros((blocks, LANES), jnp.float32)
        if levels:
            out = jnp.where(key_lev != lev, -1e9, out)
        if wrap:
            out = out + jnp.where(key_side != side, last, 0.0)
        return out

    masks = {
        (p, part, second): penalty(part, second, p == 1)
        for p in range(2)
        for part in range(2)
        for second in range(2)
    }
    for h in range(heads):
        for p in range(2):
            for third in range(3):
                line = h * lines + p + third * 18
                pieces = [
                    bias_ref[pl.ds(line + 2 * u, blocks, stride=54), :] * LOG2E for u in range(9)
                ]
                for r in range(8):
                    shift = 16 * r
                    main, nxt = pieces[r], pieces[r + 1]
                    if r:
                        main = pltpu.roll(main, LANES - shift, 1)
                        nxt = pltpu.roll(nxt, LANES - shift, 1)
                        main = jnp.where(lane < LANES - shift, main, nxt)
                    second, col = divmod(8 * third + r, WIN_LON)
                    side = col // HALF
                    place = h * QUERIES + HALF * second + col % HALF
                    at = pl.ds(place, blocks, stride=WIN_LON)
                    for part, piece in enumerate((main, nxt)):
                        table_ref[p, 1 - side, part, at, :] = piece + masks[p, part, second]


def table_kernel(count, heads, *refs):
    bias_any, field_any, *weights_any = refs[: 2 + count]
    table_ref, inner_ref, near_ref, far_ref, *weights_ref = refs[2 + count : 6 + 2 * count]
    bias_ref, sems = refs[6 + 2 * count :]
    lines = bias_ref.shape[0]
    flat = bias_any.reshape(2 * lines, LANES)
    rows, half = field_any.shape[0] - EDGE, near_ref.shape[2]
    near_at, far_at = half_places(half)
    fetches = [
        (flat.at[pl.ds(lines, lines)], bias_ref),
        (field_any.at[EDGE:, :, pl.ds(far_at, half)], far_ref.at[:rows]),
        (field_any.at[EDGE:, :, pl.ds(near_at, half)], near_ref.at[:rows]),
        (flat.at[pl.ds(0, lines)], inner_ref),
    ]
    fetches += list(zip(weights_any, weights_ref))
    fetches = [
        pltpu.make_async_copy(source, target, sems.at[n])
        for n, (source, target) in enumerate(fetches)
    ]
    for copy in fetches:
        copy.start()
    fetches[0].wait()
    build_tables(bias_ref, table_ref, heads, True)
    for copy in fetches[1:]:
        copy.wait()


def layer_norm(values, gain):
    center = values - jnp.mean(values, axis=-1, keepdims=True)
    spread = jnp.mean(center * center, axis=-1, keepdims=True)
    return center * lax.rsqrt(spread + 1e-05) * gain


def gelu(x):
    half = 0.5 * x
    return half + half * jnp.tanh(x * (GELU_0 + GELU_1 * (x * x)))


def units_kernel(chans, heads, units, extra, *refs):
    count = len(units)
    pieces, refs = refs[: 2 * count], refs[2 * count :]
    gain1_ref, qkv_ref, proj_ref, gain2_ref, fc1_ref, fc2_ref, table_ref, *refs = refs
    *refs, keys_ref, own_ref, res_ref = refs
    if extra == "ahead":
        raw_ref, far_ref, out_ref, inner_ref, far_keys, far_own, far_picked = refs
        build_tables(raw_ref, inner_ref, heads, False)
    elif extra == "send":
        far_keys, far_own, far_picked, lower_ref, out_ref, send_ref = refs
    else:
        (out_ref,) = refs
    head_dim = chans // heads
    low = lax.broadcasted_iota(jnp.int32, (1, LANES), 1) < SPARE
    odd = lax.rem(lax.axis_index("lon"), 2)
    rights = [1 - odd if near else odd for near, _ in units]

    def tokens_of(ref, at, first, count):
        both = [ref[at, part, first : first + count] for part in range(2)]
        return jnp.concatenate([both[0], both[1][:, : chans - LANES]], axis=1)

    def split(ref, row):
        for pair in range(HALF // 2):
            both = ref[row, :, pair * 2 * chans : (pair + 1) * 2 * chans].astype(jnp.float32)
            first, middle, final = (both[:, u * LANES : (u + 1) * LANES] for u in range(3))
            yield 2 * pair, (first, middle)
            middle, final = pltpu.roll(middle, SPARE, 1), pltpu.roll(final, SPARE, 1)
            yield 2 * pair + 1, (jnp.where(low, middle, final), final)

    def place_keys(n, ref, first, column, into):
        for row in range(WIN_LAT):
            for col, block in split(ref, first + row):
                at = pl.ds(row * WIN_LON + col + column, LEVELS, stride=QUERIES)
                for part in range(2):
                    into[n, part, at, :] = block[part]

    def place_own(n, ref, first, column, into, own_into):
        for row in range(WIN_LAT):
            for col, block in split(ref, first + row):
                at = pl.ds(row * WIN_LON + col + column, LEVELS, stride=QUERIES)
                place = row * HALF + col
                for part in range(2):
                    into[n, part, at, :] = block[part]
                    own_into[n, part, pl.ds(4 + place, LEVELS, stride=36), :] = block[part]
                    own_into[n, part, pl.ds(148 + place, 1), :] = block[part][:1]

    def queries(n, own_from):
        own = layer_norm(tokens_of(own_from, n, 40, 144), gain1).astype(jnp.bfloat16)
        query = jnp.dot(own, qkv_ref[:, :chans], preferred_element_type=jnp.float32)
        query = query * (head_dim ** (-0.5) * LOG2E)
        picked = []
        for p in range(2):
            q = query[p * QUERIES : (p + 1) * QUERIES]
            picked += [
                jnp.where((lane >= h * head_dim) & (lane < (h + 1) * head_dim), q, 0.0)
                for h in range(heads)
            ]
        return jnp.concatenate(picked, axis=0).astype(jnp.bfloat16)

    if extra == "send":
        keys_ref[...] = far_keys[...]
        own_ref = far_own
    for n, (near, window) in enumerate(units):
        own_piece, halo_piece = pieces[2 * n], pieces[2 * n + 1]
        first = 0 if near else window * WIN_LAT
        if extra != "send":
            place_own(n, own_piece, first, HALF - rights[n] * HALF, keys_ref, own_ref)
        place_keys(n, halo_piece, first, rights[n] * HALF, keys_ref)

    gain1 = gain1_ref[...]
    lane = lax.broadcasted_iota(jnp.int32, (1, chans), 1)
    ones = jnp.ones((TOKENS, 2 * LANES - chans), jnp.float32)
    scores, values, mixed = {}, {}, []
    for n in range(count):
        picked = far_picked[...] if extra == "send" else queries(n, own_ref)
        normed = []
        for p in range(2):
            levels = [(2 * p + 1 + lev) % LEVELS for lev in range(WIN_LEV)]
            parts = [tokens_of(keys_ref, n, lev * QUERIES, QUERIES) for lev in levels]
            parts = [layer_norm(x, gain1) for x in parts]
            normed.append(jnp.concatenate(parts, axis=0).astype(jnp.bfloat16))
        normed = jnp.concatenate(normed, axis=0)
        keys = jnp.dot(normed, qkv_ref[:, chans : 2 * chans], preferred_element_type=jnp.float32)
        rows = heads * QUERIES
        for p in range(2):
            k = keys[p * TOKENS : (p + 1) * TOKENS].astype(jnp.bfloat16)
            scores[n, p] = lax.dot_general(
                picked[p * rows : (p + 1) * rows], k, NT, preferred_element_type=jnp.float32
            )
        values[n] = jnp.dot(normed, qkv_ref[:, 2 * chans :], preferred_element_type=jnp.float32)
    if extra == "ahead":
        place_own(0, far_ref, WIN_LAT, HALF - odd * HALF, far_keys, far_own)
        far_picked[...] = queries(0, far_own)
    got = {}
    for n, (_, window) in enumerate(units):
        for p in range(2):
            probs = []
            for h in range(heads):
                at = slice(h * QUERIES, (h + 1) * QUERIES)
                bias = [table_ref[p, rights[n], part, at] for part in range(2)]
                bias = jnp.concatenate([bias[0], bias[1][:, : TOKENS - LANES]], axis=1)
                part = scores[n, p][at] + bias
                probs.append(jnp.exp2(part - jnp.max(part, axis=1, keepdims=True)))
            probs = jnp.concatenate(probs, axis=0).astype(jnp.bfloat16)
            v = jnp.concatenate([values[n][p * TOKENS : (p + 1) * TOKENS], ones], axis=1)
            v = v.astype(jnp.bfloat16)
            got[n, p] = jnp.dot(probs, v, preferred_element_type=jnp.float32)
    for n in range(count):
        for p in range(2):
            out = None
            for h in range(heads):
                part = got[n, p][h * QUERIES : (h + 1) * QUERIES]
                scaled = part[:, :chans] * (1.0 / part[:, chans : chans + 1])
                out = jnp.where(lane >= h * head_dim, scaled, out) if h else scaled
            mixed.append(out)
    mixed = jnp.concatenate(mixed, axis=0).astype(jnp.bfloat16)
    attn = jnp.dot(mixed, proj_ref[...], preferred_element_type=jnp.float32)
    attn = attn.astype(jnp.bfloat16).astype(jnp.float32)
    resid, normed = [], []
    for n in range(count):
        part = tokens_of(own_ref, n, 40, 144) + attn[n * 144 : (n + 1) * 144]
        resid.append(part.astype(jnp.bfloat16).astype(jnp.float32))
        normed.append(layer_norm(resid[n], gain2_ref[...]).astype(jnp.bfloat16))
    result, normed = jnp.concatenate(resid, axis=0), jnp.concatenate(normed, axis=0)
    blocks = [slice(f, f + 2 * LANES) for f in range(0, fc1_ref.shape[1], 2 * LANES)]

    def first_product(at):
        return jnp.dot(normed, fc1_ref[:, at], preferred_element_type=jnp.float32)

    hidden = first_product(blocks[0])
    for b, at in enumerate(blocks):
        following = first_product(blocks[b + 1]) if b + 1 < len(blocks) else None
        active = gelu(hidden).astype(jnp.bfloat16)
        result = result + lax.dot_general(
            active, fc2_ref[:, at], NT, preferred_element_type=jnp.float32
        )
        hidden = following
    for n in range(count):
        mine = result[n * 144 : (n + 1) * 144]
        for part, lanes in enumerate((slice(0, LANES), slice(LANES, chans))):
            width = min(LANES, chans - part * LANES)
            res_ref[n, part, 40:184, :width] = mine[:, lanes]
            res_ref[n, part, 0:40, :width] = mine[104:144, lanes]
        for row in range(WIN_LAT):
            for pair in range(HALF // 2):
                tiles = []
                for col in (2 * pair, 2 * pair + 1):
                    at = pl.ds(4 + row * HALF + col, LEVELS, stride=36)
                    tiles += [res_ref[n, part, at, :] for part in range(2)]
                shifted = [pltpu.roll(x, SPARE, 1) for x in tiles[2:]]
                tiles = [tiles[0], jnp.where(low, tiles[1], shifted[0])]
                tiles.append(jnp.where(low, shifted[0], shifted[1]))
                tiles = jnp.concatenate(tiles, axis=1).astype(jnp.bfloat16)
                out_ref[n, row, :, pair * 2 * chans : (pair + 1) * 2 * chans] = tiles
    if extra == "send":
        send_ref[0] = lower_ref[0, EDGE:]
        send_ref[1] = out_ref[0, EDGE:]


def run_units(units, near, far, weights, chans, heads, table, extra=None, *extra_in):
    count = len(units)
    pieces = [x for is_near, w in units for x in (near[w] if is_near else far)]
    piece = pieces[0]
    outs = [jax.ShapeDtypeStruct((count, WIN_LAT) + piece.shape[1:], piece.dtype)]
    operands = (*pieces, *weights, table, *extra_in)
    if extra == "send":
        outs.append(jax.ShapeDtypeStruct((2, EDGE) + piece.shape[1:], piece.dtype))
    elif extra == "ahead":
        outs += [
            jax.ShapeDtypeStruct(table.shape, table.dtype),
            jax.ShapeDtypeStruct((1, 2, LEVELS * QUERIES, LANES), jnp.float32),
            jax.ShapeDtypeStruct((1, 2, 184, LANES), jnp.float32),
            jax.ShapeDtypeStruct((2 * heads * QUERIES, chans), jnp.bfloat16),
        ]
    vmem = pl.BlockSpec(memory_space=pltpu.VMEM)
    return pl.pallas_call(
        functools.partial(units_kernel, chans, heads, units, extra),
        out_shape=outs,
        in_specs=[vmem] * len(operands),
        out_specs=[vmem] * len(outs),
        scratch_shapes=[
            pltpu.VMEM((count, 2, LEVELS * QUERIES, LANES), jnp.float32),
            pltpu.VMEM((count, 2, 184, LANES), jnp.float32),
            pltpu.VMEM((count, 2, 184, LANES), jnp.float32),
        ],
        compiler_params=pltpu.CompilerParams(vmem_limit_bytes=VMEM_BYTES),
        cost_estimate=pl.CostEstimate(
            flops=200_000_000 * count, bytes_accessed=3_000_000, transcendentals=250_000 * count
        ),
        name="swin_windows",
    )(*operands)


def shards(
    field_in, norm1_gain, qkv_weight, proj_weight, earth_bias, norm2_gain, fc1_weight, fc2_weight
):
    levels, rows, flat = field_in.shape
    chans = qkv_weight.shape[0]
    heads = earth_bias.shape[2]
    half = HALF * chans
    field = jnp.transpose(field_in, (1, 0, 2))
    south = moved(field[:EDGE], "lat", -1)
    weights = (
        norm1_gain.reshape(1, chans),
        qkv_weight,
        proj_weight,
        norm2_gain.reshape(1, chans),
        fc1_weight,
        jnp.transpose(fc2_weight),
    )
    vmem = pl.BlockSpec(memory_space=pltpu.VMEM)
    anywhere = pl.BlockSpec(memory_space=pl.ANY)
    piece = jax.ShapeDtypeStruct((rows, levels, half), field.dtype)
    table = jax.ShapeDtypeStruct((2, 2, 2, heads * QUERIES, LANES), jnp.float32)
    windows, zwin, _, entries = earth_bias.shape
    tiles = entries // LANES
    bias = earth_bias.reshape(windows, zwin, heads, tiles, LANES).transpose(0, 2, 3, 1, 4)
    sources = (bias, field) + weights
    raw = jax.ShapeDtypeStruct((bias.size // windows // LANES, LANES), bias.dtype)
    sources = [pltpu.with_memory_space_constraint(x, pltpu.HBM) for x in sources]
    outs = [table, raw, piece, piece] + [jax.ShapeDtypeStruct(x.shape, x.dtype) for x in weights]
    table, inner, near, far, *weights = pl.pallas_call(
        functools.partial(table_kernel, len(weights), heads),
        out_shape=outs,
        in_specs=[pl.BlockSpec(memory_space=pltpu.HBM)] * len(sources),
        out_specs=[vmem] * len(outs),
        scratch_shapes=[
            pltpu.VMEM(raw.shape, raw.dtype),
            pltpu.SemaphoreType.DMA((4 + len(weights),)),
        ],
        compiler_params=pltpu.CompilerParams(vmem_limit_bytes=VMEM_BYTES),
        cost_estimate=pl.CostEstimate(flops=4_000_000, bytes_accessed=6_000_000, transcendentals=0),
        name="bias_tables",
    )(*sources)

    def pack(kernel, outs, *operands):
        return pl.pallas_call(
            kernel,
            out_shape=outs,
            in_specs=[vmem] * 2 + [anywhere] * (len(operands) - 2),
            out_specs=[vmem] * len(outs),
            compiler_params=pltpu.CompilerParams(vmem_limit_bytes=VMEM_BYTES),
            cost_estimate=pl.CostEstimate(flops=0, bytes_accessed=250_000, transcendentals=0),
            name="pack_half",
        )(*operands)

    (far,) = pack(pack_far_kernel, [piece], south, far)
    far_halo = swapped(far, "lon", 1)
    window = jax.ShapeDtypeStruct((WIN_LAT, levels, half), field.dtype)
    near_parts = pack(pack_near_kernel, [window, window], south, near, far)
    low, high = ((part, swapped(part, "lon", 0)) for part in near_parts)
    near, far = (high, low), (far, far_halo)
    common = (near, far, weights, chans, heads)
    near_low, inner, *ahead = run_units(
        ((True, 1),), *common, table, "ahead", inner, far[0]
    )
    far_low, send = run_units(((False, 1),), *common, table, "send", *ahead, near_low)
    top = moved(send, "lat", 1)
    (high,) = run_units(((True, 0), (False, 0)), *common, inner)
    done = pl.pallas_call(
        last_kernel,
        out_shape=jax.ShapeDtypeStruct(field.shape, field.dtype),
        in_specs=[vmem] * 4,
        out_specs=anywhere,
        scratch_shapes=[pltpu.SemaphoreType.DMA((6,))],
        compiler_params=pltpu.CompilerParams(vmem_limit_bytes=VMEM_BYTES),
        cost_estimate=pl.CostEstimate(flops=0, bytes_accessed=400_000, transcendentals=0),
        name="last_rows",
    )(top, high, near_low, far_low)
    return jnp.transpose(done, (1, 0, 2))


def solution(mesh):
    in_specs = (P(None, "lat", "lon"), P(), P(), P(), P("lat", None, None, None), P(), P(), P())
    out_specs = P(None, "lat", "lon")
    return jax.shard_map(shards, mesh=mesh, in_specs=in_specs, out_specs=out_specs, check_vma=False)
```

```python
import functools

import jax
import jax.numpy as jnp
from jax import lax
from jax.experimental import pallas as pl
from jax.experimental.pallas import tpu as pltpu
from jax.sharding import PartitionSpec as P

LEVELS = 4
WIN_LEV = 2
WIN_LAT = 6
WIN_LON = 12
EDGE = WIN_LAT // 2
HALF = WIN_LON // 2
TOKENS = WIN_LEV * WIN_LAT * WIN_LON
QUERIES = TOKENS // 2
LOG2E = 1.4426950408889634
GELU_0 = 0.7978845608028654
GELU_1 = 0.044715 * GELU_0
LANES = 128
SPARE = 64
VMEM_BYTES = 8 * 2**20
NT = (((1,), (1,)), ((), ()))


def moved(x, axis, by):
    size = lax.axis_size(axis)
    return lax.ppermute(x, axis, [(i, (i + by) % size) for i in range(size)])


def swapped(x, axis, first):
    size = lax.axis_size(axis)
    pairs = []
    for i in range(first, size, 2):
        j = (i + 1) % size
        pairs += [(i, j), (j, i)]
    return lax.ppermute(x, axis, pairs)


def half_places(half):
    odd = lax.rem(lax.axis_index("lon"), 2)
    return pl.multiple_of((1 - odd) * half, LANES), pl.multiple_of(odd * half, LANES)


def pack_far_kernel(south_ref, kept_ref, far_ref):
    at = half_places(far_ref.shape[2])[1]
    rows = far_ref.shape[0] - EDGE
    far_ref[:rows] = kept_ref[:rows]
    far_ref[rows:] = south_ref[:, :, pl.ds(at, far_ref.shape[2])]


def pack_near_kernel(south_ref, kept_ref, _, low_ref, high_ref):
    at = half_places(low_ref.shape[2])[0]
    high_ref[...] = kept_ref[:WIN_LAT]
    low_ref[:EDGE] = kept_ref[WIN_LAT : WIN_LAT + EDGE]
    low_ref[EDGE:] = south_ref[:, :, pl.ds(at, low_ref.shape[2])]


def last_kernel(top_ref, near_ref, far_low_ref, far_high_ref, out_ref, sems):
    half = top_ref.shape[3]
    parts = ((near_ref.at[0], near_ref.at[1]), (far_low_ref.at[0], far_high_ref.at[0]))
    copies = []
    for n, at in enumerate(half_places(half)):
        target = out_ref.at[:, :, pl.ds(at, half)]
        low, high = parts[n]
        for source, first in (
            (high, EDGE),
            (low.at[:EDGE], EDGE + WIN_LAT),
            (top_ref.at[n], 0),
        ):
            rows = pl.ds(first, source.shape[0])
            copy = pltpu.make_async_copy(source, target.at[rows], sems.at[len(copies)])
            copy.start()
            copies.append(copy)
    for copy in copies:
        copy.wait()


def build_tables(bias_ref, start, table_ref, heads, wrap):
    lines = bias_ref.shape[0] // 2 // heads
    blocks = WIN_LEV * WIN_LAT // 2
    lane = lax.broadcasted_iota(jnp.int32, (blocks, LANES), 1)
    block = lax.broadcasted_iota(jnp.int32, (blocks, LANES), 0)
    is_last = lax.axis_index("lat") == lax.axis_size("lat") - 1
    last = jnp.where(is_last, -1e9, 0.0).astype(jnp.float32)

    def penalty(part, second, levels):
        key = lane + part * LANES
        key_lev = key // QUERIES
        key_side = (key - key_lev * QUERIES) // (QUERIES // 2)
        row = 2 * block + second
        lev = row // WIN_LAT
        side = (row - lev * WIN_LAT) // EDGE
        out = jnp.zeros((blocks, LANES), jnp.float32)
        if levels:
            out = jnp.where(key_lev != lev, -1e9, out)
        if wrap:
            out = out + jnp.where(key_side != side, last, 0.0)
        return out

    masks = {
        (p, part, second): penalty(part, second, p == 1)
        for p in range(2)
        for part in range(2)
        for second in range(2)
    }
    for h in range(heads):
        for p in range(2):
            for third in range(3):
                line = start + h * lines + p + third * 18
                pieces = [
                    bias_ref[pl.ds(line + 2 * u, blocks, stride=54), :] * LOG2E for u in range(9)
                ]
                for r in range(8):
                    shift = 16 * r
                    main, nxt = pieces[r], pieces[r + 1]
                    if r:
                        main = pltpu.roll(main, LANES - shift, 1)
                        nxt = pltpu.roll(nxt, LANES - shift, 1)
                        main = jnp.where(lane < LANES - shift, main, nxt)
                    second, col = divmod(8 * third + r, WIN_LON)
                    side = col // HALF
                    place = h * QUERIES + HALF * second + col % HALF
                    at = pl.ds(place, blocks, stride=WIN_LON)
                    for part, piece in enumerate((main, nxt)):
                        table_ref[p, 1 - side, part, at, :] = piece + masks[p, part, second]


def table_kernel(count, heads, *refs):
    bias_any, field_any, *weights_any = refs[: 2 + count]
    high_ref, low_ref, near_ref, far_ref, *weights_ref = refs[2 + count : 6 + 2 * count]
    bias_ref, sems = refs[6 + 2 * count :]
    lines = bias_ref.shape[0] // 2
    flat = bias_any.reshape(2 * lines, LANES)
    rows, half = field_any.shape[0] - EDGE, near_ref.shape[2]
    near_at, far_at = half_places(half)
    inner, straddling = pl.ds(0, lines), pl.ds(lines, lines)
    fetches = [
        (flat.at[straddling], bias_ref.at[straddling]),
        (flat.at[inner], bias_ref.at[inner]),
        (field_any.at[EDGE:, :, pl.ds(far_at, half)], far_ref.at[:rows]),
        (field_any.at[EDGE:, :, pl.ds(near_at, half)], near_ref.at[:rows]),
    ]
    fetches += list(zip(weights_any, weights_ref))
    fetches = [
        pltpu.make_async_copy(source, target, sems.at[n])
        for n, (source, target) in enumerate(fetches)
    ]
    for copy in fetches:
        copy.start()
    fetches[0].wait()
    build_tables(bias_ref, lines, low_ref, heads, True)
    fetches[1].wait()
    build_tables(bias_ref, 0, high_ref, heads, False)
    for copy in fetches[2:]:
        copy.wait()


def layer_norm(values, gain):
    center = values - jnp.mean(values, axis=-1, keepdims=True)
    spread = jnp.mean(center * center, axis=-1, keepdims=True)
    return center * lax.rsqrt(spread + 1e-05) * gain


def gelu(x):
    half = 0.5 * x
    return half + half * jnp.tanh(x * (GELU_0 + GELU_1 * (x * x)))


def units_kernel(chans, heads, units, extra, *refs):
    count = len(units)
    pieces, refs = refs[: 2 * count], refs[2 * count :]
    gain1_ref, qkv_ref, proj_ref, gain2_ref, fc1_ref, fc2_ref, *refs = refs
    tables, refs = refs[:2], refs[2:]
    *refs, keys_ref, own_ref, res_ref = refs
    if extra == "ahead":
        far_ref, out_ref, far_keys, far_own, far_picked = refs
    elif extra == "send":
        far_keys, far_own, far_picked, lower_ref, out_ref, send_ref = refs
    else:
        (out_ref,) = refs
    head_dim = chans // heads
    low = lax.broadcasted_iota(jnp.int32, (1, LANES), 1) < SPARE
    odd = lax.rem(lax.axis_index("lon"), 2)
    rights = [1 - odd if near else odd for near, _ in units]

    def tokens_of(ref, at, first, count):
        both = [ref[at, part, first : first + count] for part in range(2)]
        return jnp.concatenate([both[0], both[1][:, : chans - LANES]], axis=1)

    def split(ref, row):
        for pair in range(HALF // 2):
            both = ref[row, :, pair * 2 * chans : (pair + 1) * 2 * chans].astype(jnp.float32)
            first, middle, final = (both[:, u * LANES : (u + 1) * LANES] for u in range(3))
            yield 2 * pair, (first, middle)
            middle, final = pltpu.roll(middle, SPARE, 1), pltpu.roll(final, SPARE, 1)
            yield 2 * pair + 1, (jnp.where(low, middle, final), final)

    def place_keys(n, ref, first, column, into):
        for row in range(WIN_LAT):
            for col, block in split(ref, first + row):
                at = pl.ds(row * WIN_LON + col + column, LEVELS, stride=QUERIES)
                for part in range(2):
                    into[n, part, at, :] = block[part]

    def place_own(n, ref, first, column, into, own_into):
        for row in range(WIN_LAT):
            for col, block in split(ref, first + row):
                at = pl.ds(row * WIN_LON + col + column, LEVELS, stride=QUERIES)
                place = row * HALF + col
                for part in range(2):
                    into[n, part, at, :] = block[part]
                    own_into[n, part, pl.ds(4 + place, LEVELS, stride=36), :] = block[part]
                    own_into[n, part, pl.ds(148 + place, 1), :] = block[part][:1]

    def queries(n, own_from):
        own = layer_norm(tokens_of(own_from, n, 40, 144), gain1).astype(jnp.bfloat16)
        query = jnp.dot(own, qkv_ref[:, :chans], preferred_element_type=jnp.float32)
        query = query * (head_dim ** (-0.5) * LOG2E)
        picked = []
        for p in range(2):
            q = query[p * QUERIES : (p + 1) * QUERIES]
            picked += [
                jnp.where((lane >= h * head_dim) & (lane < (h + 1) * head_dim), q, 0.0)
                for h in range(heads)
            ]
        return jnp.concatenate(picked, axis=0).astype(jnp.bfloat16)

    if extra == "send":
        keys_ref[...] = far_keys[...]
        own_ref = far_own
    for n, (near, window) in enumerate(units):
        own_piece, halo_piece = pieces[2 * n], pieces[2 * n + 1]
        first = 0 if near else window * WIN_LAT
        if extra != "send":
            place_own(n, own_piece, first, HALF - rights[n] * HALF, keys_ref, own_ref)
        place_keys(n, halo_piece, first, rights[n] * HALF, keys_ref)

    gain1 = gain1_ref[...]
    lane = lax.broadcasted_iota(jnp.int32, (1, chans), 1)
    ones = jnp.ones((TOKENS, 2 * LANES - chans), jnp.float32)
    scores, values, mixed = {}, {}, []
    for n in range(count):
        picked = far_picked[...] if extra == "send" else queries(n, own_ref)
        normed = []
        for p in range(2):
            levels = [(2 * p + 1 + lev) % LEVELS for lev in range(WIN_LEV)]
            parts = [tokens_of(keys_ref, n, lev * QUERIES, QUERIES) for lev in levels]
            parts = [layer_norm(x, gain1) for x in parts]
            normed.append(jnp.concatenate(parts, axis=0).astype(jnp.bfloat16))
        normed = jnp.concatenate(normed, axis=0)
        keys = jnp.dot(normed, qkv_ref[:, chans : 2 * chans], preferred_element_type=jnp.float32)
        rows = heads * QUERIES
        for p in range(2):
            k = keys[p * TOKENS : (p + 1) * TOKENS].astype(jnp.bfloat16)
            scores[n, p] = lax.dot_general(
                picked[p * rows : (p + 1) * rows], k, NT, preferred_element_type=jnp.float32
            )
        values[n] = jnp.dot(normed, qkv_ref[:, 2 * chans :], preferred_element_type=jnp.float32)
    if extra == "ahead":
        place_own(0, far_ref, WIN_LAT, HALF - odd * HALF, far_keys, far_own)
        far_picked[...] = queries(0, far_own)
    got = {}
    for n, (_, window) in enumerate(units):
        for p in range(2):
            probs = []
            for h in range(heads):
                at = slice(h * QUERIES, (h + 1) * QUERIES)
                bias = [tables[window][p, rights[n], part, at] for part in range(2)]
                bias = jnp.concatenate([bias[0], bias[1][:, : TOKENS - LANES]], axis=1)
                part = scores[n, p][at] + bias
                probs.append(jnp.exp2(part - jnp.max(part, axis=1, keepdims=True)))
            probs = jnp.concatenate(probs, axis=0).astype(jnp.bfloat16)
            v = jnp.concatenate([values[n][p * TOKENS : (p + 1) * TOKENS], ones], axis=1)
            v = v.astype(jnp.bfloat16)
            got[n, p] = jnp.dot(probs, v, preferred_element_type=jnp.float32)
    for n in range(count):
        for p in range(2):
            out = None
            for h in range(heads):
                part = got[n, p][h * QUERIES : (h + 1) * QUERIES]
                scaled = part[:, :chans] * (1.0 / part[:, chans : chans + 1])
                out = jnp.where(lane >= h * head_dim, scaled, out) if h else scaled
            mixed.append(out)
    mixed = jnp.concatenate(mixed, axis=0).astype(jnp.bfloat16)
    attn = jnp.dot(mixed, proj_ref[...], preferred_element_type=jnp.float32)
    attn = attn.astype(jnp.bfloat16).astype(jnp.float32)
    resid, normed = [], []
    for n in range(count):
        part = tokens_of(own_ref, n, 40, 144) + attn[n * 144 : (n + 1) * 144]
        resid.append(part.astype(jnp.bfloat16).astype(jnp.float32))
        normed.append(layer_norm(resid[n], gain2_ref[...]).astype(jnp.bfloat16))
    result, normed = jnp.concatenate(resid, axis=0), jnp.concatenate(normed, axis=0)
    blocks = [slice(f, f + 2 * LANES) for f in range(0, fc1_ref.shape[1], 2 * LANES)]

    def first_product(at):
        return jnp.dot(normed, fc1_ref[:, at], preferred_element_type=jnp.float32)

    hidden = first_product(blocks[0])
    for b, at in enumerate(blocks):
        following = first_product(blocks[b + 1]) if b + 1 < len(blocks) else None
        active = gelu(hidden).astype(jnp.bfloat16)
        result = result + lax.dot_general(
            active, fc2_ref[:, at], NT, preferred_element_type=jnp.float32
        )
        hidden = following
    for n in range(count):
        mine = result[n * 144 : (n + 1) * 144]
        for part, lanes in enumerate((slice(0, LANES), slice(LANES, chans))):
            width = min(LANES, chans - part * LANES)
            res_ref[n, part, 40:184, :width] = mine[:, lanes]
            res_ref[n, part, 0:40, :width] = mine[104:144, lanes]
        for row in range(WIN_LAT):
            for pair in range(HALF // 2):
                tiles = []
                for col in (2 * pair, 2 * pair + 1):
                    at = pl.ds(4 + row * HALF + col, LEVELS, stride=36)
                    tiles += [res_ref[n, part, at, :] for part in range(2)]
                shifted = [pltpu.roll(x, SPARE, 1) for x in tiles[2:]]
                tiles = [tiles[0], jnp.where(low, tiles[1], shifted[0])]
                tiles.append(jnp.where(low, shifted[0], shifted[1]))
                tiles = jnp.concatenate(tiles, axis=1).astype(jnp.bfloat16)
                out_ref[n, row, :, pair * 2 * chans : (pair + 1) * 2 * chans] = tiles
    if extra == "send":
        send_ref[0] = lower_ref[0, EDGE:]
        send_ref[1] = out_ref[0, EDGE:]


def run_units(units, near, far, weights, chans, heads, tables, extra=None, *extra_in):
    count = len(units)
    pieces = [x for is_near, w in units for x in (near[w] if is_near else far)]
    piece = pieces[0]
    outs = [jax.ShapeDtypeStruct((count, WIN_LAT) + piece.shape[1:], piece.dtype)]
    operands = (*pieces, *weights, *tables, *extra_in)
    if extra == "send":
        outs.append(jax.ShapeDtypeStruct((2, EDGE) + piece.shape[1:], piece.dtype))
    elif extra == "ahead":
        outs += [
            jax.ShapeDtypeStruct((1, 2, LEVELS * QUERIES, LANES), jnp.float32),
            jax.ShapeDtypeStruct((1, 2, 184, LANES), jnp.float32),
            jax.ShapeDtypeStruct((2 * heads * QUERIES, chans), jnp.bfloat16),
        ]
    vmem = pl.BlockSpec(memory_space=pltpu.VMEM)
    return pl.pallas_call(
        functools.partial(units_kernel, chans, heads, units, extra),
        out_shape=outs,
        in_specs=[vmem] * len(operands),
        out_specs=[vmem] * len(outs),
        scratch_shapes=[
            pltpu.VMEM((count, 2, LEVELS * QUERIES, LANES), jnp.float32),
            pltpu.VMEM((count, 2, 184, LANES), jnp.float32),
            pltpu.VMEM((count, 2, 184, LANES), jnp.float32),
        ],
        compiler_params=pltpu.CompilerParams(vmem_limit_bytes=VMEM_BYTES),
        cost_estimate=pl.CostEstimate(
            flops=200_000_000 * count, bytes_accessed=3_000_000, transcendentals=250_000 * count
        ),
        name="swin_windows",
    )(*operands)


def shards(
    field_in, norm1_gain, qkv_weight, proj_weight, earth_bias, norm2_gain, fc1_weight, fc2_weight
):
    levels, rows, flat = field_in.shape
    chans = qkv_weight.shape[0]
    heads = earth_bias.shape[2]
    half = HALF * chans
    field = jnp.transpose(field_in, (1, 0, 2))
    south = moved(field[:EDGE], "lat", -1)
    weights = (
        norm1_gain.reshape(1, chans),
        qkv_weight,
        proj_weight,
        norm2_gain.reshape(1, chans),
        fc1_weight,
        jnp.transpose(fc2_weight),
    )
    vmem = pl.BlockSpec(memory_space=pltpu.VMEM)
    anywhere = pl.BlockSpec(memory_space=pl.ANY)
    piece = jax.ShapeDtypeStruct((rows, levels, half), field.dtype)
    table = jax.ShapeDtypeStruct((2, 2, 2, heads * QUERIES, LANES), jnp.float32)
    windows, zwin, _, entries = earth_bias.shape
    tiles = entries // LANES
    bias = earth_bias.reshape(windows, zwin, heads, tiles, LANES).transpose(0, 2, 3, 1, 4)
    sources = (bias, field) + weights
    sources = [pltpu.with_memory_space_constraint(x, pltpu.HBM) for x in sources]
    outs = [table, table, piece, piece] + [jax.ShapeDtypeStruct(x.shape, x.dtype) for x in weights]
    high_table, low_table, near, far, *weights = pl.pallas_call(
        functools.partial(table_kernel, len(weights), heads),
        out_shape=outs,
        in_specs=[pl.BlockSpec(memory_space=pltpu.HBM)] * len(sources),
        out_specs=[vmem] * len(outs),
        scratch_shapes=[
            pltpu.VMEM((bias.size // LANES, LANES), bias.dtype),
            pltpu.SemaphoreType.DMA((4 + len(weights),)),
        ],
        compiler_params=pltpu.CompilerParams(vmem_limit_bytes=VMEM_BYTES),
        cost_estimate=pl.CostEstimate(flops=4_000_000, bytes_accessed=6_000_000, transcendentals=0),
        name="bias_tables",
    )(*sources)

    def pack(kernel, outs, *operands):
        return pl.pallas_call(
            kernel,
            out_shape=outs,
            in_specs=[vmem] * 2 + [anywhere] * (len(operands) - 2),
            out_specs=[vmem] * len(outs),
            compiler_params=pltpu.CompilerParams(vmem_limit_bytes=VMEM_BYTES),
            cost_estimate=pl.CostEstimate(flops=0, bytes_accessed=250_000, transcendentals=0),
            name="pack_half",
        )(*operands)

    (far,) = pack(pack_far_kernel, [piece], south, far)
    far_halo = swapped(far, "lon", 1)
    window = jax.ShapeDtypeStruct((WIN_LAT, levels, half), field.dtype)
    near_parts = pack(pack_near_kernel, [window, window], south, near, far)
    low, high = ((part, swapped(part, "lon", 0)) for part in near_parts)
    near, far = (high, low), (far, far_halo)
    common = (near, far, weights, chans, heads, (high_table, low_table))
    near_both, *ahead = run_units(((True, 1), (True, 0)), *common, "ahead", far[0])
    far_low, send = run_units(((False, 1),), *common, "send", *ahead, near_both)
    top = moved(send, "lat", 1)
    (far_high,) = run_units(((False, 0),), *common)
    done = pl.pallas_call(
        last_kernel,
        out_shape=jax.ShapeDtypeStruct(field.shape, field.dtype),
        in_specs=[vmem] * 4,
        out_specs=anywhere,
        scratch_shapes=[pltpu.SemaphoreType.DMA((6,))],
        compiler_params=pltpu.CompilerParams(vmem_limit_bytes=VMEM_BYTES),
        cost_estimate=pl.CostEstimate(flops=0, bytes_accessed=400_000, transcendentals=0),
        name="last_rows",
    )(top, near_both, far_low, far_high)
    return jnp.transpose(done, (1, 0, 2))


def solution(mesh):
    in_specs = (P(None, "lat", "lon"), P(), P(), P(), P("lat", None, None, None), P(), P(), P())
    out_specs = P(None, "lat", "lon")
    return jax.shard_map(shards, mesh=mesh, in_specs=in_specs, out_specs=out_specs, check_vma=False)
```

```python
import functools

import jax
import jax.numpy as jnp
from jax import lax
from jax.experimental import pallas as pl
from jax.experimental.pallas import tpu as pltpu
from jax.sharding import PartitionSpec as P

LEVELS = 4
WIN_LEV = 2
WIN_LAT = 6
WIN_LON = 12
EDGE = WIN_LAT // 2
HALF = WIN_LON // 2
TOKENS = WIN_LEV * WIN_LAT * WIN_LON
QUERIES = TOKENS // 2
LOG2E = 1.4426950408889634
GELU_0 = 0.7978845608028654
GELU_1 = 0.044715 * GELU_0
LANES = 128
SPARE = 64
VMEM_BYTES = 12 * 2**20
NT = (((1,), (1,)), ((), ()))


def moved(x, axis, by):
    size = lax.axis_size(axis)
    return lax.ppermute(x, axis, [(i, (i + by) % size) for i in range(size)])


def swapped(x, axis, first):
    size = lax.axis_size(axis)
    pairs = []
    for i in range(first, size, 2):
        j = (i + 1) % size
        pairs += [(i, j), (j, i)]
    return lax.ppermute(x, axis, pairs)


def half_places(half):
    odd = lax.rem(lax.axis_index("lon"), 2)
    return pl.multiple_of((1 - odd) * half, LANES), pl.multiple_of(odd * half, LANES)


def pack_far_kernel(south_ref, kept_ref, far_ref):
    at = half_places(far_ref.shape[2])[1]
    rows = far_ref.shape[0] - EDGE
    far_ref[:rows] = kept_ref[:rows]
    far_ref[rows:] = south_ref[:, :, pl.ds(at, far_ref.shape[2])]


def pack_near_kernel(south_ref, kept_ref, _, low_ref, high_ref):
    at = half_places(low_ref.shape[2])[0]
    high_ref[...] = kept_ref[:WIN_LAT]
    low_ref[:EDGE] = kept_ref[WIN_LAT : WIN_LAT + EDGE]
    low_ref[EDGE:] = south_ref[:, :, pl.ds(at, low_ref.shape[2])]


def last_kernel(top_ref, high_ref, near_low_ref, far_low_ref, out_ref, sems):
    half = top_ref.shape[3]
    copies = []
    for n, at in enumerate(half_places(half)):
        target = out_ref.at[:, :, pl.ds(at, half)]
        low_ref = (near_low_ref, far_low_ref)[n]
        for source, first in (
            (high_ref.at[n], EDGE),
            (low_ref.at[0, :EDGE], EDGE + WIN_LAT),
            (top_ref.at[n], 0),
        ):
            rows = pl.ds(first, source.shape[0])
            copy = pltpu.make_async_copy(source, target.at[rows], sems.at[len(copies)])
            copy.start()
            copies.append(copy)
    for copy in copies:
        copy.wait()


def build_tables(bias_ref, table_ref, heads, wrap):
    lines = bias_ref.shape[0] // heads
    blocks = WIN_LEV * WIN_LAT // 2
    lane = lax.broadcasted_iota(jnp.int32, (blocks, LANES), 1)
    block = lax.broadcasted_iota(jnp.int32, (blocks, LANES), 0)
    is_last = lax.axis_index("lat") == lax.axis_size("lat") - 1
    last = jnp.where(is_last, -1e9, 0.0).astype(jnp.float32)

    def penalty(part, second, levels):
        key = lane + part * LANES
        key_lev = key // QUERIES
        key_side = (key - key_lev * QUERIES) // (QUERIES // 2)
        row = 2 * block + second
        lev = row // WIN_LAT
        side = (row - lev * WIN_LAT) // EDGE
        out = jnp.zeros((blocks, LANES), jnp.float32)
        if levels:
            out = jnp.where(key_lev != lev, -1e9, out)
        if wrap:
            out = out + jnp.where(key_side != side, last, 0.0)
        return out

    masks = {
        (p, part, second): penalty(part, second, p == 1)
        for p in range(2)
        for part in range(2)
        for second in range(2)
    }
    for h in range(heads):
        for p in range(2):
            for third in range(3):
                line = h * lines + p + third * 18
                pieces = [
                    bias_ref[pl.ds(line + 2 * u, blocks, stride=54), :] * LOG2E for u in range(9)
                ]
                for r in range(8):
                    shift = 16 * r
                    main, nxt = pieces[r], pieces[r + 1]
                    if r:
                        main = pltpu.roll(main, LANES - shift, 1)
                        nxt = pltpu.roll(nxt, LANES - shift, 1)
                        main = jnp.where(lane < LANES - shift, main, nxt)
                    second, col = divmod(8 * third + r, WIN_LON)
                    side = col // HALF
                    place = h * QUERIES + HALF * second + col % HALF
                    at = pl.ds(place, blocks, stride=WIN_LON)
                    for part, piece in enumerate((main, nxt)):
                        table_ref[p, 1 - side, part, at, :] = piece + masks[p, part, second]


def table_kernel(count, heads, *refs):
    bias_any, field_any, *weights_any = refs[: 2 + count]
    table_ref, inner_ref, near_ref, far_ref, *weights_ref = refs[2 + count : 6 + 2 * count]
    bias_ref, sems = refs[6 + 2 * count :]
    lines = bias_ref.shape[0]
    flat = bias_any.reshape(2 * lines, LANES)
    rows, half = field_any.shape[0] - EDGE, near_ref.shape[2]
    near_at, far_at = half_places(half)
    fetches = [
        (flat.at[pl.ds(lines, lines)], bias_ref),
        (field_any.at[EDGE:, :, pl.ds(far_at, half)], far_ref.at[:rows]),
        (field_any.at[EDGE:, :, pl.ds(near_at, half)], near_ref.at[:rows]),
        (flat.at[pl.ds(0, lines)], inner_ref),
    ]
    fetches += list(zip(weights_any, weights_ref))
    fetches = [
        pltpu.make_async_copy(source, target, sems.at[n])
        for n, (source, target) in enumerate(fetches)
    ]
    for copy in fetches:
        copy.start()
    fetches[0].wait()
    build_tables(bias_ref, table_ref, heads, True)
    for copy in fetches[1:]:
        copy.wait()


def layer_norm(values, gain):
    center = values - jnp.mean(values, axis=-1, keepdims=True)
    spread = jnp.mean(center * center, axis=-1, keepdims=True)
    return center * lax.rsqrt(spread + 1e-05) * gain


def gelu(x):
    half = 0.5 * x
    return half + half * jnp.tanh(x * (GELU_0 + GELU_1 * (x * x)))


def units_kernel(chans, heads, units, extra, *refs):
    count = len(units)
    pieces, refs = refs[: 2 * count], refs[2 * count :]
    gain1_ref, qkv_ref, proj_ref, gain2_ref, fc1_ref, fc2_ref, table_ref, *refs = refs
    *refs, keys_ref, own_ref, res_ref = refs
    if extra == "ahead":
        raw_ref, far_ref, high_ref, out_ref, inner_ref, all_keys, all_own, all_picked = refs
        build_tables(raw_ref, inner_ref, heads, False)
    elif extra == "send":
        all_keys, all_own, all_picked, lower_ref, out_ref, send_ref = refs
    else:
        all_keys, all_own, all_picked, out_ref = refs
    slots = {(True, 1): None, (False, 1): 0, (True, 0): 1, (False, 0): 2}
    head_dim = chans // heads
    low = lax.broadcasted_iota(jnp.int32, (1, LANES), 1) < SPARE
    odd = lax.rem(lax.axis_index("lon"), 2)
    rights = [1 - odd if near else odd for near, _ in units]

    def tokens_of(ref, at, first, count):
        both = [ref[at, part, first : first + count] for part in range(2)]
        return jnp.concatenate([both[0], both[1][:, : chans - LANES]], axis=1)

    def split(ref, row):
        for pair in range(HALF // 2):
            both = ref[row, :, pair * 2 * chans : (pair + 1) * 2 * chans].astype(jnp.float32)
            first, middle, final = (both[:, u * LANES : (u + 1) * LANES] for u in range(3))
            yield 2 * pair, (first, middle)
            middle, final = pltpu.roll(middle, SPARE, 1), pltpu.roll(final, SPARE, 1)
            yield 2 * pair + 1, (jnp.where(low, middle, final), final)

    def place_keys(n, ref, first, column, into):
        for row in range(WIN_LAT):
            for col, block in split(ref, first + row):
                at = pl.ds(row * WIN_LON + col + column, LEVELS, stride=QUERIES)
                for part in range(2):
                    into[n, part, at, :] = block[part]

    def place_own(n, ref, first, column, into, own_into):
        for row in range(WIN_LAT):
            for col, block in split(ref, first + row):
                at = pl.ds(row * WIN_LON + col + column, LEVELS, stride=QUERIES)
                place = row * HALF + col
                for part in range(2):
                    into[n, part, at, :] = block[part]
                    own_into[n, part, pl.ds(4 + place, LEVELS, stride=36), :] = block[part]
                    own_into[n, part, pl.ds(148 + place, 1), :] = block[part][:1]

    def queries(n, own_from):
        own = layer_norm(tokens_of(own_from, n, 40, 144), gain1).astype(jnp.bfloat16)
        query = jnp.dot(own, qkv_ref[:, :chans], preferred_element_type=jnp.float32)
        query = query * (head_dim ** (-0.5) * LOG2E)
        picked = []
        for p in range(2):
            q = query[p * QUERIES : (p + 1) * QUERIES]
            picked += [
                jnp.where((lane >= h * head_dim) & (lane < (h + 1) * head_dim), q, 0.0)
                for h in range(heads)
            ]
        return jnp.concatenate(picked, axis=0).astype(jnp.bfloat16)

    owns = {n: (own_ref, n) for n in range(count)}
    for n, (near, window) in enumerate(units):
        if extra != "ahead":
            slot = slots[near, window]
            keys_ref[n] = all_keys[slot]
            owns[n] = (all_own, slot)
        own_piece, halo_piece = pieces[2 * n], pieces[2 * n + 1]
        first = 0 if near else window * WIN_LAT
        if extra == "ahead":
            place_own(n, own_piece, first, HALF - rights[n] * HALF, keys_ref, own_ref)
        place_keys(n, halo_piece, first, rights[n] * HALF, keys_ref)

    gain1 = gain1_ref[...]
    lane = lax.broadcasted_iota(jnp.int32, (1, chans), 1)
    ones = jnp.ones((TOKENS, 2 * LANES - chans), jnp.float32)
    scores, values, mixed = {}, {}, []
    for n in range(count):
        picked = queries(n, own_ref) if extra == "ahead" else all_picked[owns[n][1]]
        normed = []
        for p in range(2):
            levels = [(2 * p + 1 + lev) % LEVELS for lev in range(WIN_LEV)]
            parts = [tokens_of(keys_ref, n, lev * QUERIES, QUERIES) for lev in levels]
            parts = [layer_norm(x, gain1) for x in parts]
            normed.append(jnp.concatenate(parts, axis=0).astype(jnp.bfloat16))
        normed = jnp.concatenate(normed, axis=0)
        keys = jnp.dot(normed, qkv_ref[:, chans : 2 * chans], preferred_element_type=jnp.float32)
        rows = heads * QUERIES
        for p in range(2):
            k = keys[p * TOKENS : (p + 1) * TOKENS].astype(jnp.bfloat16)
            scores[n, p] = lax.dot_general(
                picked[p * rows : (p + 1) * rows], k, NT, preferred_element_type=jnp.float32
            )
        values[n] = jnp.dot(normed, qkv_ref[:, 2 * chans :], preferred_element_type=jnp.float32)
    if extra == "ahead":
        ahead = ((far_ref, WIN_LAT, odd), (high_ref, 0, 1 - odd), (far_ref, 0, odd))
        for slot, (ref, first, right) in enumerate(ahead):
            place_own(slot, ref, first, HALF - right * HALF, all_keys, all_own)
            all_picked[slot] = queries(slot, all_own)
    got = {}
    for n, (_, window) in enumerate(units):
        for p in range(2):
            probs = []
            for h in range(heads):
                at = slice(h * QUERIES, (h + 1) * QUERIES)
                bias = [table_ref[p, rights[n], part, at] for part in range(2)]
                bias = jnp.concatenate([bias[0], bias[1][:, : TOKENS - LANES]], axis=1)
                part = scores[n, p][at] + bias
                probs.append(jnp.exp2(part - jnp.max(part, axis=1, keepdims=True)))
            probs = jnp.concatenate(probs, axis=0).astype(jnp.bfloat16)
            v = jnp.concatenate([values[n][p * TOKENS : (p + 1) * TOKENS], ones], axis=1)
            v = v.astype(jnp.bfloat16)
            got[n, p] = jnp.dot(probs, v, preferred_element_type=jnp.float32)
    for n in range(count):
        for p in range(2):
            out = None
            for h in range(heads):
                part = got[n, p][h * QUERIES : (h + 1) * QUERIES]
                scaled = part[:, :chans] * (1.0 / part[:, chans : chans + 1])
                out = jnp.where(lane >= h * head_dim, scaled, out) if h else scaled
            mixed.append(out)
    mixed = jnp.concatenate(mixed, axis=0).astype(jnp.bfloat16)
    attn = jnp.dot(mixed, proj_ref[...], preferred_element_type=jnp.float32)
    attn = attn.astype(jnp.bfloat16).astype(jnp.float32)
    resid, normed = [], []
    for n in range(count):
        part = tokens_of(*owns[n], 40, 144) + attn[n * 144 : (n + 1) * 144]
        resid.append(part.astype(jnp.bfloat16).astype(jnp.float32))
        normed.append(layer_norm(resid[n], gain2_ref[...]).astype(jnp.bfloat16))
    result, normed = jnp.concatenate(resid, axis=0), jnp.concatenate(normed, axis=0)
    blocks = [slice(f, f + 2 * LANES) for f in range(0, fc1_ref.shape[1], 2 * LANES)]

    def first_product(at):
        return jnp.dot(normed, fc1_ref[:, at], preferred_element_type=jnp.float32)

    hidden = first_product(blocks[0])
    for b, at in enumerate(blocks):
        following = first_product(blocks[b + 1]) if b + 1 < len(blocks) else None
        active = gelu(hidden).astype(jnp.bfloat16)
        result = result + lax.dot_general(
            active, fc2_ref[:, at], NT, preferred_element_type=jnp.float32
        )
        hidden = following
    for n in range(count):
        mine = result[n * 144 : (n + 1) * 144]
        for part, lanes in enumerate((slice(0, LANES), slice(LANES, chans))):
            width = min(LANES, chans - part * LANES)
            res_ref[n, part, 40:184, :width] = mine[:, lanes]
            res_ref[n, part, 0:40, :width] = mine[104:144, lanes]
        for row in range(WIN_LAT):
            for pair in range(HALF // 2):
                tiles = []
                for col in (2 * pair, 2 * pair + 1):
                    at = pl.ds(4 + row * HALF + col, LEVELS, stride=36)
                    tiles += [res_ref[n, part, at, :] for part in range(2)]
                shifted = [pltpu.roll(x, SPARE, 1) for x in tiles[2:]]
                tiles = [tiles[0], jnp.where(low, tiles[1], shifted[0])]
                tiles.append(jnp.where(low, shifted[0], shifted[1]))
                tiles = jnp.concatenate(tiles, axis=1).astype(jnp.bfloat16)
                out_ref[n, row, :, pair * 2 * chans : (pair + 1) * 2 * chans] = tiles
    if extra == "send":
        send_ref[0] = lower_ref[0, EDGE:]
        send_ref[1] = out_ref[0, EDGE:]


def run_units(units, near, far, weights, chans, heads, table, extra=None, *extra_in):
    count = len(units)
    pieces = [x for is_near, w in units for x in (near[w] if is_near else far)]
    piece = pieces[0]
    outs = [jax.ShapeDtypeStruct((count, WIN_LAT) + piece.shape[1:], piece.dtype)]
    operands = (*pieces, *weights, table, *extra_in)
    if extra == "send":
        outs.append(jax.ShapeDtypeStruct((2, EDGE) + piece.shape[1:], piece.dtype))
    elif extra == "ahead":
        outs += [
            jax.ShapeDtypeStruct(table.shape, table.dtype),
            jax.ShapeDtypeStruct((3, 2, LEVELS * QUERIES, LANES), jnp.float32),
            jax.ShapeDtypeStruct((3, 2, 184, LANES), jnp.float32),
            jax.ShapeDtypeStruct((3, 2 * heads * QUERIES, chans), jnp.bfloat16),
        ]
    vmem = pl.BlockSpec(memory_space=pltpu.VMEM)
    return pl.pallas_call(
        functools.partial(units_kernel, chans, heads, units, extra),
        out_shape=outs,
        in_specs=[vmem] * len(operands),
        out_specs=[vmem] * len(outs),
        scratch_shapes=[
            pltpu.VMEM((count, 2, LEVELS * QUERIES, LANES), jnp.float32),
            pltpu.VMEM((count, 2, 184, LANES), jnp.float32),
            pltpu.VMEM((count, 2, 184, LANES), jnp.float32),
        ],
        compiler_params=pltpu.CompilerParams(vmem_limit_bytes=VMEM_BYTES),
        cost_estimate=pl.CostEstimate(
            flops=200_000_000 * count, bytes_accessed=3_000_000, transcendentals=250_000 * count
        ),
        name="swin_windows",
    )(*operands)


def shards(
    field_in, norm1_gain, qkv_weight, proj_weight, earth_bias, norm2_gain, fc1_weight, fc2_weight
):
    levels, rows, flat = field_in.shape
    chans = qkv_weight.shape[0]
    heads = earth_bias.shape[2]
    half = HALF * chans
    field = jnp.transpose(field_in, (1, 0, 2))
    south = moved(field[:EDGE], "lat", -1)
    weights = (
        norm1_gain.reshape(1, chans),
        qkv_weight,
        proj_weight,
        norm2_gain.reshape(1, chans),
        fc1_weight,
        jnp.transpose(fc2_weight),
    )
    vmem = pl.BlockSpec(memory_space=pltpu.VMEM)
    anywhere = pl.BlockSpec(memory_space=pl.ANY)
    piece = jax.ShapeDtypeStruct((rows, levels, half), field.dtype)
    table = jax.ShapeDtypeStruct((2, 2, 2, heads * QUERIES, LANES), jnp.float32)
    windows, zwin, _, entries = earth_bias.shape
    tiles = entries // LANES
    bias = earth_bias.reshape(windows, zwin, heads, tiles, LANES).transpose(0, 2, 3, 1, 4)
    sources = (bias, field) + weights
    raw = jax.ShapeDtypeStruct((bias.size // windows // LANES, LANES), bias.dtype)
    sources = [pltpu.with_memory_space_constraint(x, pltpu.HBM) for x in sources]
    outs = [table, raw, piece, piece] + [jax.ShapeDtypeStruct(x.shape, x.dtype) for x in weights]
    table, inner, near, far, *weights = pl.pallas_call(
        functools.partial(table_kernel, len(weights), heads),
        out_shape=outs,
        in_specs=[pl.BlockSpec(memory_space=pltpu.HBM)] * len(sources),
        out_specs=[vmem] * len(outs),
        scratch_shapes=[
            pltpu.VMEM(raw.shape, raw.dtype),
            pltpu.SemaphoreType.DMA((4 + len(weights),)),
        ],
        compiler_params=pltpu.CompilerParams(vmem_limit_bytes=VMEM_BYTES),
        cost_estimate=pl.CostEstimate(flops=4_000_000, bytes_accessed=6_000_000, transcendentals=0),
        name="bias_tables",
    )(*sources)

    def pack(kernel, outs, *operands):
        return pl.pallas_call(
            kernel,
            out_shape=outs,
            in_specs=[vmem] * 2 + [anywhere] * (len(operands) - 2),
            out_specs=[vmem] * len(outs),
            compiler_params=pltpu.CompilerParams(vmem_limit_bytes=VMEM_BYTES),
            cost_estimate=pl.CostEstimate(flops=0, bytes_accessed=250_000, transcendentals=0),
            name="pack_half",
        )(*operands)

    (far,) = pack(pack_far_kernel, [piece], south, far)
    far_halo = swapped(far, "lon", 1)
    window = jax.ShapeDtypeStruct((WIN_LAT, levels, half), field.dtype)
    near_parts = pack(pack_near_kernel, [window, window], south, near, far)
    low, high = ((part, swapped(part, "lon", 0)) for part in near_parts)
    near, far = (high, low), (far, far_halo)
    common = (near, far, weights, chans, heads)
    near_low, inner, *ahead = run_units(
        ((True, 1),), *common, table, "ahead", inner, far[0], high[0]
    )
    far_low, send = run_units(((False, 1),), *common, table, "send", *ahead, near_low)
    top = moved(send, "lat", 1)
    (high,) = run_units(((True, 0), (False, 0)), *common, inner, None, *ahead)
    done = pl.pallas_call(
        last_kernel,
        out_shape=jax.ShapeDtypeStruct(field.shape, field.dtype),
        in_specs=[vmem] * 4,
        out_specs=anywhere,
        scratch_shapes=[pltpu.SemaphoreType.DMA((6,))],
        compiler_params=pltpu.CompilerParams(vmem_limit_bytes=VMEM_BYTES),
        cost_estimate=pl.CostEstimate(flops=0, bytes_accessed=400_000, transcendentals=0),
        name="last_rows",
    )(top, high, near_low, far_low)
    return jnp.transpose(done, (1, 0, 2))


def solution(mesh):
    in_specs = (P(None, "lat", "lon"), P(), P(), P(), P("lat", None, None, None), P(), P(), P())
    out_specs = P(None, "lat", "lon")
    return jax.shard_map(shards, mesh=mesh, in_specs=in_specs, out_specs=out_specs, check_vma=False)
```

```python
import functools

import jax
import jax.numpy as jnp
from jax import lax
from jax.experimental import pallas as pl
from jax.experimental.pallas import tpu as pltpu
from jax.sharding import PartitionSpec as P

LEVELS = 4
WIN_LEV = 2
WIN_LAT = 6
WIN_LON = 12
EDGE = WIN_LAT // 2
HALF = WIN_LON // 2
TOKENS = WIN_LEV * WIN_LAT * WIN_LON
QUERIES = TOKENS // 2
LOG2E = 1.4426950408889634
GELU_0 = 0.7978845608028654
GELU_1 = 0.044715 * GELU_0
LANES = 128
SPARE = 64
VMEM_BYTES = 12 * 2**20
NT = (((1,), (1,)), ((), ()))


def moved(x, axis, by):
    size = lax.axis_size(axis)
    return lax.ppermute(x, axis, [(i, (i + by) % size) for i in range(size)])


def swapped(x, axis, first):
    size = lax.axis_size(axis)
    pairs = []
    for i in range(first, size, 2):
        j = (i + 1) % size
        pairs += [(i, j), (j, i)]
    return lax.ppermute(x, axis, pairs)


def half_places(half):
    odd = lax.rem(lax.axis_index("lon"), 2)
    return pl.multiple_of((1 - odd) * half, LANES), pl.multiple_of(odd * half, LANES)


def pack_far_kernel(south_ref, kept_ref, far_ref):
    at = half_places(far_ref.shape[2])[1]
    rows = far_ref.shape[0] - EDGE
    far_ref[:rows] = kept_ref[:rows]
    far_ref[rows:] = south_ref[:, :, pl.ds(at, far_ref.shape[2])]


def pack_near_kernel(south_ref, kept_ref, _, low_ref, high_ref):
    at = half_places(low_ref.shape[2])[0]
    high_ref[...] = kept_ref[:WIN_LAT]
    low_ref[:EDGE] = kept_ref[WIN_LAT : WIN_LAT + EDGE]
    low_ref[EDGE:] = south_ref[:, :, pl.ds(at, low_ref.shape[2])]


def last_kernel(top_ref, high_ref, near_low_ref, far_low_ref, out_ref, sems):
    half = top_ref.shape[3]
    copies = []
    for n, at in enumerate(half_places(half)):
        target = out_ref.at[:, :, pl.ds(at, half)]
        low_ref = (near_low_ref, far_low_ref)[n]
        for source, first in (
            (high_ref.at[n], EDGE),
            (low_ref.at[0, :EDGE], EDGE + WIN_LAT),
            (top_ref.at[n], 0),
        ):
            rows = pl.ds(first, source.shape[0])
            copy = pltpu.make_async_copy(source, target.at[rows], sems.at[len(copies)])
            copy.start()
            copies.append(copy)
    for copy in copies:
        copy.wait()


def build_tables(bias_ref, table_ref, heads, wrap):
    lines = bias_ref.shape[0] // heads
    blocks = WIN_LEV * WIN_LAT // 2
    lane = lax.broadcasted_iota(jnp.int32, (blocks, LANES), 1)
    block = lax.broadcasted_iota(jnp.int32, (blocks, LANES), 0)
    is_last = lax.axis_index("lat") == lax.axis_size("lat") - 1
    last = jnp.where(is_last, -1e9, 0.0).astype(jnp.float32)

    def penalty(part, second, levels):
        key = lane + part * LANES
        key_lev = key // QUERIES
        key_side = (key - key_lev * QUERIES) // (QUERIES // 2)
        row = 2 * block + second
        lev = row // WIN_LAT
        side = (row - lev * WIN_LAT) // EDGE
        out = jnp.zeros((blocks, LANES), jnp.float32)
        if levels:
            out = jnp.where(key_lev != lev, -1e9, out)
        if wrap:
            out = out + jnp.where(key_side != side, last, 0.0)
        return out

    masks = {
        (p, part, second): penalty(part, second, p == 1)
        for p in range(2)
        for part in range(2)
        for second in range(2)
    }
    for h in range(heads):
        for p in range(2):
            for third in range(3):
                line = h * lines + p + third * 18
                pieces = [
                    bias_ref[pl.ds(line + 2 * u, blocks, stride=54), :] * LOG2E for u in range(9)
                ]
                for r in range(8):
                    shift = 16 * r
                    main, nxt = pieces[r], pieces[r + 1]
                    if r:
                        main = pltpu.roll(main, LANES - shift, 1)
                        nxt = pltpu.roll(nxt, LANES - shift, 1)
                        main = jnp.where(lane < LANES - shift, main, nxt)
                    second, col = divmod(8 * third + r, WIN_LON)
                    side = col // HALF
                    place = h * QUERIES + HALF * second + col % HALF
                    at = pl.ds(place, blocks, stride=WIN_LON)
                    for part, piece in enumerate((main, nxt)):
                        table_ref[p, 1 - side, part, at, :] = piece + masks[p, part, second]


def table_kernel(count, heads, *refs):
    bias_any, field_any, *weights_any = refs[: 2 + count]
    table_ref, inner_ref, near_ref, far_ref, *weights_ref = refs[2 + count : 6 + 2 * count]
    bias_ref, sems = refs[6 + 2 * count :]
    lines = bias_ref.shape[0]
    flat = bias_any.reshape(2 * lines, LANES)
    rows, half = field_any.shape[0] - EDGE, near_ref.shape[2]
    near_at, far_at = half_places(half)
    fetches = [
        (flat.at[pl.ds(lines, lines)], bias_ref),
        (field_any.at[EDGE:, :, pl.ds(far_at, half)], far_ref.at[:rows]),
        (field_any.at[EDGE:, :, pl.ds(near_at, half)], near_ref.at[:rows]),
        (flat.at[pl.ds(0, lines)], inner_ref),
    ]
    fetches += list(zip(weights_any, weights_ref))
    fetches = [
        pltpu.make_async_copy(source, target, sems.at[n])
        for n, (source, target) in enumerate(fetches)
    ]
    for copy in fetches:
        copy.start()
    fetches[0].wait()
    build_tables(bias_ref, table_ref, heads, True)
    for copy in fetches[1:]:
        copy.wait()


def layer_norm(values, gain):
    center = values - jnp.mean(values, axis=-1, keepdims=True)
    spread = jnp.mean(center * center, axis=-1, keepdims=True)
    return center * lax.rsqrt(spread + 1e-05) * gain


def gelu(x):
    one, zero = jnp.asarray(GELU_1, x.dtype), jnp.asarray(GELU_0, x.dtype)
    half = jnp.asarray(0.5, x.dtype) * x
    return half + half * jnp.tanh(x * (zero + one * (x * x)))


def units_kernel(chans, heads, units, extra, *refs):
    count = len(units)
    pieces, refs = refs[: 2 * count], refs[2 * count :]
    gain1_ref, qkv_ref, proj_ref, gain2_ref, fc1_ref, fc2_ref, table_ref, *refs = refs
    *refs, keys_ref, own_ref, res_ref = refs
    if extra == "ahead":
        raw_ref, far_ref, high_ref, out_ref, inner_ref, all_keys, all_own, all_picked = refs
        build_tables(raw_ref, inner_ref, heads, False)
    elif extra == "send":
        all_keys, all_own, all_picked, lower_ref, out_ref, send_ref = refs
    else:
        all_keys, all_own, all_picked, out_ref = refs
    slots = {(True, 1): None, (False, 1): 0, (True, 0): 1, (False, 0): 2}
    head_dim = chans // heads
    low = lax.broadcasted_iota(jnp.int32, (1, LANES), 1) < SPARE
    odd = lax.rem(lax.axis_index("lon"), 2)
    rights = [1 - odd if near else odd for near, _ in units]

    def tokens_of(ref, at, first, count):
        both = [ref[at, part, first : first + count] for part in range(2)]
        return jnp.concatenate([both[0], both[1][:, : chans - LANES]], axis=1)

    def split(ref, row):
        for pair in range(HALF // 2):
            both = ref[row, :, pair * 2 * chans : (pair + 1) * 2 * chans].astype(jnp.float32)
            first, middle, final = (both[:, u * LANES : (u + 1) * LANES] for u in range(3))
            yield 2 * pair, (first, middle)
            middle, final = pltpu.roll(middle, SPARE, 1), pltpu.roll(final, SPARE, 1)
            yield 2 * pair + 1, (jnp.where(low, middle, final), final)

    def place_keys(n, ref, first, column, into):
        for row in range(WIN_LAT):
            for col, block in split(ref, first + row):
                at = pl.ds(row * WIN_LON + col + column, LEVELS, stride=QUERIES)
                for part in range(2):
                    into[n, part, at, :] = block[part]

    def place_own(n, ref, first, column, into, own_into):
        for row in range(WIN_LAT):
            for col, block in split(ref, first + row):
                at = pl.ds(row * WIN_LON + col + column, LEVELS, stride=QUERIES)
                place = row * HALF + col
                for part in range(2):
                    into[n, part, at, :] = block[part]
                    own_into[n, part, pl.ds(4 + place, LEVELS, stride=36), :] = block[part]
                    own_into[n, part, pl.ds(148 + place, 1), :] = block[part][:1]

    def queries(n, own_from):
        own = layer_norm(tokens_of(own_from, n, 40, 144), gain1).astype(jnp.bfloat16)
        query = jnp.dot(own, qkv_ref[:, :chans], preferred_element_type=jnp.float32)
        query = query * (head_dim ** (-0.5) * LOG2E)
        picked = []
        for p in range(2):
            q = query[p * QUERIES : (p + 1) * QUERIES]
            picked += [
                jnp.where((lane >= h * head_dim) & (lane < (h + 1) * head_dim), q, 0.0)
                for h in range(heads)
            ]
        return jnp.concatenate(picked, axis=0).astype(jnp.bfloat16)

    owns = {n: (own_ref, n) for n in range(count)}
    for n, (near, window) in enumerate(units):
        if extra != "ahead":
            slot = slots[near, window]
            keys_ref[n] = all_keys[slot]
            owns[n] = (all_own, slot)
        own_piece, halo_piece = pieces[2 * n], pieces[2 * n + 1]
        first = 0 if near else window * WIN_LAT
        if extra == "ahead":
            place_own(n, own_piece, first, HALF - rights[n] * HALF, keys_ref, own_ref)
        place_keys(n, halo_piece, first, rights[n] * HALF, keys_ref)

    gain1 = gain1_ref[...]
    lane = lax.broadcasted_iota(jnp.int32, (1, chans), 1)
    ones = jnp.ones((TOKENS, 2 * LANES - chans), jnp.float32)
    scores, values, mixed = {}, {}, []
    for n in range(count):
        picked = queries(n, own_ref) if extra == "ahead" else all_picked[owns[n][1]]
        normed = []
        for p in range(2):
            levels = [(2 * p + 1 + lev) % LEVELS for lev in range(WIN_LEV)]
            parts = [tokens_of(keys_ref, n, lev * QUERIES, QUERIES) for lev in levels]
            parts = [layer_norm(x, gain1) for x in parts]
            normed.append(jnp.concatenate(parts, axis=0).astype(jnp.bfloat16))
        normed = jnp.concatenate(normed, axis=0)
        keys = jnp.dot(normed, qkv_ref[:, chans : 2 * chans], preferred_element_type=jnp.float32)
        rows = heads * QUERIES
        for p in range(2):
            k = keys[p * TOKENS : (p + 1) * TOKENS].astype(jnp.bfloat16)
            scores[n, p] = lax.dot_general(
                picked[p * rows : (p + 1) * rows], k, NT, preferred_element_type=jnp.float32
            )
        values[n] = jnp.dot(normed, qkv_ref[:, 2 * chans :], preferred_element_type=jnp.float32)
    if extra == "ahead":
        ahead = ((far_ref, WIN_LAT, odd), (high_ref, 0, 1 - odd), (far_ref, 0, odd))
        for slot, (ref, first, right) in enumerate(ahead):
            place_own(slot, ref, first, HALF - right * HALF, all_keys, all_own)
            all_picked[slot] = queries(slot, all_own)
    got = {}
    for n, (_, window) in enumerate(units):
        for p in range(2):
            probs = []
            for h in range(heads):
                at = slice(h * QUERIES, (h + 1) * QUERIES)
                bias = [table_ref[p, rights[n], part, at] for part in range(2)]
                bias = jnp.concatenate([bias[0], bias[1][:, : TOKENS - LANES]], axis=1)
                part = scores[n, p][at] + bias
                probs.append(jnp.exp2(part - jnp.max(part, axis=1, keepdims=True)))
            probs = jnp.concatenate(probs, axis=0).astype(jnp.bfloat16)
            v = jnp.concatenate([values[n][p * TOKENS : (p + 1) * TOKENS], ones], axis=1)
            v = v.astype(jnp.bfloat16)
            got[n, p] = jnp.dot(probs, v, preferred_element_type=jnp.float32)
    for n in range(count):
        for p in range(2):
            out = None
            for h in range(heads):
                part = got[n, p][h * QUERIES : (h + 1) * QUERIES]
                scaled = part[:, :chans] * (1.0 / part[:, chans : chans + 1])
                out = jnp.where(lane >= h * head_dim, scaled, out) if h else scaled
            mixed.append(out)
    mixed = jnp.concatenate(mixed, axis=0).astype(jnp.bfloat16)
    attn = jnp.dot(mixed, proj_ref[...], preferred_element_type=jnp.float32)
    attn = attn.astype(jnp.bfloat16).astype(jnp.float32)
    resid, normed = [], []
    for n in range(count):
        part = tokens_of(*owns[n], 40, 144) + attn[n * 144 : (n + 1) * 144]
        resid.append(part.astype(jnp.bfloat16).astype(jnp.float32))
        normed.append(layer_norm(resid[n], gain2_ref[...]).astype(jnp.bfloat16))
    result, normed = jnp.concatenate(resid, axis=0), jnp.concatenate(normed, axis=0)
    blocks = [slice(f, f + 2 * LANES) for f in range(0, fc1_ref.shape[1], 2 * LANES)]

    def first_product(at):
        return jnp.dot(normed, fc1_ref[:, at], preferred_element_type=jnp.float32)

    hidden = first_product(blocks[0])
    for b, at in enumerate(blocks):
        following = first_product(blocks[b + 1]) if b + 1 < len(blocks) else None
        active = gelu(hidden.astype(jnp.bfloat16))
        result = result + lax.dot_general(
            active, fc2_ref[:, at], NT, preferred_element_type=jnp.float32
        )
        hidden = following
    for n in range(count):
        mine = result[n * 144 : (n + 1) * 144]
        for part, lanes in enumerate((slice(0, LANES), slice(LANES, chans))):
            width = min(LANES, chans - part * LANES)
            res_ref[n, part, 40:184, :width] = mine[:, lanes]
            res_ref[n, part, 0:40, :width] = mine[104:144, lanes]
        for row in range(WIN_LAT):
            for pair in range(HALF // 2):
                tiles = []
                for col in (2 * pair, 2 * pair + 1):
                    at = pl.ds(4 + row * HALF + col, LEVELS, stride=36)
                    tiles += [res_ref[n, part, at, :] for part in range(2)]
                shifted = [pltpu.roll(x, SPARE, 1) for x in tiles[2:]]
                tiles = [tiles[0], jnp.where(low, tiles[1], shifted[0])]
                tiles.append(jnp.where(low, shifted[0], shifted[1]))
                tiles = jnp.concatenate(tiles, axis=1).astype(jnp.bfloat16)
                out_ref[n, row, :, pair * 2 * chans : (pair + 1) * 2 * chans] = tiles
    if extra == "send":
        send_ref[0] = lower_ref[0, EDGE:]
        send_ref[1] = out_ref[0, EDGE:]


def run_units(units, near, far, weights, chans, heads, table, extra=None, *extra_in):
    count = len(units)
    pieces = [x for is_near, w in units for x in (near[w] if is_near else far)]
    piece = pieces[0]
    outs = [jax.ShapeDtypeStruct((count, WIN_LAT) + piece.shape[1:], piece.dtype)]
    operands = (*pieces, *weights, table, *extra_in)
    if extra == "send":
        outs.append(jax.ShapeDtypeStruct((2, EDGE) + piece.shape[1:], piece.dtype))
    elif extra == "ahead":
        outs += [
            jax.ShapeDtypeStruct(table.shape, table.dtype),
            jax.ShapeDtypeStruct((3, 2, LEVELS * QUERIES, LANES), jnp.float32),
            jax.ShapeDtypeStruct((3, 2, 184, LANES), jnp.float32),
            jax.ShapeDtypeStruct((3, 2 * heads * QUERIES, chans), jnp.bfloat16),
        ]
    vmem = pl.BlockSpec(memory_space=pltpu.VMEM)
    return pl.pallas_call(
        functools.partial(units_kernel, chans, heads, units, extra),
        out_shape=outs,
        in_specs=[vmem] * len(operands),
        out_specs=[vmem] * len(outs),
        scratch_shapes=[
            pltpu.VMEM((count, 2, LEVELS * QUERIES, LANES), jnp.float32),
            pltpu.VMEM((count, 2, 184, LANES), jnp.float32),
            pltpu.VMEM((count, 2, 184, LANES), jnp.float32),
        ],
        compiler_params=pltpu.CompilerParams(vmem_limit_bytes=VMEM_BYTES),
        cost_estimate=pl.CostEstimate(
            flops=200_000_000 * count, bytes_accessed=3_000_000, transcendentals=250_000 * count
        ),
        name="swin_windows",
    )(*operands)


def shards(
    field_in, norm1_gain, qkv_weight, proj_weight, earth_bias, norm2_gain, fc1_weight, fc2_weight
):
    levels, rows, flat = field_in.shape
    chans = qkv_weight.shape[0]
    heads = earth_bias.shape[2]
    half = HALF * chans
    field = jnp.transpose(field_in, (1, 0, 2))
    south = moved(field[:EDGE], "lat", -1)
    weights = (
        norm1_gain.reshape(1, chans),
        qkv_weight,
        proj_weight,
        norm2_gain.reshape(1, chans),
        fc1_weight,
        jnp.transpose(fc2_weight),
    )
    vmem = pl.BlockSpec(memory_space=pltpu.VMEM)
    anywhere = pl.BlockSpec(memory_space=pl.ANY)
    piece = jax.ShapeDtypeStruct((rows, levels, half), field.dtype)
    table = jax.ShapeDtypeStruct((2, 2, 2, heads * QUERIES, LANES), jnp.float32)
    windows, zwin, _, entries = earth_bias.shape
    tiles = entries // LANES
    bias = earth_bias.reshape(windows, zwin, heads, tiles, LANES).transpose(0, 2, 3, 1, 4)
    sources = (bias, field) + weights
    raw = jax.ShapeDtypeStruct((bias.size // windows // LANES, LANES), bias.dtype)
    sources = [pltpu.with_memory_space_constraint(x, pltpu.HBM) for x in sources]
    outs = [table, raw, piece, piece] + [jax.ShapeDtypeStruct(x.shape, x.dtype) for x in weights]
    table, inner, near, far, *weights = pl.pallas_call(
        functools.partial(table_kernel, len(weights), heads),
        out_shape=outs,
        in_specs=[pl.BlockSpec(memory_space=pltpu.HBM)] * len(sources),
        out_specs=[vmem] * len(outs),
        scratch_shapes=[
            pltpu.VMEM(raw.shape, raw.dtype),
            pltpu.SemaphoreType.DMA((4 + len(weights),)),
        ],
        compiler_params=pltpu.CompilerParams(vmem_limit_bytes=VMEM_BYTES),
        cost_estimate=pl.CostEstimate(flops=4_000_000, bytes_accessed=6_000_000, transcendentals=0),
        name="bias_tables",
    )(*sources)

    def pack(kernel, outs, *operands):
        return pl.pallas_call(
            kernel,
            out_shape=outs,
            in_specs=[vmem] * 2 + [anywhere] * (len(operands) - 2),
            out_specs=[vmem] * len(outs),
            compiler_params=pltpu.CompilerParams(vmem_limit_bytes=VMEM_BYTES),
            cost_estimate=pl.CostEstimate(flops=0, bytes_accessed=250_000, transcendentals=0),
            name="pack_half",
        )(*operands)

    (far,) = pack(pack_far_kernel, [piece], south, far)
    far_halo = swapped(far, "lon", 1)
    window = jax.ShapeDtypeStruct((WIN_LAT, levels, half), field.dtype)
    near_parts = pack(pack_near_kernel, [window, window], south, near, far)
    low, high = ((part, swapped(part, "lon", 0)) for part in near_parts)
    near, far = (high, low), (far, far_halo)
    common = (near, far, weights, chans, heads)
    near_low, inner, *ahead = run_units(
        ((True, 1),), *common, table, "ahead", inner, far[0], high[0]
    )
    far_low, send = run_units(((False, 1),), *common, table, "send", *ahead, near_low)
    top = moved(send, "lat", 1)
    (high,) = run_units(((True, 0), (False, 0)), *common, inner, None, *ahead)
    done = pl.pallas_call(
        last_kernel,
        out_shape=jax.ShapeDtypeStruct(field.shape, field.dtype),
        in_specs=[vmem] * 4,
        out_specs=anywhere,
        scratch_shapes=[pltpu.SemaphoreType.DMA((6,))],
        compiler_params=pltpu.CompilerParams(vmem_limit_bytes=VMEM_BYTES),
        cost_estimate=pl.CostEstimate(flops=0, bytes_accessed=400_000, transcendentals=0),
        name="last_rows",
    )(top, high, near_low, far_low)
    return jnp.transpose(done, (1, 0, 2))


def solution(mesh):
    in_specs = (P(None, "lat", "lon"), P(), P(), P(), P("lat", None, None, None), P(), P(), P())
    out_specs = P(None, "lat", "lon")
    return jax.shard_map(shards, mesh=mesh, in_specs=in_specs, out_specs=out_specs, check_vma=False)
```

```python
import functools

import jax
import jax.numpy as jnp
from jax import lax
from jax.experimental import pallas as pl
from jax.experimental.pallas import tpu as pltpu
from jax.sharding import PartitionSpec as P

LEVELS = 4
WIN_LEV = 2
WIN_LAT = 6
WIN_LON = 12
EDGE = WIN_LAT // 2
HALF = WIN_LON // 2
TOKENS = WIN_LEV * WIN_LAT * WIN_LON
QUERIES = TOKENS // 2
LOG2E = 1.4426950408889634
GELU_0 = 0.7978845608028654
GELU_1 = 0.044715 * GELU_0
LANES = 128
SPARE = 64
VMEM_BYTES = 12 * 2**20
NT = (((1,), (1,)), ((), ()))


def moved(x, axis, by):
    size = lax.axis_size(axis)
    return lax.ppermute(x, axis, [(i, (i + by) % size) for i in range(size)])


def swapped(x, axis, first):
    size = lax.axis_size(axis)
    pairs = []
    for i in range(first, size, 2):
        j = (i + 1) % size
        pairs += [(i, j), (j, i)]
    return lax.ppermute(x, axis, pairs)


def half_places(half):
    odd = lax.rem(lax.axis_index("lon"), 2)
    return pl.multiple_of((1 - odd) * half, LANES), pl.multiple_of(odd * half, LANES)


def pack_far_kernel(south_ref, kept_ref, far_ref):
    at = half_places(far_ref.shape[2])[1]
    rows = far_ref.shape[0] - EDGE
    far_ref[:rows] = kept_ref[:rows]
    far_ref[rows:] = south_ref[:, :, pl.ds(at, far_ref.shape[2])]


def pack_near_kernel(south_ref, kept_ref, _, low_ref, high_ref):
    at = half_places(low_ref.shape[2])[0]
    high_ref[...] = kept_ref[:WIN_LAT]
    low_ref[:EDGE] = kept_ref[WIN_LAT : WIN_LAT + EDGE]
    low_ref[EDGE:] = south_ref[:, :, pl.ds(at, low_ref.shape[2])]


def last_kernel(top_ref, high_ref, near_low_ref, far_low_ref, out_ref, sems):
    half = top_ref.shape[3]
    copies = []
    for n, at in enumerate(half_places(half)):
        target = out_ref.at[:, :, pl.ds(at, half)]
        low_ref = (near_low_ref, far_low_ref)[n]
        for source, first in (
            (high_ref.at[n], EDGE),
            (low_ref.at[0, :EDGE], EDGE + WIN_LAT),
            (top_ref.at[n], 0),
        ):
            rows = pl.ds(first, source.shape[0])
            copy = pltpu.make_async_copy(source, target.at[rows], sems.at[len(copies)])
            copy.start()
            copies.append(copy)
    for copy in copies:
        copy.wait()


def build_tables(bias_ref, table_ref, heads, wrap):
    lines = bias_ref.shape[0] // heads
    blocks = WIN_LEV * WIN_LAT // 2
    lane = lax.broadcasted_iota(jnp.int32, (blocks, LANES), 1)
    block = lax.broadcasted_iota(jnp.int32, (blocks, LANES), 0)
    is_last = lax.axis_index("lat") == lax.axis_size("lat") - 1
    last = jnp.where(is_last, -1e9, 0.0).astype(jnp.float32)

    def penalty(part, second, levels):
        key = lane + part * LANES
        key_lev = key // QUERIES
        key_side = (key - key_lev * QUERIES) // (QUERIES // 2)
        row = 2 * block + second
        lev = row // WIN_LAT
        side = (row - lev * WIN_LAT) // EDGE
        out = jnp.zeros((blocks, LANES), jnp.float32)
        if levels:
            out = jnp.where(key_lev != lev, -1e9, out)
        if wrap:
            out = out + jnp.where(key_side != side, last, 0.0)
        return out

    masks = {
        (p, part, second): penalty(part, second, p == 1)
        for p in range(2)
        for part in range(2)
        for second in range(2)
    }
    for h in range(heads):
        for p in range(2):
            for third in range(3):
                line = h * lines + p + third * 18
                pieces = [
                    bias_ref[pl.ds(line + 2 * u, blocks, stride=54), :] * LOG2E for u in range(9)
                ]
                for r in range(8):
                    shift = 16 * r
                    main, nxt = pieces[r], pieces[r + 1]
                    if r:
                        main = pltpu.roll(main, LANES - shift, 1)
                        nxt = pltpu.roll(nxt, LANES - shift, 1)
                        main = jnp.where(lane < LANES - shift, main, nxt)
                    second, col = divmod(8 * third + r, WIN_LON)
                    side = col // HALF
                    place = h * QUERIES + HALF * second + col % HALF
                    at = pl.ds(place, blocks, stride=WIN_LON)
                    for part, piece in enumerate((main, nxt)):
                        table_ref[p, 1 - side, part, at, :] = piece + masks[p, part, second]


def table_kernel(count, heads, *refs):
    bias_any, field_any, *weights_any = refs[: 2 + count]
    table_ref, inner_ref, near_ref, far_ref, *weights_ref = refs[2 + count : 6 + 2 * count]
    bias_ref, sems = refs[6 + 2 * count :]
    lines = bias_ref.shape[0]
    flat = bias_any.reshape(2 * lines, LANES)
    rows, half = field_any.shape[0] - EDGE, near_ref.shape[2]
    near_at, far_at = half_places(half)
    fetches = [
        (flat.at[pl.ds(lines, lines)], bias_ref),
        (field_any.at[EDGE:, :, pl.ds(far_at, half)], far_ref.at[:rows]),
        (field_any.at[EDGE:, :, pl.ds(near_at, half)], near_ref.at[:rows]),
        (flat.at[pl.ds(0, lines)], inner_ref),
    ]
    fetches += list(zip(weights_any, weights_ref))
    fetches = [
        pltpu.make_async_copy(source, target, sems.at[n])
        for n, (source, target) in enumerate(fetches)
    ]
    for copy in fetches:
        copy.start()
    fetches[0].wait()
    build_tables(bias_ref, table_ref, heads, True)
    for copy in fetches[1:]:
        copy.wait()


def layer_norm(values, gain):
    center = values - jnp.mean(values, axis=-1, keepdims=True)
    spread = jnp.mean(center * center, axis=-1, keepdims=True)
    return center * lax.rsqrt(spread + 1e-05) * gain


def gelu(x):
    one, zero = jnp.asarray(GELU_1, x.dtype), jnp.asarray(GELU_0, x.dtype)
    half = jnp.asarray(0.5, x.dtype) * x
    return half + half * jnp.tanh(x * (zero + one * (x * x)))


def units_kernel(chans, heads, units, extra, *refs):
    count = len(units)
    pieces, refs = refs[: 2 * count], refs[2 * count :]
    gain1_ref, qkv_ref, proj_ref, gain2_ref, fc1_ref, fc2_ref, table_ref, *refs = refs
    *refs, keys_ref, own_ref, res_ref = refs
    if extra == "ahead":
        raw_ref, far_ref, high_ref, out_ref, inner_ref, all_keys, all_own, all_picked = refs
        build_tables(raw_ref, inner_ref, heads, False)
    elif extra == "send":
        all_keys, all_own, all_picked, lower_ref, out_ref, send_ref = refs
    else:
        all_keys, all_own, all_picked, out_ref = refs
    slots = {(True, 1): None, (False, 1): 0, (True, 0): 1, (False, 0): 2}
    head_dim = chans // heads
    low = lax.broadcasted_iota(jnp.int32, (1, LANES), 1) < SPARE
    odd = lax.rem(lax.axis_index("lon"), 2)
    rights = [1 - odd if near else odd for near, _ in units]

    def tokens_of(ref, at, first, count):
        both = [ref[at, part, first : first + count] for part in range(2)]
        return jnp.concatenate([both[0], both[1][:, : chans - LANES]], axis=1)

    def split(ref, row):
        for pair in range(HALF // 2):
            both = ref[row, :, pair * 2 * chans : (pair + 1) * 2 * chans].astype(jnp.float32)
            first, middle, final = (both[:, u * LANES : (u + 1) * LANES] for u in range(3))
            yield 2 * pair, (first, middle)
            middle, final = pltpu.roll(middle, SPARE, 1), pltpu.roll(final, SPARE, 1)
            yield 2 * pair + 1, (jnp.where(low, middle, final), final)

    def place_keys(n, ref, first, column, into):
        for row in range(WIN_LAT):
            for col, block in split(ref, first + row):
                at = pl.ds(row * WIN_LON + col + column, LEVELS, stride=QUERIES)
                for part in range(2):
                    into[n, part, at, :] = block[part]

    def place_own(n, ref, first, column, into, own_into):
        for row in range(WIN_LAT):
            for col, block in split(ref, first + row):
                at = pl.ds(row * WIN_LON + col + column, LEVELS, stride=QUERIES)
                place = row * HALF + col
                for part in range(2):
                    into[n, part, at, :] = block[part]
                    own_into[n, part, pl.ds(4 + place, LEVELS, stride=36), :] = block[part]
                    own_into[n, part, pl.ds(148 + place, 1), :] = block[part][:1]

    def queries(n, own_from):
        own = layer_norm(tokens_of(own_from, n, 40, 144), gain1).astype(jnp.bfloat16)
        query = jnp.dot(own, qkv_ref[:, :chans], preferred_element_type=jnp.float32)
        query = query * (head_dim ** (-0.5) * LOG2E)
        picked = []
        for p in range(2):
            q = query[p * QUERIES : (p + 1) * QUERIES]
            picked += [
                jnp.where((lane >= h * head_dim) & (lane < (h + 1) * head_dim), q, 0.0)
                for h in range(heads)
            ]
        return jnp.concatenate(picked, axis=0).astype(jnp.bfloat16)

    owns = {n: (own_ref, n) for n in range(count)}
    for n, (near, window) in enumerate(units):
        if extra != "ahead":
            slot = slots[near, window]
            keys_ref[n] = all_keys[slot]
            owns[n] = (all_own, slot)
        own_piece, halo_piece = pieces[2 * n], pieces[2 * n + 1]
        first = 0 if near else window * WIN_LAT
        if extra == "ahead":
            place_own(n, own_piece, first, HALF - rights[n] * HALF, keys_ref, own_ref)
        place_keys(n, halo_piece, first, rights[n] * HALF, keys_ref)

    gain1 = gain1_ref[...]
    lane = lax.broadcasted_iota(jnp.int32, (1, chans), 1)
    ones = jnp.ones((TOKENS, 2 * LANES - chans), jnp.float32)
    scores, values, mixed = {}, {}, []
    for n in range(count):
        picked = queries(n, own_ref) if extra == "ahead" else all_picked[owns[n][1]]
        normed = []
        for p in range(2):
            levels = [(2 * p + 1 + lev) % LEVELS for lev in range(WIN_LEV)]
            parts = [tokens_of(keys_ref, n, lev * QUERIES, QUERIES) for lev in levels]
            parts = [layer_norm(x, gain1) for x in parts]
            normed.append(jnp.concatenate(parts, axis=0).astype(jnp.bfloat16))
        normed = jnp.concatenate(normed, axis=0)
        keys = jnp.dot(normed, qkv_ref[:, chans : 2 * chans], preferred_element_type=jnp.float32)
        rows = heads * QUERIES
        for p in range(2):
            k = keys[p * TOKENS : (p + 1) * TOKENS].astype(jnp.bfloat16)
            scores[n, p] = lax.dot_general(
                picked[p * rows : (p + 1) * rows], k, NT, preferred_element_type=jnp.float32
            )
        values[n] = jnp.dot(normed, qkv_ref[:, 2 * chans :], preferred_element_type=jnp.float32)
    if extra == "ahead":
        ahead = ((far_ref, WIN_LAT, odd), (high_ref, 0, 1 - odd), (far_ref, 0, odd))
        for slot, (ref, first, right) in enumerate(ahead):
            place_own(slot, ref, first, HALF - right * HALF, all_keys, all_own)
            all_picked[slot] = queries(slot, all_own)
    got = {}
    for n, (_, window) in enumerate(units):
        for p in range(2):
            probs = []
            for h in range(heads):
                at = slice(h * QUERIES, (h + 1) * QUERIES)
                bias = [table_ref[p, rights[n], part, at] for part in range(2)]
                bias = jnp.concatenate([bias[0], bias[1][:, : TOKENS - LANES]], axis=1)
                part = scores[n, p][at] + bias
                probs.append(jnp.exp2(part - jnp.max(part, axis=1, keepdims=True)))
            probs = jnp.concatenate(probs, axis=0).astype(jnp.bfloat16)
            v = jnp.concatenate([values[n][p * TOKENS : (p + 1) * TOKENS], ones], axis=1)
            v = v.astype(jnp.bfloat16)
            got[n, p] = jnp.dot(probs, v, preferred_element_type=jnp.float32)
    for n in range(count):
        for p in range(2):
            out = None
            for h in range(heads):
                part = got[n, p][h * QUERIES : (h + 1) * QUERIES]
                total = part[:, chans : chans + 1]
                inverse = pl.reciprocal(total, approx=True)
                scaled = part[:, :chans] * (inverse * (2.0 - total * inverse))
                out = jnp.where(lane >= h * head_dim, scaled, out) if h else scaled
            mixed.append(out)
    mixed = jnp.concatenate(mixed, axis=0).astype(jnp.bfloat16)
    attn = jnp.dot(mixed, proj_ref[...], preferred_element_type=jnp.float32)
    attn = attn.astype(jnp.bfloat16).astype(jnp.float32)
    resid, normed = [], []
    for n in range(count):
        part = tokens_of(*owns[n], 40, 144) + attn[n * 144 : (n + 1) * 144]
        resid.append(part.astype(jnp.bfloat16).astype(jnp.float32))
        normed.append(layer_norm(resid[n], gain2_ref[...]).astype(jnp.bfloat16))
    result, normed = jnp.concatenate(resid, axis=0), jnp.concatenate(normed, axis=0)
    blocks = [slice(f, f + 2 * LANES) for f in range(0, fc1_ref.shape[1], 2 * LANES)]

    def first_product(at):
        return jnp.dot(normed, fc1_ref[:, at], preferred_element_type=jnp.float32)

    hidden = first_product(blocks[0])
    for b, at in enumerate(blocks):
        following = first_product(blocks[b + 1]) if b + 1 < len(blocks) else None
        active = gelu(hidden.astype(jnp.bfloat16))
        result = result + lax.dot_general(
            active, fc2_ref[:, at], NT, preferred_element_type=jnp.float32
        )
        hidden = following
    for n in range(count):
        mine = result[n * 144 : (n + 1) * 144]
        for part, lanes in enumerate((slice(0, LANES), slice(LANES, chans))):
            width = min(LANES, chans - part * LANES)
            res_ref[n, part, 40:184, :width] = mine[:, lanes]
            res_ref[n, part, 0:40, :width] = mine[104:144, lanes]
        for row in range(WIN_LAT):
            for pair in range(HALF // 2):
                tiles = []
                for col in (2 * pair, 2 * pair + 1):
                    at = pl.ds(4 + row * HALF + col, LEVELS, stride=36)
                    tiles += [res_ref[n, part, at, :] for part in range(2)]
                shifted = [pltpu.roll(x, SPARE, 1) for x in tiles[2:]]
                tiles = [tiles[0], jnp.where(low, tiles[1], shifted[0])]
                tiles.append(jnp.where(low, shifted[0], shifted[1]))
                tiles = jnp.concatenate(tiles, axis=1).astype(jnp.bfloat16)
                out_ref[n, row, :, pair * 2 * chans : (pair + 1) * 2 * chans] = tiles
    if extra == "send":
        send_ref[0] = lower_ref[0, EDGE:]
        send_ref[1] = out_ref[0, EDGE:]


def run_units(units, near, far, weights, chans, heads, table, extra=None, *extra_in):
    count = len(units)
    pieces = [x for is_near, w in units for x in (near[w] if is_near else far)]
    piece = pieces[0]
    outs = [jax.ShapeDtypeStruct((count, WIN_LAT) + piece.shape[1:], piece.dtype)]
    operands = (*pieces, *weights, table, *extra_in)
    if extra == "send":
        outs.append(jax.ShapeDtypeStruct((2, EDGE) + piece.shape[1:], piece.dtype))
    elif extra == "ahead":
        outs += [
            jax.ShapeDtypeStruct(table.shape, table.dtype),
            jax.ShapeDtypeStruct((3, 2, LEVELS * QUERIES, LANES), jnp.float32),
            jax.ShapeDtypeStruct((3, 2, 184, LANES), jnp.float32),
            jax.ShapeDtypeStruct((3, 2 * heads * QUERIES, chans), jnp.bfloat16),
        ]
    vmem = pl.BlockSpec(memory_space=pltpu.VMEM)
    return pl.pallas_call(
        functools.partial(units_kernel, chans, heads, units, extra),
        out_shape=outs,
        in_specs=[vmem] * len(operands),
        out_specs=[vmem] * len(outs),
        scratch_shapes=[
            pltpu.VMEM((count, 2, LEVELS * QUERIES, LANES), jnp.float32),
            pltpu.VMEM((count, 2, 184, LANES), jnp.float32),
            pltpu.VMEM((count, 2, 184, LANES), jnp.float32),
        ],
        compiler_params=pltpu.CompilerParams(vmem_limit_bytes=VMEM_BYTES),
        cost_estimate=pl.CostEstimate(
            flops=200_000_000 * count, bytes_accessed=3_000_000, transcendentals=250_000 * count
        ),
        name="swin_windows",
    )(*operands)


def shards(
    field_in, norm1_gain, qkv_weight, proj_weight, earth_bias, norm2_gain, fc1_weight, fc2_weight
):
    levels, rows, flat = field_in.shape
    chans = qkv_weight.shape[0]
    heads = earth_bias.shape[2]
    half = HALF * chans
    field = jnp.transpose(field_in, (1, 0, 2))
    south = moved(field[:EDGE], "lat", -1)
    weights = (
        norm1_gain.reshape(1, chans),
        qkv_weight,
        proj_weight,
        norm2_gain.reshape(1, chans),
        fc1_weight,
        jnp.transpose(fc2_weight),
    )
    vmem = pl.BlockSpec(memory_space=pltpu.VMEM)
    anywhere = pl.BlockSpec(memory_space=pl.ANY)
    piece = jax.ShapeDtypeStruct((rows, levels, half), field.dtype)
    table = jax.ShapeDtypeStruct((2, 2, 2, heads * QUERIES, LANES), jnp.float32)
    windows, zwin, _, entries = earth_bias.shape
    tiles = entries // LANES
    bias = earth_bias.reshape(windows, zwin, heads, tiles, LANES).transpose(0, 2, 3, 1, 4)
    sources = (bias, field) + weights
    raw = jax.ShapeDtypeStruct((bias.size // windows // LANES, LANES), bias.dtype)
    sources = [pltpu.with_memory_space_constraint(x, pltpu.HBM) for x in sources]
    outs = [table, raw, piece, piece] + [jax.ShapeDtypeStruct(x.shape, x.dtype) for x in weights]
    table, inner, near, far, *weights = pl.pallas_call(
        functools.partial(table_kernel, len(weights), heads),
        out_shape=outs,
        in_specs=[pl.BlockSpec(memory_space=pltpu.HBM)] * len(sources),
        out_specs=[vmem] * len(outs),
        scratch_shapes=[
            pltpu.VMEM(raw.shape, raw.dtype),
            pltpu.SemaphoreType.DMA((4 + len(weights),)),
        ],
        compiler_params=pltpu.CompilerParams(vmem_limit_bytes=VMEM_BYTES),
        cost_estimate=pl.CostEstimate(flops=4_000_000, bytes_accessed=6_000_000, transcendentals=0),
        name="bias_tables",
    )(*sources)

    def pack(kernel, outs, *operands):
        return pl.pallas_call(
            kernel,
            out_shape=outs,
            in_specs=[vmem] * 2 + [anywhere] * (len(operands) - 2),
            out_specs=[vmem] * len(outs),
            compiler_params=pltpu.CompilerParams(vmem_limit_bytes=VMEM_BYTES),
            cost_estimate=pl.CostEstimate(flops=0, bytes_accessed=250_000, transcendentals=0),
            name="pack_half",
        )(*operands)

    (far,) = pack(pack_far_kernel, [piece], south, far)
    far_halo = swapped(far, "lon", 1)
    window = jax.ShapeDtypeStruct((WIN_LAT, levels, half), field.dtype)
    near_parts = pack(pack_near_kernel, [window, window], south, near, far)
    low, high = ((part, swapped(part, "lon", 0)) for part in near_parts)
    near, far = (high, low), (far, far_halo)
    common = (near, far, weights, chans, heads)
    near_low, inner, *ahead = run_units(
        ((True, 1),), *common, table, "ahead", inner, far[0], high[0]
    )
    far_low, send = run_units(((False, 1),), *common, table, "send", *ahead, near_low)
    top = moved(send, "lat", 1)
    (high,) = run_units(((True, 0), (False, 0)), *common, inner, None, *ahead)
    done = pl.pallas_call(
        last_kernel,
        out_shape=jax.ShapeDtypeStruct(field.shape, field.dtype),
        in_specs=[vmem] * 4,
        out_specs=anywhere,
        scratch_shapes=[pltpu.SemaphoreType.DMA((6,))],
        compiler_params=pltpu.CompilerParams(vmem_limit_bytes=VMEM_BYTES),
        cost_estimate=pl.CostEstimate(flops=0, bytes_accessed=400_000, transcendentals=0),
        name="last_rows",
    )(top, high, near_low, far_low)
    return jnp.transpose(done, (1, 0, 2))


def solution(mesh):
    in_specs = (P(None, "lat", "lon"), P(), P(), P(), P("lat", None, None, None), P(), P(), P())
    out_specs = P(None, "lat", "lon")
    return jax.shard_map(shards, mesh=mesh, in_specs=in_specs, out_specs=out_specs, check_vma=False)
```

```python
import functools

import jax
import jax.numpy as jnp
from jax import lax
from jax.experimental import pallas as pl
from jax.experimental.pallas import tpu as pltpu
from jax.sharding import PartitionSpec as P

LEVELS = 4
WIN_LEV = 2
WIN_LAT = 6
WIN_LON = 12
EDGE = WIN_LAT // 2
HALF = WIN_LON // 2
TOKENS = WIN_LEV * WIN_LAT * WIN_LON
QUERIES = TOKENS // 2
LOG2E = 1.4426950408889634
GELU_0 = 0.7978845608028654
GELU_1 = 0.044715 * GELU_0
LANES = 128
SPARE = 64
VMEM_BYTES = 12 * 2**20
NT = (((1,), (1,)), ((), ()))


def moved(x, axis, by):
    size = lax.axis_size(axis)
    return lax.ppermute(x, axis, [(i, (i + by) % size) for i in range(size)])


def swapped(x, axis, first):
    size = lax.axis_size(axis)
    pairs = []
    for i in range(first, size, 2):
        j = (i + 1) % size
        pairs += [(i, j), (j, i)]
    return lax.ppermute(x, axis, pairs)


def half_places(half):
    odd = lax.rem(lax.axis_index("lon"), 2)
    return pl.multiple_of((1 - odd) * half, LANES), pl.multiple_of(odd * half, LANES)


def pack_far_kernel(south_ref, kept_ref, far_ref):
    at = half_places(far_ref.shape[2])[1]
    rows = far_ref.shape[0] - EDGE
    far_ref[:rows] = kept_ref[:rows]
    far_ref[rows:] = south_ref[:, :, pl.ds(at, far_ref.shape[2])]


def pack_near_kernel(south_ref, kept_ref, _, low_ref, high_ref):
    at = half_places(low_ref.shape[2])[0]
    high_ref[...] = kept_ref[:WIN_LAT]
    low_ref[:EDGE] = kept_ref[WIN_LAT : WIN_LAT + EDGE]
    low_ref[EDGE:] = south_ref[:, :, pl.ds(at, low_ref.shape[2])]


def last_kernel(top_ref, high_ref, near_low_ref, far_low_ref, out_ref, sems):
    half = top_ref.shape[3]
    copies = []
    for n, at in enumerate(half_places(half)):
        target = out_ref.at[:, :, pl.ds(at, half)]
        low_ref = (near_low_ref, far_low_ref)[n]
        for source, first in (
            (high_ref.at[n], EDGE),
            (low_ref.at[0, :EDGE], EDGE + WIN_LAT),
            (top_ref.at[n], 0),
        ):
            rows = pl.ds(first, source.shape[0])
            copy = pltpu.make_async_copy(source, target.at[rows], sems.at[len(copies)])
            copy.start()
            copies.append(copy)
    for copy in copies:
        copy.wait()


def build_tables(bias_ref, table_ref, heads, wrap):
    lines = 2 * TOKENS * TOKENS // LANES
    blocks = WIN_LEV * WIN_LAT // 2
    lane = lax.broadcasted_iota(jnp.int32, (blocks, LANES), 1)
    block = lax.broadcasted_iota(jnp.int32, (blocks, LANES), 0)
    is_last = lax.axis_index("lat") == lax.axis_size("lat") - 1
    last = jnp.where(is_last, -1e9, 0.0).astype(jnp.float32)

    def penalty(part, second, levels):
        key = lane + part * LANES
        key_lev = key // QUERIES
        key_side = (key - key_lev * QUERIES) // (QUERIES // 2)
        row = 2 * block + second
        lev = row // WIN_LAT
        side = (row - lev * WIN_LAT) // EDGE
        out = jnp.zeros((blocks, LANES), jnp.float32)
        if levels:
            out = jnp.where(key_lev != lev, -1e9, out)
        if wrap:
            out = out + jnp.where(key_side != side, last, 0.0)
        return out

    masks = {
        (p, part, second): penalty(part, second, p == 1)
        for p in range(2)
        for part in range(2)
        for second in range(2)
    }
    for h in range(heads):
        for p in range(2):
            for third in range(3):
                line = h * lines + p + third * 18
                pieces = [
                    bias_ref[pl.ds(line + 2 * u, blocks, stride=54), :] * LOG2E for u in range(9)
                ]
                for r in range(8):
                    shift = 16 * r
                    main, nxt = pieces[r], pieces[r + 1]
                    if r:
                        main = pltpu.roll(main, LANES - shift, 1)
                        nxt = pltpu.roll(nxt, LANES - shift, 1)
                        main = jnp.where(lane < LANES - shift, main, nxt)
                    second, col = divmod(8 * third + r, WIN_LON)
                    side = col // HALF
                    place = h * QUERIES + HALF * second + col % HALF
                    at = pl.ds(place, blocks, stride=WIN_LON)
                    for part, piece in enumerate((main, nxt)):
                        table_ref[p, 1 - side, part, at, :] = piece + masks[p, part, second]


def table_kernel(count, heads, *refs):
    bias_any, field_any, *weights_any = refs[: 2 + count]
    table_ref, inner_ref, near_ref, far_ref, *weights_ref = refs[2 + count : 6 + 2 * count]
    bias_ref, sems = refs[6 + 2 * count :]
    lines = heads * 2 * TOKENS * TOKENS // LANES
    flat = bias_any.reshape(2 * lines, LANES)
    rows, half = field_any.shape[0] - EDGE, near_ref.shape[2]
    near_at, far_at = half_places(half)
    fetches = [
        (flat.at[pl.ds(lines, lines)], bias_ref.at[pl.ds(0, lines)]),
        (field_any.at[EDGE:, :, pl.ds(far_at, half)], far_ref.at[:rows]),
        (field_any.at[EDGE:, :, pl.ds(near_at, half)], near_ref.at[:rows]),
        (flat.at[pl.ds(0, lines)], inner_ref.at[pl.ds(0, lines)]),
    ]
    fetches += list(zip(weights_any, weights_ref))
    fetches = [
        pltpu.make_async_copy(source, target, sems.at[n])
        for n, (source, target) in enumerate(fetches)
    ]
    for copy in fetches:
        copy.start()
    fetches[0].wait()
    build_tables(bias_ref, table_ref, heads, True)
    for copy in fetches[1:]:
        copy.wait()


def layer_norm(values, gain):
    center = values - jnp.mean(values, axis=-1, keepdims=True)
    spread = jnp.mean(center * center, axis=-1, keepdims=True)
    return center * lax.rsqrt(spread + 1e-05) * gain


def gelu(x):
    one, zero = jnp.asarray(GELU_1, x.dtype), jnp.asarray(GELU_0, x.dtype)
    half = jnp.asarray(0.5, x.dtype) * x
    return half + half * jnp.tanh(x * (zero + one * (x * x)))


def units_kernel(chans, heads, units, extra, *refs):
    count = len(units)
    pieces, refs = refs[: 2 * count], refs[2 * count :]
    gain1_ref, qkv_ref, proj_ref, gain2_ref, fc1_ref, fc2_ref, table_ref, *refs = refs
    *refs, keys_ref, own_ref, res_ref = refs
    if extra == "ahead":
        raw_ref, far_ref, high_ref, out_ref, inner_ref, all_keys, all_own, all_picked = refs
        build_tables(raw_ref, inner_ref, heads, False)
    elif extra == "send":
        all_keys, all_own, all_picked, lower_ref, out_ref, send_ref = refs
    else:
        all_keys, all_own, all_picked, out_ref = refs
    slots = {(True, 1): None, (False, 1): 0, (True, 0): 1, (False, 0): 2}
    head_dim = chans // heads
    low = lax.broadcasted_iota(jnp.int32, (1, LANES), 1) < SPARE
    odd = lax.rem(lax.axis_index("lon"), 2)
    rights = [1 - odd if near else odd for near, _ in units]

    def tokens_of(ref, at, first, count):
        both = [ref[at, part, first : first + count] for part in range(2)]
        return jnp.concatenate([both[0], both[1][:, : chans - LANES]], axis=1)

    def split(ref, row):
        for pair in range(HALF // 2):
            both = ref[row, :, pair * 2 * chans : (pair + 1) * 2 * chans].astype(jnp.float32)
            first, middle, final = (both[:, u * LANES : (u + 1) * LANES] for u in range(3))
            yield 2 * pair, (first, middle)
            middle, final = pltpu.roll(middle, SPARE, 1), pltpu.roll(final, SPARE, 1)
            yield 2 * pair + 1, (jnp.where(low, middle, final), final)

    def place_keys(n, ref, first, column, into):
        for row in range(WIN_LAT):
            for col, block in split(ref, first + row):
                at = pl.ds(row * WIN_LON + col + column, LEVELS, stride=QUERIES)
                for part in range(2):
                    into[n, part, at, :] = block[part]

    def place_own(n, ref, first, column, into, own_into):
        for row in range(WIN_LAT):
            for col, block in split(ref, first + row):
                at = pl.ds(row * WIN_LON + col + column, LEVELS, stride=QUERIES)
                place = row * HALF + col
                for part in range(2):
                    into[n, part, at, :] = block[part]
                    own_into[n, part, pl.ds(4 + place, LEVELS, stride=36), :] = block[part]
                    own_into[n, part, pl.ds(148 + place, 1), :] = block[part][:1]

    def queries(n, own_from):
        own = layer_norm(tokens_of(own_from, n, 40, 144), gain1).astype(jnp.bfloat16)
        query = jnp.dot(own, qkv_ref[:, :chans], preferred_element_type=jnp.float32)
        query = query * (head_dim ** (-0.5) * LOG2E)
        picked = []
        for p in range(2):
            q = query[p * QUERIES : (p + 1) * QUERIES]
            picked += [
                jnp.where((lane >= h * head_dim) & (lane < (h + 1) * head_dim), q, 0.0)
                for h in range(heads)
            ]
        return jnp.concatenate(picked, axis=0).astype(jnp.bfloat16)

    owns = {n: (own_ref, n) for n in range(count)}
    for n, (near, window) in enumerate(units):
        if extra != "ahead":
            slot = slots[near, window]
            keys_ref[n] = all_keys[slot]
            owns[n] = (all_own, slot)
        own_piece, halo_piece = pieces[2 * n], pieces[2 * n + 1]
        first = 0 if near else window * WIN_LAT
        if extra == "ahead":
            place_own(n, own_piece, first, HALF - rights[n] * HALF, keys_ref, own_ref)
        place_keys(n, halo_piece, first, rights[n] * HALF, keys_ref)

    gain1 = gain1_ref[...]
    lane = lax.broadcasted_iota(jnp.int32, (1, chans), 1)
    ones = jnp.ones((TOKENS, 2 * LANES - chans), jnp.float32)
    scores, values, mixed = {}, {}, []
    for n in range(count):
        picked = queries(n, own_ref) if extra == "ahead" else all_picked[owns[n][1]]
        normed = []
        for p in range(2):
            levels = [(2 * p + 1 + lev) % LEVELS for lev in range(WIN_LEV)]
            parts = [tokens_of(keys_ref, n, lev * QUERIES, QUERIES) for lev in levels]
            parts = [layer_norm(x, gain1) for x in parts]
            normed.append(jnp.concatenate(parts, axis=0).astype(jnp.bfloat16))
        normed = jnp.concatenate(normed, axis=0)
        keys = jnp.dot(normed, qkv_ref[:, chans : 2 * chans], preferred_element_type=jnp.float32)
        rows = heads * QUERIES
        for p in range(2):
            k = keys[p * TOKENS : (p + 1) * TOKENS].astype(jnp.bfloat16)
            scores[n, p] = lax.dot_general(
                picked[p * rows : (p + 1) * rows], k, NT, preferred_element_type=jnp.float32
            )
        values[n] = jnp.dot(normed, qkv_ref[:, 2 * chans :], preferred_element_type=jnp.float32)
    if extra == "ahead":
        ahead = ((far_ref, WIN_LAT, odd), (high_ref, 0, 1 - odd), (far_ref, 0, odd))
        for slot, (ref, first, right) in enumerate(ahead):
            place_own(slot, ref, first, HALF - right * HALF, all_keys, all_own)
            all_picked[slot] = queries(slot, all_own)
    got = {}
    for n, (_, window) in enumerate(units):
        for p in range(2):
            probs = []
            for h in range(heads):
                at = slice(h * QUERIES, (h + 1) * QUERIES)
                bias = [table_ref[p, rights[n], part, at] for part in range(2)]
                bias = jnp.concatenate([bias[0], bias[1][:, : TOKENS - LANES]], axis=1)
                part = scores[n, p][at] + bias
                probs.append(jnp.exp2(part - jnp.max(part, axis=1, keepdims=True)))
            probs = jnp.concatenate(probs, axis=0).astype(jnp.bfloat16)
            v = jnp.concatenate([values[n][p * TOKENS : (p + 1) * TOKENS], ones], axis=1)
            v = v.astype(jnp.bfloat16)
            got[n, p] = jnp.dot(probs, v, preferred_element_type=jnp.float32)
    for n in range(count):
        for p in range(2):
            out = None
            for h in range(heads):
                part = got[n, p][h * QUERIES : (h + 1) * QUERIES]
                scaled = part[:, :chans] * (1.0 / part[:, chans : chans + 1])
                out = jnp.where(lane >= h * head_dim, scaled, out) if h else scaled
            mixed.append(out)
    mixed = jnp.concatenate(mixed, axis=0).astype(jnp.bfloat16)
    attn = jnp.dot(mixed, proj_ref[...], preferred_element_type=jnp.float32)
    attn = attn.astype(jnp.bfloat16).astype(jnp.float32)
    resid, normed = [], []
    for n in range(count):
        part = tokens_of(*owns[n], 40, 144) + attn[n * 144 : (n + 1) * 144]
        resid.append(part.astype(jnp.bfloat16).astype(jnp.float32))
        normed.append(layer_norm(resid[n], gain2_ref[...]).astype(jnp.bfloat16))
    result, normed = jnp.concatenate(resid, axis=0), jnp.concatenate(normed, axis=0)
    blocks = [slice(f, f + 2 * LANES) for f in range(0, fc1_ref.shape[1], 2 * LANES)]

    def first_product(at):
        return jnp.dot(normed, fc1_ref[:, at], preferred_element_type=jnp.float32)

    hidden = first_product(blocks[0])
    for b, at in enumerate(blocks):
        following = first_product(blocks[b + 1]) if b + 1 < len(blocks) else None
        active = gelu(hidden.astype(jnp.bfloat16))
        result = result + lax.dot_general(
            active, fc2_ref[:, at], NT, preferred_element_type=jnp.float32
        )
        hidden = following
    for n in range(count):
        mine = result[n * 144 : (n + 1) * 144]
        for part, lanes in enumerate((slice(0, LANES), slice(LANES, chans))):
            width = min(LANES, chans - part * LANES)
            res_ref[n, part, 40:184, :width] = mine[:, lanes]
            res_ref[n, part, 0:40, :width] = mine[104:144, lanes]
        for row in range(WIN_LAT):
            for pair in range(HALF // 2):
                tiles = []
                for col in (2 * pair, 2 * pair + 1):
                    at = pl.ds(4 + row * HALF + col, LEVELS, stride=36)
                    tiles += [res_ref[n, part, at, :] for part in range(2)]
                shifted = [pltpu.roll(x, SPARE, 1) for x in tiles[2:]]
                tiles = [tiles[0], jnp.where(low, tiles[1], shifted[0])]
                tiles.append(jnp.where(low, shifted[0], shifted[1]))
                tiles = jnp.concatenate(tiles, axis=1).astype(jnp.bfloat16)
                out_ref[n, row, :, pair * 2 * chans : (pair + 1) * 2 * chans] = tiles
    if extra == "send":
        send_ref[0] = lower_ref[0, EDGE:]
        send_ref[1] = out_ref[0, EDGE:]


def run_units(units, near, far, weights, chans, heads, table, extra=None, *extra_in):
    count = len(units)
    pieces = [x for is_near, w in units for x in (near[w] if is_near else far)]
    piece = pieces[0]
    outs = [jax.ShapeDtypeStruct((count, WIN_LAT) + piece.shape[1:], piece.dtype)]
    operands = (*pieces, *weights, table, *extra_in)
    if extra == "send":
        outs.append(jax.ShapeDtypeStruct((2, EDGE) + piece.shape[1:], piece.dtype))
    elif extra == "ahead":
        outs += [
            jax.ShapeDtypeStruct(table.shape, table.dtype),
            jax.ShapeDtypeStruct((4, 2, LEVELS * QUERIES, LANES), jnp.float32),
            jax.ShapeDtypeStruct((4, 2, 184, LANES), jnp.float32),
            jax.ShapeDtypeStruct((3, 2 * heads * QUERIES, chans), jnp.bfloat16),
        ]
    vmem = pl.BlockSpec(memory_space=pltpu.VMEM)
    return pl.pallas_call(
        functools.partial(units_kernel, chans, heads, units, extra),
        out_shape=outs,
        in_specs=[vmem] * len(operands),
        out_specs=[vmem] * len(outs),
        scratch_shapes=[
            pltpu.VMEM((count + 1, 2, LEVELS * QUERIES, LANES), jnp.float32),
            pltpu.VMEM((count + 1, 2, 184, LANES), jnp.float32),
            pltpu.VMEM((count + 1, 2, 184, LANES), jnp.float32),
        ],
        compiler_params=pltpu.CompilerParams(vmem_limit_bytes=VMEM_BYTES),
        cost_estimate=pl.CostEstimate(
            flops=200_000_000 * count, bytes_accessed=3_000_000, transcendentals=250_000 * count
        ),
        name="swin_windows",
    )(*operands)


def shards(
    field_in, norm1_gain, qkv_weight, proj_weight, earth_bias, norm2_gain, fc1_weight, fc2_weight
):
    levels, rows, flat = field_in.shape
    chans = qkv_weight.shape[0]
    heads = earth_bias.shape[2]
    half = HALF * chans
    field = jnp.transpose(field_in, (1, 0, 2))
    south = moved(field[:EDGE], "lat", -1)
    weights = (
        norm1_gain.reshape(1, chans),
        qkv_weight,
        proj_weight,
        norm2_gain.reshape(1, chans),
        fc1_weight,
        jnp.transpose(fc2_weight),
    )
    vmem = pl.BlockSpec(memory_space=pltpu.VMEM)
    anywhere = pl.BlockSpec(memory_space=pl.ANY)
    piece = jax.ShapeDtypeStruct((rows, levels, half), field.dtype)
    table = jax.ShapeDtypeStruct((2, 2, 2, heads * QUERIES + 24, LANES), jnp.float32)
    windows, zwin, _, entries = earth_bias.shape
    tiles = entries // LANES
    bias = earth_bias.reshape(windows, zwin, heads, tiles, LANES).transpose(0, 2, 3, 1, 4)
    sources = (bias, field) + weights
    raw = jax.ShapeDtypeStruct((bias.size // windows // LANES + 112, LANES), bias.dtype)
    sources = [pltpu.with_memory_space_constraint(x, pltpu.HBM) for x in sources]
    outs = [table, raw, piece, piece] + [jax.ShapeDtypeStruct(x.shape, x.dtype) for x in weights]
    table, inner, near, far, *weights = pl.pallas_call(
        functools.partial(table_kernel, len(weights), heads),
        out_shape=outs,
        in_specs=[pl.BlockSpec(memory_space=pltpu.HBM)] * len(sources),
        out_specs=[vmem] * len(outs),
        scratch_shapes=[
            pltpu.VMEM(raw.shape, raw.dtype),
            pltpu.SemaphoreType.DMA((4 + len(weights),)),
        ],
        compiler_params=pltpu.CompilerParams(vmem_limit_bytes=VMEM_BYTES),
        cost_estimate=pl.CostEstimate(flops=4_000_000, bytes_accessed=6_000_000, transcendentals=0),
        name="bias_tables",
    )(*sources)

    def pack(kernel, outs, *operands):
        return pl.pallas_call(
            kernel,
            out_shape=outs,
            in_specs=[vmem] * 2 + [anywhere] * (len(operands) - 2),
            out_specs=[vmem] * len(outs),
            compiler_params=pltpu.CompilerParams(vmem_limit_bytes=VMEM_BYTES),
            cost_estimate=pl.CostEstimate(flops=0, bytes_accessed=250_000, transcendentals=0),
            name="pack_half",
        )(*operands)

    (far,) = pack(pack_far_kernel, [piece], south, far)
    far_halo = swapped(far, "lon", 1)
    window = jax.ShapeDtypeStruct((WIN_LAT, levels, half), field.dtype)
    near_parts = pack(pack_near_kernel, [window, window], south, near, far)
    low, high = ((part, swapped(part, "lon", 0)) for part in near_parts)
    near, far = (high, low), (far, far_halo)
    common = (near, far, weights, chans, heads)
    near_low, inner, *ahead = run_units(
        ((True, 1),), *common, table, "ahead", inner, far[0], high[0]
    )
    far_low, send = run_units(((False, 1),), *common, table, "send", *ahead, near_low)
    top = moved(send, "lat", 1)
    (high,) = run_units(((True, 0), (False, 0)), *common, inner, None, *ahead)
    done = pl.pallas_call(
        last_kernel,
        out_shape=jax.ShapeDtypeStruct(field.shape, field.dtype),
        in_specs=[vmem] * 4,
        out_specs=anywhere,
        scratch_shapes=[pltpu.SemaphoreType.DMA((6,))],
        compiler_params=pltpu.CompilerParams(vmem_limit_bytes=VMEM_BYTES),
        cost_estimate=pl.CostEstimate(flops=0, bytes_accessed=400_000, transcendentals=0),
        name="last_rows",
    )(top, high, near_low, far_low)
    return jnp.transpose(done, (1, 0, 2))


def solution(mesh):
    in_specs = (P(None, "lat", "lon"), P(), P(), P(), P("lat", None, None, None), P(), P(), P())
    out_specs = P(None, "lat", "lon")
    return jax.shard_map(shards, mesh=mesh, in_specs=in_specs, out_specs=out_specs, check_vma=False)
```
